32 devices in a mesh: tensor: 8 (over y, x, core), dp: 4 (over z).
Axes of the slice: x: 2, y: 2, z: 4, core: 2. Of those that a mesh axis runs over, the one named last changes fastest.
Arguments:
- tokens: bfloat16 [6144, 6144], P('dp', 'tensor'), may hold values from -9 to 9
- expert_ids: int32 [6144, 2], P('dp'), may hold values from 0 to 7, as said below
- gate_probs: float32 [6144, 2], P('dp'), may hold values from 0.2 to 1
- gate_weight: bfloat16 [6144, 8192], P(None, 'tensor'), may hold values from -0.078125 to 0.078125
- up_weight: bfloat16 [6144, 8192], P(None, 'tensor'), may hold values from -0.078125 to 0.078125
- down_weight: bfloat16 [8192, 6144], P('tensor'), may hold values from -0.09375 to 0.09375
Outputs:
- expert_out: bfloat16 [6144, 6144], P('dp', 'tensor')
- peaks: float32 [2], replicated
The draws below stay inside these ranges and needn't reach their ends.
Inputs may be any that keep to these rules, and one draw needn't show every extreme that they name: `expert_ids`: each row names two different experts. In each aligned block of 1536 rows at most 768 rows name expert 0, and in some block exactly 768 do.
All inputs are finite; a program needn't handle non-finite values.
Results may differ from the reference program's by a relative error of at most 0.02.
Values may be sent and summed in bfloat16 or wider, within the bound.
No kernel may reach another device: no remote copies, remote signals or barrier semaphores. Data moves between devices by JAX's collectives and lax.ppermute only.
A program may use at most 128 MiB of HBM per device.

```python
import math
import jax
import jax.numpy as jnp
from jax import lax

D = 6144
EXPERTS = 8
FF_WIN = 8192
TOP = 2
TOK_DEV = 1536
CAP = 768
TOKENS = 6144
N_TENSOR = 8


def draw_tokens(key, part):
    subkeys = jax.random.split(key, 2)
    place_in = jnp.arange(TOKENS, dtype=jnp.float32) / max(TOKENS - 1, 1)
    row_rise = 3.0 ** place_in
    roughness = jax.random.uniform(subkeys[0], (TOKENS,), jnp.float32, 0.5, 1.5)
    base_draw = jnp.clip(0.5 * jax.random.normal(subkeys[1], (TOKENS, D), jnp.float32), -2.0, 2.0)
    return (base_draw * (row_rise * roughness)[:, None]).astype(jnp.bfloat16)


def draw_expert_ids(key, part):
    blocks = TOKENS // TOK_DEV
    subkeys = jax.random.split(jax.random.fold_in(key, 17), 6)
    counts = jax.random.randint(subkeys[0], (blocks,), CAP // 2, CAP + 1)
    fullest = jax.random.randint(subkeys[1], (), 0, blocks)
    counts = jnp.where(jnp.arange(blocks) == fullest, CAP, counts)
    orders = jax.vmap(lambda sub_key: jax.random.permutation(sub_key, TOK_DEV))(jax.random.split(subkeys[2], blocks))
    rank_of = jnp.argsort(orders, axis=1, stable=True)
    chosen = (rank_of < counts[:, None]).reshape(TOKENS)
    first_pick = jax.random.randint(subkeys[3], (TOKENS,), 1, EXPERTS)
    second = 1 + (first_pick - 1 + jax.random.randint(subkeys[4], (TOKENS,), 1, EXPERTS - 1)) % (EXPERTS - 1)
    second = jnp.where(chosen, 0, second)
    swapped = jax.random.randint(subkeys[5], (TOKENS,), 0, 2) == 1
    column_a = jnp.where(swapped, second, first_pick)
    column_b = jnp.where(swapped, first_pick, second)
    return jnp.stack([column_a, column_b], axis=1).astype(jnp.int32)


def raised(result, stream_key, source, target, blocks, factor):
    owner, partner = [(jnp.arange(result.shape[dim]) // (result.shape[dim] // blocks)).reshape([-1 if axis == dim else 1 for axis in range(result.ndim)]) for dim in (source, target)]
    chosen = jax.random.permutation(stream_key, blocks)[partner]
    strong = (owner == chosen) | (owner == (partner + blocks // 2) % blocks)
    return jnp.where(strong, factor * result, result)


def block_levels(stream_key, shape, cuts, low, largest):
    factor_of, own = 1.0, jax.random.fold_in(stream_key, 6)
    for axis_at, shards_of in cuts:
        steps = jnp.exp(jax.random.uniform(jax.random.fold_in(own, axis_at), (shards_of,), jnp.float32, low / len(cuts), largest / len(cuts)))
        factor_of = factor_of * jnp.repeat(steps, shape[axis_at] // shards_of).reshape([-1 if axis == axis_at else 1 for axis in range(len(shape))])
    return factor_of


def gaussian(own_key, shape, spread, limit, pieces=(), held_as=jnp.bfloat16):
    array = spread * jax.random.normal(own_key, shape, jnp.float32)
    if pieces:
        array = array * block_levels(own_key, shape, pieces, -0.22, 0.18)
    return jnp.clip(array, -limit, limit).astype(held_as)


def noise_with(rng, dims, width, limit, shards, heavy, kind=jnp.bfloat16):
    result = width * jax.random.normal(rng, dims, jnp.float32)
    if shards:
        result = result * block_levels(rng, dims, shards, -0.22, 0.18)
    return jnp.clip(raised(result, jax.random.fold_in(rng, 3), *heavy), -limit, limit).astype(kind)


def setup_inputs(seed: int = 0) -> dict:
    streams_of = jax.random.split(jax.random.key(seed), 7)
    tokens = draw_tokens(jax.random.fold_in(streams_of[6], 71), 0)
    expert_ids = draw_expert_ids(jax.random.fold_in(streams_of[6], 71), 0)
    gate_probs = jnp.clip(0.2 + 0.8 * jax.random.uniform(streams_of[2], (TOKENS, TOP), jnp.float32) ** block_levels(streams_of[2], (TOKENS, TOP), ((0, 4),), -0.2, 0.2), 0.2, 1.0)
    gate_weight = gaussian(streams_of[3], (D, FF_WIN), D ** -0.5, 0.078125, ((1, 8),))
    up_weight = gaussian(streams_of[4], (D, FF_WIN), D ** -0.5, 0.078125, ((1, 8),))
    down_weight = noise_with(streams_of[5], (FF_WIN, D), FF_WIN ** -0.5, 0.09375, ((0, 8),), (0, 1, 8, 2.0))
    return {"tokens": tokens, "expert_ids": expert_ids, "gate_probs": gate_probs, "gate_weight": gate_weight, "up_weight": up_weight, "down_weight": down_weight}


clip_share = 0.25

def sylvester(order_size):
    index_row = jnp.arange(order_size, dtype=jnp.int32)
    common = index_row[:, None] & index_row[None, :]
    parity = jnp.zeros((order_size, order_size), jnp.int32)
    for bit_pos in range(order_size.bit_length() - 1):
        parity = parity ^ common >> bit_pos & 1
    return (1 - 2 * parity).astype(jnp.float32)

def routing(expert_ids, gate_probs, capacity):
    hits = expert_ids == 0
    routed = jnp.any(hits, axis=1)
    share_of = lax.optimization_barrier(jnp.sum(jnp.where(hits, gate_probs, 0.0), axis=1))
    position = (jnp.cumsum(routed.astype(jnp.int32)) - 1).astype(jnp.int32)
    routed_count = jnp.sum(routed.astype(jnp.int32)).astype(jnp.int32)
    target_slot = jnp.where(routed, position, capacity).astype(jnp.int32)
    row_numbers = jnp.arange(expert_ids.shape[0], dtype=jnp.int32)
    source = jnp.zeros((capacity,), jnp.int32).at[target_slot].set(row_numbers, mode='drop')
    filled = jnp.arange(capacity, dtype=jnp.int32) < routed_count
    slot_of_row = jnp.clip(position, 0, capacity - 1).astype(jnp.int32)
    return (routed, share_of, source, filled, slot_of_row)

def rotate(hidden):
    bits = FF_WIN.bit_length() - 1
    outer_size = 2 ** (bits // 2)
    inner_size = FF_WIN // outer_size
    grid = hidden.astype(jnp.float32).reshape(hidden.shape[0], outer_size, inner_size)
    first_pass = jnp.einsum('rab,bd->rad', grid, sylvester(inner_size), precision=lax.Precision.HIGHEST)
    second_pass = jnp.einsum('rad,ac->rcd', first_pass, sylvester(outer_size), precision=lax.Precision.HIGHEST)
    return second_pass.reshape(hidden.shape[0], FF_WIN) * (1.0 / math.sqrt(FF_WIN))

def reference(tokens, expert_ids, gate_probs, gate_weight, up_weight, down_weight):
    blocks = TOKENS // TOK_DEV
    routes = []
    rotations = []
    input_peaks = []
    for block_idx in range(blocks):
        lower = block_idx * TOK_DEV
        token_block = tokens[lower:lower + TOK_DEV]
        info = routing(expert_ids[lower:lower + TOK_DEV], gate_probs[lower:lower + TOK_DEV], CAP)
        routes.append(info)
        picked = jnp.where(info[3][:, None], token_block[info[2]], jnp.zeros((), tokens.dtype))
        input_peaks.append(jnp.max(jnp.abs(picked)).astype(jnp.float32))
        gate_part = jnp.dot(picked, gate_weight, preferred_element_type=jnp.float32)
        up_part = jnp.dot(picked, up_weight, preferred_element_type=jnp.float32)
        hidden = (jax.nn.silu(gate_part) * up_part).astype(jnp.bfloat16)
        rotations.append(rotate(hidden))
    peak_in = jnp.max(jnp.stack(input_peaks))
    peak_rot = jnp.max(jnp.stack([jnp.max(jnp.abs(item)) for item in rotations]))
    clip_level = clip_share * peak_rot
    group_width = FF_WIN // N_TENSOR
    outputs = []
    for block_idx in range(blocks):
        routed, share_of, source, filled, slot_of_row = routes[block_idx]
        clipped = jnp.clip(rotations[block_idx], -clip_level, clip_level).astype(jnp.bfloat16)
        summed = jnp.zeros((CAP, D), jnp.float32)
        for group in range(N_TENSOR):
            lower = group * group_width
            term = jnp.dot(clipped[:, lower:lower + group_width], down_weight[lower:lower + group_width], preferred_element_type=jnp.float32)
            rounded = lax.optimization_barrier(term.astype(jnp.bfloat16))
            summed = summed + rounded.astype(jnp.float32)
        block_out = jnp.where(routed[:, None], share_of[:, None] * summed[slot_of_row], 0.0)
        outputs.append(block_out.astype(jnp.bfloat16))
    return (jnp.concatenate(outputs, axis=0), jnp.stack([peak_in, peak_rot]))
```

```python
import math

import jax
import jax.numpy as jnp
from jax import lax
from jax.experimental import pallas as pl
from jax.experimental.pallas import tpu as pltpu
from jax.sharding import PartitionSpec as P

CAP = 768
CLIP_SHARE = 0.25
LANES = 128
ROW_CHUNKS = 2
FEATURE_CHUNKS = 3
BF16 = jnp.bfloat16
F32 = jnp.float32
MIB = 1 << 20


def params(mib):
    return pltpu.CompilerParams(vmem_limit_bytes=mib * MIB)


def cost(flops, moved):
    return pl.CostEstimate(flops=int(flops), bytes_accessed=int(moved), transcendentals=0)


def across(block, bit):
    count = lax.axis_size("tensor")
    return lax.ppermute(block, "tensor", [(r, r ^ 1 << bit) for r in range(count)])


def iota(shape, dim):
    return lax.broadcasted_iota(jnp.int32, shape, dim)


def slots_of(ids_ref):
    tokens = ids_ref.shape[1]
    rows = tokens // LANES
    padded = (rows + 15) // 16 * 16
    hit = jnp.where((ids_ref[0:1, :] == 0) | (ids_ref[1:2, :] == 0), 1.0, 0.0)
    grid = jnp.concatenate(
        [hit[:, LANES * k : LANES * (k + 1)] for k in range(rows)]
        + [jnp.zeros((padded - rows, LANES), F32)],
        axis=0,
    )
    flat = grid.astype(BF16)
    upto = (iota((LANES, LANES), 0) <= iota((LANES, LANES), 1)).astype(F32).astype(BF16)
    before = (iota((padded, padded), 1) < iota((padded, padded), 0)).astype(F32).astype(BF16)
    within = jnp.dot(flat, upto, preferred_element_type=F32)
    offset = jnp.sum(jnp.dot(before, flat, preferred_element_type=F32), axis=1, keepdims=True)
    return jnp.where(grid > 0.0, within + offset - 1.0, -1.0)


def pick_body(first, ids_ref, tokens_ref, picked_ref, peak_ref):
    rows = picked_ref.shape[0]
    slots = slots_of(ids_ref).astype(jnp.int32)
    wanted = iota((rows, LANES), 0) + first
    hot = jnp.concatenate(
        [
            jnp.where(wanted == slots[k : k + 1, :], 1.0, 0.0).astype(BF16)
            for k in range(ids_ref.shape[1] // LANES)
        ],
        axis=1,
    )
    picked = jnp.dot(hot, tokens_ref[...], preferred_element_type=F32)
    picked_ref[...] = picked.astype(BF16)
    peak_ref[...] = jnp.broadcast_to(jnp.max(jnp.abs(picked)), peak_ref.shape)


def pick_rows(ids, tokens, first, rows):
    count, width = tokens.shape
    return pl.pallas_call(
        lambda *refs: pick_body(first, *refs),
        out_shape=(
            jax.ShapeDtypeStruct((rows, width), BF16),
            jax.ShapeDtypeStruct((8, LANES), F32),
        ),
        compiler_params=params(32),
        cost_estimate=cost(2 * rows * count * width, 2 * count * width),
        name="pick_rows",
    )(ids, tokens)


def signs(size):
    common = iota((size, size), 0) & iota((size, size), 1)
    shift = 1
    while shift < size.bit_length():
        shift *= 2
    while shift > 1:
        shift //= 2
        common = common ^ (common >> shift)
    return (1 - 2 * (common & 1)).astype(F32).astype(BF16)


def expand_body(layout, me_ref, *refs):
    parts = refs[: len(layout)]
    gate_ref, up_ref, out_ref, rows_ref, turned, table, arrived = refs[len(layout) :]
    step = pl.program_id(0)
    steps = turned.shape[0]
    tile = gate_ref.shape[1]

    @pl.when(step == 0)
    def _():
        copies = []
        for index, (part, (mask, low)) in enumerate(zip(parts, layout)):
            rows, width = part.shape
            at = pl.multiple_of((me_ref[0] ^ mask) * width, LANES)
            copies.append(
                pltpu.make_async_copy(
                    part, rows_ref.at[pl.ds(low, rows), pl.ds(at, width)], arrived.at[index]
                )
            )
        for copy in copies:
            copy.start()
        table[...] = signs(tile)
        for copy in copies:
            copy.wait()

    block = rows_ref[...]
    gate = jnp.dot(block, gate_ref[...], preferred_element_type=F32)
    up = jnp.dot(block, up_ref[...], preferred_element_type=F32)
    hidden = (gate * (1.0 / (1.0 + jnp.exp(-gate))) * up).astype(BF16)
    turned[step] = jnp.dot(hidden, table[...], preferred_element_type=F32)

    @pl.when(step == steps - 1)
    def _():
        values = [turned[i] for i in range(steps)]
        gap = 1
        while gap < steps:
            values = [
                values[i] + values[i ^ gap] if not i & gap else values[i ^ gap] - values[i]
                for i in range(steps)
            ]
            gap *= 2
        for i in range(steps):
            out_ref[:, i * tile : (i + 1) * tile] = values[i].astype(BF16)


def expand(parts, layout, rows, me, gate_weight, up_weight):
    depth, width = gate_weight.shape
    tile = 256
    steps = width // tile
    return pl.pallas_call(
        lambda *refs: expand_body(layout, *refs),
        grid_spec=pltpu.PrefetchScalarGridSpec(
            num_scalar_prefetch=1,
            grid=(steps,),
            in_specs=[pl.BlockSpec(memory_space=pl.ANY)] * len(parts)
            + [pl.BlockSpec((depth, tile), lambda i, me: (0, i))] * 2,
            out_specs=pl.BlockSpec((rows, width), lambda i, me: (0, 0)),
            scratch_shapes=[
                pltpu.VMEM((rows, depth), BF16),
                pltpu.VMEM((steps, rows, tile), F32),
                pltpu.VMEM((tile, tile), BF16),
                pltpu.SemaphoreType.DMA((len(parts),)),
            ],
        ),
        out_shape=jax.ShapeDtypeStruct((rows, width), BF16),
        compiler_params=params(48),
        cost_estimate=cost(4 * rows * depth * width, 4 * depth * width),
        name="expand",
    )(me, *parts, gate_weight, up_weight)


def clip_into(held, level_ref, rotated):
    level = level_ref[0]
    low = 0
    for part in rotated:
        rows = part.shape[0]
        held[low : low + rows, :] = jnp.clip(part[...].astype(F32), -level, level).astype(BF16)
        low += rows


def down_send_body(count, me_ref, level_ref, *refs):
    rotated, (weight_ref, out_ref, held) = refs[:count], refs[count:]

    @pl.when(pl.program_id(0) == 0)
    def _():
        clip_into(held, level_ref, rotated)

    out_ref[0] = jnp.dot(held[...], weight_ref[...], preferred_element_type=F32).astype(BF16)


def down_keep_body(count, places, me_ref, level_ref, *refs):
    rotated, (weight_ref, came_ref) = refs[:count], refs[count : count + 2]
    outs, held = refs[count + 2 : -1], refs[-1]
    step = pl.program_id(0)

    @pl.when(step == 0)
    def _():
        clip_into(held, level_ref, rotated)

    total = jnp.dot(held[...], weight_ref[...], preferred_element_type=F32)
    total = (total + came_ref[0].astype(F32)).astype(BF16)
    half = total.shape[0] // 2
    for at, where in enumerate(places):

        @pl.when(step == at)
        def _(where=where):
            for h, (out, slot) in enumerate(where):
                outs[out][slot] = total[h * half : (h + 1) * half, :]


def down(rotated, weight, me, level, chunk, masks, came=None, places=None):
    depth = weight.shape[0]
    features = weight.shape[1] // lax.axis_size("tensor")
    rows = sum(part.shape[0] for part in rotated)
    fc = features // FEATURE_CHUNKS
    steps = len(masks)
    count = len(rotated)
    by_step = masks[0]
    in_specs = [
        pl.BlockSpec(part.shape, lambda i, me, level: (0, 0)) for part in rotated
    ] + [
        pl.BlockSpec(
            (depth, fc),
            lambda i, me, level: (0, (me[0] ^ (2 * i + by_step)) * FEATURE_CHUNKS + chunk),
        )
    ]
    args = [me, level, *rotated, weight]
    block = pl.BlockSpec((1, rows, fc), lambda i, me, level: (i, 0, 0))
    if came is None:
        body = lambda *refs: down_send_body(count, *refs)
        out_specs = block
        out_shape = jax.ShapeDtypeStruct((steps, rows, fc), BF16)
    else:
        body = lambda *refs: down_keep_body(count, places, *refs)
        in_specs.append(block)
        args.append(came)
        half = (max(1, steps // 2), rows // 2, fc)
        out_specs = [pl.BlockSpec(half, lambda i, me, level: (0, 0, 0))] * 4
        out_shape = [jax.ShapeDtypeStruct(half, BF16)] * 4
    return pl.pallas_call(
        body,
        grid_spec=pltpu.PrefetchScalarGridSpec(
            num_scalar_prefetch=2,
            grid=(steps,),
            in_specs=in_specs,
            out_specs=out_specs,
            scratch_shapes=[pltpu.VMEM((rows, depth), BF16)],
        ),
        out_shape=out_shape,
        compiler_params=params(40),
        cost_estimate=cost(2 * steps * rows * depth * fc, 2 * steps * depth * fc),
        name="down_send" if came is None else "down_keep",
    )(*args)


def spread_body(count, ids_ref, probs_ref, *refs):
    mine, theirs = refs[:count], refs[count : 2 * count]
    out_ref = refs[-1]
    tokens = ids_ref.shape[1]
    summed = jnp.concatenate(
        [(a[0].astype(F32) + b[0].astype(F32)).astype(BF16) for a, b in zip(mine, theirs)], axis=0
    )
    slots = slots_of(ids_ref)
    share = jnp.where(ids_ref[0:1, :] == 0, probs_ref[0:1, :], 0.0) + jnp.where(
        ids_ref[1:2, :] == 0, probs_ref[1:2, :], 0.0
    )
    blocks = tokens // LANES
    share = jnp.concatenate(
        [share[:, LANES * k : LANES * (k + 1)] for k in range(blocks)]
        + [jnp.zeros((LANES - blocks, LANES), F32)],
        axis=0,
    ).T
    slots = jnp.concatenate(
        [slots, jnp.zeros((LANES - slots.shape[0], LANES), F32)], axis=0
    ).T.astype(jnp.int32)
    at = iota((LANES, summed.shape[0]), 1)
    for k in range(blocks):
        hot = jnp.where(at == slots[:, k : k + 1], 1.0, 0.0).astype(BF16)
        rows = jnp.dot(hot, summed, preferred_element_type=F32)
        out_ref[LANES * k : LANES * (k + 1), :] = (rows * share[:, k : k + 1]).astype(BF16)


def spread(ids, probs, mine, theirs, chunk, out):
    tokens = ids.shape[1]
    count = len(mine)
    _, rows, fc = mine[0].shape
    whole = lambda x: pl.BlockSpec(x.shape, lambda i: (0,) * x.ndim)
    args = [ids, probs, *mine, *theirs]
    in_specs = [whole(x) for x in args]
    aliases = {}
    if out is not None:
        aliases = {len(args): 0}
        args.append(out)
        in_specs.append(pl.BlockSpec(memory_space=pl.ANY))
    return pl.pallas_call(
        lambda *refs: spread_body(count, *refs[: 2 + 2 * count], refs[-1]),
        grid=(1,),
        in_specs=in_specs,
        out_specs=pl.BlockSpec((tokens, fc), lambda i: (0, chunk)),
        out_shape=jax.ShapeDtypeStruct((tokens, fc * FEATURE_CHUNKS), BF16),
        input_output_aliases=aliases,
        compiler_params=params(40),
        cost_estimate=cost(2 * tokens * rows * count * fc, 2 * tokens * fc),
        name="spread",
    )(*args)


def gather_rows(own, orders):
    rows = own.shape[0]
    half = rows // len(orders)
    full = {0: own}
    part = {}

    def get(mask, h):
        if (mask, h) in part:
            return part[mask, h]
        return full[mask][h * half : (h + 1) * half]

    for bit in orders[0]:
        full[1 << bit] = across(own, bit)
    have = [[0, 1 << order[0]] for order in orders]
    for at in range(1, len(orders[0])):
        for h, order in enumerate(orders):
            bit = order[at]
            for mask in list(have[h]):
                there = mask | 1 << bit
                if there not in full:
                    part[there, h] = across(get(mask, h), bit)
                have[h].append(there)
    pieces = {(mask, 0): block for mask, block in full.items()}
    pieces |= {(mask, h * half): block for (mask, h), block in part.items()}
    return pieces


def butterfly(own, came, bit, me):
    flip = (1 - 2 * (me >> bit & 1)).astype(F32)
    return came.astype(F32) + own.astype(F32) * flip


def largest(values):
    count = lax.axis_size("tensor")
    bits = count.bit_length() - 1
    for low in range(0, bits, 2):
        top = min(bits, low + 2)
        others = [
            lax.ppermute(values, "tensor", [(r, r ^ m << low) for r in range(count)])
            for m in range(1, 1 << (top - low))
        ]
        for other in others:
            values = jnp.maximum(values, other)
    blocks = lax.axis_size("dp")
    others = [
        lax.ppermute(values, "dp", [(r, (r + s) % blocks) for r in range(blocks)])
        for s in range(1, blocks)
    ]
    for other in others:
        values = jnp.maximum(values, other)
    return values


def on_device(tokens, expert_ids, gate_probs, gate_weight, up_weight, down_weight):
    count = lax.axis_size("tensor")
    bits = count.bit_length() - 1
    outer = list(range(1, bits))
    orders = [outer, outer[::-1]]
    me = lax.axis_index("tensor")
    me_arr = me.astype(jnp.int32).reshape(1)
    ids, probs = expert_ids.T, gate_probs.T
    rows = CAP // ROW_CHUNKS
    half = rows // 2
    scale = 1.0 / math.sqrt(gate_weight.shape[1] * count)

    peak_in = None
    rotated, tops = [], []
    for chunk in range(ROW_CHUNKS):
        own, top = pick_rows(ids, tokens, chunk * rows, rows)
        peak_in = top if peak_in is None else jnp.maximum(peak_in, top)
        pieces = gather_rows(own, orders)
        pieces |= {(mask | 1, low): across(block, 0) for (mask, low), block in pieces.items()}
        layout = sorted(pieces)
        local = expand([pieces[key] for key in layout], layout, rows, me_arr, gate_weight, up_weight)
        paired = butterfly(local, across(local, 0), 0, me).astype(BF16)
        done = []
        for h, order in enumerate(orders):
            block = paired[h * half : (h + 1) * half]
            for bit in order:
                block = butterfly(block, across(block.astype(BF16), bit), bit, me)
                if bit != order[-1]:
                    block = block.astype(BF16)
            block = block * scale
            tops.append(jnp.max(jnp.abs(block)))
            rotated.append(block.astype(BF16))

    peak_rot = tops[0]
    for top in tops[1:]:
        peak_rot = jnp.maximum(peak_rot, top)
    rot_rows = jnp.broadcast_to(peak_rot, (4, LANES))
    peaks = largest(jnp.concatenate([peak_in[:4], rot_rows], axis=0))
    level = (CLIP_SHARE * peaks[4, :1]).reshape(1)

    sent = [2 * i + 1 for i in range(count // 2)]
    kept = [2 * i for i in range(count // 2)]
    places = []
    for mask in kept:
        where = []
        for h, order in enumerate(orders):
            first = 1 << order[0]
            rest = [m for m in kept if not m & first]
            where.append((2 * h + (1 if mask & first else 0), rest.index(mask & ~first)))
        places.append(where)

    out = None
    for chunk in range(FEATURE_CHUNKS):
        away = down(rotated, down_weight, me_arr, level, chunk, sent)
        came = across(away, 0)
        halves = down(rotated, down_weight, me_arr, level, chunk, kept, came, places)
        mine, theirs = [], []
        for h, order in enumerate(orders):
            keep, send = halves[2 * h], halves[2 * h + 1]
            masks = [m for m in kept if not m & 1 << order[0]]
            for at, bit in enumerate(order):
                recv = across(send, bit)
                if at == len(order) - 1:
                    mine.append(keep)
                    theirs.append(recv)
                    break
                total = (keep.astype(F32) + recv.astype(F32)).astype(BF16)
                after = 1 << order[at + 1]
                keep = jnp.stack([total[i] for i, m in enumerate(masks) if not m & after])
                send = jnp.stack([total[i] for i, m in enumerate(masks) if m & after])
                masks = [m for m in masks if not m & after]
        out = spread(ids, probs, mine, theirs, chunk, out)
    return out, jnp.stack([peaks[0, 0], peaks[4, 0]])


def solution(mesh):
    in_specs = (
        P("dp", "tensor"),
        P("dp", None),
        P("dp", None),
        P(None, "tensor"),
        P(None, "tensor"),
        P("tensor", None),
    )
    out_specs = (P("dp", "tensor"), P())
    return jax.shard_map(
        on_device, mesh=mesh, in_specs=in_specs, out_specs=out_specs, check_vma=False
    )
```

```python
import math

import jax
import jax.numpy as jnp
from jax import lax
from jax.experimental import pallas as pl
from jax.experimental.pallas import tpu as pltpu
from jax.sharding import PartitionSpec as P

CAP = 768
CLIP_SHARE = 0.25
LANES = 128
ROW_CHUNKS = 2
FEATURE_CHUNKS = 3
BF16 = jnp.bfloat16
F32 = jnp.float32
MIB = 1 << 20
EXPAND_MIB = 36


def params(mib):
    return pltpu.CompilerParams(vmem_limit_bytes=mib * MIB)


def cost(flops, moved):
    return pl.CostEstimate(flops=int(flops), bytes_accessed=int(moved), transcendentals=0)


def across(block, bit):
    count = lax.axis_size("tensor")
    return lax.ppermute(block, "tensor", [(r, r ^ 1 << bit) for r in range(count)])


def iota(shape, dim):
    return lax.broadcasted_iota(jnp.int32, shape, dim)


def slots_of(ids_ref):
    tokens = ids_ref.shape[1]
    rows = tokens // LANES
    padded = (rows + 15) // 16 * 16
    hit = jnp.where((ids_ref[0:1, :] == 0) | (ids_ref[1:2, :] == 0), 1.0, 0.0)
    grid = jnp.concatenate(
        [hit[:, LANES * k : LANES * (k + 1)] for k in range(rows)]
        + [jnp.zeros((padded - rows, LANES), F32)],
        axis=0,
    )
    flat = grid.astype(BF16)
    upto = (iota((LANES, LANES), 0) <= iota((LANES, LANES), 1)).astype(F32).astype(BF16)
    before = (iota((padded, padded), 1) < iota((padded, padded), 0)).astype(F32).astype(BF16)
    within = jnp.dot(flat, upto, preferred_element_type=F32)
    offset = jnp.sum(jnp.dot(before, flat, preferred_element_type=F32), axis=1, keepdims=True)
    return jnp.where(grid > 0.0, within + offset - 1.0, -1.0)


def pick_body(first, ids_ref, tokens_ref, *refs):
    picked_ref, peak_ref = refs[-2:]
    rows = picked_ref.shape[0]
    slots = slots_of(ids_ref).astype(jnp.int32)
    wanted = iota((rows, LANES), 0) + first
    hot = jnp.concatenate(
        [
            jnp.where(wanted == slots[k : k + 1, :], 1.0, 0.0).astype(BF16)
            for k in range(ids_ref.shape[1] // LANES)
        ],
        axis=1,
    )
    picked = jnp.dot(hot, tokens_ref[...], preferred_element_type=F32)
    picked_ref[...] = picked.astype(BF16)
    peak_ref[...] = jnp.broadcast_to(jnp.max(jnp.abs(picked)), peak_ref.shape)


def pick_rows(ids, tokens, first, rows, follow=()):
    count, width = tokens.shape
    return pl.pallas_call(
        lambda *refs: pick_body(first, *refs),
        out_shape=(
            jax.ShapeDtypeStruct((rows, width), BF16),
            jax.ShapeDtypeStruct((8, LANES), F32),
        ),
        in_specs=[pl.BlockSpec(memory_space=pltpu.VMEM)] * 2
        + [pl.BlockSpec(memory_space=pl.ANY)] * len(follow),
        compiler_params=params(16),
        cost_estimate=cost(2 * rows * count * width, 2 * count * width),
        name="pick_rows",
    )(ids, tokens, *follow)


def signs(size):
    common = iota((size, size), 0) & iota((size, size), 1)
    shift = 1
    while shift < size.bit_length():
        shift *= 2
    while shift > 1:
        shift //= 2
        common = common ^ (common >> shift)
    return (1 - 2 * (common & 1)).astype(F32).astype(BF16)


def gather_parts(parts, layout, me_ref, rows_ref, arrived):
    copies = []
    for index, (part, mask) in enumerate(zip(parts, layout)):
        width = part.shape[1]
        at = pl.multiple_of((me_ref[0] ^ mask) * width, LANES)
        copies.append(
            pltpu.make_async_copy(part, rows_ref.at[:, pl.ds(at, width)], arrived.at[index])
        )
    return copies


def expand_body(layout, first, last, me_ref, *refs):
    parts, refs = refs[: len(layout)], refs[len(layout) :]
    before_ref = None
    if last:
        before_ref, refs = refs[0], refs[1:]
    gate_hbm, up_hbm, *outs, rows_ref, gate_ref, up_ref, arrived, loaded = refs
    count, _, tile = gate_ref.shape
    copies = gather_parts(parts, layout, me_ref, rows_ref, arrived)
    loads = []
    for i in range(count):
        columns = pl.ds((first + i) * tile, tile)
        for at, (hbm, held) in enumerate(((gate_hbm, gate_ref), (up_hbm, up_ref))):
            loads.append(
                pltpu.make_async_copy(hbm.at[:, columns], held.at[i], loaded.at[2 * i + at])
            )
    for copy in copies + loads:
        copy.start()
    table = signs(tile)
    for copy in copies:
        copy.wait()
    values = []
    for i in range(count):
        loads[2 * i].wait()
        gate = jnp.dot(rows_ref[...], gate_ref[i], preferred_element_type=F32)
        loads[2 * i + 1].wait()
        up = jnp.dot(rows_ref[...], up_ref[i], preferred_element_type=F32)
        hidden = (gate * (1.0 / (1.0 + jnp.exp(-gate))) * up).astype(BF16)
        values.append(jnp.dot(hidden, table, preferred_element_type=F32))
        if not last:
            outs[0][i] = values[i]
    if not last:
        return
    values = [before_ref[i] for i in range(first)] + values
    steps = len(values)
    gap = 1
    while gap < steps:
        values = [
            values[i] + values[i ^ gap] if not i & gap else values[i ^ gap] - values[i]
            for i in range(steps)
        ]
        gap *= 2
    for i in range(steps):
        low = 0
        for out in outs:
            rows = out.shape[0]
            out[:, i * tile : (i + 1) * tile] = values[i][low : low + rows].astype(BF16)
            low += rows


def expand(parts, layout, rows, me, gate_weight, up_weight, before=None, follow=()):
    depth, width = gate_weight.shape
    tile = 256
    steps = width // tile
    last = before is not None
    first = steps // 2 if last else 0
    mine = steps - first if last else steps // 2
    spaces = [pltpu.SMEM] + [pl.ANY] * len(parts) + [pltpu.VMEM] * last + [pltpu.HBM] * 2
    args = [me, *parts] + ([before] if last else []) + [gate_weight, up_weight]
    if last:
        out_shape = [jax.ShapeDtypeStruct((rows // 2, width), BF16)] * 2
    else:
        out_shape = [jax.ShapeDtypeStruct((mine, rows, tile), F32)]
    used = len(args)
    return pl.pallas_call(
        lambda *refs: expand_body(
            layout, first, last, *refs[:used], *refs[used + len(follow) :]
        ),
        in_specs=[pl.BlockSpec(memory_space=space) for space in spaces]
        + [pl.BlockSpec(memory_space=pl.ANY)] * len(follow),
        out_specs=[pl.BlockSpec(memory_space=pltpu.VMEM)] * len(out_shape),
        out_shape=out_shape,
        scratch_shapes=[
            pltpu.VMEM((rows, depth), BF16),
            pltpu.VMEM((mine, depth, tile), BF16),
            pltpu.VMEM((mine, depth, tile), BF16),
            pltpu.SemaphoreType.DMA((len(parts),)),
            pltpu.SemaphoreType.DMA((2 * mine,)),
        ],
        compiler_params=params(EXPAND_MIB),
        cost_estimate=cost(8 * rows * depth * tile * mine, 4 * depth * tile * mine),
        name="expand_last" if last else "expand_first",
    )(*args, *follow)


def down_body(count, me_ref, *refs):
    rotated, (peaks_ref, weight_ref), (out_ref, held) = refs[:count], refs[count : count + 2], refs[-2:]

    @pl.when(pl.program_id(0) == 0)
    def _():
        level = CLIP_SHARE * jnp.max(peaks_ref[8:, :])
        low = 0
        for part in rotated:
            rows = part.shape[0]
            held[low : low + rows, :] = jnp.clip(part[...].astype(F32), -level, level).astype(BF16)
            low += rows

    out_ref[0] = jnp.dot(held[...], weight_ref[...], preferred_element_type=F32).astype(BF16)


def down(rotated, peaks, weight, me, chunk, odd, follow=()):
    depth = weight.shape[0]
    owners = lax.axis_size("tensor")
    steps = owners // 2
    rows = sum(part.shape[0] for part in rotated)
    fc = weight.shape[1] // owners // FEATURE_CHUNKS
    count = len(rotated)
    return pl.pallas_call(
        lambda *refs: down_body(count, *refs),
        grid_spec=pltpu.PrefetchScalarGridSpec(
            num_scalar_prefetch=1,
            grid=(steps,),
            in_specs=[pl.BlockSpec(x.shape, lambda i, me: (0, 0)) for x in [*rotated, peaks]]
            + [
                pl.BlockSpec(
                    (depth, fc),
                    lambda i, me: (0, (me[0] ^ (2 * i + odd)) * FEATURE_CHUNKS + chunk),
                )
            ]
            + [pl.BlockSpec(memory_space=pl.ANY)] * len(follow),
            out_specs=pl.BlockSpec((1, rows, fc), lambda i, me: (i, 0, 0)),
            scratch_shapes=[pltpu.VMEM((rows, depth), BF16)],
        ),
        out_shape=jax.ShapeDtypeStruct((steps, rows, fc), BF16),
        compiler_params=params(16),
        cost_estimate=cost(4 * steps * rows * depth * fc, 2 * steps * depth * fc),
        name="down_other" if odd else "down_same",
    )(me, *rotated, peaks, weight, *follow)


def spread_body(count, ids_ref, probs_ref, *refs):
    mine, theirs = refs[:count], refs[count : 2 * count]
    out_ref = refs[-1]
    tokens = ids_ref.shape[1]
    summed = jnp.concatenate(
        [(a[0].astype(F32) + b[0].astype(F32)).astype(BF16) for a, b in zip(mine, theirs)], axis=0
    )
    slots = slots_of(ids_ref)
    share = jnp.where(ids_ref[0:1, :] == 0, probs_ref[0:1, :], 0.0) + jnp.where(
        ids_ref[1:2, :] == 0, probs_ref[1:2, :], 0.0
    )
    blocks = tokens // LANES
    share = jnp.concatenate(
        [share[:, LANES * k : LANES * (k + 1)] for k in range(blocks)]
        + [jnp.zeros((LANES - blocks, LANES), F32)],
        axis=0,
    ).T
    slots = jnp.concatenate(
        [slots, jnp.zeros((LANES - slots.shape[0], LANES), F32)], axis=0
    ).T.astype(jnp.int32)
    at = iota((LANES, summed.shape[0]), 1)
    for k in range(blocks):
        hot = jnp.where(at == slots[:, k : k + 1], 1.0, 0.0).astype(BF16)
        rows = jnp.dot(hot, summed, preferred_element_type=F32)
        out_ref[LANES * k : LANES * (k + 1), :] = (rows * share[:, k : k + 1]).astype(BF16)


def spread(ids, probs, state, chunk, out, follow=()):
    mine, theirs = [x[0] for x in state], [x[1] for x in state]
    tokens = ids.shape[1]
    count = len(mine)
    _, rows, fc = mine[0].shape
    args = [ids, probs, *mine, *theirs]
    in_specs = [pl.BlockSpec(x.shape, lambda i, d=x.ndim: (0,) * d) for x in args]
    aliases = {}
    if out is not None:
        aliases = {len(args): 0}
        follow = [out, *follow]
    return pl.pallas_call(
        lambda *refs: spread_body(count, *refs[: 2 + 2 * count], refs[-1]),
        grid=(1,),
        in_specs=in_specs + follows(follow),
        out_specs=pl.BlockSpec((tokens, fc), lambda i: (0, chunk)),
        out_shape=jax.ShapeDtypeStruct((tokens, fc * FEATURE_CHUNKS), BF16),
        input_output_aliases=aliases,
        compiler_params=params(16),
        cost_estimate=cost(2 * tokens * rows * count * fc, 2 * tokens * fc),
        name="spread",
    )(*args, *follow)


def follows(arrays):
    return [pl.BlockSpec(memory_space=pl.ANY)] * len(arrays)


def small(body, args, shapes, name, follow=()):
    vmem = pl.BlockSpec(memory_space=pltpu.VMEM)
    count = len(args)
    specs = [pl.BlockSpec(memory_space=pltpu.SMEM) if x.ndim == 1 else vmem for x in args]
    return pl.pallas_call(
        lambda *refs: body(refs[:count], refs[count + len(follow) :]),
        in_specs=specs + follows(follow),
        out_specs=[vmem] * len(shapes),
        out_shape=[jax.ShapeDtypeStruct(*x) for x in shapes],
        compiler_params=params(16),
        name=name,
    )(*args, *follow)


def gather_near(own, orders):
    return {0: own} | {1 << bit: across(own, bit) for bit in orders[0]}


def cut_body(ins, outs):
    for h, (block, out) in enumerate(zip(ins, outs)):
        rows = out.shape[0]
        out[...] = block[h * rows : (h + 1) * rows, :]


def join_body(ins, outs):
    for i, out in enumerate(outs):
        rows = out.shape[0] // 2
        out[:rows, :] = ins[2 * i][...]
        out[rows:, :] = ins[2 * i + 1][...]


def gather_far(full, orders, before_cut, before_join):
    rows, width = full[0].shape
    half = rows // len(orders)
    firsts = [1 << order[0] for order in orders]
    cuts = small(
        cut_body, [full[m] for m in firsts], [((half, width), BF16)] * 2, "cut", before_cut
    )
    part = {}

    def get(mask, h):
        if (mask, h) in part:
            return part[mask, h]
        return cuts[h] if mask == firsts[h] else full[mask][h * half : (h + 1) * half]

    have = [[0, first] for first in firsts]
    for at in range(1, len(orders[0])):
        for h, order in enumerate(orders):
            bit = order[at]
            for mask in list(have[h]):
                there = mask | 1 << bit
                if there not in full:
                    part[there, h] = across(get(mask, h), bit)
                have[h].append(there)
    masks = sorted({mask for mask, _ in part})
    halves = [part[mask, h] for mask in masks for h in range(2)]
    joined = small(
        join_body, halves, [((rows, width), BF16)] * len(masks), "join", before_join
    )
    return dict(zip(masks, joined))


def paired(pieces):
    return pieces | {mask | 1: across(block, 0) for mask, block in pieces.items()}


def turn_body(bits, scale, ins, outs):
    me_ref, ins = ins[0], ins[1:]
    tops = []
    for h, bit in enumerate(bits):
        flip = (1 - 2 * ((me_ref[0] >> bit) & 1)).astype(F32)
        value = ins[2 * h + 1][...].astype(F32) + ins[2 * h][...].astype(F32) * flip
        if scale is not None:
            value = value * scale
            tops.append(jnp.max(jnp.abs(value), axis=0, keepdims=True))
        outs[h][...] = value.astype(BF16)
    if scale is not None:
        top = jnp.maximum(*tops)
        wide = top[:, :LANES]
        for k in range(1, top.shape[1] // LANES):
            wide = jnp.maximum(wide, top[:, k * LANES : (k + 1) * LANES])
        outs[-1][...] = jnp.broadcast_to(wide, outs[-1].shape)


def turn(me, blocks, came, bits, follow=(), scale=None):
    args = [me] + [x for pair in zip(blocks, came) for x in pair]
    shapes = [(x.shape, BF16) for x in blocks]
    if scale is not None:
        shapes.append(((8, LANES), F32))
    return small(
        lambda ins, outs: turn_body(bits, scale, ins, outs), args, shapes, "turn", follow
    )


def largest(values):
    count = lax.axis_size("tensor")
    bits = count.bit_length() - 1
    for low in range(0, bits, 2):
        top = min(bits, low + 2)
        others = [
            lax.ppermute(values, "tensor", [(r, r ^ m << low) for r in range(count)])
            for m in range(1, 1 << (top - low))
        ]
        for other in others:
            values = jnp.maximum(values, other)
    blocks = lax.axis_size("dp")
    others = [
        lax.ppermute(values, "dp", [(r, (r + s) % blocks) for r in range(blocks)])
        for s in range(1, blocks)
    ]
    for other in others:
        values = jnp.maximum(values, other)
    return values


def on_device(tokens, expert_ids, gate_probs, gate_weight, up_weight, down_weight):
    count = lax.axis_size("tensor")
    bits = count.bit_length() - 1
    outer = list(range(1, bits))
    orders = [outer, outer[::-1]]
    me = lax.axis_index("tensor")
    me_arr = me.astype(jnp.int32).reshape(1)
    ids, probs = expert_ids.T, gate_probs.T
    rows = CAP // ROW_CHUNKS
    half = rows // 2
    scale = 1.0 / math.sqrt(gate_weight.shape[1] * count)
    weights = (me_arr, gate_weight, up_weight)
    layout = list(range(count))
    stages = [[order[at] for order in orders] for at in range(len(outer))]

    def send(blocks, bits):
        return [across(x, bit) for x, bit in zip(blocks, bits)]

    def start_turn(halves, follow=()):
        blocks = turn(me_arr, halves, send(halves, [0, 0]), [0, 0], follow)
        return blocks, send(blocks, stages[0])

    def go_on(blocks, came, at, follow=()):
        blocks = turn(me_arr, blocks, came, stages[at], follow)
        return blocks, send(blocks, stages[at + 1])

    def end_turn(blocks, came, follow=()):
        *blocks, top = turn(me_arr, blocks, came, stages[-1], follow, scale)
        return blocks, top

    own_a, top_a = pick_rows(ids, tokens, 0, rows, [me_arr])
    near_a = gather_near(own_a, orders)
    got_a = [near_a[1 << bit] for bit in outer]
    own_b, top_b = pick_rows(ids, tokens, rows, rows, got_a)
    far_a = gather_far(near_a, orders, [], [own_b])
    near_b = gather_near(own_b, orders)
    got_b = [near_b[1 << bit] for bit in outer]
    parts_a = paired(near_a | far_a)
    parts_a = [parts_a[mask] for mask in layout]
    first_a = expand(parts_a, layout, rows, *weights)
    local_a = expand(parts_a, layout, rows, *weights, *first_a, got_b)
    far_b = gather_far(near_b, orders, first_a, local_a)
    blocks_a, came_a = start_turn(local_a)
    parts_b = paired(near_b | far_b)
    parts_b = [parts_b[mask] for mask in layout]
    first_b = expand(parts_b, layout, rows, *weights, None, blocks_a)
    for at in range(len(outer) - 1):
        blocks_a, came_a = go_on(blocks_a, came_a, at, first_b)
    local_b = expand(parts_b, layout, rows, *weights, *first_b, blocks_a)
    blocks_b, came_b = start_turn(local_b)
    turned_a, rot_a = end_turn(blocks_a, came_a, blocks_b)
    for at in range(len(outer) - 1):
        blocks_b, came_b = go_on(blocks_b, came_b, at, [rot_a] if at == 0 else [])
    turned_b, rot_b = end_turn(blocks_b, came_b)
    rotated = turned_a + turned_b

    top_in = jnp.maximum(top_a, top_b)
    peaks = largest(jnp.concatenate([top_in, jnp.maximum(rot_a, rot_b)], axis=0))

    tops = pl.pallas_call(
        peaks_body,
        out_specs=pl.BlockSpec(memory_space=pltpu.SMEM),
        out_shape=jax.ShapeDtypeStruct((2,), F32),
        name="peaks",
    )(peaks)
    states, wait, out = [], [], None
    for chunk in range(FEATURE_CHUNKS):
        other = down(rotated, peaks, down_weight, me_arr, chunk, 1, wait)
        came = across(other, 0)
        same = down(rotated, peaks, down_weight, me_arr, chunk, 0, [other])
        states.append(fold_cores(same, came, stages[0]))
        wait = [keep for keep, _, _ in states[chunk]]
        if chunk > 0:
            states[chunk - 1] = finish(states[chunk - 1], stages, [same])
            wait += [keep for keep, _, _ in states[chunk - 1]]
        if chunk > 1:
            out = spread(ids, probs, states[chunk - 2], chunk - 2, out, [same])
    last = FEATURE_CHUNKS - 1
    states[last] = finish(states[last], stages, [] if out is None else [out])
    for chunk in range(max(0, last - 1), FEATURE_CHUNKS):
        out = spread(ids, probs, states[chunk], chunk, out)
    return out, tops


def peaks_body(values_ref, out_ref):
    out_ref[0] = jnp.max(values_ref[:8, :])
    out_ref[1] = jnp.max(values_ref[8:, :])


def fold_body(plan, ins, outs):
    for out, (at, slots, low) in zip(outs, plan):
        rows = out.shape[1]
        for slot, i in enumerate(slots):
            total = ins[2 * at][i, low : low + rows, :].astype(F32)
            total += ins[2 * at + 1][i, low : low + rows, :].astype(F32)
            out[slot] = total.astype(BF16)


def fold(pairs, masks, lows, rows, bits, follow):
    plan, shapes, lefts = [], [], []
    for h, bit in enumerate(bits):
        at = min(h, len(pairs) - 1)
        for side in (0, 1):
            slots = [i for i, m in enumerate(masks[h]) if m >> bit & 1 == side]
            plan.append((at, slots, lows[h]))
            shapes.append(((len(slots), rows, pairs[at][0].shape[2]), BF16))
        lefts.append([m for m in masks[h] if not m >> bit & 1])
    made = small(
        lambda ins, outs: fold_body(plan, ins, outs),
        [x for pair in pairs for x in pair],
        shapes,
        "fold",
        follow,
    )
    return [
        (made[2 * h], across(made[2 * h + 1], bit), lefts[h]) for h, bit in enumerate(bits)
    ]


def fold_cores(same, came, bits):
    half = same.shape[1] // 2
    masks = [2 * i for i in range(same.shape[0])]
    return fold([(same, came)], [masks, masks], [0, half], half, bits, [])


def finish(state, stages, follow):
    for bits in stages[1:]:
        pairs = [(keep, recv) for keep, recv, _ in state]
        masks = [left for _, _, left in state]
        state = fold(pairs, masks, [0, 0], pairs[0][0].shape[1], bits, follow)
    return state


def solution(mesh):
    in_specs = (
        P("dp", "tensor"),
        P("dp", None),
        P("dp", None),
        P(None, "tensor"),
        P(None, "tensor"),
        P("tensor", None),
    )
    out_specs = (P("dp", "tensor"), P())
    return jax.shard_map(
        on_device, mesh=mesh, in_specs=in_specs, out_specs=out_specs, check_vma=False
    )
```

```python
import math

import jax
import jax.numpy as jnp
from jax import lax
from jax.experimental import pallas as pl
from jax.experimental.pallas import tpu as pltpu
from jax.sharding import PartitionSpec as P

CAP = 768
CLIP_SHARE = 0.25
LANES = 128
ROW_CHUNKS = 2
FEATURE_CHUNKS = 3
BF16 = jnp.bfloat16
F32 = jnp.float32
MIB = 1 << 20
EXPAND_MIB = 24
AHEAD = 3


def params(mib):
    return pltpu.CompilerParams(vmem_limit_bytes=mib * MIB)


TINY = pl.CostEstimate(flops=1, bytes_accessed=1, transcendentals=0)


def across(block, bit):
    count = lax.axis_size("tensor")
    return lax.ppermute(block, "tensor", [(r, r ^ 1 << bit) for r in range(count)])


def iota(shape, dim):
    return lax.broadcasted_iota(jnp.int32, shape, dim)


def slots_of(ids_ref):
    tokens = ids_ref.shape[1]
    rows = tokens // LANES
    padded = (rows + 15) // 16 * 16
    hit = jnp.where((ids_ref[0:1, :] == 0) | (ids_ref[1:2, :] == 0), 1.0, 0.0)
    grid = jnp.concatenate(
        [hit[:, LANES * k : LANES * (k + 1)] for k in range(rows)]
        + [jnp.zeros((padded - rows, LANES), F32)],
        axis=0,
    )
    flat = grid.astype(BF16)
    upto = (iota((LANES, LANES), 0) <= iota((LANES, LANES), 1)).astype(F32).astype(BF16)
    before = (iota((padded, padded), 1) < iota((padded, padded), 0)).astype(F32).astype(BF16)
    within = jnp.dot(flat, upto, preferred_element_type=F32)
    offset = jnp.sum(jnp.dot(before, flat, preferred_element_type=F32), axis=1, keepdims=True)
    return jnp.where(grid > 0.0, within + offset - 1.0, -1.0)


def pick_body(first, ids_ref, tokens_ref, *refs):
    picked_ref, peak_ref = refs[-2:]
    rows = picked_ref.shape[0]
    slots = slots_of(ids_ref).astype(jnp.int32)
    wanted = iota((rows, LANES), 0) + first
    hot = jnp.concatenate(
        [
            jnp.where(wanted == slots[k : k + 1, :], 1.0, 0.0).astype(BF16)
            for k in range(ids_ref.shape[1] // LANES)
        ],
        axis=1,
    )
    picked = jnp.dot(hot, tokens_ref[...], preferred_element_type=F32)
    picked_ref[...] = picked.astype(BF16)
    peak_ref[...] = jnp.broadcast_to(jnp.max(jnp.abs(picked)), peak_ref.shape)


def pick_rows(ids, tokens, first, rows, follow=()):
    count, width = tokens.shape
    return pl.pallas_call(
        lambda *refs: pick_body(first, *refs),
        out_shape=(
            jax.ShapeDtypeStruct((rows, width), BF16),
            jax.ShapeDtypeStruct((8, LANES), F32),
        ),
        in_specs=[pl.BlockSpec(memory_space=pltpu.VMEM)] * 2
        + [pl.BlockSpec(memory_space=pl.ANY)] * len(follow),
        compiler_params=params(16),
        cost_estimate=TINY,
        name="pick_rows",
    )(ids, tokens, *follow)


def signs(size):
    common = iota((size, size), 0) & iota((size, size), 1)
    shift = 1
    while shift < size.bit_length():
        shift *= 2
    while shift > 1:
        shift //= 2
        common = common ^ (common >> shift)
    return (1 - 2 * (common & 1)).astype(F32).astype(BF16)


def expand_body(first, count, last, me_ref, *refs):
    parts, refs = refs[:count], refs[count:]
    before_ref = None
    if last:
        before_ref, refs = refs[0], refs[1:]
    gate_hbm, up_hbm, *outs, total, held, loaded = refs
    width = parts[0].shape[1]
    columns = total.shape[2]
    tile = min(256, columns)

    def load(mask):
        rows = pl.ds(pl.multiple_of((me_ref[0] ^ mask) * width, LANES), width)
        return [
            pltpu.make_async_copy(
                weight.at[rows, pl.ds(first, columns)], held.at[mask, at], loaded.at[mask, at]
            )
            for at, weight in enumerate((gate_hbm, up_hbm))
        ]

    loads = [load(mask) for mask in range(count)]
    for copies in loads[:AHEAD]:
        for copy in copies:
            copy.start()
    table = signs(tile)
    for mask, part in enumerate(parts):
        for copies in loads[mask + AHEAD : mask + AHEAD + 1]:
            for copy in copies:
                copy.start()
        for at in range(2):
            loads[mask][at].wait()
            term = jnp.dot(part[...], held[mask, at], preferred_element_type=F32)
            if mask == 0:
                total[at] = term
            else:
                total[at] += term
    values = []
    for i in range(columns // tile):
        gate = total[0, :, i * tile : (i + 1) * tile]
        up = total[1, :, i * tile : (i + 1) * tile]
        hidden = (gate * (1.0 / (1.0 + jnp.exp(-gate))) * up).astype(BF16)
        values.append(jnp.dot(hidden, table, preferred_element_type=F32))
        if not last:
            outs[0][i] = values[i]
    if not last:
        return
    values = [before_ref[i] for i in range(before_ref.shape[0])] + values
    steps = len(values)
    gap = 1
    while gap < steps:
        values = [
            values[i] + values[i ^ gap] if not i & gap else values[i ^ gap] - values[i]
            for i in range(steps)
        ]
        gap *= 2
    for i in range(steps):
        low = 0
        for out in outs:
            rows = out.shape[0]
            out[:, i * tile : (i + 1) * tile] = values[i][low : low + rows].astype(BF16)
            low += rows


def expand(parts, rows, me, gate_weight, up_weight, before=None, follow=()):
    depth, width = gate_weight.shape
    last = before is not None
    columns = width // 2
    first = columns if last else 0
    tile = min(256, columns)
    count = len(parts)
    vmem = pl.BlockSpec(memory_space=pltpu.VMEM)
    in_hbm = [pltpu.with_memory_space_constraint(x, pltpu.HBM) for x in (gate_weight, up_weight)]
    args = [me, *parts] + ([before] if last else [])
    used = len(args) + 2
    if last:
        out_shape = [jax.ShapeDtypeStruct((rows // 2, width), BF16)] * 2
    else:
        out_shape = [jax.ShapeDtypeStruct((columns // tile, rows, tile), F32)]
    return pl.pallas_call(
        lambda *refs: expand_body(first, count, last, *refs[:used], *refs[used + len(follow) :]),
        in_specs=[pl.BlockSpec(memory_space=pltpu.SMEM)]
        + [vmem] * (used - 3)
        + [pl.BlockSpec(memory_space=pltpu.HBM)] * 2
        + follows(follow),
        out_specs=[vmem] * len(out_shape),
        out_shape=out_shape,
        scratch_shapes=[
            pltpu.VMEM((2, rows, columns), F32),
            pltpu.VMEM((count, 2, depth // count, columns), BF16),
            pltpu.SemaphoreType.DMA((count, 2)),
        ],
        compiler_params=params(EXPAND_MIB),
        cost_estimate=TINY,
        name="expand_last" if last else "expand_first",
    )(*args, *in_hbm, *follow)


def down_body(count, me_ref, *refs):
    rotated, (peaks_ref, weight_ref), (out_ref, held) = refs[:count], refs[count : count + 2], refs[-2:]

    @pl.when(pl.program_id(0) == 0)
    def _():
        level = CLIP_SHARE * jnp.max(peaks_ref[8:, :])
        low = 0
        for part in rotated:
            rows = part.shape[0]
            held[low : low + rows, :] = jnp.clip(part[...].astype(F32), -level, level).astype(BF16)
            low += rows

    out_ref[0] = jnp.dot(held[...], weight_ref[...], preferred_element_type=F32).astype(BF16)


def down(rotated, peaks, weight, me, chunk, odd, follow=()):
    depth = weight.shape[0]
    owners = lax.axis_size("tensor")
    steps = owners // 2
    rows = sum(part.shape[0] for part in rotated)
    fc = weight.shape[1] // owners // FEATURE_CHUNKS
    count = len(rotated)
    return pl.pallas_call(
        lambda *refs: down_body(count, *refs),
        grid_spec=pltpu.PrefetchScalarGridSpec(
            num_scalar_prefetch=1,
            grid=(steps,),
            in_specs=[pl.BlockSpec(x.shape, lambda i, me: (0, 0)) for x in [*rotated, peaks]]
            + [
                pl.BlockSpec(
                    (depth, fc),
                    lambda i, me: (0, (me[0] ^ (2 * i + odd)) * FEATURE_CHUNKS + chunk),
                )
            ]
            + [pl.BlockSpec(memory_space=pl.ANY)] * len(follow),
            out_specs=pl.BlockSpec((1, rows, fc), lambda i, me: (i, 0, 0)),
            scratch_shapes=[pltpu.VMEM((rows, depth), BF16)],
        ),
        out_shape=jax.ShapeDtypeStruct((steps, rows, fc), BF16),
        compiler_params=params(16),
        cost_estimate=TINY,
        name="down_other" if odd else "down_same",
    )(me, *rotated, peaks, weight, *follow)


def spread_body(count, ids_ref, probs_ref, *refs):
    mine, theirs = refs[:count], refs[count : 2 * count]
    out_ref = refs[-1]
    tokens = ids_ref.shape[1]
    summed = jnp.concatenate(
        [(a[0].astype(F32) + b[0].astype(F32)).astype(BF16) for a, b in zip(mine, theirs)], axis=0
    )
    slots = slots_of(ids_ref)
    share = jnp.where(ids_ref[0:1, :] == 0, probs_ref[0:1, :], 0.0) + jnp.where(
        ids_ref[1:2, :] == 0, probs_ref[1:2, :], 0.0
    )
    blocks = tokens // LANES
    share = jnp.concatenate(
        [share[:, LANES * k : LANES * (k + 1)] for k in range(blocks)]
        + [jnp.zeros((LANES - blocks, LANES), F32)],
        axis=0,
    ).T
    slots = jnp.concatenate(
        [slots, jnp.zeros((LANES - slots.shape[0], LANES), F32)], axis=0
    ).T.astype(jnp.int32)
    at = iota((LANES, summed.shape[0]), 1)
    for k in range(blocks):
        hot = jnp.where(at == slots[:, k : k + 1], 1.0, 0.0).astype(BF16)
        rows = jnp.dot(hot, summed, preferred_element_type=F32)
        out_ref[LANES * k : LANES * (k + 1), :] = (rows * share[:, k : k + 1]).astype(BF16)


def spread(ids, probs, state, chunk, out, follow=()):
    mine, theirs = [x[0] for x in state], [x[1] for x in state]
    tokens = ids.shape[1]
    count = len(mine)
    _, rows, fc = mine[0].shape
    args = [ids, probs, *mine, *theirs]
    in_specs = [pl.BlockSpec(x.shape, lambda i, d=x.ndim: (0,) * d) for x in args]
    aliases = {}
    if out is not None:
        aliases = {len(args): 0}
        follow = [out, *follow]
    return pl.pallas_call(
        lambda *refs: spread_body(count, *refs[: 2 + 2 * count], refs[-1]),
        grid=(1,),
        in_specs=in_specs + follows(follow),
        out_specs=pl.BlockSpec((tokens, fc), lambda i: (0, chunk)),
        out_shape=jax.ShapeDtypeStruct((tokens, fc * FEATURE_CHUNKS), BF16),
        input_output_aliases=aliases,
        compiler_params=params(16),
        cost_estimate=TINY,
        name="spread",
    )(*args, *follow)


def follows(arrays):
    return [pl.BlockSpec(memory_space=pl.ANY)] * len(arrays)


def small(body, args, shapes, name, follow=()):
    vmem = pl.BlockSpec(memory_space=pltpu.VMEM)
    count = len(args)
    specs = [pl.BlockSpec(memory_space=pltpu.SMEM) if x.ndim == 1 else vmem for x in args]
    return pl.pallas_call(
        lambda *refs: body(refs[:count], refs[count + len(follow) :]),
        in_specs=specs + follows(follow),
        out_specs=[vmem] * len(shapes),
        out_shape=[jax.ShapeDtypeStruct(*x) for x in shapes],
        compiler_params=params(16),
        cost_estimate=TINY,
        name=name,
    )(*args, *follow)


def gather_near(own, orders):
    return {0: own} | {1 << bit: across(own, bit) for bit in orders[0]}


def cut_body(firsts, ins, outs):
    for h, at in enumerate(firsts):
        rows = outs[h].shape[0]
        outs[h][...] = ins[at][h * rows : (h + 1) * rows, :]
    for block, out in zip(ins, outs[2:]):
        out[...] = block[...]


def join_body(ins, outs):
    for i, out in enumerate(outs):
        rows = out.shape[0] // 2
        out[:rows, :] = ins[2 * i][...]
        out[rows:, :] = ins[2 * i + 1][...]


def cut(full, orders, follow, passed=False):
    rows, width = full[0].shape
    masks = [mask for mask in full if mask]
    firsts = [masks.index(1 << order[0]) for order in orders]
    shapes = [((rows // 2, width), BF16)] * 2 + [((rows, width), BF16)] * len(masks) * passed
    outs = small(
        lambda ins, outs: cut_body(firsts, ins, outs),
        [full[mask] for mask in masks],
        shapes,
        "cut",
        follow,
    )
    return outs[:2], full | dict(zip(masks, outs[2:]))


def gather_far(full, cuts, orders):
    half = full[0].shape[0] // len(orders)
    firsts = [1 << order[0] for order in orders]
    part = {}

    def get(mask, h):
        if (mask, h) in part:
            return part[mask, h]
        return cuts[h] if mask == firsts[h] else full[mask][h * half : (h + 1) * half]

    have = [[0, first] for first in firsts]
    for at in range(1, len(orders[0])):
        for h, order in enumerate(orders):
            bit = order[at]
            for mask in list(have[h]):
                there = mask | 1 << bit
                if there not in full:
                    part[there, h] = across(get(mask, h), bit)
                have[h].append(there)
    return part


def join(part, follow):
    masks = sorted({mask for mask, _ in part})
    halves = [part[mask, h] for mask in masks for h in range(2)]
    half, width = halves[0].shape
    joined = small(join_body, halves, [((2 * half, width), BF16)] * len(masks), "join", follow)
    return dict(zip(masks, joined))


def paired(pieces):
    return pieces | {mask | 1: across(block, 0) for mask, block in pieces.items()}


def turn_body(bits, scale, ins, outs):
    me_ref, ins = ins[0], ins[1:]
    tops = []
    for h, bit in enumerate(bits):
        flip = (1 - 2 * ((me_ref[0] >> bit) & 1)).astype(F32)
        value = ins[2 * h + 1][...].astype(F32) + ins[2 * h][...].astype(F32) * flip
        if scale is not None:
            value = value * scale
            tops.append(jnp.max(jnp.abs(value), axis=0, keepdims=True))
        outs[h][...] = value.astype(BF16)
    if scale is not None:
        top = jnp.maximum(*tops)
        wide = top[:, :LANES]
        for k in range(1, top.shape[1] // LANES):
            wide = jnp.maximum(wide, top[:, k * LANES : (k + 1) * LANES])
        outs[-1][...] = jnp.broadcast_to(wide, outs[-1].shape)


def turn(me, blocks, came, bits, follow=(), scale=None):
    args = [me] + [x for pair in zip(blocks, came) for x in pair]
    shapes = [(x.shape, BF16) for x in blocks]
    if scale is not None:
        shapes.append(((8, LANES), F32))
    return small(
        lambda ins, outs: turn_body(bits, scale, ins, outs), args, shapes, "turn", follow
    )


def largest(values):
    count = lax.axis_size("tensor")
    bits = count.bit_length() - 1
    for low in range(0, bits, 2):
        top = min(bits, low + 2)
        others = [
            lax.ppermute(values, "tensor", [(r, r ^ m << low) for r in range(count)])
            for m in range(1, 1 << (top - low))
        ]
        for other in others:
            values = jnp.maximum(values, other)
    blocks = lax.axis_size("dp")
    others = [
        lax.ppermute(values, "dp", [(r, (r + s) % blocks) for r in range(blocks)])
        for s in range(1, blocks)
    ]
    for other in others:
        values = jnp.maximum(values, other)
    return values


def on_device(tokens, expert_ids, gate_probs, gate_weight, up_weight, down_weight):
    count = lax.axis_size("tensor")
    bits = count.bit_length() - 1
    outer = list(range(1, bits))
    orders = [outer, outer[::-1]]
    me = lax.axis_index("tensor")
    me_arr = me.astype(jnp.int32).reshape(1)
    ids, probs = expert_ids.T, gate_probs.T
    rows = CAP // ROW_CHUNKS
    half = rows // 2
    scale = 1.0 / math.sqrt(gate_weight.shape[1] * count)
    stages = [[order[at] for order in orders] for at in range(len(outer))]

    def send(blocks, bits):
        return [across(x, bit) for x, bit in zip(blocks, bits)]

    def start_turn(halves, follow=()):
        blocks = turn(me_arr, halves, send(halves, [0, 0]), [0, 0], follow)
        return blocks, send(blocks, stages[0])

    def go_on(blocks, came, at, follow=()):
        blocks = turn(me_arr, blocks, came, stages[at], follow)
        return blocks, send(blocks, stages[at + 1])

    def end_turn(blocks, came, follow=()):
        *blocks, top = turn(me_arr, blocks, came, stages[-1], follow, scale)
        return blocks, top

    own_a, top_a = pick_rows(ids, tokens, 0, rows, [me_arr])
    near_a = gather_near(own_a, orders)
    weights = (me_arr, gate_weight, up_weight)
    cuts_a, near_a = cut(near_a, orders, [])
    own_b, top_b = pick_rows(ids, tokens, rows, rows, cuts_a)
    far_a = join(gather_far(near_a, cuts_a, orders), [own_b])
    near_b = gather_near(own_b, orders)
    parts_a = paired(near_a | far_a)
    parts_a = [parts_a[mask] for mask in range(count)]
    first_a = expand(parts_a, rows, *weights)
    cuts_b, near_b = cut(near_b, orders, first_a, True)
    local_a = expand(parts_a, rows, *weights, *first_a, cuts_b)
    parts_b = paired(near_b)
    theirs_b = [block for mask, block in parts_b.items() if mask & 1]
    far_b = join(gather_far(near_b, cuts_b, orders), list(local_a) + theirs_b)
    parts_b |= paired(far_b)
    parts_b = [parts_b[mask] for mask in range(count)]
    blocks_a, came_a = start_turn(local_a)
    first_b = expand(parts_b, rows, *weights, None, blocks_a)
    for at in range(len(outer) - 1):
        blocks_a, came_a = go_on(blocks_a, came_a, at, first_b)
    local_b = expand(parts_b, rows, *weights, *first_b, blocks_a)
    turned_a, rot_a = end_turn(blocks_a, came_a, local_b)
    blocks_b, came_b = start_turn(local_b, [rot_a])
    for at in range(len(outer) - 1):
        blocks_b, came_b = go_on(blocks_b, came_b, at)
    turned_b, rot_b = end_turn(blocks_b, came_b)
    rotated = turned_a + turned_b

    top_in = jnp.maximum(top_a, top_b)
    peaks = largest(jnp.concatenate([top_in, jnp.maximum(rot_a, rot_b)], axis=0))

    tops = pl.pallas_call(
        peaks_body,
        out_specs=pl.BlockSpec(memory_space=pltpu.SMEM),
        out_shape=jax.ShapeDtypeStruct((2,), F32),
        name="peaks",
    )(peaks)
    states, out = [], None
    other = down(rotated, peaks, down_weight, me_arr, 0, 1)
    wait = [other]
    for chunk in range(FEATURE_CHUNKS):
        came = across(other, 0)
        same = down(rotated, peaks, down_weight, me_arr, chunk, 0, wait)
        state = fold_cores(same, came, stages[0])
        wait = [keep for keep, _, _ in state]
        if chunk > 0:
            out = spread(ids, probs, states[-1], chunk - 1, out, wait)
            wait.append(out)
        if chunk + 1 < FEATURE_CHUNKS:
            other = down(rotated, peaks, down_weight, me_arr, chunk + 1, 1, wait)
            wait = [other]
        states.append(finish(state, stages, wait))
        wait = [keep for keep, _, _ in states[-1]]
    out = spread(ids, probs, states[-1], FEATURE_CHUNKS - 1, out)
    return out, tops


def peaks_body(values_ref, out_ref):
    out_ref[0] = jnp.max(values_ref[:8, :])
    out_ref[1] = jnp.max(values_ref[8:, :])


def fold_body(plan, ins, outs):
    for out, (at, slots, low) in zip(outs, plan):
        rows = out.shape[1]
        for slot, i in enumerate(slots):
            total = ins[2 * at][i, low : low + rows, :].astype(F32)
            total += ins[2 * at + 1][i, low : low + rows, :].astype(F32)
            out[slot] = total.astype(BF16)


def fold(pairs, masks, lows, rows, bits, follow):
    plan, shapes, lefts = [], [], []
    for h, bit in enumerate(bits):
        at = min(h, len(pairs) - 1)
        for side in (0, 1):
            slots = [i for i, m in enumerate(masks[h]) if m >> bit & 1 == side]
            plan.append((at, slots, lows[h]))
            shapes.append(((len(slots), rows, pairs[at][0].shape[2]), BF16))
        lefts.append([m for m in masks[h] if not m >> bit & 1])
    made = small(
        lambda ins, outs: fold_body(plan, ins, outs),
        [x for pair in pairs for x in pair],
        shapes,
        "fold",
        follow,
    )
    return [
        (made[2 * h], across(made[2 * h + 1], bit), lefts[h]) for h, bit in enumerate(bits)
    ]


def fold_cores(same, came, bits):
    half = same.shape[1] // 2
    masks = [2 * i for i in range(same.shape[0])]
    return fold([(same, came)], [masks, masks], [0, half], half, bits, [])


def finish(state, stages, follow):
    for bits in stages[1:]:
        pairs = [(keep, recv) for keep, recv, _ in state]
        masks = [left for _, _, left in state]
        state = fold(pairs, masks, [0, 0], pairs[0][0].shape[1], bits, follow)
    return state


def solution(mesh):
    in_specs = (
        P("dp", "tensor"),
        P("dp", None),
        P("dp", None),
        P(None, "tensor"),
        P(None, "tensor"),
        P("tensor", None),
    )
    out_specs = (P("dp", "tensor"), P())
    return jax.shard_map(
        on_device, mesh=mesh, in_specs=in_specs, out_specs=out_specs, check_vma=False
    )
```

```python
import math

import jax
import jax.numpy as jnp
from jax import lax
from jax.experimental import pallas as pl
from jax.experimental.pallas import tpu as pltpu
from jax.sharding import PartitionSpec as P

CAP = 768
CLIP_SHARE = 0.25
LANES = 128
ROW_CHUNKS = 2
BF16 = jnp.bfloat16
F32 = jnp.float32
MIB = 1 << 20
EXPAND_MIB = 24
AHEAD = 3


def params(mib):
    return pltpu.CompilerParams(vmem_limit_bytes=mib * MIB)


TINY = pl.CostEstimate(flops=1, bytes_accessed=1, transcendentals=0)


def across(block, bit):
    count = lax.axis_size("tensor")
    return lax.ppermute(block, "tensor", [(r, r ^ 1 << bit) for r in range(count)])


def iota(shape, dim):
    return lax.broadcasted_iota(jnp.int32, shape, dim)


def slots_of(ids_ref):
    tokens = ids_ref.shape[1]
    rows = tokens // LANES
    padded = (rows + 15) // 16 * 16
    hit = jnp.where((ids_ref[0:1, :] == 0) | (ids_ref[1:2, :] == 0), 1.0, 0.0)
    grid = jnp.concatenate(
        [hit[:, LANES * k : LANES * (k + 1)] for k in range(rows)]
        + [jnp.zeros((padded - rows, LANES), F32)],
        axis=0,
    )
    flat = grid.astype(BF16)
    upto = (iota((LANES, LANES), 0) <= iota((LANES, LANES), 1)).astype(F32).astype(BF16)
    before = (iota((padded, padded), 1) < iota((padded, padded), 0)).astype(F32).astype(BF16)
    within = jnp.dot(flat, upto, preferred_element_type=F32)
    offset = jnp.sum(jnp.dot(before, flat, preferred_element_type=F32), axis=1, keepdims=True)
    return jnp.where(grid > 0.0, within + offset - 1.0, -1.0)


def pick_body(first, ids_ref, tokens_ref, *refs):
    picked_ref, peak_ref = refs[-2:]
    rows = picked_ref.shape[0]
    slots = slots_of(ids_ref).astype(jnp.int32)
    wanted = iota((rows, LANES), 0) + first
    hot = jnp.concatenate(
        [
            jnp.where(wanted == slots[k : k + 1, :], 1.0, 0.0).astype(BF16)
            for k in range(ids_ref.shape[1] // LANES)
        ],
        axis=1,
    )
    picked = jnp.dot(hot, tokens_ref[...], preferred_element_type=F32)
    picked_ref[...] = picked.astype(BF16)
    peak_ref[...] = jnp.broadcast_to(jnp.max(jnp.abs(picked)), peak_ref.shape)


def pick_rows(ids, tokens, first, rows, follow=()):
    count, width = tokens.shape
    return pl.pallas_call(
        lambda *refs: pick_body(first, *refs),
        out_shape=(
            jax.ShapeDtypeStruct((rows, width), BF16),
            jax.ShapeDtypeStruct((8, LANES), F32),
        ),
        in_specs=[pl.BlockSpec(memory_space=pltpu.VMEM)] * 2
        + [pl.BlockSpec(memory_space=pl.ANY)] * len(follow),
        compiler_params=params(16),
        cost_estimate=TINY,
        name="pick_rows",
    )(ids, tokens, *follow)


def signs(size):
    common = iota((size, size), 0) & iota((size, size), 1)
    shift = 1
    while shift < size.bit_length():
        shift *= 2
    while shift > 1:
        shift //= 2
        common = common ^ (common >> shift)
    return (1 - 2 * (common & 1)).astype(F32).astype(BF16)


def expand_body(first, count, last, me_ref, *refs):
    parts, refs = refs[:count], refs[count:]
    before_ref = None
    if last:
        before_ref, refs = refs[0], refs[1:]
    gate_hbm, up_hbm, *outs, total, held, loaded = refs
    width = parts[0].shape[1]
    columns = total.shape[2]
    tile = min(256, columns)

    def load(mask):
        rows = pl.ds(pl.multiple_of((me_ref[0] ^ mask) * width, LANES), width)
        return [
            pltpu.make_async_copy(
                weight.at[rows, pl.ds(first, columns)], held.at[mask, at], loaded.at[mask, at]
            )
            for at, weight in enumerate((gate_hbm, up_hbm))
        ]

    loads = [load(mask) for mask in range(count)]
    for copies in loads[:AHEAD]:
        for copy in copies:
            copy.start()
    table = signs(tile)
    for mask, part in enumerate(parts):
        for copies in loads[mask + AHEAD : mask + AHEAD + 1]:
            for copy in copies:
                copy.start()
        for at in range(2):
            loads[mask][at].wait()
            term = jnp.dot(part[...], held[mask, at], preferred_element_type=F32)
            if mask == 0:
                total[at] = term
            else:
                total[at] += term
    values = []
    for i in range(columns // tile):
        gate = total[0, :, i * tile : (i + 1) * tile]
        up = total[1, :, i * tile : (i + 1) * tile]
        hidden = (gate * (1.0 / (1.0 + jnp.exp(-gate))) * up).astype(BF16)
        values.append(jnp.dot(hidden, table, preferred_element_type=F32))
        if not last:
            outs[0][i] = values[i]
    if not last:
        return
    values = [before_ref[i] for i in range(before_ref.shape[0])] + values
    steps = len(values)
    gap = 1
    while gap < steps:
        values = [
            values[i] + values[i ^ gap] if not i & gap else values[i ^ gap] - values[i]
            for i in range(steps)
        ]
        gap *= 2
    for i in range(steps):
        low = 0
        for out in outs:
            rows = out.shape[0]
            out[:, i * tile : (i + 1) * tile] = values[i][low : low + rows].astype(BF16)
            low += rows


def expand(parts, rows, me, gate_weight, up_weight, before=None, follow=()):
    depth, width = gate_weight.shape
    last = before is not None
    columns = width // 2
    first = columns if last else 0
    tile = min(256, columns)
    count = len(parts)
    vmem = pl.BlockSpec(memory_space=pltpu.VMEM)
    in_hbm = [pltpu.with_memory_space_constraint(x, pltpu.HBM) for x in (gate_weight, up_weight)]
    args = [me, *parts] + ([before] if last else [])
    used = len(args) + 2
    if last:
        out_shape = [jax.ShapeDtypeStruct((rows // 2, width), BF16)] * 2
    else:
        out_shape = [jax.ShapeDtypeStruct((columns // tile, rows, tile), F32)]
    return pl.pallas_call(
        lambda *refs: expand_body(first, count, last, *refs[:used], *refs[used + len(follow) :]),
        in_specs=[pl.BlockSpec(memory_space=pltpu.SMEM)]
        + [vmem] * (used - 3)
        + [pl.BlockSpec(memory_space=pltpu.HBM)] * 2
        + follows(follow),
        out_specs=[vmem] * len(out_shape),
        out_shape=out_shape,
        scratch_shapes=[
            pltpu.VMEM((2, rows, columns), F32),
            pltpu.VMEM((count, 2, depth // count, columns), BF16),
            pltpu.SemaphoreType.DMA((count, 2)),
        ],
        compiler_params=params(EXPAND_MIB),
        cost_estimate=TINY,
        name="expand_last" if last else "expand_first",
    )(*args, *in_hbm, *follow)


def clip_body(ins, outs):
    level = CLIP_SHARE * jnp.max(ins[0][8:, :])
    low = 0
    for part in ins[1:]:
        rows = part.shape[0]
        outs[0][low : low + rows, :] = jnp.clip(part[...].astype(F32), -level, level).astype(BF16)
        low += rows


def down_body(first, me_ref, clipped_ref, weight_hbm, *refs):
    owners = lax.axis_size("tensor")
    half = owners // 2
    *outs, held, loaded = refs[-half - 3 :]
    *others, same_ref = outs
    fc = same_ref.shape[2]
    stride = weight_hbm.shape[1] // owners
    masks = [2 * i + 1 for i in range(half)] + [2 * i for i in range(half)]

    def load(i):
        column = pl.multiple_of((me_ref[0] ^ masks[i]) * stride + first, LANES)
        return pltpu.make_async_copy(
            weight_hbm.at[:, pl.ds(column, fc)],
            held.at[i // 2, :, pl.ds(i % 2 * fc, fc)],
            loaded.at[i],
        )

    loads = [load(i) for i in range(owners)]
    for copy in loads[: 2 * AHEAD]:
        copy.start()
    for pair in range(half):
        for copy in loads[2 * (pair + AHEAD) : 2 * (pair + AHEAD + 1)]:
            copy.start()
        for copy in loads[2 * pair : 2 * pair + 2]:
            copy.wait()
        terms = jnp.dot(clipped_ref[...], held[pair], preferred_element_type=F32).astype(BF16)
        for side in range(2):
            i = 2 * pair + side
            term = terms[:, side * fc : (side + 1) * fc]
            if i < half:
                others[i][0] = term
            else:
                same_ref[i - half] = term


def down(clipped, weight, me, units, first, follow=()):
    depth = weight.shape[0]
    owners = lax.axis_size("tensor")
    half = owners // 2
    rows = clipped.shape[0]
    fc = units * LANES
    vmem = pl.BlockSpec(memory_space=pltpu.VMEM)
    *other, same = pl.pallas_call(
        lambda *refs: down_body(first * LANES, *refs),
        in_specs=[
            pl.BlockSpec(memory_space=pltpu.SMEM),
            vmem,
            pl.BlockSpec(memory_space=pltpu.HBM),
        ]
        + follows(follow),
        out_specs=[vmem] * (half + 1),
        out_shape=[jax.ShapeDtypeStruct((1, rows, fc), BF16)] * half
        + [jax.ShapeDtypeStruct((half, rows, fc), BF16)],
        scratch_shapes=[
            pltpu.VMEM((half, depth, 2 * fc), BF16),
            pltpu.SemaphoreType.DMA((owners,)),
        ],
        compiler_params=params(16),
        cost_estimate=TINY,
        name="down",
    )(me, clipped, pltpu.with_memory_space_constraint(weight, pltpu.HBM), *follow)
    return other, same


def spread_body(count, ids_ref, probs_ref, *refs):
    mine, theirs = refs[:count], refs[count : 2 * count]
    out_ref, mark_ref = refs[-2:]
    mark_ref[...] = jnp.zeros_like(mark_ref)
    tokens = ids_ref.shape[1]
    summed = jnp.concatenate(
        [(a[0].astype(F32) + b[0].astype(F32)).astype(BF16) for a, b in zip(mine, theirs)], axis=0
    )
    slots = slots_of(ids_ref)
    share = jnp.where(ids_ref[0:1, :] == 0, probs_ref[0:1, :], 0.0) + jnp.where(
        ids_ref[1:2, :] == 0, probs_ref[1:2, :], 0.0
    )
    blocks = tokens // LANES
    share = jnp.concatenate(
        [share[:, LANES * k : LANES * (k + 1)] for k in range(blocks)]
        + [jnp.zeros((LANES - blocks, LANES), F32)],
        axis=0,
    ).T
    slots = jnp.concatenate(
        [slots, jnp.zeros((LANES - slots.shape[0], LANES), F32)], axis=0
    ).T.astype(jnp.int32)
    at = iota((LANES, summed.shape[0]), 1)
    for k in range(blocks):
        hot = jnp.where(at == slots[:, k : k + 1], 1.0, 0.0).astype(BF16)
        rows = jnp.dot(hot, summed, preferred_element_type=F32)
        out_ref[LANES * k : LANES * (k + 1), :] = (rows * share[:, k : k + 1]).astype(BF16)


def spread(ids, probs, state, first, features, out, follow=()):
    mine, theirs = [x[0] for x in state], [x[1] for x in state]
    tokens = ids.shape[1]
    count = len(mine)
    _, rows, fc = mine[0].shape
    args = [ids, probs, *mine, *theirs]
    in_specs = [pl.BlockSpec(x.shape, lambda i, d=x.ndim: (0,) * d) for x in args]
    aliases = {}
    if out is not None:
        aliases = {len(args): 0}
        follow = [out, *follow]
    return pl.pallas_call(
        lambda *refs: spread_body(count, *refs[: 2 + 2 * count], *refs[-2:]),
        grid=(1,),
        in_specs=in_specs + follows(follow),
        out_specs=[
            pl.BlockSpec((pl.Element(tokens), pl.Element(fc)), lambda i: (0, first * LANES)),
            pl.BlockSpec((8, LANES), lambda i: (0, 0)),
        ],
        out_shape=[
            jax.ShapeDtypeStruct((tokens, features), BF16),
            jax.ShapeDtypeStruct((8, LANES), F32),
        ],
        input_output_aliases=aliases,
        compiler_params=params(16),
        cost_estimate=TINY,
        name="spread",
    )(*args, *follow)


def follows(arrays):
    return [pl.BlockSpec(memory_space=pl.ANY)] * len(arrays)


def small(body, args, shapes, name, follow=()):
    vmem = pl.BlockSpec(memory_space=pltpu.VMEM)
    count = len(args)
    specs = [pl.BlockSpec(memory_space=pltpu.SMEM) if x.ndim == 1 else vmem for x in args]
    return pl.pallas_call(
        lambda *refs: body(refs[:count], refs[count + len(follow) :]),
        in_specs=specs + follows(follow),
        out_specs=[vmem] * len(shapes),
        out_shape=[jax.ShapeDtypeStruct(*x) for x in shapes],
        compiler_params=params(16),
        cost_estimate=TINY,
        name=name,
    )(*args, *follow)


def gather_near(own, orders):
    return {0: own} | {1 << bit: across(own, bit) for bit in orders[0]}


def cut_body(firsts, ins, outs):
    for h, at in enumerate(firsts):
        rows = outs[h].shape[0]
        outs[h][...] = ins[at][h * rows : (h + 1) * rows, :]
    for block, out in zip(ins, outs[2:]):
        out[...] = block[...]


def join_body(ins, outs):
    for i, out in enumerate(outs):
        rows = out.shape[0] // 2
        out[:rows, :] = ins[2 * i][...]
        out[rows:, :] = ins[2 * i + 1][...]


def cut(full, orders, follow, passed=False):
    rows, width = full[0].shape
    masks = [mask for mask in full if mask]
    firsts = [masks.index(1 << order[0]) for order in orders]
    shapes = [((rows // 2, width), BF16)] * 2 + [((rows, width), BF16)] * len(masks) * passed
    outs = small(
        lambda ins, outs: cut_body(firsts, ins, outs),
        [full[mask] for mask in masks],
        shapes,
        "cut",
        follow,
    )
    return outs[:2], full | dict(zip(masks, outs[2:]))


def gather_far(full, cuts, orders):
    half = full[0].shape[0] // len(orders)
    firsts = [1 << order[0] for order in orders]
    part = {}

    def get(mask, h):
        if (mask, h) in part:
            return part[mask, h]
        return cuts[h] if mask == firsts[h] else full[mask][h * half : (h + 1) * half]

    have = [[0, first] for first in firsts]
    for at in range(1, len(orders[0])):
        for h, order in enumerate(orders):
            bit = order[at]
            for mask in list(have[h]):
                there = mask | 1 << bit
                if there not in full:
                    part[there, h] = across(get(mask, h), bit)
                have[h].append(there)
    return part


def join(part, follow):
    masks = sorted({mask for mask, _ in part})
    halves = [part[mask, h] for mask in masks for h in range(2)]
    half, width = halves[0].shape
    joined = small(join_body, halves, [((2 * half, width), BF16)] * len(masks), "join", follow)
    return dict(zip(masks, joined))


def paired(pieces):
    return pieces | {mask | 1: across(block, 0) for mask, block in pieces.items()}


def turn_body(bits, scale, ins, outs):
    me_ref, ins = ins[0], ins[1:]
    count = len(bits)
    for h, bit in enumerate(bits):
        flip = (1 - 2 * ((me_ref[0] >> bit) & 1)).astype(F32)
        own = ins[2 * h][...].astype(F32)
        came = ins[2 * h + 1][...].astype(F32)
        value = came + own * flip
        if scale is not None:
            value = value * scale
            top = jnp.max(jnp.abs(own) + jnp.abs(came), axis=0, keepdims=True) * scale
            wide = top[:, :LANES]
            for k in range(1, top.shape[1] // LANES):
                wide = jnp.maximum(wide, top[:, k * LANES : (k + 1) * LANES])
            outs[count + h][...] = jnp.broadcast_to(wide, outs[count + h].shape)
        outs[h][...] = value.astype(BF16)


def turn(me, blocks, came, bits, follow=(), scale=None):
    args = [me] + [x for pair in zip(blocks, came) for x in pair]
    shapes = [(x.shape, BF16) for x in blocks]
    if scale is not None:
        shapes += [((8, LANES), F32)] * len(blocks)
    return small(
        lambda ins, outs: turn_body(bits, scale, ins, outs), args, shapes, "turn", follow
    )


def largest(top_in, tops, lasts):
    bits = range(lax.axis_size("tensor").bit_length() - 1)
    values = jnp.concatenate([top_in, *tops], axis=0)
    for bit in bits:
        if bit not in lasts:
            values = jnp.maximum(values, across(values, bit))
    n = top_in.shape[0]
    top_in, first, second = values[:n], values[n : 2 * n], values[2 * n :]
    if lasts[0] != lasts[1]:
        pair = jnp.concatenate([top_in, second], axis=0)
        came_first, came_pair = across(first, lasts[1]), across(pair, lasts[0])
        first = jnp.maximum(first, came_first)
        pair = jnp.maximum(pair, came_pair)
        top_in, second = pair[:n], pair[n:]
    values = jnp.concatenate([top_in, jnp.maximum(first, second)], axis=0)
    blocks = lax.axis_size("dp")
    others = [
        lax.ppermute(values, "dp", [(r, (r + s) % blocks) for r in range(blocks)])
        for s in range(1, blocks)
    ]
    for other in others:
        values = jnp.maximum(values, other)
    return values


def on_device(tokens, expert_ids, gate_probs, gate_weight, up_weight, down_weight):
    count = lax.axis_size("tensor")
    bits = count.bit_length() - 1
    outer = list(range(1, bits))
    orders = [outer, outer[::-1]]
    me = lax.axis_index("tensor")
    me_arr = me.astype(jnp.int32).reshape(1)
    ids, probs = expert_ids.T, gate_probs.T
    rows = CAP // ROW_CHUNKS
    half = rows // 2
    scale = 1.0 / math.sqrt(gate_weight.shape[1] * count)
    stages = [[order[at] for order in orders] for at in range(len(outer))]
    early_bit = stages[-1][1]

    def send(blocks, bits):
        return [across(x, bit) for x, bit in zip(blocks, bits)]

    def start_turn(halves, follow=()):
        blocks = turn(me_arr, halves, send(halves, [0, 0]), [0, 0], follow)
        return blocks, send(blocks, stages[0])

    def go_on(blocks, came, at, follow=()):
        blocks = turn(me_arr, blocks, came, stages[at], follow)
        return blocks, send(blocks, stages[at + 1])

    def end_turn(blocks, came, follow=()):
        made = turn(me_arr, blocks, came, stages[-1], follow, scale)
        return made[: len(blocks)], made[len(blocks) :]

    own_a, top_a = pick_rows(ids, tokens, 0, rows, [me_arr])
    near_a = gather_near(own_a, orders)
    weights = (me_arr, gate_weight, up_weight)
    cuts_a, near_a = cut(near_a, orders, [])
    own_b, top_b = pick_rows(ids, tokens, rows, rows, cuts_a)
    top_in = jnp.maximum(top_a, top_b)
    top_in = jnp.maximum(top_in, across(top_in, early_bit))
    far_a = join(gather_far(near_a, cuts_a, orders), [own_b, top_in])
    near_b = gather_near(own_b, orders)
    parts_a = paired(near_a | far_a)
    parts_a = [parts_a[mask] for mask in range(count)]
    first_a = expand(parts_a, rows, *weights)
    cuts_b, near_b = cut(near_b, orders, first_a, True)
    local_a = expand(parts_a, rows, *weights, *first_a, cuts_b)
    parts_b = paired(near_b)
    theirs_b = [block for mask, block in parts_b.items() if mask & 1]
    far_b = join(gather_far(near_b, cuts_b, orders), list(local_a) + theirs_b)
    parts_b |= paired(far_b)
    parts_b = [parts_b[mask] for mask in range(count)]
    blocks_a, came_a = start_turn(local_a)
    first_b = expand(parts_b, rows, *weights, None, blocks_a)
    for at in range(len(outer) - 1):
        blocks_a, came_a = go_on(blocks_a, came_a, at, first_b)
    local_b = expand(parts_b, rows, *weights, *first_b, blocks_a)
    turned_a, rot_a = end_turn(blocks_a, came_a, local_b)
    blocks_b, came_b = start_turn(local_b, rot_a)
    for at in range(len(outer) - 1):
        blocks_b, came_b = go_on(blocks_b, came_b, at)
    turned_b, rot_b = end_turn(blocks_b, came_b)
    rotated = turned_a + turned_b

    peaks = largest(top_in, [jnp.maximum(x, y) for x, y in zip(rot_a, rot_b)], stages[-1])
    clipped = small(
        clip_body, [peaks, *rotated], [((CAP, gate_weight.shape[1]), BF16)], "clip"
    )[0]

    tops = pl.pallas_call(
        peaks_body,
        out_specs=pl.BlockSpec(memory_space=pltpu.SMEM),
        out_shape=jax.ShapeDtypeStruct((2,), F32),
        name="peaks",
    )(peaks)
    units = tokens.shape[1] // LANES
    sizes = chunks_of(units)
    firsts = [sum(sizes[:i]) for i in range(len(sizes))]
    total = len(sizes)
    def product(chunk, follow=()):
        return down(clipped, down_weight, me_arr, sizes[chunk], firsts[chunk], follow)

    def back(out, chunk):
        return spread(ids, probs, ended[chunk], firsts[chunk], tokens.shape[1], out)

    begun, ended = [], []
    ready = [product(0)]
    for chunk in range(total):
        other, same = ready[chunk]
        came = [across(x, 0) for x in other]
        wait = [keep for keep, _, _ in begun[-1]] if begun else []
        passed = []
        if chunk + 1 < total:
            passed, same_next = product(chunk + 1, [other[0], *wait])
            wait = [same_next]
        if chunk > 0:
            state, passed = finish(begun[-1], stages, wait, passed)
            ended.append(state)
        if chunk + 1 < total:
            ready.append((passed, same_next))
        begun.append(fold_cores(same, came, stages[0], wait))
    out, wait = None, [keep for keep, _, _ in begun[-1]]
    for chunk in range(total):
        if chunk == len(ended):
            ended.append(finish(begun[chunk], stages, wait)[0])
        out, mark = back(out, chunk)
        wait = [mark]
    return out, tops


def chunks_of(units):
    return [2] * (units // 2) + [1] * (units % 2)


def peaks_body(values_ref, out_ref):
    out_ref[0] = jnp.max(values_ref[:8, :])
    out_ref[1] = jnp.max(values_ref[8:, :])


def fold_body(plan, passed, ins, outs):
    for i in range(passed):
        outs[len(plan) + i][...] = ins[len(ins) - passed + i][...]
    for out, (slots, low) in zip(outs, plan):
        rows = out.shape[1]
        for slot, terms in enumerate(slots):
            total = 0.0
            for at, i in terms:
                total = total + ins[at][i, low : low + rows, :].astype(F32)
            out[slot] = total.astype(BF16)


def fold(args, terms, masks, lows, rows, bits, follow, passed=()):
    plan, shapes, lefts = [], [], []
    width = args[0].shape[2]
    for h, bit in enumerate(bits):
        for side in (0, 1):
            chosen = [m for m in masks[h] if m >> bit & 1 == side]
            plan.append(([terms[h][m] for m in chosen], lows[h]))
            shapes.append(((len(chosen), rows, width), BF16))
        lefts.append([m for m in masks[h] if not m >> bit & 1])
    shapes += [(x.shape, x.dtype) for x in passed]
    made = small(
        lambda ins, outs: fold_body(plan, len(passed), ins, outs),
        [*args, *passed],
        shapes,
        "fold",
        follow,
    )
    state = [
        (made[2 * h], across(made[2 * h + 1], bit), lefts[h]) for h, bit in enumerate(bits)
    ]
    return state, made[len(plan) :]


def fold_cores(same, came, bits, follow):
    half = same.shape[1] // 2
    masks = [2 * i for i in range(len(came))]
    terms = {m: ((0, i), (1 + i, 0)) for i, m in enumerate(masks)}
    return fold([same, *came], [terms] * 2, [masks] * 2, [0, half], half, bits, follow)[0]


def finish(state, stages, follow, passed=()):
    for bits in stages[1:]:
        args = [x for keep, recv, _ in state for x in (keep, recv)]
        masks = [left for _, _, left in state]
        terms = [
            {m: ((2 * h, i), (2 * h + 1, i)) for i, m in enumerate(left)}
            for h, left in enumerate(masks)
        ]
        state, passed = fold(
            args, terms, masks, [0, 0], args[0].shape[1], bits, follow, passed
        )
    return state, passed


def solution(mesh):
    in_specs = (
        P("dp", "tensor"),
        P("dp", None),
        P("dp", None),
        P(None, "tensor"),
        P(None, "tensor"),
        P("tensor", None),
    )
    out_specs = (P("dp", "tensor"), P())
    return jax.shard_map(
        on_device, mesh=mesh, in_specs=in_specs, out_specs=out_specs, check_vma=False
    )
```

```python
import math

import jax
import jax.numpy as jnp
from jax import lax
from jax.experimental import pallas as pl
from jax.experimental.pallas import tpu as pltpu
from jax.sharding import PartitionSpec as P

CAP = 768
CLIP_SHARE = 0.25
LANES = 128
ROW_CHUNKS = 2
BF16 = jnp.bfloat16
F32 = jnp.float32
MIB = 1 << 20
EXPAND_MIB = 24
AHEAD = 3


def params(mib):
    return pltpu.CompilerParams(vmem_limit_bytes=mib * MIB)


TINY = pl.CostEstimate(flops=1, bytes_accessed=1, transcendentals=0)


def across(block, bit):
    count = lax.axis_size("tensor")
    return lax.ppermute(block, "tensor", [(r, r ^ 1 << bit) for r in range(count)])


def iota(shape, dim):
    return lax.broadcasted_iota(jnp.int32, shape, dim)


def slots_of(ids_ref):
    tokens = ids_ref.shape[1]
    rows = tokens // LANES
    padded = (rows + 15) // 16 * 16
    hit = jnp.where((ids_ref[0:1, :] == 0) | (ids_ref[1:2, :] == 0), 1.0, 0.0)
    grid = jnp.concatenate(
        [hit[:, LANES * k : LANES * (k + 1)] for k in range(rows)]
        + [jnp.zeros((padded - rows, LANES), F32)],
        axis=0,
    )
    flat = grid.astype(BF16)
    upto = (iota((LANES, LANES), 0) <= iota((LANES, LANES), 1)).astype(F32).astype(BF16)
    before = (iota((padded, padded), 1) < iota((padded, padded), 0)).astype(F32).astype(BF16)
    within = jnp.dot(flat, upto, preferred_element_type=F32)
    offset = jnp.sum(jnp.dot(before, flat, preferred_element_type=F32), axis=1, keepdims=True)
    return jnp.where(grid > 0.0, within + offset - 1.0, -1.0)


def pick_body(first, ids_hbm, tokens_hbm, *refs):
    picked_ref, peak_ref, ids_ref, tokens_ref, loaded = refs[-5:]
    rows = picked_ref.shape[0]
    count = tokens_ref.shape[0]
    pieces = loaded.shape[0] - 1
    step = count // pieces
    ids_copy = pltpu.make_async_copy(ids_hbm, ids_ref, loaded.at[pieces])
    ids_copy.start()
    copies = [
        pltpu.make_async_copy(
            tokens_hbm.at[pl.ds(i * step, step), :],
            tokens_ref.at[pl.ds(i * step, step), :],
            loaded.at[i],
        )
        for i in range(pieces)
    ]
    for copy in copies:
        copy.start()
    ids_copy.wait()
    slots = slots_of(ids_ref).astype(jnp.int32)
    wanted = iota((rows, LANES), 0) + first
    picked = jnp.zeros(picked_ref.shape, F32)
    for i, copy in enumerate(copies):
        hot = jnp.concatenate(
            [
                jnp.where(wanted == slots[k : k + 1, :], 1.0, 0.0).astype(BF16)
                for k in range(i * step // LANES, (i + 1) * step // LANES)
            ],
            axis=1,
        )
        copy.wait()
        picked += jnp.dot(
            hot, tokens_ref[i * step : (i + 1) * step, :], preferred_element_type=F32
        )
    picked_ref[...] = picked.astype(BF16)
    peak_ref[...] = jnp.broadcast_to(jnp.max(jnp.abs(picked)), peak_ref.shape)


def pick_rows(ids, tokens, first, rows, follow=()):
    count, width = tokens.shape
    blocks = count // LANES
    pieces = math.gcd(blocks, 4)
    in_hbm = [pltpu.with_memory_space_constraint(x, pltpu.HBM) for x in (ids, tokens)]
    return pl.pallas_call(
        lambda *refs: pick_body(first, *refs),
        out_shape=(
            jax.ShapeDtypeStruct((rows, width), BF16),
            jax.ShapeDtypeStruct((8, LANES), F32),
        ),
        in_specs=[pl.BlockSpec(memory_space=pltpu.HBM)] * 2 + follows(follow),
        out_specs=[pl.BlockSpec(memory_space=pltpu.VMEM)] * 2,
        scratch_shapes=[
            pltpu.VMEM(ids.shape, ids.dtype),
            pltpu.VMEM(tokens.shape, tokens.dtype),
            pltpu.SemaphoreType.DMA((pieces + 1,)),
        ],
        compiler_params=params(16),
        cost_estimate=TINY,
        name="pick_rows",
    )(*in_hbm, *follow)


def signs(size):
    common = iota((size, size), 0) & iota((size, size), 1)
    shift = 1
    while shift < size.bit_length():
        shift *= 2
    while shift > 1:
        shift //= 2
        common = common ^ (common >> shift)
    return (1 - 2 * (common & 1)).astype(F32).astype(BF16)


def expand_body(first, count, last, me_ref, *refs):
    parts, refs = refs[:count], refs[count:]
    before_ref = None
    if last:
        before_ref, refs = refs[0], refs[1:]
    gate_hbm, up_hbm, *outs, total, held, loaded = refs
    width = parts[0].shape[1]
    columns = total.shape[2]
    tile = min(256, columns)

    def load(mask):
        rows = pl.ds(pl.multiple_of((me_ref[0] ^ mask) * width, LANES), width)
        return [
            pltpu.make_async_copy(
                weight.at[rows, pl.ds(first, columns)], held.at[mask, at], loaded.at[mask, at]
            )
            for at, weight in enumerate((gate_hbm, up_hbm))
        ]

    loads = [load(mask) for mask in range(count)]
    for copies in loads[:AHEAD]:
        for copy in copies:
            copy.start()
    table = signs(tile)
    for mask, part in enumerate(parts):
        for copies in loads[mask + AHEAD : mask + AHEAD + 1]:
            for copy in copies:
                copy.start()
        for at in range(2):
            loads[mask][at].wait()
            term = jnp.dot(part[...], held[mask, at], preferred_element_type=F32)
            if mask == 0:
                total[at] = term
            else:
                total[at] += term
    values = []
    for i in range(columns // tile):
        gate = total[0, :, i * tile : (i + 1) * tile]
        up = total[1, :, i * tile : (i + 1) * tile]
        hidden = (gate * (1.0 / (1.0 + jnp.exp(-gate))) * up).astype(BF16)
        values.append(jnp.dot(hidden, table, preferred_element_type=F32))
        if not last:
            outs[0][i] = values[i]
    if not last:
        return
    values = [before_ref[i] for i in range(before_ref.shape[0])] + values
    steps = len(values)
    gap = 1
    while gap < steps:
        values = [
            values[i] + values[i ^ gap] if not i & gap else values[i ^ gap] - values[i]
            for i in range(steps)
        ]
        gap *= 2
    for i in range(steps):
        low = 0
        for out in outs:
            rows = out.shape[0]
            out[:, i * tile : (i + 1) * tile] = values[i][low : low + rows].astype(BF16)
            low += rows


def expand(parts, rows, me, gate_weight, up_weight, before=None, follow=()):
    depth, width = gate_weight.shape
    last = before is not None
    columns = width // 2
    first = columns if last else 0
    tile = min(256, columns)
    count = len(parts)
    vmem = pl.BlockSpec(memory_space=pltpu.VMEM)
    in_hbm = [pltpu.with_memory_space_constraint(x, pltpu.HBM) for x in (gate_weight, up_weight)]
    args = [me, *parts] + ([before] if last else [])
    used = len(args) + 2
    if last:
        out_shape = [jax.ShapeDtypeStruct((rows // 2, width), BF16)] * 2
    else:
        out_shape = [jax.ShapeDtypeStruct((columns // tile, rows, tile), F32)]
    return pl.pallas_call(
        lambda *refs: expand_body(first, count, last, *refs[:used], *refs[used + len(follow) :]),
        in_specs=[pl.BlockSpec(memory_space=pltpu.SMEM)]
        + [vmem] * (used - 3)
        + [pl.BlockSpec(memory_space=pltpu.HBM)] * 2
        + follows(follow),
        out_specs=[vmem] * len(out_shape),
        out_shape=out_shape,
        scratch_shapes=[
            pltpu.VMEM((2, rows, columns), F32),
            pltpu.VMEM((count, 2, depth // count, columns), BF16),
            pltpu.SemaphoreType.DMA((count, 2)),
        ],
        compiler_params=params(EXPAND_MIB),
        cost_estimate=TINY,
        name="expand_last" if last else "expand_first",
    )(*args, *in_hbm, *follow)


def clip_body(ins, outs):
    level = CLIP_SHARE * jnp.max(ins[0][8:, :])
    low = 0
    for part in ins[1:]:
        rows = part.shape[0]
        outs[0][low : low + rows, :] = jnp.clip(part[...].astype(F32), -level, level).astype(BF16)
        low += rows


def down_body(first, me_ref, clipped_ref, weight_hbm, *refs):
    owners = lax.axis_size("tensor")
    half = owners // 2
    *outs, held, loaded = refs[-half - 3 :]
    *others, same_ref = outs
    fc = same_ref.shape[2]
    stride = weight_hbm.shape[1] // owners
    masks = [2 * i + 1 for i in range(half)] + [2 * i for i in range(half)]

    def load(i):
        column = pl.multiple_of((me_ref[0] ^ masks[i]) * stride + first, LANES)
        return pltpu.make_async_copy(
            weight_hbm.at[:, pl.ds(column, fc)],
            held.at[i // 2, :, pl.ds(i % 2 * fc, fc)],
            loaded.at[i],
        )

    loads = [load(i) for i in range(owners)]
    for copy in loads[: 2 * AHEAD]:
        copy.start()
    for pair in range(half):
        for copy in loads[2 * (pair + AHEAD) : 2 * (pair + AHEAD + 1)]:
            copy.start()
        for copy in loads[2 * pair : 2 * pair + 2]:
            copy.wait()
        terms = jnp.dot(clipped_ref[...], held[pair], preferred_element_type=F32).astype(BF16)
        for side in range(2):
            i = 2 * pair + side
            term = terms[:, side * fc : (side + 1) * fc]
            if i < half:
                others[i][0] = term
            else:
                same_ref[i - half] = term


def down(clipped, weight, me, units, first, follow=()):
    depth = weight.shape[0]
    owners = lax.axis_size("tensor")
    half = owners // 2
    rows = clipped.shape[0]
    fc = units * LANES
    vmem = pl.BlockSpec(memory_space=pltpu.VMEM)
    *other, same = pl.pallas_call(
        lambda *refs: down_body(first * LANES, *refs),
        in_specs=[
            pl.BlockSpec(memory_space=pltpu.SMEM),
            vmem,
            pl.BlockSpec(memory_space=pltpu.HBM),
        ]
        + follows(follow),
        out_specs=[vmem] * (half + 1),
        out_shape=[jax.ShapeDtypeStruct((1, rows, fc), BF16)] * half
        + [jax.ShapeDtypeStruct((half, rows, fc), BF16)],
        scratch_shapes=[
            pltpu.VMEM((half, depth, 2 * fc), BF16),
            pltpu.SemaphoreType.DMA((owners,)),
        ],
        compiler_params=params(16),
        cost_estimate=TINY,
        name="down",
    )(me, clipped, pltpu.with_memory_space_constraint(weight, pltpu.HBM), *follow)
    return other, same


def spread_body(count, ids_ref, probs_ref, *refs):
    mine, theirs = refs[:count], refs[count : 2 * count]
    out_ref, mark_ref = refs[-2:]
    mark_ref[...] = jnp.zeros_like(mark_ref)
    tokens = ids_ref.shape[1]
    summed = jnp.concatenate(
        [(a[0].astype(F32) + b[0].astype(F32)).astype(BF16) for a, b in zip(mine, theirs)], axis=0
    )
    slots = slots_of(ids_ref)
    share = jnp.where(ids_ref[0:1, :] == 0, probs_ref[0:1, :], 0.0) + jnp.where(
        ids_ref[1:2, :] == 0, probs_ref[1:2, :], 0.0
    )
    blocks = tokens // LANES
    share = jnp.concatenate(
        [share[:, LANES * k : LANES * (k + 1)] for k in range(blocks)]
        + [jnp.zeros((LANES - blocks, LANES), F32)],
        axis=0,
    ).T
    slots = jnp.concatenate(
        [slots, jnp.zeros((LANES - slots.shape[0], LANES), F32)], axis=0
    ).T.astype(jnp.int32)
    at = iota((LANES, summed.shape[0]), 1)
    for k in range(blocks):
        hot = jnp.where(at == slots[:, k : k + 1], 1.0, 0.0).astype(BF16)
        rows = jnp.dot(hot, summed, preferred_element_type=F32)
        out_ref[LANES * k : LANES * (k + 1), :] = (rows * share[:, k : k + 1]).astype(BF16)


def spread(ids, probs, state, first, features, out, follow=()):
    mine, theirs = [x[0] for x in state], [x[1] for x in state]
    tokens = ids.shape[1]
    count = len(mine)
    _, rows, fc = mine[0].shape
    args = [ids, probs, *mine, *theirs]
    in_specs = [pl.BlockSpec(x.shape, lambda i, d=x.ndim: (0,) * d) for x in args]
    aliases = {}
    if out is not None:
        aliases = {len(args): 0}
        follow = [out, *follow]
    return pl.pallas_call(
        lambda *refs: spread_body(count, *refs[: 2 + 2 * count], *refs[-2:]),
        grid=(1,),
        in_specs=in_specs + follows(follow),
        out_specs=[
            pl.BlockSpec((pl.Element(tokens), pl.Element(fc)), lambda i: (0, first * LANES)),
            pl.BlockSpec((8, LANES), lambda i: (0, 0)),
        ],
        out_shape=[
            jax.ShapeDtypeStruct((tokens, features), BF16),
            jax.ShapeDtypeStruct((8, LANES), F32),
        ],
        input_output_aliases=aliases,
        compiler_params=params(16),
        cost_estimate=TINY,
        name="spread",
    )(*args, *follow)


def follows(arrays):
    return [pl.BlockSpec(memory_space=pl.ANY)] * len(arrays)


def small(body, args, shapes, name, follow=()):
    vmem = pl.BlockSpec(memory_space=pltpu.VMEM)
    count = len(args)
    specs = [pl.BlockSpec(memory_space=pltpu.SMEM) if x.ndim == 1 else vmem for x in args]
    return pl.pallas_call(
        lambda *refs: body(refs[:count], refs[count + len(follow) :]),
        in_specs=specs + follows(follow),
        out_specs=[vmem] * len(shapes),
        out_shape=[jax.ShapeDtypeStruct(*x) for x in shapes],
        compiler_params=params(16),
        cost_estimate=TINY,
        name=name,
    )(*args, *follow)


def gather_near(own, orders):
    return {0: own} | {1 << bit: across(own, bit) for bit in orders[0]}


def cut_body(firsts, ins, outs):
    for h, at in enumerate(firsts):
        rows = outs[h].shape[0]
        outs[h][...] = ins[at][h * rows : (h + 1) * rows, :]
    for block, out in zip(ins, outs[2:]):
        out[...] = block[...]


def join_body(ins, outs):
    for i, out in enumerate(outs):
        rows = out.shape[0] // 2
        out[:rows, :] = ins[2 * i][...]
        out[rows:, :] = ins[2 * i + 1][...]


def cut(full, orders, follow, passed=False):
    rows, width = full[0].shape
    masks = [mask for mask in full if mask]
    firsts = [masks.index(1 << order[0]) for order in orders]
    shapes = [((rows // 2, width), BF16)] * 2 + [((rows, width), BF16)] * len(masks) * passed
    outs = small(
        lambda ins, outs: cut_body(firsts, ins, outs),
        [full[mask] for mask in masks],
        shapes,
        "cut",
        follow,
    )
    return outs[:2], full | dict(zip(masks, outs[2:]))


def gather_far(full, cuts, orders):
    half = full[0].shape[0] // len(orders)
    firsts = [1 << order[0] for order in orders]
    part = {}

    def get(mask, h):
        if (mask, h) in part:
            return part[mask, h]
        return cuts[h] if mask == firsts[h] else full[mask][h * half : (h + 1) * half]

    have = [[0, first] for first in firsts]
    for at in range(1, len(orders[0])):
        for h, order in enumerate(orders):
            bit = order[at]
            for mask in list(have[h]):
                there = mask | 1 << bit
                if there not in full:
                    part[there, h] = across(get(mask, h), bit)
                have[h].append(there)
    return part


def join(part, follow):
    masks = sorted({mask for mask, _ in part})
    halves = [part[mask, h] for mask in masks for h in range(2)]
    half, width = halves[0].shape
    joined = small(join_body, halves, [((2 * half, width), BF16)] * len(masks), "join", follow)
    return dict(zip(masks, joined))


def paired(pieces):
    return pieces | {mask | 1: across(block, 0) for mask, block in pieces.items()}


def turn_body(bits, scale, ins, outs):
    me_ref, ins = ins[0], ins[1:]
    count = len(bits)
    for h, bit in enumerate(bits):
        flip = (1 - 2 * ((me_ref[0] >> bit) & 1)).astype(F32)
        own = ins[2 * h][...].astype(F32)
        came = ins[2 * h + 1][...].astype(F32)
        value = came + own * flip
        if scale is not None:
            value = value * scale
            top = jnp.max(jnp.abs(own) + jnp.abs(came), axis=0, keepdims=True) * scale
            wide = top[:, :LANES]
            for k in range(1, top.shape[1] // LANES):
                wide = jnp.maximum(wide, top[:, k * LANES : (k + 1) * LANES])
            outs[count + h][...] = jnp.broadcast_to(wide, outs[count + h].shape)
        outs[h][...] = value.astype(BF16)


def turn(me, blocks, came, bits, follow=(), scale=None):
    args = [me] + [x for pair in zip(blocks, came) for x in pair]
    shapes = [(x.shape, BF16) for x in blocks]
    if scale is not None:
        shapes += [((8, LANES), F32)] * len(blocks)
    return small(
        lambda ins, outs: turn_body(bits, scale, ins, outs), args, shapes, "turn", follow
    )


def largest(top_in, tops, lasts):
    bits = range(lax.axis_size("tensor").bit_length() - 1)
    values = jnp.concatenate([top_in, *tops], axis=0)
    for bit in bits:
        if bit not in lasts:
            values = jnp.maximum(values, across(values, bit))
    n = top_in.shape[0]
    top_in, first, second = values[:n], values[n : 2 * n], values[2 * n :]
    if lasts[0] != lasts[1]:
        pair = jnp.concatenate([top_in, second], axis=0)
        came_first, came_pair = across(first, lasts[1]), across(pair, lasts[0])
        first = jnp.maximum(first, came_first)
        pair = jnp.maximum(pair, came_pair)
        top_in, second = pair[:n], pair[n:]
    values = jnp.concatenate([top_in, jnp.maximum(first, second)], axis=0)
    blocks = lax.axis_size("dp")
    far = 1
    while far < blocks:
        pairs = [(r, r ^ far) for r in range(blocks)]
        values = jnp.maximum(values, lax.ppermute(values, "dp", pairs))
        far *= 2
    return values


def on_device(tokens, expert_ids, gate_probs, gate_weight, up_weight, down_weight):
    count = lax.axis_size("tensor")
    bits = count.bit_length() - 1
    outer = list(range(1, bits))
    orders = [outer, outer[::-1]]
    me = lax.axis_index("tensor")
    me_arr = me.astype(jnp.int32).reshape(1)
    ids, probs = expert_ids.T, gate_probs.T
    rows = CAP // ROW_CHUNKS
    half = rows // 2
    scale = 1.0 / math.sqrt(gate_weight.shape[1] * count)
    stages = [[order[at] for order in orders] for at in range(len(outer))]
    early_bit = stages[-1][1]

    def send(blocks, bits):
        return [across(x, bit) for x, bit in zip(blocks, bits)]

    def start_turn(halves, follow=()):
        blocks = turn(me_arr, halves, send(halves, [0, 0]), [0, 0], follow)
        return blocks, send(blocks, stages[0])

    def go_on(blocks, came, at, follow=()):
        blocks = turn(me_arr, blocks, came, stages[at], follow)
        return blocks, send(blocks, stages[at + 1])

    def end_turn(blocks, came, follow=()):
        made = turn(me_arr, blocks, came, stages[-1], follow, scale)
        return made[: len(blocks)], made[len(blocks) :]

    own_a, top_a = pick_rows(ids, tokens, 0, rows, [me_arr])
    near_a = gather_near(own_a, orders)
    weights = (me_arr, gate_weight, up_weight)
    cuts_a, near_a = cut(near_a, orders, [])
    own_b, top_b = pick_rows(ids, tokens, rows, rows, cuts_a)
    top_in = jnp.maximum(top_a, top_b)
    top_in = jnp.maximum(top_in, across(top_in, early_bit))
    far_a = join(gather_far(near_a, cuts_a, orders), [own_b, top_in])
    near_b = gather_near(own_b, orders)
    parts_a = paired(near_a | far_a)
    parts_a = [parts_a[mask] for mask in range(count)]
    first_a = expand(parts_a, rows, *weights)
    cuts_b, near_b = cut(near_b, orders, first_a, True)
    local_a = expand(parts_a, rows, *weights, *first_a, cuts_b)
    parts_b = paired(near_b)
    theirs_b = [block for mask, block in parts_b.items() if mask & 1]
    far_b = join(gather_far(near_b, cuts_b, orders), list(local_a) + theirs_b)
    parts_b |= paired(far_b)
    parts_b = [parts_b[mask] for mask in range(count)]
    blocks_a, came_a = start_turn(local_a)
    first_b = expand(parts_b, rows, *weights, None, blocks_a)
    for at in range(len(outer) - 1):
        blocks_a, came_a = go_on(blocks_a, came_a, at, first_b)
    local_b = expand(parts_b, rows, *weights, *first_b, blocks_a)
    turned_a, rot_a = end_turn(blocks_a, came_a, local_b)
    blocks_b, came_b = start_turn(local_b, rot_a)
    for at in range(len(outer) - 1):
        blocks_b, came_b = go_on(blocks_b, came_b, at)
    turned_b, rot_b = end_turn(blocks_b, came_b)
    rotated = turned_a + turned_b

    peaks = largest(top_in, [jnp.maximum(x, y) for x, y in zip(rot_a, rot_b)], stages[-1])
    clipped = small(
        clip_body, [peaks, *rotated], [((CAP, gate_weight.shape[1]), BF16)], "clip"
    )[0]

    tops = pl.pallas_call(
        peaks_body,
        out_specs=pl.BlockSpec(memory_space=pltpu.SMEM),
        out_shape=jax.ShapeDtypeStruct((2,), F32),
        name="peaks",
    )(peaks)
    units = tokens.shape[1] // LANES
    sizes = chunks_of(units)
    firsts = [sum(sizes[:i]) for i in range(len(sizes))]
    total = len(sizes)
    def product(chunk, follow=()):
        return down(clipped, down_weight, me_arr, sizes[chunk], firsts[chunk], follow)

    def back(out, chunk):
        return spread(ids, probs, ended[chunk], firsts[chunk], tokens.shape[1], out)

    begun, ended = [], []
    ready = [product(0)]
    for chunk in range(total):
        other, same = ready[chunk]
        came = [across(x, 0) for x in other]
        wait = [keep for keep, _, _ in begun[-1]] if begun else []
        passed = []
        if chunk + 1 < total:
            passed, same_next = product(chunk + 1, [other[0], *wait])
            wait = [same_next]
        if chunk > 0:
            state, passed = finish(begun[-1], stages, wait, passed)
            ended.append(state)
        if chunk + 1 < total:
            ready.append((passed, same_next))
        begun.append(fold_cores(same, came, stages[0], wait))
    out, marks = None, []
    for chunk in range(total):
        if chunk == len(ended):
            wait = marks[-1:] if chunk > 1 else [keep for keep, _, _ in begun[-1]]
            ended.append(finish(begun[chunk], stages, wait)[0])
        if chunk > 0:
            out, mark = back(out, chunk - 1)
            marks.append(mark)
    out, _ = back(out, total - 1)
    return out, tops


def chunks_of(units):
    return [2] * (units // 2) + [1] * (units % 2)


def peaks_body(values_ref, out_ref):
    out_ref[0] = jnp.max(values_ref[:8, :])
    out_ref[1] = jnp.max(values_ref[8:, :])


def fold_body(plan, passed, ins, outs):
    for i in range(passed):
        outs[len(plan) + i][...] = ins[len(ins) - passed + i][...]
    for out, (slots, low) in zip(outs, plan):
        rows = out.shape[1]
        for slot, terms in enumerate(slots):
            total = 0.0
            for at, i in terms:
                total = total + ins[at][i, low : low + rows, :].astype(F32)
            out[slot] = total.astype(BF16)


def fold(args, terms, masks, lows, rows, bits, follow, passed=()):
    plan, shapes, lefts = [], [], []
    width = args[0].shape[2]
    for h, bit in enumerate(bits):
        for side in (0, 1):
            chosen = [m for m in masks[h] if m >> bit & 1 == side]
            plan.append(([terms[h][m] for m in chosen], lows[h]))
            shapes.append(((len(chosen), rows, width), BF16))
        lefts.append([m for m in masks[h] if not m >> bit & 1])
    shapes += [(x.shape, x.dtype) for x in passed]
    made = small(
        lambda ins, outs: fold_body(plan, len(passed), ins, outs),
        [*args, *passed],
        shapes,
        "fold",
        follow,
    )
    state = [
        (made[2 * h], across(made[2 * h + 1], bit), lefts[h]) for h, bit in enumerate(bits)
    ]
    return state, made[len(plan) :]


def fold_cores(same, came, bits, follow):
    half = same.shape[1] // 2
    masks = [2 * i for i in range(len(came))]
    terms = {m: ((0, i), (1 + i, 0)) for i, m in enumerate(masks)}
    return fold([same, *came], [terms] * 2, [masks] * 2, [0, half], half, bits, follow)[0]


def finish(state, stages, follow, passed=()):
    for bits in stages[1:]:
        args = [x for keep, recv, _ in state for x in (keep, recv)]
        masks = [left for _, _, left in state]
        terms = [
            {m: ((2 * h, i), (2 * h + 1, i)) for i, m in enumerate(left)}
            for h, left in enumerate(masks)
        ]
        state, passed = fold(
            args, terms, masks, [0, 0], args[0].shape[1], bits, follow, passed
        )
    return state, passed


def solution(mesh):
    in_specs = (
        P("dp", "tensor"),
        P("dp", None),
        P("dp", None),
        P(None, "tensor"),
        P(None, "tensor"),
        P("tensor", None),
    )
    out_specs = (P("dp", "tensor"), P())
    return jax.shard_map(
        on_device, mesh=mesh, in_specs=in_specs, out_specs=out_specs, check_vma=False
    )
```

```python
import math

import jax
import jax.numpy as jnp
from jax import lax
from jax.experimental import pallas as pl
from jax.experimental.pallas import tpu as pltpu
from jax.sharding import PartitionSpec as P

CAP = 768
CLIP_SHARE = 0.25
LANES = 128
ROW_CHUNKS = 2
BF16 = jnp.bfloat16
F32 = jnp.float32
MIB = 1 << 20
EXPAND_MIB = 24
AHEAD = 3


def params(mib):
    return pltpu.CompilerParams(vmem_limit_bytes=mib * MIB)


TINY = pl.CostEstimate(flops=1, bytes_accessed=1, transcendentals=0)


def across(block, bit):
    count = lax.axis_size("tensor")
    return lax.ppermute(block, "tensor", [(r, r ^ 1 << bit) for r in range(count)])


def iota(shape, dim):
    return lax.broadcasted_iota(jnp.int32, shape, dim)


def slots_of(ids_ref):
    tokens = ids_ref.shape[1]
    rows = tokens // LANES
    padded = (rows + 15) // 16 * 16
    hit = jnp.where((ids_ref[0:1, :] == 0) | (ids_ref[1:2, :] == 0), 1.0, 0.0)
    grid = jnp.concatenate(
        [hit[:, LANES * k : LANES * (k + 1)] for k in range(rows)]
        + [jnp.zeros((padded - rows, LANES), F32)],
        axis=0,
    )
    flat = grid.astype(BF16)
    upto = (iota((LANES, LANES), 0) <= iota((LANES, LANES), 1)).astype(F32).astype(BF16)
    before = (iota((padded, padded), 1) < iota((padded, padded), 0)).astype(F32).astype(BF16)
    within = jnp.dot(flat, upto, preferred_element_type=F32)
    offset = jnp.sum(jnp.dot(before, flat, preferred_element_type=F32), axis=1, keepdims=True)
    return jnp.where(grid > 0.0, within + offset - 1.0, -1.0)


def pick_body(first, ids_hbm, tokens_hbm, *refs):
    picked_ref, peak_ref, ids_ref, tokens_ref, loaded = refs[-5:]
    rows = picked_ref.shape[0]
    count = tokens_ref.shape[0]
    pieces = loaded.shape[0] - 1
    step = count // pieces
    ids_copy = pltpu.make_async_copy(ids_hbm, ids_ref, loaded.at[pieces])
    ids_copy.start()
    copies = [
        pltpu.make_async_copy(
            tokens_hbm.at[pl.ds(i * step, step), :],
            tokens_ref.at[pl.ds(i * step, step), :],
            loaded.at[i],
        )
        for i in range(pieces)
    ]
    for copy in copies:
        copy.start()
    ids_copy.wait()
    slots = slots_of(ids_ref).astype(jnp.int32)
    wanted = iota((rows, LANES), 0) + first
    picked = jnp.zeros(picked_ref.shape, F32)
    for i, copy in enumerate(copies):
        hot = jnp.concatenate(
            [
                jnp.where(wanted == slots[k : k + 1, :], 1.0, 0.0).astype(BF16)
                for k in range(i * step // LANES, (i + 1) * step // LANES)
            ],
            axis=1,
        )
        copy.wait()
        picked += jnp.dot(
            hot, tokens_ref[i * step : (i + 1) * step, :], preferred_element_type=F32
        )
    picked_ref[...] = picked.astype(BF16)
    peak_ref[...] = jnp.broadcast_to(jnp.max(jnp.abs(picked)), peak_ref.shape)


def pick_rows(ids, tokens, first, rows, follow=()):
    count, width = tokens.shape
    blocks = count // LANES
    pieces = math.gcd(blocks, 4)
    in_hbm = [pltpu.with_memory_space_constraint(x, pltpu.HBM) for x in (ids, tokens)]
    return pl.pallas_call(
        lambda *refs: pick_body(first, *refs),
        out_shape=(
            jax.ShapeDtypeStruct((rows, width), BF16),
            jax.ShapeDtypeStruct((8, LANES), F32),
        ),
        in_specs=[pl.BlockSpec(memory_space=pltpu.HBM)] * 2 + follows(follow),
        out_specs=[pl.BlockSpec(memory_space=pltpu.VMEM)] * 2,
        scratch_shapes=[
            pltpu.VMEM(ids.shape, ids.dtype),
            pltpu.VMEM(tokens.shape, tokens.dtype),
            pltpu.SemaphoreType.DMA((pieces + 1,)),
        ],
        compiler_params=params(16),
        cost_estimate=TINY,
        name="pick_rows",
    )(*in_hbm, *follow)


def signs(size):
    common = iota((size, size), 0) & iota((size, size), 1)
    shift = 1
    while shift < size.bit_length():
        shift *= 2
    while shift > 1:
        shift //= 2
        common = common ^ (common >> shift)
    return (1 - 2 * (common & 1)).astype(F32).astype(BF16)


def expand_body(first, count, last, me_ref, *refs):
    parts, refs = refs[:count], refs[count:]
    before_ref = None
    if last:
        before_ref, refs = refs[0], refs[1:]
    gate_hbm, up_hbm, *outs, total, held, loaded = refs
    width = parts[0].shape[1]
    columns = total.shape[2]
    tile = min(256, columns)

    def load(mask):
        rows = pl.ds(pl.multiple_of((me_ref[0] ^ mask) * width, LANES), width)
        return [
            pltpu.make_async_copy(
                weight.at[rows, pl.ds(first, columns)], held.at[mask, at], loaded.at[mask, at]
            )
            for at, weight in enumerate((gate_hbm, up_hbm))
        ]

    loads = [load(mask) for mask in range(count)]
    for copies in loads[:AHEAD]:
        for copy in copies:
            copy.start()
    table = signs(tile)
    for mask, part in enumerate(parts):
        for copies in loads[mask + AHEAD : mask + AHEAD + 1]:
            for copy in copies:
                copy.start()
        for at in range(2):
            loads[mask][at].wait()
            term = jnp.dot(part[...], held[mask, at], preferred_element_type=F32)
            if mask == 0:
                total[at] = term
            else:
                total[at] += term
    values = []
    for i in range(columns // tile):
        gate = total[0, :, i * tile : (i + 1) * tile]
        up = total[1, :, i * tile : (i + 1) * tile]
        hidden = (gate * (1.0 / (1.0 + jnp.exp(-gate))) * up).astype(BF16)
        values.append(jnp.dot(hidden, table, preferred_element_type=F32))
        if not last:
            outs[0][i] = values[i]
    if not last:
        return
    values = [before_ref[i] for i in range(before_ref.shape[0])] + values
    steps = len(values)
    gap = 1
    while gap < steps:
        values = [
            values[i] + values[i ^ gap] if not i & gap else values[i ^ gap] - values[i]
            for i in range(steps)
        ]
        gap *= 2
    for i in range(steps):
        low = 0
        for out in outs:
            rows = out.shape[0]
            out[:, i * tile : (i + 1) * tile] = values[i][low : low + rows].astype(BF16)
            low += rows


def expand(parts, rows, me, gate_weight, up_weight, before=None, follow=()):
    depth, width = gate_weight.shape
    last = before is not None
    columns = width // 2
    first = columns if last else 0
    tile = min(256, columns)
    count = len(parts)
    vmem = pl.BlockSpec(memory_space=pltpu.VMEM)
    in_hbm = [pltpu.with_memory_space_constraint(x, pltpu.HBM) for x in (gate_weight, up_weight)]
    args = [me, *parts] + ([before] if last else [])
    used = len(args) + 2
    if last:
        out_shape = [jax.ShapeDtypeStruct((rows // 2, width), BF16)] * 2
    else:
        out_shape = [jax.ShapeDtypeStruct((columns // tile, rows, tile), F32)]
    return pl.pallas_call(
        lambda *refs: expand_body(first, count, last, *refs[:used], *refs[used + len(follow) :]),
        in_specs=[pl.BlockSpec(memory_space=pltpu.SMEM)]
        + [vmem] * (used - 3)
        + [pl.BlockSpec(memory_space=pltpu.HBM)] * 2
        + follows(follow),
        out_specs=[vmem] * len(out_shape),
        out_shape=out_shape,
        scratch_shapes=[
            pltpu.VMEM((2, rows, columns), F32),
            pltpu.VMEM((count, 2, depth // count, columns), BF16),
            pltpu.SemaphoreType.DMA((count, 2)),
        ],
        compiler_params=params(EXPAND_MIB),
        cost_estimate=TINY,
        name="expand_last" if last else "expand_first",
    )(*args, *in_hbm, *follow)


def clip_body(ins, outs):
    level = CLIP_SHARE * jnp.max(ins[0][8:, :])
    low = 0
    for part in ins[1:]:
        rows = part.shape[0]
        outs[0][low : low + rows, :] = jnp.clip(part[...].astype(F32), -level, level).astype(BF16)
        low += rows


def down_body(first, me_ref, clipped_ref, weight_hbm, *refs):
    owners = lax.axis_size("tensor")
    half = owners // 2
    other_ref, same_ref, held, loaded = refs[-4:]
    fc = same_ref.shape[2]
    stride = weight_hbm.shape[1] // owners
    masks = [2 * i + 1 for i in range(half)] + [2 * i for i in range(half)]

    def load(i):
        column = pl.multiple_of((me_ref[0] ^ masks[i]) * stride + first, LANES)
        return pltpu.make_async_copy(
            weight_hbm.at[:, pl.ds(column, fc)],
            held.at[i // 2, :, pl.ds(i % 2 * fc, fc)],
            loaded.at[i],
        )

    loads = [load(i) for i in range(owners)]
    for copy in loads[: 2 * AHEAD]:
        copy.start()
    for pair in range(half):
        for copy in loads[2 * (pair + AHEAD) : 2 * (pair + AHEAD + 1)]:
            copy.start()
        for copy in loads[2 * pair : 2 * pair + 2]:
            copy.wait()
        terms = jnp.dot(clipped_ref[...], held[pair], preferred_element_type=F32).astype(BF16)
        for side in range(2):
            i = 2 * pair + side
            term = terms[:, side * fc : (side + 1) * fc]
            if i < half:
                other_ref[i] = term
            else:
                same_ref[i - half] = term


def down(clipped, weight, me, units, first, follow=()):
    depth = weight.shape[0]
    owners = lax.axis_size("tensor")
    half = owners // 2
    rows = clipped.shape[0]
    fc = units * LANES
    vmem = pl.BlockSpec(memory_space=pltpu.VMEM)
    shape = jax.ShapeDtypeStruct((half, rows, fc), BF16)
    return pl.pallas_call(
        lambda *refs: down_body(first * LANES, *refs),
        in_specs=[
            pl.BlockSpec(memory_space=pltpu.SMEM),
            vmem,
            pl.BlockSpec(memory_space=pltpu.HBM),
        ]
        + follows(follow),
        out_specs=[vmem] * 2,
        out_shape=[shape] * 2,
        scratch_shapes=[
            pltpu.VMEM((half, depth, 2 * fc), BF16),
            pltpu.SemaphoreType.DMA((owners,)),
        ],
        compiler_params=params(16),
        cost_estimate=TINY,
        name="down",
    )(me, clipped, pltpu.with_memory_space_constraint(weight, pltpu.HBM), *follow)


def spread_body(count, ids_ref, probs_ref, *refs):
    mine, theirs = refs[:count], refs[count : 2 * count]
    out_ref, mark_ref = refs[-2:]
    mark_ref[...] = jnp.zeros_like(mark_ref)
    tokens = ids_ref.shape[1]
    summed = jnp.concatenate(
        [(a[0].astype(F32) + b[0].astype(F32)).astype(BF16) for a, b in zip(mine, theirs)], axis=0
    )
    slots = slots_of(ids_ref)
    share = jnp.where(ids_ref[0:1, :] == 0, probs_ref[0:1, :], 0.0) + jnp.where(
        ids_ref[1:2, :] == 0, probs_ref[1:2, :], 0.0
    )
    blocks = tokens // LANES
    share = jnp.concatenate(
        [share[:, LANES * k : LANES * (k + 1)] for k in range(blocks)]
        + [jnp.zeros((LANES - blocks, LANES), F32)],
        axis=0,
    ).T
    slots = jnp.concatenate(
        [slots, jnp.zeros((LANES - slots.shape[0], LANES), F32)], axis=0
    ).T.astype(jnp.int32)
    at = iota((LANES, summed.shape[0]), 1)
    for k in range(blocks):
        hot = jnp.where(at == slots[:, k : k + 1], 1.0, 0.0).astype(BF16)
        rows = jnp.dot(hot, summed, preferred_element_type=F32)
        out_ref[LANES * k : LANES * (k + 1), :] = (rows * share[:, k : k + 1]).astype(BF16)


def spread(ids, probs, state, first, features, out, follow=()):
    mine, theirs = [x[0] for x in state], [x[1] for x in state]
    tokens = ids.shape[1]
    count = len(mine)
    _, rows, fc = mine[0].shape
    args = [ids, probs, *mine, *theirs]
    in_specs = [pl.BlockSpec(x.shape, lambda i, d=x.ndim: (0,) * d) for x in args]
    aliases = {}
    if out is not None:
        aliases = {len(args): 0}
        follow = [out, *follow]
    return pl.pallas_call(
        lambda *refs: spread_body(count, *refs[: 2 + 2 * count], *refs[-2:]),
        grid=(1,),
        in_specs=in_specs + follows(follow),
        out_specs=[
            pl.BlockSpec((pl.Element(tokens), pl.Element(fc)), lambda i: (0, first * LANES)),
            pl.BlockSpec((8, LANES), lambda i: (0, 0)),
        ],
        out_shape=[
            jax.ShapeDtypeStruct((tokens, features), BF16),
            jax.ShapeDtypeStruct((8, LANES), F32),
        ],
        input_output_aliases=aliases,
        compiler_params=params(16),
        cost_estimate=TINY,
        name="spread",
    )(*args, *follow)


def follows(arrays):
    return [pl.BlockSpec(memory_space=pl.ANY)] * len(arrays)


def small(body, args, shapes, name, follow=()):
    vmem = pl.BlockSpec(memory_space=pltpu.VMEM)
    count = len(args)
    specs = [pl.BlockSpec(memory_space=pltpu.SMEM) if x.ndim == 1 else vmem for x in args]
    return pl.pallas_call(
        lambda *refs: body(refs[:count], refs[count + len(follow) :]),
        in_specs=specs + follows(follow),
        out_specs=[vmem] * len(shapes),
        out_shape=[jax.ShapeDtypeStruct(*x) for x in shapes],
        compiler_params=params(16),
        cost_estimate=TINY,
        name=name,
    )(*args, *follow)


def gather_near(own, orders):
    return {0: own} | {1 << bit: across(own, bit) for bit in orders[0]}


def cut_body(firsts, ins, outs):
    for h, at in enumerate(firsts):
        rows = outs[h].shape[0]
        outs[h][...] = ins[at][h * rows : (h + 1) * rows, :]
    for block, out in zip(ins, outs[2:]):
        out[...] = block[...]


def join_body(ins, outs):
    for i, out in enumerate(outs):
        rows = out.shape[0] // 2
        out[:rows, :] = ins[2 * i][...]
        out[rows:, :] = ins[2 * i + 1][...]


def cut(full, orders, follow, passed=False):
    rows, width = full[0].shape
    masks = [mask for mask in full if mask]
    firsts = [masks.index(1 << order[0]) for order in orders]
    shapes = [((rows // 2, width), BF16)] * 2 + [((rows, width), BF16)] * len(masks) * passed
    outs = small(
        lambda ins, outs: cut_body(firsts, ins, outs),
        [full[mask] for mask in masks],
        shapes,
        "cut",
        follow,
    )
    return outs[:2], full | dict(zip(masks, outs[2:]))


def gather_far(full, cuts, orders):
    half = full[0].shape[0] // len(orders)
    firsts = [1 << order[0] for order in orders]
    part = {}

    def get(mask, h):
        if (mask, h) in part:
            return part[mask, h]
        return cuts[h] if mask == firsts[h] else full[mask][h * half : (h + 1) * half]

    have = [[0, first] for first in firsts]
    for at in range(1, len(orders[0])):
        for h, order in enumerate(orders):
            bit = order[at]
            for mask in list(have[h]):
                there = mask | 1 << bit
                if there not in full:
                    part[there, h] = across(get(mask, h), bit)
                have[h].append(there)
    return part


def join(part, follow):
    masks = sorted({mask for mask, _ in part})
    halves = [part[mask, h] for mask in masks for h in range(2)]
    half, width = halves[0].shape
    joined = small(join_body, halves, [((2 * half, width), BF16)] * len(masks), "join", follow)
    return dict(zip(masks, joined))


def paired(pieces):
    return pieces | {mask | 1: across(block, 0) for mask, block in pieces.items()}


def turn_body(bits, scale, ins, outs):
    me_ref, ins = ins[0], ins[1:]
    count = len(bits)
    for h, bit in enumerate(bits):
        flip = (1 - 2 * ((me_ref[0] >> bit) & 1)).astype(F32)
        own = ins[2 * h][...].astype(F32)
        came = ins[2 * h + 1][...].astype(F32)
        value = came + own * flip
        if scale is not None:
            value = value * scale
            top = jnp.max(jnp.abs(own) + jnp.abs(came), axis=0, keepdims=True) * scale
            wide = top[:, :LANES]
            for k in range(1, top.shape[1] // LANES):
                wide = jnp.maximum(wide, top[:, k * LANES : (k + 1) * LANES])
            outs[count + h][...] = jnp.broadcast_to(wide, outs[count + h].shape)
        outs[h][...] = value.astype(BF16)


def turn(me, blocks, came, bits, follow=(), scale=None):
    args = [me] + [x for pair in zip(blocks, came) for x in pair]
    shapes = [(x.shape, BF16) for x in blocks]
    if scale is not None:
        shapes += [((8, LANES), F32)] * len(blocks)
    return small(
        lambda ins, outs: turn_body(bits, scale, ins, outs), args, shapes, "turn", follow
    )


def largest(top_in, tops, lasts):
    bits = range(lax.axis_size("tensor").bit_length() - 1)
    values = jnp.concatenate([top_in, *tops], axis=0)
    for bit in bits:
        if bit not in lasts:
            values = jnp.maximum(values, across(values, bit))
    n = top_in.shape[0]
    top_in, first, second = values[:n], values[n : 2 * n], values[2 * n :]
    if lasts[0] != lasts[1]:
        pair = jnp.concatenate([top_in, second], axis=0)
        came_first, came_pair = across(first, lasts[1]), across(pair, lasts[0])
        first = jnp.maximum(first, came_first)
        pair = jnp.maximum(pair, came_pair)
        top_in, second = pair[:n], pair[n:]
    values = jnp.concatenate([top_in, jnp.maximum(first, second)], axis=0)
    blocks = lax.axis_size("dp")
    far = 1
    while far < blocks:
        pairs = [(r, r ^ far) for r in range(blocks)]
        values = jnp.maximum(values, lax.ppermute(values, "dp", pairs))
        far *= 2
    return values


def on_device(tokens, expert_ids, gate_probs, gate_weight, up_weight, down_weight):
    count = lax.axis_size("tensor")
    bits = count.bit_length() - 1
    outer = list(range(1, bits))
    orders = [outer, outer[::-1]]
    me = lax.axis_index("tensor")
    me_arr = me.astype(jnp.int32).reshape(1)
    ids, probs = expert_ids.T, gate_probs.T
    rows = CAP // ROW_CHUNKS
    half = rows // 2
    scale = 1.0 / math.sqrt(gate_weight.shape[1] * count)
    stages = [[order[at] for order in orders] for at in range(len(outer))]
    early_bit = stages[-1][1]

    def send(blocks, bits):
        return [across(x, bit) for x, bit in zip(blocks, bits)]

    def start_turn(halves, follow=()):
        blocks = turn(me_arr, halves, send(halves, [0, 0]), [0, 0], follow)
        return blocks, send(blocks, stages[0])

    def go_on(blocks, came, at, follow=()):
        blocks = turn(me_arr, blocks, came, stages[at], follow)
        return blocks, send(blocks, stages[at + 1])

    def end_turn(blocks, came, follow=()):
        made = turn(me_arr, blocks, came, stages[-1], follow, scale)
        return made[: len(blocks)], made[len(blocks) :]

    own_a, top_a = pick_rows(ids, tokens, 0, rows, [me_arr])
    near_a = gather_near(own_a, orders)
    weights = (me_arr, gate_weight, up_weight)
    cuts_a, near_a = cut(near_a, orders, [])
    own_b, top_b = pick_rows(ids, tokens, rows, rows, cuts_a)
    top_in = jnp.maximum(top_a, top_b)
    top_in = jnp.maximum(top_in, across(top_in, early_bit))
    far_a = join(gather_far(near_a, cuts_a, orders), [own_b, top_in])
    near_b = gather_near(own_b, orders)
    parts_a = paired(near_a | far_a)
    parts_a = [parts_a[mask] for mask in range(count)]
    first_a = expand(parts_a, rows, *weights)
    cuts_b, near_b = cut(near_b, orders, first_a, True)
    local_a = expand(parts_a, rows, *weights, *first_a, cuts_b)
    parts_b = paired(near_b)
    theirs_b = [block for mask, block in parts_b.items() if mask & 1]
    far_b = join(gather_far(near_b, cuts_b, orders), list(local_a) + theirs_b)
    parts_b |= paired(far_b)
    parts_b = [parts_b[mask] for mask in range(count)]
    blocks_a, came_a = start_turn(local_a)
    first_b = expand(parts_b, rows, *weights, None, blocks_a)
    for at in range(len(outer) - 1):
        blocks_a, came_a = go_on(blocks_a, came_a, at, first_b)
    local_b = expand(parts_b, rows, *weights, *first_b, blocks_a)
    turned_a, rot_a = end_turn(blocks_a, came_a, local_b)
    blocks_b, came_b = start_turn(local_b, rot_a)
    for at in range(len(outer) - 1):
        blocks_b, came_b = go_on(blocks_b, came_b, at)
    turned_b, rot_b = end_turn(blocks_b, came_b)
    rotated = turned_a + turned_b

    peaks = largest(top_in, [jnp.maximum(x, y) for x, y in zip(rot_a, rot_b)], stages[-1])
    clipped = small(
        clip_body, [peaks, *rotated], [((CAP, gate_weight.shape[1]), BF16)], "clip"
    )[0]

    tops = pl.pallas_call(
        peaks_body,
        out_specs=pl.BlockSpec(memory_space=pltpu.SMEM),
        out_shape=jax.ShapeDtypeStruct((2,), F32),
        name="peaks",
    )(peaks)
    units = tokens.shape[1] // LANES
    sizes = chunks_of(units)
    firsts = [sum(sizes[:i]) for i in range(len(sizes))]
    total = len(sizes)
    def product(chunk, follow=()):
        return down(clipped, down_weight, me_arr, sizes[chunk], firsts[chunk], follow)

    def back(out, chunk, follow):
        return spread(ids, probs, ended[chunk], firsts[chunk], tokens.shape[1], out, follow)

    begun, ended = [], []
    ready = [product(0)]
    out, marks = None, []
    for chunk in range(total):
        other, same = ready[chunk]
        came = across(other, 0)
        wait = [keep for keep, _, _ in begun[-1]] if begun else []
        passed, late = [], []
        if chunk + 1 < total:
            *passed, same_next = product(chunk + 1, [same, *wait])
            late = [same_next]
        if len(ended) > 0:
            late += [recv for _, recv, _ in ended[-1]]
        if chunk > 0:
            state, passed = finish(begun[-1], stages, late, passed)
            ended.append(state)
            late += [keep for keep, _, _ in state]
        if chunk + 1 < total:
            ready.append((passed[0], same_next))
        begun.append(fold_cores(same, came, stages[0], late))
        if chunk > 1:
            out, mark = back(out, chunk - 2, [keep for keep, _, _ in begun[-1]])
            marks.append(mark)
    late = marks + ([recv for _, recv, _ in ended[-1]] if ended else [])
    ended.append(finish(begun[-1], stages, late)[0])
    for chunk in range(len(marks), total):
        out, _ = back(out, chunk, [keep for keep, _, _ in ended[-1]])
    return out, tops


def chunks_of(units):
    return [2] * (units // 2) + [1] * (units % 2)


def peaks_body(values_ref, out_ref):
    out_ref[0] = jnp.max(values_ref[:8, :])
    out_ref[1] = jnp.max(values_ref[8:, :])


def fold_body(plan, passed, ins, outs):
    for i in range(passed):
        outs[len(plan) + i][...] = ins[len(ins) - passed + i][...]
    for out, (slots, low) in zip(outs, plan):
        rows = out.shape[1]
        for slot, terms in enumerate(slots):
            total = 0.0
            for at, i in terms:
                total = total + ins[at][i, low : low + rows, :].astype(F32)
            out[slot] = total.astype(BF16)


def fold(args, terms, masks, lows, rows, bits, follow, passed=()):
    plan, shapes, lefts = [], [], []
    width = args[0].shape[2]
    for h, bit in enumerate(bits):
        for side in (0, 1):
            chosen = [m for m in masks[h] if m >> bit & 1 == side]
            plan.append(([terms[h][m] for m in chosen], lows[h]))
            shapes.append(((len(chosen), rows, width), BF16))
        lefts.append([m for m in masks[h] if not m >> bit & 1])
    shapes += [(x.shape, x.dtype) for x in passed]
    made = small(
        lambda ins, outs: fold_body(plan, len(passed), ins, outs),
        [*args, *passed],
        shapes,
        "fold",
        follow,
    )
    state = [
        (made[2 * h], across(made[2 * h + 1], bit), lefts[h]) for h, bit in enumerate(bits)
    ]
    return state, made[len(plan) :]


def fold_cores(same, came, bits, follow):
    half = same.shape[1] // 2
    masks = [2 * i for i in range(same.shape[0])]
    terms = {m: ((0, i), (1, i)) for i, m in enumerate(masks)}
    return fold([same, came], [terms] * 2, [masks] * 2, [0, half], half, bits, follow)[0]


def finish(state, stages, follow, passed=()):
    for bits in stages[1:]:
        args = [x for keep, recv, _ in state for x in (keep, recv)]
        masks = [left for _, _, left in state]
        terms = [
            {m: ((2 * h, i), (2 * h + 1, i)) for i, m in enumerate(left)}
            for h, left in enumerate(masks)
        ]
        state, passed = fold(
            args, terms, masks, [0, 0], args[0].shape[1], bits, follow, passed
        )
    return state, passed


def solution(mesh):
    in_specs = (
        P("dp", "tensor"),
        P("dp", None),
        P("dp", None),
        P(None, "tensor"),
        P(None, "tensor"),
        P("tensor", None),
    )
    out_specs = (P("dp", "tensor"), P())
    return jax.shard_map(
        on_device, mesh=mesh, in_specs=in_specs, out_specs=out_specs, check_vma=False
    )
```

```python
import math

import jax
import jax.numpy as jnp
from jax import lax
from jax.experimental import pallas as pl
from jax.experimental.pallas import tpu as pltpu
from jax.sharding import PartitionSpec as P

CAP = 768
CLIP_SHARE = 0.25
LANES = 128
ROW_CHUNKS = 2
BF16 = jnp.bfloat16
F32 = jnp.float32
MIB = 1 << 20
EXPAND_MIB = 24
AHEAD = 3


def params(mib):
    return pltpu.CompilerParams(vmem_limit_bytes=mib * MIB)


TINY = pl.CostEstimate(flops=1, bytes_accessed=1, transcendentals=0)


def across(block, bit):
    count = lax.axis_size("tensor")
    return lax.ppermute(block, "tensor", [(r, r ^ 1 << bit) for r in range(count)])


def iota(shape, dim):
    return lax.broadcasted_iota(jnp.int32, shape, dim)


def slots_of(ids_ref):
    tokens = ids_ref.shape[1]
    rows = tokens // LANES
    padded = (rows + 15) // 16 * 16
    hit = jnp.where((ids_ref[0:1, :] == 0) | (ids_ref[1:2, :] == 0), 1.0, 0.0)
    grid = jnp.concatenate(
        [hit[:, LANES * k : LANES * (k + 1)] for k in range(rows)]
        + [jnp.zeros((padded - rows, LANES), F32)],
        axis=0,
    )
    flat = grid.astype(BF16)
    upto = (iota((LANES, LANES), 0) <= iota((LANES, LANES), 1)).astype(F32).astype(BF16)
    before = (iota((padded, padded), 1) < iota((padded, padded), 0)).astype(F32).astype(BF16)
    within = jnp.dot(flat, upto, preferred_element_type=F32)
    offset = jnp.sum(jnp.dot(before, flat, preferred_element_type=F32), axis=1, keepdims=True)
    return jnp.where(grid > 0.0, within + offset - 1.0, -1.0)


def pick_body(first, ids_hbm, tokens_hbm, *refs):
    picked_ref, peak_ref, ids_ref, tokens_ref, loaded = refs[-5:]
    rows = picked_ref.shape[0]
    count = tokens_ref.shape[0]
    pieces = loaded.shape[0] - 1
    step = count // pieces
    ids_copy = pltpu.make_async_copy(ids_hbm, ids_ref, loaded.at[pieces])
    ids_copy.start()
    copies = [
        pltpu.make_async_copy(
            tokens_hbm.at[pl.ds(i * step, step), :],
            tokens_ref.at[pl.ds(i * step, step), :],
            loaded.at[i],
        )
        for i in range(pieces)
    ]
    for copy in copies:
        copy.start()
    ids_copy.wait()
    slots = slots_of(ids_ref).astype(jnp.int32)
    wanted = iota((rows, LANES), 0) + first
    picked = jnp.zeros(picked_ref.shape, F32)
    for i, copy in enumerate(copies):
        hot = jnp.concatenate(
            [
                jnp.where(wanted == slots[k : k + 1, :], 1.0, 0.0).astype(BF16)
                for k in range(i * step // LANES, (i + 1) * step // LANES)
            ],
            axis=1,
        )
        copy.wait()
        picked += jnp.dot(
            hot, tokens_ref[i * step : (i + 1) * step, :], preferred_element_type=F32
        )
    picked_ref[...] = picked.astype(BF16)
    peak_ref[...] = jnp.broadcast_to(jnp.max(jnp.abs(picked)), peak_ref.shape)


def pick_rows(ids, tokens, first, rows, follow=()):
    count, width = tokens.shape
    blocks = count // LANES
    pieces = math.gcd(blocks, 4)
    in_hbm = [pltpu.with_memory_space_constraint(x, pltpu.HBM) for x in (ids, tokens)]
    return pl.pallas_call(
        lambda *refs: pick_body(first, *refs),
        out_shape=(
            jax.ShapeDtypeStruct((rows, width), BF16),
            jax.ShapeDtypeStruct((8, LANES), F32),
        ),
        in_specs=[pl.BlockSpec(memory_space=pltpu.HBM)] * 2 + follows(follow),
        out_specs=[pl.BlockSpec(memory_space=pltpu.VMEM)] * 2,
        scratch_shapes=[
            pltpu.VMEM(ids.shape, ids.dtype),
            pltpu.VMEM(tokens.shape, tokens.dtype),
            pltpu.SemaphoreType.DMA((pieces + 1,)),
        ],
        compiler_params=params(16),
        cost_estimate=TINY,
        name="pick_rows",
    )(*in_hbm, *follow)


def signs(size):
    common = iota((size, size), 0) & iota((size, size), 1)
    shift = 1
    while shift < size.bit_length():
        shift *= 2
    while shift > 1:
        shift //= 2
        common = common ^ (common >> shift)
    return (1 - 2 * (common & 1)).astype(F32).astype(BF16)


def expand_body(first, count, last, me_ref, *refs):
    parts, refs = refs[:count], refs[count:]
    before_ref = None
    if last:
        before_ref, refs = refs[0], refs[1:]
    gate_hbm, up_hbm, *outs, total, held, loaded = refs
    width = parts[0].shape[1]
    columns = total.shape[2]
    tile = min(256, columns)

    def load(mask):
        rows = pl.ds(pl.multiple_of((me_ref[0] ^ mask) * width, LANES), width)
        return [
            pltpu.make_async_copy(
                weight.at[rows, pl.ds(first, columns)], held.at[mask, at], loaded.at[mask, at]
            )
            for at, weight in enumerate((gate_hbm, up_hbm))
        ]

    loads = [load(mask) for mask in range(count)]
    for copies in loads[:AHEAD]:
        for copy in copies:
            copy.start()
    table = signs(tile)
    for mask, part in enumerate(parts):
        for copies in loads[mask + AHEAD : mask + AHEAD + 1]:
            for copy in copies:
                copy.start()
        for at in range(2):
            loads[mask][at].wait()
            term = jnp.dot(part[...], held[mask, at], preferred_element_type=F32)
            if mask == 0:
                total[at] = term
            else:
                total[at] += term
    values = []
    for i in range(columns // tile):
        gate = total[0, :, i * tile : (i + 1) * tile]
        up = total[1, :, i * tile : (i + 1) * tile]
        hidden = (gate * (1.0 / (1.0 + jnp.exp(-gate))) * up).astype(BF16)
        values.append(jnp.dot(hidden, table, preferred_element_type=F32))
        if not last:
            outs[0][i] = values[i]
    if not last:
        return
    values = [before_ref[i] for i in range(before_ref.shape[0])] + values
    steps = len(values)
    gap = 1
    while gap < steps:
        values = [
            values[i] + values[i ^ gap] if not i & gap else values[i ^ gap] - values[i]
            for i in range(steps)
        ]
        gap *= 2
    for i in range(steps):
        low = 0
        for out in outs:
            rows = out.shape[0]
            out[:, i * tile : (i + 1) * tile] = values[i][low : low + rows].astype(BF16)
            low += rows


def expand(parts, rows, me, gate_weight, up_weight, before=None, follow=()):
    depth, width = gate_weight.shape
    last = before is not None
    columns = width // 2
    first = columns if last else 0
    tile = min(256, columns)
    count = len(parts)
    vmem = pl.BlockSpec(memory_space=pltpu.VMEM)
    in_hbm = [pltpu.with_memory_space_constraint(x, pltpu.HBM) for x in (gate_weight, up_weight)]
    args = [me, *parts] + ([before] if last else [])
    used = len(args) + 2
    if last:
        out_shape = [jax.ShapeDtypeStruct((rows // 2, width), BF16)] * 2
    else:
        out_shape = [jax.ShapeDtypeStruct((columns // tile, rows, tile), F32)]
    return pl.pallas_call(
        lambda *refs: expand_body(first, count, last, *refs[:used], *refs[used + len(follow) :]),
        in_specs=[pl.BlockSpec(memory_space=pltpu.SMEM)]
        + [vmem] * (used - 3)
        + [pl.BlockSpec(memory_space=pltpu.HBM)] * 2
        + follows(follow),
        out_specs=[vmem] * len(out_shape),
        out_shape=out_shape,
        scratch_shapes=[
            pltpu.VMEM((2, rows, columns), F32),
            pltpu.VMEM((count, 2, depth // count, columns), BF16),
            pltpu.SemaphoreType.DMA((count, 2)),
        ],
        compiler_params=params(EXPAND_MIB),
        cost_estimate=TINY,
        name="expand_last" if last else "expand_first",
    )(*args, *in_hbm, *follow)


def clip_body(ins, outs):
    level = CLIP_SHARE * jnp.max(ins[0][8:, :])
    low = 0
    for part in ins[1:]:
        rows = part.shape[0]
        outs[0][low : low + rows, :] = jnp.clip(part[...].astype(F32), -level, level).astype(BF16)
        low += rows


def down_body(first, me_ref, clipped_ref, weight_hbm, *refs):
    owners = lax.axis_size("tensor")
    half = owners // 2
    other_ref, same_ref, held, loaded = refs[-4:]
    fc = same_ref.shape[2]
    stride = weight_hbm.shape[1] // owners
    masks = [2 * i + 1 for i in range(half)] + [2 * i for i in range(half)]

    def load(i):
        column = pl.multiple_of((me_ref[0] ^ masks[i]) * stride + first, LANES)
        return pltpu.make_async_copy(
            weight_hbm.at[:, pl.ds(column, fc)],
            held.at[i // 2, :, pl.ds(i % 2 * fc, fc)],
            loaded.at[i],
        )

    loads = [load(i) for i in range(owners)]
    for copy in loads[: 2 * AHEAD]:
        copy.start()
    for pair in range(half):
        for copy in loads[2 * (pair + AHEAD) : 2 * (pair + AHEAD + 1)]:
            copy.start()
        for copy in loads[2 * pair : 2 * pair + 2]:
            copy.wait()
        terms = jnp.dot(clipped_ref[...], held[pair], preferred_element_type=F32).astype(BF16)
        for side in range(2):
            i = 2 * pair + side
            term = terms[:, side * fc : (side + 1) * fc]
            if i < half:
                other_ref[i] = term
            else:
                same_ref[i - half] = term


def down(clipped, weight, me, units, first, follow=()):
    depth = weight.shape[0]
    owners = lax.axis_size("tensor")
    half = owners // 2
    rows = clipped.shape[0]
    fc = units * LANES
    vmem = pl.BlockSpec(memory_space=pltpu.VMEM)
    shape = jax.ShapeDtypeStruct((half, rows, fc), BF16)
    return pl.pallas_call(
        lambda *refs: down_body(first * LANES, *refs),
        in_specs=[
            pl.BlockSpec(memory_space=pltpu.SMEM),
            vmem,
            pl.BlockSpec(memory_space=pltpu.HBM),
        ]
        + follows(follow),
        out_specs=[vmem] * 2,
        out_shape=[shape] * 2,
        scratch_shapes=[
            pltpu.VMEM((half, depth, 2 * fc), BF16),
            pltpu.SemaphoreType.DMA((owners,)),
        ],
        compiler_params=params(16),
        cost_estimate=TINY,
        name="down",
    )(me, clipped, pltpu.with_memory_space_constraint(weight, pltpu.HBM), *follow)


def spread_body(count, ids_ref, probs_ref, *refs):
    mine, theirs = refs[:count], refs[count : 2 * count]
    out_ref, mark_ref = refs[-2:]
    mark_ref[...] = jnp.zeros_like(mark_ref)
    tokens = ids_ref.shape[1]
    summed = jnp.concatenate(
        [(a[0].astype(F32) + b[0].astype(F32)).astype(BF16) for a, b in zip(mine, theirs)], axis=0
    )
    slots = slots_of(ids_ref)
    share = jnp.where(ids_ref[0:1, :] == 0, probs_ref[0:1, :], 0.0) + jnp.where(
        ids_ref[1:2, :] == 0, probs_ref[1:2, :], 0.0
    )
    blocks = tokens // LANES
    share = jnp.concatenate(
        [share[:, LANES * k : LANES * (k + 1)] for k in range(blocks)]
        + [jnp.zeros((LANES - blocks, LANES), F32)],
        axis=0,
    ).T
    slots = jnp.concatenate(
        [slots, jnp.zeros((LANES - slots.shape[0], LANES), F32)], axis=0
    ).T.astype(jnp.int32)
    at = iota((LANES, summed.shape[0]), 1)
    for k in range(blocks):
        hot = jnp.where(at == slots[:, k : k + 1], 1.0, 0.0).astype(BF16)
        rows = jnp.dot(hot, summed, preferred_element_type=F32)
        out_ref[LANES * k : LANES * (k + 1), :] = (rows * share[:, k : k + 1]).astype(BF16)


def spread(ids, probs, state, first, features, out, follow=()):
    mine, theirs = [x[0] for x in state], [x[1] for x in state]
    tokens = ids.shape[1]
    count = len(mine)
    _, rows, fc = mine[0].shape
    args = [ids, probs, *mine, *theirs]
    in_specs = [pl.BlockSpec(x.shape, lambda i, d=x.ndim: (0,) * d) for x in args]
    aliases = {}
    if out is not None:
        aliases = {len(args): 0}
        follow = [out, *follow]
    return pl.pallas_call(
        lambda *refs: spread_body(count, *refs[: 2 + 2 * count], *refs[-2:]),
        grid=(1,),
        in_specs=in_specs + follows(follow),
        out_specs=[
            pl.BlockSpec((pl.Element(tokens), pl.Element(fc)), lambda i: (0, first * LANES)),
            pl.BlockSpec((8, LANES), lambda i: (0, 0)),
        ],
        out_shape=[
            jax.ShapeDtypeStruct((tokens, features), BF16),
            jax.ShapeDtypeStruct((8, LANES), F32),
        ],
        input_output_aliases=aliases,
        compiler_params=params(16),
        cost_estimate=TINY,
        name="spread",
    )(*args, *follow)


def follows(arrays):
    return [pl.BlockSpec(memory_space=pl.ANY)] * len(arrays)


def small(body, args, shapes, name, follow=()):
    vmem = pl.BlockSpec(memory_space=pltpu.VMEM)
    count = len(args)
    specs = [pl.BlockSpec(memory_space=pltpu.SMEM) if x.ndim == 1 else vmem for x in args]
    return pl.pallas_call(
        lambda *refs: body(refs[:count], refs[count + len(follow) :]),
        in_specs=specs + follows(follow),
        out_specs=[vmem] * len(shapes),
        out_shape=[jax.ShapeDtypeStruct(*x) for x in shapes],
        compiler_params=params(16),
        cost_estimate=TINY,
        name=name,
    )(*args, *follow)


def gather_near(own, orders):
    return {0: own} | {1 << bit: across(own, bit) for bit in orders[0]}


def cut_body(firsts, ins, outs):
    for h, at in enumerate(firsts):
        rows = outs[h].shape[0]
        outs[h][...] = ins[at][h * rows : (h + 1) * rows, :]
    for block, out in zip(ins, outs[2:]):
        out[...] = block[...]


def join_body(ins, outs):
    for i, out in enumerate(outs):
        rows = out.shape[0] // 2
        out[:rows, :] = ins[2 * i][...]
        out[rows:, :] = ins[2 * i + 1][...]


def cut(full, orders, follow, passed=False):
    rows, width = full[0].shape
    masks = [mask for mask in full if mask]
    firsts = [masks.index(1 << order[0]) for order in orders]
    shapes = [((rows // 2, width), BF16)] * 2 + [((rows, width), BF16)] * len(masks) * passed
    outs = small(
        lambda ins, outs: cut_body(firsts, ins, outs),
        [full[mask] for mask in masks],
        shapes,
        "cut",
        follow,
    )
    return outs[:2], full | dict(zip(masks, outs[2:]))


def gather_far(full, cuts, orders):
    half = full[0].shape[0] // len(orders)
    firsts = [1 << order[0] for order in orders]
    part = {}

    def get(mask, h):
        if (mask, h) in part:
            return part[mask, h]
        return cuts[h] if mask == firsts[h] else full[mask][h * half : (h + 1) * half]

    have = [[0, first] for first in firsts]
    for at in range(1, len(orders[0])):
        for h, order in enumerate(orders):
            bit = order[at]
            for mask in list(have[h]):
                there = mask | 1 << bit
                if there not in full:
                    part[there, h] = across(get(mask, h), bit)
                have[h].append(there)
    return part


def join(part, follow):
    masks = sorted({mask for mask, _ in part})
    halves = [part[mask, h] for mask in masks for h in range(2)]
    half, width = halves[0].shape
    joined = small(join_body, halves, [((2 * half, width), BF16)] * len(masks), "join", follow)
    return dict(zip(masks, joined))


def paired(pieces):
    return pieces | {mask | 1: across(block, 0) for mask, block in pieces.items()}


def turn_body(bits, scale, ins, outs):
    me_ref, ins = ins[0], ins[1:]
    count = len(bits)
    for h, bit in enumerate(bits):
        flip = (1 - 2 * ((me_ref[0] >> bit) & 1)).astype(F32)
        own = ins[2 * h][...].astype(F32)
        came = ins[2 * h + 1][...].astype(F32)
        value = came + own * flip
        if scale is not None:
            value = value * scale
            top = jnp.max(jnp.abs(own) + jnp.abs(came), axis=0, keepdims=True) * scale
            wide = top[:, :LANES]
            for k in range(1, top.shape[1] // LANES):
                wide = jnp.maximum(wide, top[:, k * LANES : (k + 1) * LANES])
            outs[count + h][...] = jnp.broadcast_to(wide, outs[count + h].shape)
        outs[h][...] = value.astype(BF16)


def turn(me, blocks, came, bits, follow=(), scale=None):
    args = [me] + [x for pair in zip(blocks, came) for x in pair]
    shapes = [(x.shape, BF16) for x in blocks]
    if scale is not None:
        shapes += [((8, LANES), F32)] * len(blocks)
    return small(
        lambda ins, outs: turn_body(bits, scale, ins, outs), args, shapes, "turn", follow
    )


def largest(top_in, tops, lasts):
    bits = range(lax.axis_size("tensor").bit_length() - 1)
    values = jnp.concatenate([top_in, *tops], axis=0)
    for bit in bits:
        if bit not in lasts:
            values = jnp.maximum(values, across(values, bit))
    n = top_in.shape[0]
    top_in, first, second = values[:n], values[n : 2 * n], values[2 * n :]
    if lasts[0] != lasts[1]:
        pair = jnp.concatenate([top_in, second], axis=0)
        came_first, came_pair = across(first, lasts[1]), across(pair, lasts[0])
        first = jnp.maximum(first, came_first)
        pair = jnp.maximum(pair, came_pair)
        top_in, second = pair[:n], pair[n:]
    values = jnp.concatenate([top_in, jnp.maximum(first, second)], axis=0)
    blocks = lax.axis_size("dp")
    far = 1
    while far < blocks:
        pairs = [(r, r ^ far) for r in range(blocks)]
        values = jnp.maximum(values, lax.ppermute(values, "dp", pairs))
        far *= 2
    return values


def on_device(tokens, expert_ids, gate_probs, gate_weight, up_weight, down_weight):
    count = lax.axis_size("tensor")
    bits = count.bit_length() - 1
    outer = list(range(1, bits))
    orders = [outer, outer[::-1]]
    me = lax.axis_index("tensor")
    me_arr = me.astype(jnp.int32).reshape(1)
    ids, probs = expert_ids.T, gate_probs.T
    rows = CAP // ROW_CHUNKS
    half = rows // 2
    scale = 1.0 / math.sqrt(gate_weight.shape[1] * count)
    stages = [[order[at] for order in orders] for at in range(len(outer))]
    early_bit = stages[-1][1]

    def send(blocks, bits):
        return [across(x, bit) for x, bit in zip(blocks, bits)]

    def start_turn(halves, follow=()):
        blocks = turn(me_arr, halves, send(halves, [0, 0]), [0, 0], follow)
        return blocks, send(blocks, stages[0])

    def go_on(blocks, came, at, follow=()):
        blocks = turn(me_arr, blocks, came, stages[at], follow)
        return blocks, send(blocks, stages[at + 1])

    def end_turn(blocks, came, follow=()):
        made = turn(me_arr, blocks, came, stages[-1], follow, scale)
        return made[: len(blocks)], made[len(blocks) :]

    own_a, top_a = pick_rows(ids, tokens, 0, rows, [me_arr])
    near_a = gather_near(own_a, orders)
    weights = (me_arr, gate_weight, up_weight)
    cuts_a, near_a = cut(near_a, orders, [])
    own_b, top_b = pick_rows(ids, tokens, rows, rows, cuts_a)
    top_in = jnp.maximum(top_a, top_b)
    top_in = jnp.maximum(top_in, across(top_in, early_bit))
    far_a = join(gather_far(near_a, cuts_a, orders), [own_b, top_in])
    near_b = gather_near(own_b, orders)
    parts_a = paired(near_a | far_a)
    parts_a = [parts_a[mask] for mask in range(count)]
    first_a = expand(parts_a, rows, *weights)
    cuts_b, near_b = cut(near_b, orders, first_a, True)
    local_a = expand(parts_a, rows, *weights, *first_a, cuts_b)
    parts_b = paired(near_b)
    theirs_b = [block for mask, block in parts_b.items() if mask & 1]
    far_b = join(gather_far(near_b, cuts_b, orders), list(local_a) + theirs_b)
    parts_b |= paired(far_b)
    parts_b = [parts_b[mask] for mask in range(count)]
    blocks_a, came_a = start_turn(local_a)
    first_b = expand(parts_b, rows, *weights, None, blocks_a)
    for at in range(len(outer) - 1):
        blocks_a, came_a = go_on(blocks_a, came_a, at, first_b)
    local_b = expand(parts_b, rows, *weights, *first_b, blocks_a)
    turned_a, rot_a = end_turn(blocks_a, came_a, local_b)
    blocks_b, came_b = start_turn(local_b, rot_a)
    for at in range(len(outer) - 1):
        blocks_b, came_b = go_on(blocks_b, came_b, at)
    turned_b, rot_b = end_turn(blocks_b, came_b)
    rotated = turned_a + turned_b

    peaks = largest(top_in, [jnp.maximum(x, y) for x, y in zip(rot_a, rot_b)], stages[-1])
    clipped = small(
        clip_body, [peaks, *rotated], [((CAP, gate_weight.shape[1]), BF16)], "clip"
    )[0]

    tops = pl.pallas_call(
        peaks_body,
        out_specs=pl.BlockSpec(memory_space=pltpu.SMEM),
        out_shape=jax.ShapeDtypeStruct((2,), F32),
        name="peaks",
    )(peaks)
    units = tokens.shape[1] // LANES
    sizes = chunks_of(units)
    firsts = [sum(sizes[:i]) for i in range(len(sizes))]
    total = len(sizes)
    products, begun, ended, out, last = {}, {}, {}, None, []
    for step, chunk in sums_order(total):
        if step == "product":
            products[chunk] = down(
                clipped, down_weight, me_arr, sizes[chunk], firsts[chunk], last
            )
            last = [products[chunk][1]]
        elif step == "begin":
            other, same = products[chunk]
            begun[chunk] = fold_cores(same, across(other, 0), stages[0], last)
            last = [keep for keep, _, _ in begun[chunk]]
        elif step == "finish":
            ahead = [c for c in products if c not in begun]
            passed = [products[c][0] for c in ahead]
            ended[chunk], passed = finish(begun[chunk], stages, last, passed)
            for c, other in zip(ahead, passed):
                products[c] = (other, products[c][1])
            last = [keep for keep, _, _ in ended[chunk]]
        else:
            out, mark = spread(
                ids, probs, ended[chunk], firsts[chunk], tokens.shape[1], out, last
            )
            last = [mark]
    return out, tops


def chunks_of(units):
    return [2] * (units // 2) + [1] * (units % 2)


def sums_order(total):
    order = [("product", 0)]
    for chunk in range(total):
        if chunk + 1 < total:
            order.append(("product", chunk + 1))
        order.append(("begin", chunk))
        if chunk > 0:
            order.append(("finish", chunk - 1))
        if chunk > 1:
            order.append(("spread", chunk - 2))
    order.append(("finish", total - 1))
    return order + [("spread", chunk) for chunk in range(max(0, total - 2), total)]


def peaks_body(values_ref, out_ref):
    out_ref[0] = jnp.max(values_ref[:8, :])
    out_ref[1] = jnp.max(values_ref[8:, :])


def fold_body(plan, passed, ins, outs):
    for i in range(passed):
        outs[len(plan) + i][...] = ins[len(ins) - passed + i][...]
    for out, (slots, low) in zip(outs, plan):
        rows = out.shape[1]
        for slot, terms in enumerate(slots):
            total = 0.0
            for at, i in terms:
                total = total + ins[at][i, low : low + rows, :].astype(F32)
            out[slot] = total.astype(BF16)


def fold(args, terms, masks, lows, rows, bits, follow, passed=()):
    plan, shapes, lefts = [], [], []
    width = args[0].shape[2]
    for h, bit in enumerate(bits):
        for side in (0, 1):
            chosen = [m for m in masks[h] if m >> bit & 1 == side]
            plan.append(([terms[h][m] for m in chosen], lows[h]))
            shapes.append(((len(chosen), rows, width), BF16))
        lefts.append([m for m in masks[h] if not m >> bit & 1])
    shapes += [(x.shape, x.dtype) for x in passed]
    made = small(
        lambda ins, outs: fold_body(plan, len(passed), ins, outs),
        [*args, *passed],
        shapes,
        "fold",
        follow,
    )
    state = [
        (made[2 * h], across(made[2 * h + 1], bit), lefts[h]) for h, bit in enumerate(bits)
    ]
    return state, made[len(plan) :]


def fold_cores(same, came, bits, follow):
    half = same.shape[1] // 2
    masks = [2 * i for i in range(same.shape[0])]
    terms = {m: ((0, i), (1, i)) for i, m in enumerate(masks)}
    return fold([same, came], [terms] * 2, [masks] * 2, [0, half], half, bits, follow)[0]


def finish(state, stages, follow, passed=()):
    for bits in stages[1:]:
        args = [x for keep, recv, _ in state for x in (keep, recv)]
        masks = [left for _, _, left in state]
        terms = [
            {m: ((2 * h, i), (2 * h + 1, i)) for i, m in enumerate(left)}
            for h, left in enumerate(masks)
        ]
        state, passed = fold(
            args, terms, masks, [0, 0], args[0].shape[1], bits, follow, passed
        )
    return state, passed


def solution(mesh):
    in_specs = (
        P("dp", "tensor"),
        P("dp", None),
        P("dp", None),
        P(None, "tensor"),
        P(None, "tensor"),
        P("tensor", None),
    )
    out_specs = (P("dp", "tensor"), P())
    return jax.shard_map(
        on_device, mesh=mesh, in_specs=in_specs, out_specs=out_specs, check_vma=False
    )
```

```python
import math

import jax
import jax.numpy as jnp
from jax import lax
from jax.experimental import pallas as pl
from jax.experimental.pallas import tpu as pltpu
from jax.sharding import PartitionSpec as P

CAP = 768
CLIP_SHARE = 0.25
LANES = 128
ROW_CHUNKS = 2
BF16 = jnp.bfloat16
F32 = jnp.float32
MIB = 1 << 20
EXPAND_MIB = 24
AHEAD = 3


def params(mib):
    return pltpu.CompilerParams(vmem_limit_bytes=mib * MIB)


TINY = pl.CostEstimate(flops=1, bytes_accessed=1, transcendentals=0)


def across(block, bit):
    count = lax.axis_size("tensor")
    return lax.ppermute(block, "tensor", [(r, r ^ 1 << bit) for r in range(count)])


def iota(shape, dim):
    return lax.broadcasted_iota(jnp.int32, shape, dim)


def slots_of(ids_ref):
    tokens = ids_ref.shape[1]
    rows = tokens // LANES
    padded = (rows + 15) // 16 * 16
    hit = jnp.where((ids_ref[0:1, :] == 0) | (ids_ref[1:2, :] == 0), 1.0, 0.0)
    grid = jnp.concatenate(
        [hit[:, LANES * k : LANES * (k + 1)] for k in range(rows)]
        + [jnp.zeros((padded - rows, LANES), F32)],
        axis=0,
    )
    flat = grid.astype(BF16)
    upto = (iota((LANES, LANES), 0) <= iota((LANES, LANES), 1)).astype(F32).astype(BF16)
    before = (iota((padded, padded), 1) < iota((padded, padded), 0)).astype(F32).astype(BF16)
    within = jnp.dot(flat, upto, preferred_element_type=F32)
    offset = jnp.sum(jnp.dot(before, flat, preferred_element_type=F32), axis=1, keepdims=True)
    return jnp.where(grid > 0.0, within + offset - 1.0, -1.0)


def pick_body(first, ids_hbm, tokens_hbm, *refs):
    picked_ref, peak_ref, ids_ref, tokens_ref, loaded = refs[-5:]
    rows = picked_ref.shape[0]
    count = tokens_ref.shape[0]
    pieces = loaded.shape[0] - 1
    step = count // pieces
    ids_copy = pltpu.make_async_copy(ids_hbm, ids_ref, loaded.at[pieces])
    ids_copy.start()
    copies = [
        pltpu.make_async_copy(
            tokens_hbm.at[pl.ds(i * step, step), :],
            tokens_ref.at[pl.ds(i * step, step), :],
            loaded.at[i],
        )
        for i in range(pieces)
    ]
    for copy in copies:
        copy.start()
    ids_copy.wait()
    slots = slots_of(ids_ref).astype(jnp.int32)
    wanted = iota((rows, LANES), 0) + first
    picked = jnp.zeros(picked_ref.shape, F32)
    for i, copy in enumerate(copies):
        hot = jnp.concatenate(
            [
                jnp.where(wanted == slots[k : k + 1, :], 1.0, 0.0).astype(BF16)
                for k in range(i * step // LANES, (i + 1) * step // LANES)
            ],
            axis=1,
        )
        copy.wait()
        picked += jnp.dot(
            hot, tokens_ref[i * step : (i + 1) * step, :], preferred_element_type=F32
        )
    picked_ref[...] = picked.astype(BF16)
    peak_ref[...] = jnp.broadcast_to(jnp.max(jnp.abs(picked)), peak_ref.shape)


def pick_rows(ids, tokens, first, rows, follow=()):
    count, width = tokens.shape
    blocks = count // LANES
    pieces = math.gcd(blocks, 4)
    in_hbm = [pltpu.with_memory_space_constraint(x, pltpu.HBM) for x in (ids, tokens)]
    return pl.pallas_call(
        lambda *refs: pick_body(first, *refs),
        out_shape=(
            jax.ShapeDtypeStruct((rows, width), BF16),
            jax.ShapeDtypeStruct((8, LANES), F32),
        ),
        in_specs=[pl.BlockSpec(memory_space=pltpu.HBM)] * 2 + follows(follow),
        out_specs=[pl.BlockSpec(memory_space=pltpu.VMEM)] * 2,
        scratch_shapes=[
            pltpu.VMEM(ids.shape, ids.dtype),
            pltpu.VMEM(tokens.shape, tokens.dtype),
            pltpu.SemaphoreType.DMA((pieces + 1,)),
        ],
        compiler_params=params(16),
        cost_estimate=TINY,
        name="pick_rows",
    )(*in_hbm, *follow)


def signs(size):
    common = iota((size, size), 0) & iota((size, size), 1)
    shift = 1
    while shift < size.bit_length():
        shift *= 2
    while shift > 1:
        shift //= 2
        common = common ^ (common >> shift)
    return (1 - 2 * (common & 1)).astype(F32).astype(BF16)


def expand_body(first, count, last, me_ref, *refs):
    parts, refs = refs[:count], refs[count:]
    before_ref = None
    if last:
        before_ref, refs = refs[0], refs[1:]
    gate_hbm, up_hbm, *outs, total, held, loaded = refs
    width = parts[0].shape[1]
    columns = total.shape[2]
    tile = min(256, columns)

    def load(mask):
        rows = pl.ds(pl.multiple_of((me_ref[0] ^ mask) * width, LANES), width)
        return [
            pltpu.make_async_copy(
                weight.at[rows, pl.ds(first, columns)], held.at[mask, at], loaded.at[mask, at]
            )
            for at, weight in enumerate((gate_hbm, up_hbm))
        ]

    loads = [load(mask) for mask in range(count)]
    for copies in loads[:AHEAD]:
        for copy in copies:
            copy.start()
    table = signs(tile)
    for mask, part in enumerate(parts):
        for copies in loads[mask + AHEAD : mask + AHEAD + 1]:
            for copy in copies:
                copy.start()
        for at in range(2):
            loads[mask][at].wait()
            term = jnp.dot(part[...], held[mask, at], preferred_element_type=F32)
            if mask == 0:
                total[at] = term
            else:
                total[at] += term
    values = []
    for i in range(columns // tile):
        gate = total[0, :, i * tile : (i + 1) * tile]
        up = total[1, :, i * tile : (i + 1) * tile]
        hidden = (gate * (1.0 / (1.0 + jnp.exp(-gate))) * up).astype(BF16)
        values.append(jnp.dot(hidden, table, preferred_element_type=F32))
        if not last:
            outs[0][i] = values[i]
    if not last:
        return
    values = [before_ref[i] for i in range(before_ref.shape[0])] + values
    steps = len(values)
    gap = 1
    while gap < steps:
        values = [
            values[i] + values[i ^ gap] if not i & gap else values[i ^ gap] - values[i]
            for i in range(steps)
        ]
        gap *= 2
    for i in range(steps):
        low = 0
        for out in outs:
            rows = out.shape[0]
            out[:, i * tile : (i + 1) * tile] = values[i][low : low + rows].astype(BF16)
            low += rows


def expand(parts, rows, me, gate_weight, up_weight, before=None, follow=()):
    depth, width = gate_weight.shape
    last = before is not None
    columns = width // 2
    first = columns if last else 0
    tile = min(256, columns)
    count = len(parts)
    vmem = pl.BlockSpec(memory_space=pltpu.VMEM)
    in_hbm = [pltpu.with_memory_space_constraint(x, pltpu.HBM) for x in (gate_weight, up_weight)]
    args = [me, *parts] + ([before] if last else [])
    used = len(args) + 2
    if last:
        out_shape = [jax.ShapeDtypeStruct((rows // 2, width), BF16)] * 2
    else:
        out_shape = [jax.ShapeDtypeStruct((columns // tile, rows, tile), F32)]
    return pl.pallas_call(
        lambda *refs: expand_body(first, count, last, *refs[:used], *refs[used + len(follow) :]),
        in_specs=[pl.BlockSpec(memory_space=pltpu.SMEM)]
        + [vmem] * (used - 3)
        + [pl.BlockSpec(memory_space=pltpu.HBM)] * 2
        + follows(follow),
        out_specs=[vmem] * len(out_shape),
        out_shape=out_shape,
        scratch_shapes=[
            pltpu.VMEM((2, rows, columns), F32),
            pltpu.VMEM((count, 2, depth // count, columns), BF16),
            pltpu.SemaphoreType.DMA((count, 2)),
        ],
        compiler_params=params(EXPAND_MIB),
        cost_estimate=TINY,
        name="expand_last" if last else "expand_first",
    )(*args, *in_hbm, *follow)


def clip_body(ins, outs):
    level = CLIP_SHARE * jnp.max(ins[0][8:, :])
    low = 0
    for part in ins[1:]:
        rows = part.shape[0]
        outs[0][low : low + rows, :] = jnp.clip(part[...].astype(F32), -level, level).astype(BF16)
        low += rows


def down_body(first, me_ref, clipped_ref, weight_hbm, *refs):
    owners = lax.axis_size("tensor")
    half = owners // 2
    other_ref, same_ref, held, loaded = refs[-4:]
    fc = same_ref.shape[2]
    stride = weight_hbm.shape[1] // owners
    masks = [2 * i + 1 for i in range(half)] + [2 * i for i in range(half)]

    def load(i):
        column = pl.multiple_of((me_ref[0] ^ masks[i]) * stride + first, LANES)
        return pltpu.make_async_copy(
            weight_hbm.at[:, pl.ds(column, fc)],
            held.at[i // 2, :, pl.ds(i % 2 * fc, fc)],
            loaded.at[i],
        )

    loads = [load(i) for i in range(owners)]
    for copy in loads[: 2 * AHEAD]:
        copy.start()
    for pair in range(half):
        for copy in loads[2 * (pair + AHEAD) : 2 * (pair + AHEAD + 1)]:
            copy.start()
        for copy in loads[2 * pair : 2 * pair + 2]:
            copy.wait()
        terms = jnp.dot(clipped_ref[...], held[pair], preferred_element_type=F32).astype(BF16)
        for side in range(2):
            i = 2 * pair + side
            term = terms[:, side * fc : (side + 1) * fc]
            if i < half:
                other_ref[i] = term
            else:
                same_ref[i - half] = term


def down(clipped, weight, me, units, first, follow=()):
    depth = weight.shape[0]
    owners = lax.axis_size("tensor")
    half = owners // 2
    rows = clipped.shape[0]
    fc = units * LANES
    vmem = pl.BlockSpec(memory_space=pltpu.VMEM)
    shape = jax.ShapeDtypeStruct((half, rows, fc), BF16)
    return pl.pallas_call(
        lambda *refs: down_body(first * LANES, *refs),
        in_specs=[
            pl.BlockSpec(memory_space=pltpu.SMEM),
            vmem,
            pl.BlockSpec(memory_space=pltpu.HBM),
        ]
        + follows(follow),
        out_specs=[vmem] * 2,
        out_shape=[shape] * 2,
        scratch_shapes=[
            pltpu.VMEM((half, depth, 2 * fc), BF16),
            pltpu.SemaphoreType.DMA((owners,)),
        ],
        compiler_params=params(16),
        cost_estimate=TINY,
        name="down",
    )(me, clipped, pltpu.with_memory_space_constraint(weight, pltpu.HBM), *follow)


def spread_body(count, ids_ref, probs_ref, *refs):
    mine, theirs = refs[:count], refs[count : 2 * count]
    out_ref, mark_ref = refs[-2:]
    mark_ref[...] = jnp.zeros_like(mark_ref)
    tokens = ids_ref.shape[1]
    summed = jnp.concatenate(
        [(a[0].astype(F32) + b[0].astype(F32)).astype(BF16) for a, b in zip(mine, theirs)], axis=0
    )
    slots = slots_of(ids_ref)
    share = jnp.where(ids_ref[0:1, :] == 0, probs_ref[0:1, :], 0.0) + jnp.where(
        ids_ref[1:2, :] == 0, probs_ref[1:2, :], 0.0
    )
    blocks = tokens // LANES
    share = jnp.concatenate(
        [share[:, LANES * k : LANES * (k + 1)] for k in range(blocks)]
        + [jnp.zeros((LANES - blocks, LANES), F32)],
        axis=0,
    ).T
    slots = jnp.concatenate(
        [slots, jnp.zeros((LANES - slots.shape[0], LANES), F32)], axis=0
    ).T.astype(jnp.int32)
    at = iota((LANES, summed.shape[0]), 1)
    for k in range(blocks):
        hot = jnp.where(at == slots[:, k : k + 1], 1.0, 0.0).astype(BF16)
        rows = jnp.dot(hot, summed, preferred_element_type=F32)
        out_ref[LANES * k : LANES * (k + 1), :] = (rows * share[:, k : k + 1]).astype(BF16)


def spread(ids, probs, state, first, features, out, follow=()):
    mine, theirs = [x[0] for x in state], [x[1] for x in state]
    tokens = ids.shape[1]
    count = len(mine)
    _, rows, fc = mine[0].shape
    args = [ids, probs, *mine, *theirs]
    in_specs = [pl.BlockSpec(x.shape, lambda i, d=x.ndim: (0,) * d) for x in args]
    aliases = {}
    if out is not None:
        aliases = {len(args): 0}
        follow = [out, *follow]
    return pl.pallas_call(
        lambda *refs: spread_body(count, *refs[: 2 + 2 * count], *refs[-2:]),
        grid=(1,),
        in_specs=in_specs + follows(follow),
        out_specs=[
            pl.BlockSpec((pl.Element(tokens), pl.Element(fc)), lambda i: (0, first * LANES)),
            pl.BlockSpec((8, LANES), lambda i: (0, 0)),
        ],
        out_shape=[
            jax.ShapeDtypeStruct((tokens, features), BF16),
            jax.ShapeDtypeStruct((8, LANES), F32),
        ],
        input_output_aliases=aliases,
        compiler_params=params(16),
        cost_estimate=TINY,
        name="spread",
    )(*args, *follow)


def follows(arrays):
    return [pl.BlockSpec(memory_space=pl.ANY)] * len(arrays)


def small(body, args, shapes, name, follow=()):
    vmem = pl.BlockSpec(memory_space=pltpu.VMEM)
    count = len(args)
    specs = [pl.BlockSpec(memory_space=pltpu.SMEM) if x.ndim == 1 else vmem for x in args]
    return pl.pallas_call(
        lambda *refs: body(refs[:count], refs[count + len(follow) :]),
        in_specs=specs + follows(follow),
        out_specs=[vmem] * len(shapes),
        out_shape=[jax.ShapeDtypeStruct(*x) for x in shapes],
        compiler_params=params(16),
        cost_estimate=TINY,
        name=name,
    )(*args, *follow)


def gather_near(own, orders):
    return {0: own} | {1 << bit: across(own, bit) for bit in orders[0]}


def cut_body(firsts, ins, outs):
    for h, at in enumerate(firsts):
        rows = outs[h].shape[0]
        outs[h][...] = ins[at][h * rows : (h + 1) * rows, :]
    for block, out in zip(ins, outs[2:]):
        out[...] = block[...]


def join_body(ins, outs):
    for i, out in enumerate(outs):
        rows = out.shape[0] // 2
        out[:rows, :] = ins[2 * i][...]
        out[rows:, :] = ins[2 * i + 1][...]


def cut(full, orders, follow, passed=False):
    rows, width = full[0].shape
    masks = [mask for mask in full if mask]
    firsts = [masks.index(1 << order[0]) for order in orders]
    shapes = [((rows // 2, width), BF16)] * 2 + [((rows, width), BF16)] * len(masks) * passed
    outs = small(
        lambda ins, outs: cut_body(firsts, ins, outs),
        [full[mask] for mask in masks],
        shapes,
        "cut",
        follow,
    )
    return outs[:2], full | dict(zip(masks, outs[2:]))


def gather_far(full, cuts, orders):
    half = full[0].shape[0] // len(orders)
    firsts = [1 << order[0] for order in orders]
    part = {}

    def get(mask, h):
        if (mask, h) in part:
            return part[mask, h]
        return cuts[h] if mask == firsts[h] else full[mask][h * half : (h + 1) * half]

    have = [[0, first] for first in firsts]
    for at in range(1, len(orders[0])):
        for h, order in enumerate(orders):
            bit = order[at]
            for mask in list(have[h]):
                there = mask | 1 << bit
                if there not in full:
                    part[there, h] = across(get(mask, h), bit)
                have[h].append(there)
    return part


def join(part, follow):
    masks = sorted({mask for mask, _ in part})
    halves = [part[mask, h] for mask in masks for h in range(2)]
    half, width = halves[0].shape
    joined = small(join_body, halves, [((2 * half, width), BF16)] * len(masks), "join", follow)
    return dict(zip(masks, joined))


def paired(pieces):
    return pieces | {mask | 1: across(block, 0) for mask, block in pieces.items()}


def turn_body(bits, scale, ins, outs):
    me_ref, ins = ins[0], ins[1:]
    count = len(bits)
    for h, bit in enumerate(bits):
        flip = (1 - 2 * ((me_ref[0] >> bit) & 1)).astype(F32)
        own = ins[2 * h][...].astype(F32)
        came = ins[2 * h + 1][...].astype(F32)
        value = came + own * flip
        if scale is not None:
            value = value * scale
            top = jnp.max(jnp.abs(own) + jnp.abs(came), axis=0, keepdims=True) * scale
            wide = top[:, :LANES]
            for k in range(1, top.shape[1] // LANES):
                wide = jnp.maximum(wide, top[:, k * LANES : (k + 1) * LANES])
            outs[count + h][...] = jnp.broadcast_to(wide, outs[count + h].shape)
        outs[h][...] = value.astype(BF16)


def turn(me, blocks, came, bits, follow=(), scale=None):
    args = [me] + [x for pair in zip(blocks, came) for x in pair]
    shapes = [(x.shape, BF16) for x in blocks]
    if scale is not None:
        shapes += [((8, LANES), F32)] * len(blocks)
    return small(
        lambda ins, outs: turn_body(bits, scale, ins, outs), args, shapes, "turn", follow
    )


def largest(top_in, tops, lasts):
    bits = range(lax.axis_size("tensor").bit_length() - 1)
    values = jnp.concatenate([top_in, *tops], axis=0)
    for bit in bits:
        if bit not in lasts:
            values = jnp.maximum(values, across(values, bit))
    n = top_in.shape[0]
    top_in, first, second = values[:n], values[n : 2 * n], values[2 * n :]
    if lasts[0] != lasts[1]:
        pair = jnp.concatenate([top_in, second], axis=0)
        came_first, came_pair = across(first, lasts[1]), across(pair, lasts[0])
        first = jnp.maximum(first, came_first)
        pair = jnp.maximum(pair, came_pair)
        top_in, second = pair[:n], pair[n:]
    values = jnp.concatenate([top_in, jnp.maximum(first, second)], axis=0)
    blocks = lax.axis_size("dp")
    far = 1
    while far < blocks:
        pairs = [(r, r ^ far) for r in range(blocks)]
        values = jnp.maximum(values, lax.ppermute(values, "dp", pairs))
        far *= 2
    return values


def on_device(tokens, expert_ids, gate_probs, gate_weight, up_weight, down_weight):
    count = lax.axis_size("tensor")
    bits = count.bit_length() - 1
    outer = list(range(1, bits))
    orders = [outer, outer[::-1]]
    me = lax.axis_index("tensor")
    me_arr = me.astype(jnp.int32).reshape(1)
    ids, probs = expert_ids.T, gate_probs.T
    rows = CAP // ROW_CHUNKS
    half = rows // 2
    scale = 1.0 / math.sqrt(gate_weight.shape[1] * count)
    stages = [[order[at] for order in orders] for at in range(len(outer))]
    early_bit = stages[-1][1]

    def send(blocks, bits):
        return [across(x, bit) for x, bit in zip(blocks, bits)]

    def start_turn(halves, follow=()):
        blocks = turn(me_arr, halves, send(halves, [0, 0]), [0, 0], follow)
        return blocks, send(blocks, stages[0])

    def go_on(blocks, came, at, follow=()):
        blocks = turn(me_arr, blocks, came, stages[at], follow)
        return blocks, send(blocks, stages[at + 1])

    def end_turn(blocks, came, follow=()):
        made = turn(me_arr, blocks, came, stages[-1], follow, scale)
        return made[: len(blocks)], made[len(blocks) :]

    own_a, top_a = pick_rows(ids, tokens, 0, rows, [me_arr])
    near_a = gather_near(own_a, orders)
    weights = (me_arr, gate_weight, up_weight)
    cuts_a, near_a = cut(near_a, orders, [])
    own_b, top_b = pick_rows(ids, tokens, rows, rows, cuts_a)
    top_in = jnp.maximum(top_a, top_b)
    top_in = jnp.maximum(top_in, across(top_in, early_bit))
    far_a = join(gather_far(near_a, cuts_a, orders), [own_b, top_in])
    near_b = gather_near(own_b, orders)
    parts_a = paired(near_a | far_a)
    parts_a = [parts_a[mask] for mask in range(count)]
    first_a = expand(parts_a, rows, *weights)
    local_a = expand(parts_a, rows, *weights, *first_a)
    cuts_b, near_b = cut(near_b, orders, local_a, True)
    parts_b = paired(near_b)
    theirs_b = [block for mask, block in parts_b.items() if mask & 1]
    blocks_a, came_a = start_turn(local_a)
    far_b = join(gather_far(near_b, cuts_b, orders), list(blocks_a) + theirs_b)
    parts_b |= paired(far_b)
    parts_b = [parts_b[mask] for mask in range(count)]
    first_b = expand(parts_b, rows, *weights, None, blocks_a)
    for at in range(len(outer) - 1):
        blocks_a, came_a = go_on(blocks_a, came_a, at, first_b)
    local_b = expand(parts_b, rows, *weights, *first_b, blocks_a)
    turned_a, rot_a = end_turn(blocks_a, came_a, local_b)
    blocks_b, came_b = start_turn(local_b, rot_a)
    for at in range(len(outer) - 1):
        blocks_b, came_b = go_on(blocks_b, came_b, at)
    turned_b, rot_b = end_turn(blocks_b, came_b)
    rotated = turned_a + turned_b

    peaks = largest(top_in, [jnp.maximum(x, y) for x, y in zip(rot_a, rot_b)], stages[-1])
    clipped = small(
        clip_body, [peaks, *rotated], [((CAP, gate_weight.shape[1]), BF16)], "clip"
    )[0]

    tops = pl.pallas_call(
        peaks_body,
        out_specs=pl.BlockSpec(memory_space=pltpu.SMEM),
        out_shape=jax.ShapeDtypeStruct((2,), F32),
        name="peaks",
    )(peaks)
    units = tokens.shape[1] // LANES
    sizes = chunks_of(units)
    firsts = [sum(sizes[:i]) for i in range(len(sizes))]
    total = len(sizes)
    products, begun, ended, out, last = {}, {}, {}, None, []
    for step, chunk in sums_order(total):
        if step == "product":
            products[chunk] = down(
                clipped, down_weight, me_arr, sizes[chunk], firsts[chunk], last
            )
            last = [products[chunk][1]]
        elif step == "begin":
            other, same = products[chunk]
            begun[chunk] = fold_cores(same, across(other, 0), stages[0], last)
            last = [keep for keep, _, _ in begun[chunk]]
        elif step == "finish":
            ahead = [c for c in products if c not in begun]
            passed = [products[c][0] for c in ahead]
            ended[chunk], passed = finish(begun[chunk], stages, last, passed)
            for c, other in zip(ahead, passed):
                products[c] = (other, products[c][1])
            last = [keep for keep, _, _ in ended[chunk]]
        else:
            out, mark = spread(
                ids, probs, ended[chunk], firsts[chunk], tokens.shape[1], out, last
            )
            last = [mark]
    return out, tops


def chunks_of(units):
    return [2] * (units // 2) + [1] * (units % 2)


def sums_order(total):
    order = [("product", 0)]
    for chunk in range(total):
        if chunk + 1 < total:
            order.append(("product", chunk + 1))
        order.append(("begin", chunk))
        if chunk > 0:
            order.append(("finish", chunk - 1))
        if chunk > 1 and chunk + 1 < total:
            order.append(("spread", chunk - 2))
    order.append(("finish", total - 1))
    return order + [("spread", c) for c in range(total) if ("spread", c) not in order]


def peaks_body(values_ref, out_ref):
    out_ref[0] = jnp.max(values_ref[:8, :])
    out_ref[1] = jnp.max(values_ref[8:, :])


def fold_body(plan, passed, ins, outs):
    for i in range(passed):
        outs[len(plan) + i][...] = ins[len(ins) - passed + i][...]
    for out, (slots, low) in zip(outs, plan):
        rows = out.shape[1]
        for slot, terms in enumerate(slots):
            total = 0.0
            for at, i in terms:
                total = total + ins[at][i, low : low + rows, :].astype(F32)
            out[slot] = total.astype(BF16)


def fold(args, terms, masks, lows, rows, bits, follow, passed=()):
    plan, shapes, lefts = [], [], []
    width = args[0].shape[2]
    for h, bit in enumerate(bits):
        for side in (0, 1):
            chosen = [m for m in masks[h] if m >> bit & 1 == side]
            plan.append(([terms[h][m] for m in chosen], lows[h]))
            shapes.append(((len(chosen), rows, width), BF16))
        lefts.append([m for m in masks[h] if not m >> bit & 1])
    shapes += [(x.shape, x.dtype) for x in passed]
    made = small(
        lambda ins, outs: fold_body(plan, len(passed), ins, outs),
        [*args, *passed],
        shapes,
        "fold",
        follow,
    )
    state = [
        (made[2 * h], across(made[2 * h + 1], bit), lefts[h]) for h, bit in enumerate(bits)
    ]
    return state, made[len(plan) :]


def fold_cores(same, came, bits, follow):
    half = same.shape[1] // 2
    masks = [2 * i for i in range(same.shape[0])]
    terms = {m: ((0, i), (1, i)) for i, m in enumerate(masks)}
    return fold([same, came], [terms] * 2, [masks] * 2, [0, half], half, bits, follow)[0]


def finish(state, stages, follow, passed=()):
    for bits in stages[1:]:
        args = [x for keep, recv, _ in state for x in (keep, recv)]
        masks = [left for _, _, left in state]
        terms = [
            {m: ((2 * h, i), (2 * h + 1, i)) for i, m in enumerate(left)}
            for h, left in enumerate(masks)
        ]
        state, passed = fold(
            args, terms, masks, [0, 0], args[0].shape[1], bits, follow, passed
        )
    return state, passed


def solution(mesh):
    in_specs = (
        P("dp", "tensor"),
        P("dp", None),
        P("dp", None),
        P(None, "tensor"),
        P(None, "tensor"),
        P("tensor", None),
    )
    out_specs = (P("dp", "tensor"), P())
    return jax.shard_map(
        on_device, mesh=mesh, in_specs=in_specs, out_specs=out_specs, check_vma=False
    )
```

```python
import math

import jax
import jax.numpy as jnp
from jax import lax
from jax.experimental import pallas as pl
from jax.experimental.pallas import tpu as pltpu
from jax.sharding import PartitionSpec as P

CAP = 768
CLIP_SHARE = 0.25
LANES = 128
ROW_CHUNKS = 2
BF16 = jnp.bfloat16
F32 = jnp.float32
MIB = 1 << 20
EXPAND_MIB = 24
AHEAD = 3
JOINED = 3


def params(mib):
    return pltpu.CompilerParams(vmem_limit_bytes=mib * MIB)


TINY = pl.CostEstimate(flops=1, bytes_accessed=1, transcendentals=0)


def across(block, bit):
    count = lax.axis_size("tensor")
    return lax.ppermute(block, "tensor", [(r, r ^ 1 << bit) for r in range(count)])


def iota(shape, dim):
    return lax.broadcasted_iota(jnp.int32, shape, dim)


def slots_of(ids_ref):
    tokens = ids_ref.shape[1]
    rows = tokens // LANES
    padded = (rows + 15) // 16 * 16
    hit = jnp.where((ids_ref[0:1, :] == 0) | (ids_ref[1:2, :] == 0), 1.0, 0.0)
    grid = jnp.concatenate(
        [hit[:, LANES * k : LANES * (k + 1)] for k in range(rows)]
        + [jnp.zeros((padded - rows, LANES), F32)],
        axis=0,
    )
    flat = grid.astype(BF16)
    upto = (iota((LANES, LANES), 0) <= iota((LANES, LANES), 1)).astype(F32).astype(BF16)
    before = (iota((padded, padded), 1) < iota((padded, padded), 0)).astype(F32).astype(BF16)
    within = jnp.dot(flat, upto, preferred_element_type=F32)
    offset = jnp.sum(jnp.dot(before, flat, preferred_element_type=F32), axis=1, keepdims=True)
    return jnp.where(grid > 0.0, within + offset - 1.0, -1.0)


def pick_body(first, ids_hbm, tokens_hbm, *refs):
    picked_ref, peak_ref, ids_ref, tokens_ref, loaded = refs[-5:]
    rows = picked_ref.shape[0]
    count = tokens_ref.shape[0]
    pieces = loaded.shape[0] - 1
    step = count // pieces
    ids_copy = pltpu.make_async_copy(ids_hbm, ids_ref, loaded.at[pieces])
    ids_copy.start()
    copies = [
        pltpu.make_async_copy(
            tokens_hbm.at[pl.ds(i * step, step), :],
            tokens_ref.at[pl.ds(i * step, step), :],
            loaded.at[i],
        )
        for i in range(pieces)
    ]
    for copy in copies:
        copy.start()
    ids_copy.wait()
    slots = slots_of(ids_ref).astype(jnp.int32)
    wanted = iota((rows, LANES), 0) + first
    picked = jnp.zeros(picked_ref.shape, F32)
    for i, copy in enumerate(copies):
        hot = jnp.concatenate(
            [
                jnp.where(wanted == slots[k : k + 1, :], 1.0, 0.0).astype(BF16)
                for k in range(i * step // LANES, (i + 1) * step // LANES)
            ],
            axis=1,
        )
        copy.wait()
        picked += jnp.dot(
            hot, tokens_ref[i * step : (i + 1) * step, :], preferred_element_type=F32
        )
    picked_ref[...] = picked.astype(BF16)
    peak_ref[...] = jnp.broadcast_to(jnp.max(jnp.abs(picked)), peak_ref.shape)


def pick_rows(ids, tokens, first, rows, follow=()):
    count, width = tokens.shape
    blocks = count // LANES
    pieces = math.gcd(blocks, 4)
    in_hbm = [pltpu.with_memory_space_constraint(x, pltpu.HBM) for x in (ids, tokens)]
    return pl.pallas_call(
        lambda *refs: pick_body(first, *refs),
        out_shape=(
            jax.ShapeDtypeStruct((rows, width), BF16),
            jax.ShapeDtypeStruct((8, LANES), F32),
        ),
        in_specs=[pl.BlockSpec(memory_space=pltpu.HBM)] * 2 + follows(follow),
        out_specs=[pl.BlockSpec(memory_space=pltpu.VMEM)] * 2,
        scratch_shapes=[
            pltpu.VMEM(ids.shape, ids.dtype),
            pltpu.VMEM(tokens.shape, tokens.dtype),
            pltpu.SemaphoreType.DMA((pieces + 1,)),
        ],
        compiler_params=params(16),
        cost_estimate=TINY,
        name="pick_rows",
    )(*in_hbm, *follow)


def signs(size):
    common = iota((size, size), 0) & iota((size, size), 1)
    shift = 1
    while shift < size.bit_length():
        shift *= 2
    while shift > 1:
        shift //= 2
        common = common ^ (common >> shift)
    return (1 - 2 * (common & 1)).astype(F32).astype(BF16)


def multiply_body(masks, cuts, resumed, last, me_ref, *refs):
    count = len(masks)
    parts = []
    for pieces in cuts:
        parts.append(refs[:pieces])
        refs = refs[pieces:]
    before_ref = None
    if resumed:
        before_ref, refs = refs[0], refs[1:]
    gate_hbm, up_hbm, *outs, held, loaded = refs
    if last:
        *outs, total = outs
    else:
        total = outs[0]
    features = parts[0][0].shape[1]
    width = total.shape[2]

    def load(i):
        rows = pl.ds(pl.multiple_of((me_ref[0] ^ masks[i]) * features, LANES), features)
        return [
            pltpu.make_async_copy(weight.at[rows, :], held.at[i, at], loaded.at[i, at])
            for at, weight in enumerate((gate_hbm, up_hbm))
        ]

    loads = [load(i) for i in range(count)]
    for copies in loads[:AHEAD]:
        for copy in copies:
            copy.start()
    columns = min(512, width)
    for i, pieces in enumerate(parts):
        part = jnp.concatenate([piece[...] for piece in pieces], axis=0)
        for copies in loads[i + AHEAD : i + AHEAD + 1]:
            for copy in copies:
                copy.start()
        for at in range(2):
            loads[i][at].wait()
            for low in range(0, width, columns):
                span = slice(low, low + columns)
                term = jnp.dot(part, held[i, at, :, span], preferred_element_type=F32)
                if i > 0:
                    term += total[at, :, span]
                elif resumed:
                    term += before_ref[at, :, span]
                total[at, :, span] = term
    if not last:
        return
    tile = min(256, width)
    steps = width // tile
    table = signs(tile)
    values = []
    for i in range(steps):
        gate = total[0, :, i * tile : (i + 1) * tile]
        up = total[1, :, i * tile : (i + 1) * tile]
        hidden = (gate * (1.0 / (1.0 + jnp.exp(-gate))) * up).astype(BF16)
        values.append(jnp.dot(hidden, table, preferred_element_type=F32))
    gap = 1
    while gap < steps:
        values = [
            values[i] + values[i ^ gap] if not i & gap else values[i ^ gap] - values[i]
            for i in range(steps)
        ]
        gap *= 2
    for i in range(steps):
        low = 0
        for out in outs:
            rows = out.shape[0]
            out[:, i * tile : (i + 1) * tile] = values[i][low : low + rows].astype(BF16)
            low += rows


def multiply(parts, me, gate_weight, up_weight, before=None, last=False, follow=()):
    masks = sorted(parts)
    depth, width = gate_weight.shape
    count = len(masks)
    pieces = [x if isinstance(x, (list, tuple)) else [x] for x in (parts[m] for m in masks)]
    cuts = [len(x) for x in pieces]
    rows, features = sum(x.shape[0] for x in pieces[0]), pieces[0][0].shape[1]
    vmem = pl.BlockSpec(memory_space=pltpu.VMEM)
    resumed = before is not None
    in_hbm = [pltpu.with_memory_space_constraint(x, pltpu.HBM) for x in (gate_weight, up_weight)]
    args = [me, *[x for group in pieces for x in group]] + ([before] if resumed else [])
    used = len(args) + 2
    scratch = [
        pltpu.VMEM((count, 2, features, width), BF16),
        pltpu.SemaphoreType.DMA((count, 2)),
    ]
    if last:
        out_shape = [jax.ShapeDtypeStruct((rows // JOINED, width), BF16)] * JOINED
        scratch.insert(0, pltpu.VMEM((2, rows, width), F32))
    else:
        out_shape = [jax.ShapeDtypeStruct((2, rows, width), F32)]
    made = pl.pallas_call(
        lambda *refs: multiply_body(
            masks, cuts, resumed, last, *refs[:used], *refs[used + len(follow) :]
        ),
        in_specs=[pl.BlockSpec(memory_space=pltpu.SMEM)]
        + [vmem] * (used - 3)
        + [pl.BlockSpec(memory_space=pltpu.HBM)] * 2
        + follows(follow),
        out_specs=[vmem] * len(out_shape),
        out_shape=out_shape,
        scratch_shapes=scratch,
        compiler_params=params(EXPAND_MIB),
        cost_estimate=TINY,
        name="multiply_last" if last else "multiply",
    )(*args, *in_hbm, *follow)
    return made if last else made[0]


def clip_body(ins, outs):
    level = CLIP_SHARE * jnp.max(ins[0][8:, :])
    low = 0
    for part in ins[1:]:
        rows = part.shape[0]
        outs[0][low : low + rows, :] = jnp.clip(part[...].astype(F32), -level, level).astype(BF16)
        low += rows


def down_body(first, me_ref, clipped_ref, weight_hbm, *refs):
    owners = lax.axis_size("tensor")
    half = owners // 2
    other_ref, same_ref, held, loaded = refs[-4:]
    fc = same_ref.shape[2]
    stride = weight_hbm.shape[1] // owners
    masks = [2 * i + 1 for i in range(half)] + [2 * i for i in range(half)]

    def load(i):
        column = pl.multiple_of((me_ref[0] ^ masks[i]) * stride + first, LANES)
        return pltpu.make_async_copy(
            weight_hbm.at[:, pl.ds(column, fc)],
            held.at[i // 2, :, pl.ds(i % 2 * fc, fc)],
            loaded.at[i],
        )

    loads = [load(i) for i in range(owners)]
    for copy in loads[: 2 * AHEAD]:
        copy.start()
    for pair in range(half):
        for copy in loads[2 * (pair + AHEAD) : 2 * (pair + AHEAD + 1)]:
            copy.start()
        for copy in loads[2 * pair : 2 * pair + 2]:
            copy.wait()
        terms = jnp.dot(clipped_ref[...], held[pair], preferred_element_type=F32).astype(BF16)
        for side in range(2):
            i = 2 * pair + side
            term = terms[:, side * fc : (side + 1) * fc]
            if i < half:
                other_ref[i] = term
            else:
                same_ref[i - half] = term


def down(clipped, weight, me, units, first, follow=()):
    depth = weight.shape[0]
    owners = lax.axis_size("tensor")
    half = owners // 2
    rows = clipped.shape[0]
    fc = units * LANES
    vmem = pl.BlockSpec(memory_space=pltpu.VMEM)
    shape = jax.ShapeDtypeStruct((half, rows, fc), BF16)
    return pl.pallas_call(
        lambda *refs: down_body(first * LANES, *refs),
        in_specs=[
            pl.BlockSpec(memory_space=pltpu.SMEM),
            vmem,
            pl.BlockSpec(memory_space=pltpu.HBM),
        ]
        + follows(follow),
        out_specs=[vmem] * 2,
        out_shape=[shape] * 2,
        scratch_shapes=[
            pltpu.VMEM((half, depth, 2 * fc), BF16),
            pltpu.SemaphoreType.DMA((owners,)),
        ],
        compiler_params=params(16),
        cost_estimate=TINY,
        name="down",
    )(me, clipped, pltpu.with_memory_space_constraint(weight, pltpu.HBM), *follow)


def spread_body(count, ids_ref, probs_ref, *refs):
    mine, theirs = refs[:count], refs[count : 2 * count]
    out_ref, mark_ref = refs[-2:]
    mark_ref[...] = jnp.zeros_like(mark_ref)
    tokens = ids_ref.shape[1]
    summed = jnp.concatenate(
        [(a[0].astype(F32) + b[0].astype(F32)).astype(BF16) for a, b in zip(mine, theirs)], axis=0
    )
    slots = slots_of(ids_ref)
    share = jnp.where(ids_ref[0:1, :] == 0, probs_ref[0:1, :], 0.0) + jnp.where(
        ids_ref[1:2, :] == 0, probs_ref[1:2, :], 0.0
    )
    blocks = tokens // LANES
    share = jnp.concatenate(
        [share[:, LANES * k : LANES * (k + 1)] for k in range(blocks)]
        + [jnp.zeros((LANES - blocks, LANES), F32)],
        axis=0,
    ).T
    slots = jnp.concatenate(
        [slots, jnp.zeros((LANES - slots.shape[0], LANES), F32)], axis=0
    ).T.astype(jnp.int32)
    at = iota((LANES, summed.shape[0]), 1)
    for k in range(blocks):
        hot = jnp.where(at == slots[:, k : k + 1], 1.0, 0.0).astype(BF16)
        rows = jnp.dot(hot, summed, preferred_element_type=F32)
        out_ref[LANES * k : LANES * (k + 1), :] = (rows * share[:, k : k + 1]).astype(BF16)


def spread(ids, probs, state, first, features, out, follow=()):
    mine, theirs = [x[0] for x in state], [x[1] for x in state]
    tokens = ids.shape[1]
    count = len(mine)
    _, rows, fc = mine[0].shape
    args = [ids, probs, *mine, *theirs]
    in_specs = [pl.BlockSpec(x.shape, lambda i, d=x.ndim: (0,) * d) for x in args]
    aliases = {}
    if out is not None:
        aliases = {len(args): 0}
        follow = [out, *follow]
    return pl.pallas_call(
        lambda *refs: spread_body(count, *refs[: 2 + 2 * count], *refs[-2:]),
        grid=(1,),
        in_specs=in_specs + follows(follow),
        out_specs=[
            pl.BlockSpec((pl.Element(tokens), pl.Element(fc)), lambda i: (0, first * LANES)),
            pl.BlockSpec((8, LANES), lambda i: (0, 0)),
        ],
        out_shape=[
            jax.ShapeDtypeStruct((tokens, features), BF16),
            jax.ShapeDtypeStruct((8, LANES), F32),
        ],
        input_output_aliases=aliases,
        compiler_params=params(16),
        cost_estimate=TINY,
        name="spread",
    )(*args, *follow)


def follows(arrays):
    return [pl.BlockSpec(memory_space=pl.ANY)] * len(arrays)


def small(body, args, shapes, name, follow=()):
    vmem = pl.BlockSpec(memory_space=pltpu.VMEM)
    count = len(args)
    specs = [pl.BlockSpec(memory_space=pltpu.SMEM) if x.ndim == 1 else vmem for x in args]
    return pl.pallas_call(
        lambda *refs: body(refs[:count], refs[count + len(follow) :]),
        in_specs=specs + follows(follow),
        out_specs=[vmem] * len(shapes),
        out_shape=[jax.ShapeDtypeStruct(*x) for x in shapes],
        compiler_params=params(16),
        cost_estimate=TINY,
        name=name,
    )(*args, *follow)


def gather_near(own, orders):
    return {0: own} | {1 << bit: across(own, bit) for bit in orders[0]}


def cut_body(firsts, ins, outs):
    for h, at in enumerate(firsts):
        rows = outs[h].shape[0]
        outs[h][...] = ins[at][h * rows : (h + 1) * rows, :]
    for block, out in zip(ins, outs[2:]):
        out[...] = block[...]


def join_body(ins, outs):
    pieces = 2 * len(outs) // len(ins)
    for i in range(len(ins) // 2):
        whole = jnp.concatenate([ins[2 * i][...], ins[2 * i + 1][...]], axis=0)
        for k in range(pieces):
            out = outs[pieces * i + k]
            rows = out.shape[0]
            out[...] = whole[k * rows : (k + 1) * rows, :]


def cut(full, orders, follow, passed=False):
    rows, width = full[0].shape
    masks = [mask for mask in full if mask]
    firsts = [masks.index(1 << order[0]) for order in orders]
    shapes = [((rows // 2, width), BF16)] * 2 + [((rows, width), BF16)] * len(masks) * passed
    outs = small(
        lambda ins, outs: cut_body(firsts, ins, outs),
        [full[mask] for mask in masks],
        shapes,
        "cut",
        follow,
    )
    return outs[:2], full | dict(zip(masks, outs[2:]))


def gather_far(full, cuts, orders):
    half = full[0].shape[0] // len(orders)
    firsts = [1 << order[0] for order in orders]
    part = {}

    def get(mask, h):
        if (mask, h) in part:
            return part[mask, h]
        return cuts[h] if mask == firsts[h] else full[mask][h * half : (h + 1) * half]

    have = [[0, first] for first in firsts]
    for at in range(1, len(orders[0])):
        for h, order in enumerate(orders):
            bit = order[at]
            for mask in list(have[h]):
                there = mask | 1 << bit
                if there not in full:
                    part[there, h] = across(get(mask, h), bit)
                have[h].append(there)
    return part


def join(part, follow):
    masks = sorted({mask for mask, _ in part})
    halves = [part[mask, h] for mask in masks for h in range(2)]
    half, width = halves[0].shape
    shapes = [((2 * half // JOINED, width), BF16)] * (JOINED * len(masks))
    joined = small(join_body, halves, shapes, "join", follow)
    return {mask: joined[JOINED * i : JOINED * (i + 1)] for i, mask in enumerate(masks)}


def paired(pieces):
    return pieces | {
        mask | 1: [across(x, 0) for x in block] if isinstance(block, list) else across(block, 0)
        for mask, block in pieces.items()
    }


def beyond_own(pieces):
    return {mask: block for mask, block in pieces.items() if mask}


def turn_body(bits, scale, ins, outs):
    me_ref, ins = ins[0], ins[1:]
    count = len(bits)
    for h, bit in enumerate(bits):
        flip = (1 - 2 * ((me_ref[0] >> bit) & 1)).astype(F32)
        own = ins[2 * h][...].astype(F32)
        came = ins[2 * h + 1][...].astype(F32)
        value = came + own * flip
        if scale is not None:
            value = value * scale
            top = jnp.max(jnp.abs(own) + jnp.abs(came), axis=0, keepdims=True) * scale
            wide = top[:, :LANES]
            for k in range(1, top.shape[1] // LANES):
                wide = jnp.maximum(wide, top[:, k * LANES : (k + 1) * LANES])
            outs[count + h][...] = jnp.broadcast_to(wide, outs[count + h].shape)
        outs[h][...] = value.astype(BF16)


def turn_cores_body(ins, outs):
    me_ref, ins = ins[0], ins[1:]
    flip = (1 - 2 * (me_ref[0] & 1)).astype(F32)
    own = jnp.concatenate([x[...] for x in ins[: len(ins) // 2]], axis=0).astype(F32)
    came = jnp.concatenate([x[...] for x in ins[len(ins) // 2 :]], axis=0).astype(F32)
    value = (came + own * flip).astype(BF16)
    rows = outs[0].shape[0]
    for h, out in enumerate(outs):
        out[...] = value[h * rows : (h + 1) * rows, :]


def turn(me, blocks, came, bits, follow=(), scale=None):
    args = [me] + [x for pair in zip(blocks, came) for x in pair]
    shapes = [(x.shape, BF16) for x in blocks]
    if scale is not None:
        shapes += [((8, LANES), F32)] * len(blocks)
    return small(
        lambda ins, outs: turn_body(bits, scale, ins, outs), args, shapes, "turn", follow
    )


def largest(top_in, tops, lasts):
    bits = range(lax.axis_size("tensor").bit_length() - 1)
    values = jnp.concatenate([top_in, *tops], axis=0)
    for bit in bits:
        if bit not in lasts:
            values = jnp.maximum(values, across(values, bit))
    n = top_in.shape[0]
    top_in, first, second = values[:n], values[n : 2 * n], values[2 * n :]
    if lasts[0] != lasts[1]:
        pair = jnp.concatenate([top_in, second], axis=0)
        came_first, came_pair = across(first, lasts[1]), across(pair, lasts[0])
        first = jnp.maximum(first, came_first)
        pair = jnp.maximum(pair, came_pair)
        top_in, second = pair[:n], pair[n:]
    values = jnp.concatenate([top_in, jnp.maximum(first, second)], axis=0)
    blocks = lax.axis_size("dp")
    far = 1
    while far < blocks:
        pairs = [(r, r ^ far) for r in range(blocks)]
        values = jnp.maximum(values, lax.ppermute(values, "dp", pairs))
        far *= 2
    return values


def on_device(tokens, expert_ids, gate_probs, gate_weight, up_weight, down_weight):
    count = lax.axis_size("tensor")
    bits = count.bit_length() - 1
    outer = list(range(1, bits))
    orders = [outer, outer[::-1]]
    me = lax.axis_index("tensor")
    me_arr = me.astype(jnp.int32).reshape(1)
    ids, probs = expert_ids.T, gate_probs.T
    rows = CAP // ROW_CHUNKS
    weights = (me_arr, gate_weight, up_weight)
    half = rows // 2
    scale = 1.0 / math.sqrt(gate_weight.shape[1] * count)
    stages = [[order[at] for order in orders] for at in range(len(outer))]
    early_bit = stages[-1][1]

    def send(blocks, bits):
        return [across(x, bit) for x, bit in zip(blocks, bits)]

    def start_turn(pieces, follow=()):
        shape = ((half, pieces[0].shape[1]), BF16)
        args = [me_arr, *pieces, *[across(x, 0) for x in pieces]]
        blocks = small(turn_cores_body, args, [shape] * 2, "turn", follow)
        return blocks, send(blocks, stages[0])

    def go_on(blocks, came, at, follow=()):
        blocks = turn(me_arr, blocks, came, stages[at], follow)
        return blocks, send(blocks, stages[at + 1])

    def end_turn(blocks, came, follow=()):
        made = turn(me_arr, blocks, came, stages[-1], follow, scale)
        return made[: len(blocks)], made[len(blocks) :]

    own_a, top_a = pick_rows(ids, tokens, 0, rows, [me_arr])
    near_a = gather_near(own_a, orders)
    total_a = multiply({0: own_a}, *weights)
    own_b, top_b = pick_rows(ids, tokens, rows, rows, [total_a])
    near_b = gather_near(own_b, orders)
    total_b = multiply({0: own_b}, *weights)
    cuts_a, near_a = cut(near_a, orders, [total_b], True)
    total_a = multiply(beyond_own(paired(near_a)), *weights, total_a)
    cuts_b, near_b = cut(near_b, orders, [total_a], True)
    total_b = multiply(beyond_own(near_b), *weights, total_b)
    top_in = jnp.maximum(top_a, top_b)
    top_in = jnp.maximum(top_in, across(top_in, early_bit))
    far_a = join(gather_far(near_a, cuts_a, orders), [total_b, top_in])
    far_b = join(gather_far(near_b, cuts_b, orders), far_a[max(far_a)])
    local_a = multiply(paired(far_a), *weights, total_a, True, far_b[max(far_b)])
    blocks_a, came_a = start_turn(local_a)
    theirs = paired({0: own_b} | beyond_own(near_b))
    theirs = {mask: block for mask, block in theirs.items() if mask & 1}
    total_b = multiply(theirs, *weights, total_b, follow=blocks_a)
    for at in range(len(outer) - 1):
        blocks_a, came_a = go_on(blocks_a, came_a, at, [total_b])
    local_b = multiply(paired(far_b), *weights, total_b, True, blocks_a)
    turned_a, rot_a = end_turn(blocks_a, came_a, local_b)
    blocks_b, came_b = start_turn(local_b, rot_a)
    for at in range(len(outer) - 1):
        blocks_b, came_b = go_on(blocks_b, came_b, at)
    turned_b, rot_b = end_turn(blocks_b, came_b)
    rotated = turned_a + turned_b

    peaks = largest(top_in, [jnp.maximum(x, y) for x, y in zip(rot_a, rot_b)], stages[-1])
    clipped = small(
        clip_body, [peaks, *rotated], [((CAP, gate_weight.shape[1]), BF16)], "clip"
    )[0]

    tops = pl.pallas_call(
        peaks_body,
        out_specs=pl.BlockSpec(memory_space=pltpu.SMEM),
        out_shape=jax.ShapeDtypeStruct((2,), F32),
        name="peaks",
    )(peaks)
    units = tokens.shape[1] // LANES
    sizes = chunks_of(units)
    firsts = [sum(sizes[:i]) for i in range(len(sizes))]
    total = len(sizes)
    products, begun, ended, out, last = {}, {}, {}, None, []
    for step, chunk in sums_order(total):
        if step == "product":
            products[chunk] = down(
                clipped, down_weight, me_arr, sizes[chunk], firsts[chunk], last
            )
            last = [products[chunk][1]]
        elif step == "begin":
            other, same = products[chunk]
            begun[chunk] = fold_cores(same, across(other, 0), stages[0], last)
            last = [keep for keep, _, _ in begun[chunk]]
        elif step == "finish":
            ahead = [c for c in products if c not in begun]
            passed = [products[c][0] for c in ahead]
            ended[chunk], passed = finish(begun[chunk], stages, last, passed)
            for c, other in zip(ahead, passed):
                products[c] = (other, products[c][1])
            last = [keep for keep, _, _ in ended[chunk]]
        else:
            out, mark = spread(
                ids, probs, ended[chunk], firsts[chunk], tokens.shape[1], out, last
            )
            last = [mark]
    return out, tops


def chunks_of(units):
    return [2] * (units // 2) + [1] * (units % 2)


def sums_order(total):
    order = [("product", 0)]
    for chunk in range(total):
        if chunk + 1 < total:
            order.append(("product", chunk + 1))
        order.append(("begin", chunk))
        if chunk > 0:
            order.append(("finish", chunk - 1))
        if chunk > 1 and chunk + 1 < total:
            order.append(("spread", chunk - 2))
    order.append(("finish", total - 1))
    return order + [("spread", c) for c in range(total) if ("spread", c) not in order]


def peaks_body(values_ref, out_ref):
    out_ref[0] = jnp.max(values_ref[:8, :])
    out_ref[1] = jnp.max(values_ref[8:, :])


def fold_body(plan, passed, ins, outs):
    for i in range(passed):
        outs[len(plan) + i][...] = ins[len(ins) - passed + i][...]
    for out, (slots, low) in zip(outs, plan):
        rows = out.shape[1]
        for slot, terms in enumerate(slots):
            total = 0.0
            for at, i in terms:
                total = total + ins[at][i, low : low + rows, :].astype(F32)
            out[slot] = total.astype(BF16)


def fold(args, terms, masks, lows, rows, bits, follow, passed=()):
    plan, shapes, lefts = [], [], []
    width = args[0].shape[2]
    for h, bit in enumerate(bits):
        for side in (0, 1):
            chosen = [m for m in masks[h] if m >> bit & 1 == side]
            plan.append(([terms[h][m] for m in chosen], lows[h]))
            shapes.append(((len(chosen), rows, width), BF16))
        lefts.append([m for m in masks[h] if not m >> bit & 1])
    shapes += [(x.shape, x.dtype) for x in passed]
    made = small(
        lambda ins, outs: fold_body(plan, len(passed), ins, outs),
        [*args, *passed],
        shapes,
        "fold",
        follow,
    )
    state = [
        (made[2 * h], across(made[2 * h + 1], bit), lefts[h]) for h, bit in enumerate(bits)
    ]
    return state, made[len(plan) :]


def fold_cores(same, came, bits, follow):
    half = same.shape[1] // 2
    masks = [2 * i for i in range(same.shape[0])]
    terms = {m: ((0, i), (1, i)) for i, m in enumerate(masks)}
    return fold([same, came], [terms] * 2, [masks] * 2, [0, half], half, bits, follow)[0]


def finish(state, stages, follow, passed=()):
    for bits in stages[1:]:
        args = [x for keep, recv, _ in state for x in (keep, recv)]
        masks = [left for _, _, left in state]
        terms = [
            {m: ((2 * h, i), (2 * h + 1, i)) for i, m in enumerate(left)}
            for h, left in enumerate(masks)
        ]
        state, passed = fold(
            args, terms, masks, [0, 0], args[0].shape[1], bits, follow, passed
        )
    return state, passed


def solution(mesh):
    in_specs = (
        P("dp", "tensor"),
        P("dp", None),
        P("dp", None),
        P(None, "tensor"),
        P(None, "tensor"),
        P("tensor", None),
    )
    out_specs = (P("dp", "tensor"), P())
    return jax.shard_map(
        on_device, mesh=mesh, in_specs=in_specs, out_specs=out_specs, check_vma=False
    )
```

```python
import math

import jax
import jax.numpy as jnp
from jax import lax
from jax.experimental import pallas as pl
from jax.experimental.pallas import tpu as pltpu
from jax.sharding import PartitionSpec as P

CAP = 768
CLIP_SHARE = 0.25
LANES = 128
ROW_CHUNKS = 2
BF16 = jnp.bfloat16
F32 = jnp.float32
MIB = 1 << 20
EXPAND_MIB = 24
AHEAD = 3
JOINED = 3


def params(mib):
    return pltpu.CompilerParams(vmem_limit_bytes=mib * MIB)


TINY = pl.CostEstimate(flops=1, bytes_accessed=1, transcendentals=0)


def across(block, bit):
    count = lax.axis_size("tensor")
    return lax.ppermute(block, "tensor", [(r, r ^ 1 << bit) for r in range(count)])


def iota(shape, dim):
    return lax.broadcasted_iota(jnp.int32, shape, dim)


def slots_of(ids_ref):
    tokens = ids_ref.shape[1]
    rows = tokens // LANES
    padded = (rows + 15) // 16 * 16
    hit = jnp.where((ids_ref[0:1, :] == 0) | (ids_ref[1:2, :] == 0), 1.0, 0.0)
    grid = jnp.concatenate(
        [hit[:, LANES * k : LANES * (k + 1)] for k in range(rows)]
        + [jnp.zeros((padded - rows, LANES), F32)],
        axis=0,
    )
    flat = grid.astype(BF16)
    upto = (iota((LANES, LANES), 0) <= iota((LANES, LANES), 1)).astype(F32).astype(BF16)
    before = (iota((padded, padded), 1) < iota((padded, padded), 0)).astype(F32).astype(BF16)
    within = jnp.dot(flat, upto, preferred_element_type=F32)
    offset = jnp.sum(jnp.dot(before, flat, preferred_element_type=F32), axis=1, keepdims=True)
    return jnp.where(grid > 0.0, within + offset - 1.0, -1.0)


def pick_body(first, ids_hbm, tokens_hbm, *refs):
    picked_ref, peak_ref, ids_ref, tokens_ref, loaded = refs[-5:]
    rows = picked_ref.shape[0]
    count = tokens_ref.shape[0]
    pieces = loaded.shape[0] - 1
    step = count // pieces
    ids_copy = pltpu.make_async_copy(ids_hbm, ids_ref, loaded.at[pieces])
    ids_copy.start()
    copies = [
        pltpu.make_async_copy(
            tokens_hbm.at[pl.ds(i * step, step), :],
            tokens_ref.at[pl.ds(i * step, step), :],
            loaded.at[i],
        )
        for i in range(pieces)
    ]
    for copy in copies:
        copy.start()
    ids_copy.wait()
    slots = slots_of(ids_ref).astype(jnp.int32)
    wanted = iota((rows, LANES), 0) + first
    picked = jnp.zeros(picked_ref.shape, F32)
    for i, copy in enumerate(copies):
        hot = jnp.concatenate(
            [
                jnp.where(wanted == slots[k : k + 1, :], 1.0, 0.0).astype(BF16)
                for k in range(i * step // LANES, (i + 1) * step // LANES)
            ],
            axis=1,
        )
        copy.wait()
        picked += jnp.dot(
            hot, tokens_ref[i * step : (i + 1) * step, :], preferred_element_type=F32
        )
    picked_ref[...] = picked.astype(BF16)
    peak_ref[...] = jnp.broadcast_to(jnp.max(jnp.abs(picked)), peak_ref.shape)


def pick_rows(ids, tokens, first, rows, follow=()):
    count, width = tokens.shape
    blocks = count // LANES
    pieces = math.gcd(blocks, 4)
    in_hbm = [pltpu.with_memory_space_constraint(x, pltpu.HBM) for x in (ids, tokens)]
    return pl.pallas_call(
        lambda *refs: pick_body(first, *refs),
        out_shape=(
            jax.ShapeDtypeStruct((rows, width), BF16),
            jax.ShapeDtypeStruct((8, LANES), F32),
        ),
        in_specs=[pl.BlockSpec(memory_space=pltpu.HBM)] * 2 + follows(follow),
        out_specs=[pl.BlockSpec(memory_space=pltpu.VMEM)] * 2,
        scratch_shapes=[
            pltpu.VMEM(ids.shape, ids.dtype),
            pltpu.VMEM(tokens.shape, tokens.dtype),
            pltpu.SemaphoreType.DMA((pieces + 1,)),
        ],
        compiler_params=params(16),
        cost_estimate=TINY,
        name="pick_rows",
    )(*in_hbm, *follow)


def signs(size):
    common = iota((size, size), 0) & iota((size, size), 1)
    shift = 1
    while shift < size.bit_length():
        shift *= 2
    while shift > 1:
        shift //= 2
        common = common ^ (common >> shift)
    return (1 - 2 * (common & 1)).astype(F32).astype(BF16)


def multiply_body(masks, cuts, resumed, last, me_ref, *refs):
    count = len(masks)
    parts = []
    for pieces in cuts:
        parts.append(refs[:pieces])
        refs = refs[pieces:]
    before_ref = None
    if resumed:
        before_ref, refs = refs[0], refs[1:]
    gate_hbm, up_hbm, *outs, held, loaded = refs
    if last:
        *outs, total = outs
    else:
        total = outs[0]
    features = parts[0][0].shape[1]
    width = total.shape[2]

    def load(i):
        rows = pl.ds(pl.multiple_of((me_ref[0] ^ masks[i]) * features, LANES), features)
        return [
            pltpu.make_async_copy(weight.at[rows, :], held.at[i, at], loaded.at[i, at])
            for at, weight in enumerate((gate_hbm, up_hbm))
        ]

    loads = [load(i) for i in range(count)]
    for copies in loads[:AHEAD]:
        for copy in copies:
            copy.start()
    columns = min(512, width)
    for i, pieces in enumerate(parts):
        part = jnp.concatenate([piece[...] for piece in pieces], axis=0)
        for copies in loads[i + AHEAD : i + AHEAD + 1]:
            for copy in copies:
                copy.start()
        for at in range(2):
            loads[i][at].wait()
            for low in range(0, width, columns):
                span = slice(low, low + columns)
                term = jnp.dot(part, held[i, at, :, span], preferred_element_type=F32)
                if i > 0:
                    term += total[at, :, span]
                elif resumed:
                    term += before_ref[at, :, span]
                total[at, :, span] = term
    if not last:
        return
    tile = min(256, width)
    steps = width // tile
    table = signs(tile)
    values = []
    for i in range(steps):
        gate = total[0, :, i * tile : (i + 1) * tile]
        up = total[1, :, i * tile : (i + 1) * tile]
        hidden = (gate * (1.0 / (1.0 + jnp.exp(-gate))) * up).astype(BF16)
        values.append(jnp.dot(hidden, table, preferred_element_type=F32))
    gap = 1
    while gap < steps:
        values = [
            values[i] + values[i ^ gap] if not i & gap else values[i ^ gap] - values[i]
            for i in range(steps)
        ]
        gap *= 2
    for i in range(steps):
        low = 0
        for out in outs:
            rows = out.shape[0]
            out[:, i * tile : (i + 1) * tile] = values[i][low : low + rows].astype(BF16)
            low += rows


def multiply(parts, me, gate_weight, up_weight, before=None, last=False, follow=()):
    masks = sorted(parts)
    depth, width = gate_weight.shape
    count = len(masks)
    pieces = [x if isinstance(x, (list, tuple)) else [x] for x in (parts[m] for m in masks)]
    cuts = [len(x) for x in pieces]
    rows, features = sum(x.shape[0] for x in pieces[0]), pieces[0][0].shape[1]
    vmem = pl.BlockSpec(memory_space=pltpu.VMEM)
    resumed = before is not None
    in_hbm = [pltpu.with_memory_space_constraint(x, pltpu.HBM) for x in (gate_weight, up_weight)]
    args = [me, *[x for group in pieces for x in group]] + ([before] if resumed else [])
    used = len(args) + 2
    scratch = [
        pltpu.VMEM((count, 2, features, width), BF16),
        pltpu.SemaphoreType.DMA((count, 2)),
    ]
    if last:
        out_shape = [jax.ShapeDtypeStruct((rows // JOINED, width), BF16)] * JOINED
        scratch.insert(0, pltpu.VMEM((2, rows, width), F32))
    else:
        out_shape = [jax.ShapeDtypeStruct((2, rows, width), F32)]
    made = pl.pallas_call(
        lambda *refs: multiply_body(
            masks, cuts, resumed, last, *refs[:used], *refs[used + len(follow) :]
        ),
        in_specs=[pl.BlockSpec(memory_space=pltpu.SMEM)]
        + [vmem] * (used - 3)
        + [pl.BlockSpec(memory_space=pltpu.HBM)] * 2
        + follows(follow),
        out_specs=[vmem] * len(out_shape),
        out_shape=out_shape,
        scratch_shapes=scratch,
        compiler_params=params(EXPAND_MIB),
        cost_estimate=TINY,
        name="multiply_last" if last else "multiply",
    )(*args, *in_hbm, *follow)
    return made if last else made[0]


def clip_body(ins, outs):
    level = CLIP_SHARE * jnp.max(ins[0][8:, :])
    low = 0
    for part in ins[1:]:
        rows = part.shape[0]
        outs[0][low : low + rows, :] = jnp.clip(part[...].astype(F32), -level, level).astype(BF16)
        low += rows


def down_body(first, me_ref, clipped_ref, weight_hbm, *refs):
    owners = lax.axis_size("tensor")
    half = owners // 2
    other_ref, same_ref, held, loaded = refs[-4:]
    fc = same_ref.shape[2]
    stride = weight_hbm.shape[1] // owners
    masks = [2 * i + 1 for i in range(half)] + [2 * i for i in range(half)]

    def load(i):
        column = pl.multiple_of((me_ref[0] ^ masks[i]) * stride + first, LANES)
        return pltpu.make_async_copy(
            weight_hbm.at[:, pl.ds(column, fc)],
            held.at[i // 2, :, pl.ds(i % 2 * fc, fc)],
            loaded.at[i],
        )

    loads = [load(i) for i in range(owners)]
    for copy in loads[: 2 * AHEAD]:
        copy.start()
    for pair in range(half):
        for copy in loads[2 * (pair + AHEAD) : 2 * (pair + AHEAD + 1)]:
            copy.start()
        for copy in loads[2 * pair : 2 * pair + 2]:
            copy.wait()
        terms = jnp.dot(clipped_ref[...], held[pair], preferred_element_type=F32).astype(BF16)
        for side in range(2):
            i = 2 * pair + side
            term = terms[:, side * fc : (side + 1) * fc]
            if i < half:
                other_ref[i] = term
            else:
                same_ref[i - half] = term


def down(clipped, weight, me, units, first, follow=()):
    depth = weight.shape[0]
    owners = lax.axis_size("tensor")
    half = owners // 2
    rows = clipped.shape[0]
    fc = units * LANES
    vmem = pl.BlockSpec(memory_space=pltpu.VMEM)
    shape = jax.ShapeDtypeStruct((half, rows, fc), BF16)
    return pl.pallas_call(
        lambda *refs: down_body(first * LANES, *refs),
        in_specs=[
            pl.BlockSpec(memory_space=pltpu.SMEM),
            vmem,
            pl.BlockSpec(memory_space=pltpu.HBM),
        ]
        + follows(follow),
        out_specs=[vmem] * 2,
        out_shape=[shape] * 2,
        scratch_shapes=[
            pltpu.VMEM((half, depth, 2 * fc), BF16),
            pltpu.SemaphoreType.DMA((owners,)),
        ],
        compiler_params=params(16),
        cost_estimate=TINY,
        name="down",
    )(me, clipped, pltpu.with_memory_space_constraint(weight, pltpu.HBM), *follow)


def spread_body(count, ids_ref, probs_ref, *refs):
    mine, theirs = refs[:count], refs[count : 2 * count]
    out_ref, mark_ref = refs[-2:]
    mark_ref[...] = jnp.zeros_like(mark_ref)
    tokens = ids_ref.shape[1]
    summed = jnp.concatenate(
        [(a[0].astype(F32) + b[0].astype(F32)).astype(BF16) for a, b in zip(mine, theirs)], axis=0
    )
    slots = slots_of(ids_ref)
    share = jnp.where(ids_ref[0:1, :] == 0, probs_ref[0:1, :], 0.0) + jnp.where(
        ids_ref[1:2, :] == 0, probs_ref[1:2, :], 0.0
    )
    blocks = tokens // LANES
    share = jnp.concatenate(
        [share[:, LANES * k : LANES * (k + 1)] for k in range(blocks)]
        + [jnp.zeros((LANES - blocks, LANES), F32)],
        axis=0,
    ).T
    slots = jnp.concatenate(
        [slots, jnp.zeros((LANES - slots.shape[0], LANES), F32)], axis=0
    ).T.astype(jnp.int32)
    at = iota((LANES, summed.shape[0]), 1)
    for k in range(blocks):
        hot = jnp.where(at == slots[:, k : k + 1], 1.0, 0.0).astype(BF16)
        rows = jnp.dot(hot, summed, preferred_element_type=F32)
        out_ref[LANES * k : LANES * (k + 1), :] = (rows * share[:, k : k + 1]).astype(BF16)


def spread(ids, probs, state, first, features, out, follow=()):
    mine, theirs = [x[0] for x in state], [x[1] for x in state]
    tokens = ids.shape[1]
    count = len(mine)
    _, rows, fc = mine[0].shape
    args = [ids, probs, *mine, *theirs]
    in_specs = [pl.BlockSpec(x.shape, lambda i, d=x.ndim: (0,) * d) for x in args]
    aliases = {}
    if out is not None:
        aliases = {len(args): 0}
        follow = [out, *follow]
    return pl.pallas_call(
        lambda *refs: spread_body(count, *refs[: 2 + 2 * count], *refs[-2:]),
        grid=(1,),
        in_specs=in_specs + follows(follow),
        out_specs=[
            pl.BlockSpec((pl.Element(tokens), pl.Element(fc)), lambda i: (0, first * LANES)),
            pl.BlockSpec((8, LANES), lambda i: (0, 0)),
        ],
        out_shape=[
            jax.ShapeDtypeStruct((tokens, features), BF16),
            jax.ShapeDtypeStruct((8, LANES), F32),
        ],
        input_output_aliases=aliases,
        compiler_params=params(16),
        cost_estimate=TINY,
        name="spread",
    )(*args, *follow)


def follows(arrays):
    return [pl.BlockSpec(memory_space=pl.ANY)] * len(arrays)


def small(body, args, shapes, name, follow=()):
    vmem = pl.BlockSpec(memory_space=pltpu.VMEM)
    count = len(args)
    specs = [pl.BlockSpec(memory_space=pltpu.SMEM) if x.ndim == 1 else vmem for x in args]
    return pl.pallas_call(
        lambda *refs: body(refs[:count], refs[count + len(follow) :]),
        in_specs=specs + follows(follow),
        out_specs=[vmem] * len(shapes),
        out_shape=[jax.ShapeDtypeStruct(*x) for x in shapes],
        compiler_params=params(16),
        cost_estimate=TINY,
        name=name,
    )(*args, *follow)


def gather_near(own, orders):
    return {0: own} | {1 << bit: across(own, bit) for bit in orders[0]}


def cut_body(firsts, ins, outs):
    for h, at in enumerate(firsts):
        rows = outs[h].shape[0]
        outs[h][...] = ins[at][h * rows : (h + 1) * rows, :]
    for block, out in zip(ins, outs[2:]):
        out[...] = block[...]


def join_body(ins, outs):
    pieces = 2 * len(outs) // len(ins)
    for i in range(len(ins) // 2):
        whole = jnp.concatenate([ins[2 * i][...], ins[2 * i + 1][...]], axis=0)
        for k in range(pieces):
            out = outs[pieces * i + k]
            rows = out.shape[0]
            out[...] = whole[k * rows : (k + 1) * rows, :]


def cut(full, orders, follow, passed=False):
    rows, width = full[0].shape
    masks = [mask for mask in full if mask]
    firsts = [masks.index(1 << order[0]) for order in orders]
    shapes = [((rows // 2, width), BF16)] * 2 + [((rows, width), BF16)] * len(masks) * passed
    outs = small(
        lambda ins, outs: cut_body(firsts, ins, outs),
        [full[mask] for mask in masks],
        shapes,
        "cut",
        follow,
    )
    return outs[:2], full | dict(zip(masks, outs[2:]))


def gather_far(full, cuts, orders):
    half = full[0].shape[0] // len(orders)
    firsts = [1 << order[0] for order in orders]
    part = {}

    def get(mask, h):
        if (mask, h) in part:
            return part[mask, h]
        return cuts[h] if mask == firsts[h] else full[mask][h * half : (h + 1) * half]

    have = [[0, first] for first in firsts]
    for at in range(1, len(orders[0])):
        for h, order in enumerate(orders):
            bit = order[at]
            for mask in list(have[h]):
                there = mask | 1 << bit
                if there not in full:
                    part[there, h] = across(get(mask, h), bit)
                have[h].append(there)
    return part


def join(part, follow):
    masks = sorted({mask for mask, _ in part})
    halves = [part[mask, h] for mask in masks for h in range(2)]
    half, width = halves[0].shape
    shapes = [((2 * half // JOINED, width), BF16)] * (JOINED * len(masks))
    joined = small(join_body, halves, shapes, "join", follow)
    return {mask: joined[JOINED * i : JOINED * (i + 1)] for i, mask in enumerate(masks)}


def paired(pieces):
    return pieces | {
        mask | 1: [across(x, 0) for x in block] if isinstance(block, list) else across(block, 0)
        for mask, block in pieces.items()
    }


def beyond_own(pieces):
    return {mask: block for mask, block in pieces.items() if mask}


def turn_body(bits, scale, ins, outs):
    me_ref, ins = ins[0], ins[1:]
    count = len(bits)
    for h, bit in enumerate(bits):
        flip = (1 - 2 * ((me_ref[0] >> bit) & 1)).astype(F32)
        own = ins[2 * h][...].astype(F32)
        came = ins[2 * h + 1][...].astype(F32)
        value = came + own * flip
        if scale is not None:
            value = value * scale
            top = jnp.max(jnp.abs(own) + jnp.abs(came), axis=0, keepdims=True) * scale
            wide = top[:, :LANES]
            for k in range(1, top.shape[1] // LANES):
                wide = jnp.maximum(wide, top[:, k * LANES : (k + 1) * LANES])
            outs[count + h][...] = jnp.broadcast_to(wide, outs[count + h].shape)
        outs[h][...] = value.astype(BF16)


def turn_cores_body(ins, outs):
    me_ref, ins = ins[0], ins[1:]
    flip = (1 - 2 * (me_ref[0] & 1)).astype(F32)
    own = jnp.concatenate([x[...] for x in ins[: len(ins) // 2]], axis=0).astype(F32)
    came = jnp.concatenate([x[...] for x in ins[len(ins) // 2 :]], axis=0).astype(F32)
    value = (came + own * flip).astype(BF16)
    rows = outs[0].shape[0]
    for h, out in enumerate(outs):
        out[...] = value[h * rows : (h + 1) * rows, :]


def turn(me, blocks, came, bits, follow=(), scale=None):
    args = [me] + [x for pair in zip(blocks, came) for x in pair]
    shapes = [(x.shape, BF16) for x in blocks]
    if scale is not None:
        shapes += [((8, LANES), F32)] * len(blocks)
    return small(
        lambda ins, outs: turn_body(bits, scale, ins, outs), args, shapes, "turn", follow
    )


def largest(top_in, tops, lasts):
    bits = range(lax.axis_size("tensor").bit_length() - 1)
    values = jnp.concatenate([top_in, *tops], axis=0)
    for bit in bits:
        if bit not in lasts:
            values = jnp.maximum(values, across(values, bit))
    n = top_in.shape[0]
    top_in, first, second = values[:n], values[n : 2 * n], values[2 * n :]
    if lasts[0] != lasts[1]:
        pair = jnp.concatenate([top_in, second], axis=0)
        came_first, came_pair = across(first, lasts[1]), across(pair, lasts[0])
        first = jnp.maximum(first, came_first)
        pair = jnp.maximum(pair, came_pair)
        top_in, second = pair[:n], pair[n:]
    values = jnp.concatenate([top_in, jnp.maximum(first, second)], axis=0)
    blocks = lax.axis_size("dp")
    far = 1
    while far < blocks:
        pairs = [(r, r ^ far) for r in range(blocks)]
        values = jnp.maximum(values, lax.ppermute(values, "dp", pairs))
        far *= 2
    return values


def on_device(tokens, expert_ids, gate_probs, gate_weight, up_weight, down_weight):
    count = lax.axis_size("tensor")
    bits = count.bit_length() - 1
    outer = list(range(1, bits))
    orders = [outer, outer[::-1]]
    me = lax.axis_index("tensor")
    me_arr = me.astype(jnp.int32).reshape(1)
    ids, probs = expert_ids.T, gate_probs.T
    rows = CAP // ROW_CHUNKS
    weights = (me_arr, gate_weight, up_weight)
    half = rows // 2
    scale = 1.0 / math.sqrt(gate_weight.shape[1] * count)
    stages = [[order[at] for order in orders] for at in range(len(outer))]
    early_bit = stages[-1][1]

    def send(blocks, bits):
        return [across(x, bit) for x, bit in zip(blocks, bits)]

    def start_turn(pieces, follow=()):
        shape = ((half, pieces[0].shape[1]), BF16)
        args = [me_arr, *pieces, *[across(x, 0) for x in pieces]]
        blocks = small(turn_cores_body, args, [shape] * 2, "turn", follow)
        return blocks, send(blocks, stages[0])

    def go_on(blocks, came, at, follow=()):
        blocks = turn(me_arr, blocks, came, stages[at], follow)
        return blocks, send(blocks, stages[at + 1])

    def end_turn(blocks, came, follow=()):
        made = turn(me_arr, blocks, came, stages[-1], follow, scale)
        return made[: len(blocks)], made[len(blocks) :]

    own_a, top_a = pick_rows(ids, tokens, 0, rows, [me_arr])
    near_a = gather_near(own_a, orders)
    total_a = multiply({0: own_a}, *weights)
    own_b, top_b = pick_rows(ids, tokens, rows, rows, [total_a])
    near_b = gather_near(own_b, orders)
    total_b = multiply({0: own_b}, *weights)
    cuts_a, near_a = cut(near_a, orders, [total_b], True)
    total_a = multiply(beyond_own(paired(near_a)), *weights, total_a)
    cuts_b, near_b = cut(near_b, orders, [total_a], True)
    total_b = multiply(beyond_own(near_b), *weights, total_b)
    top_in = jnp.maximum(top_a, top_b)
    top_in = jnp.maximum(top_in, across(top_in, early_bit))
    far_a = join(gather_far(near_a, cuts_a, orders), [total_b])
    far_b = join(gather_far(near_b, cuts_b, orders), far_a[max(far_a)])
    local_a = multiply(paired(far_a), *weights, total_a, True, far_b[max(far_b)])
    blocks_a, came_a = start_turn(local_a)
    theirs = paired({0: own_b} | beyond_own(near_b))
    theirs = {mask: block for mask, block in theirs.items() if mask & 1}
    total_b = multiply(theirs, *weights, total_b, follow=blocks_a)
    for at in range(len(outer) - 1):
        blocks_a, came_a = go_on(blocks_a, came_a, at, [total_b])
    local_b = multiply(paired(far_b), *weights, total_b, True, blocks_a)
    turned_a, rot_a = end_turn(blocks_a, came_a, [*local_b, top_in])
    blocks_b, came_b = start_turn(local_b, rot_a)
    for at in range(len(outer) - 1):
        blocks_b, came_b = go_on(blocks_b, came_b, at)
    turned_b, rot_b = end_turn(blocks_b, came_b)
    rotated = turned_a + turned_b

    peaks = largest(top_in, [jnp.maximum(x, y) for x, y in zip(rot_a, rot_b)], stages[-1])
    clipped = small(
        clip_body, [peaks, *rotated], [((CAP, gate_weight.shape[1]), BF16)], "clip"
    )[0]

    tops = pl.pallas_call(
        peaks_body,
        out_specs=pl.BlockSpec(memory_space=pltpu.SMEM),
        out_shape=jax.ShapeDtypeStruct((2,), F32),
        name="peaks",
    )(peaks)
    units = tokens.shape[1] // LANES
    sizes = chunks_of(units)
    firsts = [sum(sizes[:i]) for i in range(len(sizes))]
    total = len(sizes)
    products, begun, ended, out, last = {}, {}, {}, None, []
    for step, chunk in sums_order(total):
        if step == "product":
            products[chunk] = down(
                clipped, down_weight, me_arr, sizes[chunk], firsts[chunk], last
            )
            last = [products[chunk][1]]
        elif step == "begin":
            other, same = products[chunk]
            begun[chunk] = fold_cores(same, across(other, 0), stages[0], last)
            last = [keep for keep, _, _ in begun[chunk]]
        elif step == "finish":
            ahead = [c for c in products if c not in begun]
            passed = [products[c][0] for c in ahead]
            ended[chunk], passed = finish(begun[chunk], stages, last, passed)
            for c, other in zip(ahead, passed):
                products[c] = (other, products[c][1])
            last = [keep for keep, _, _ in ended[chunk]]
        else:
            out, mark = spread(
                ids, probs, ended[chunk], firsts[chunk], tokens.shape[1], out, last
            )
            last = [mark]
    return out, tops


def chunks_of(units):
    return [2] * (units // 2) + [1] * (units % 2)


def sums_order(total):
    order = [("product", 0)]
    for chunk in range(total):
        if chunk + 1 < total:
            order.append(("product", chunk + 1))
        order.append(("begin", chunk))
        if chunk > 0:
            order.append(("finish", chunk - 1))
        if chunk > 1 and chunk + 1 < total:
            order.append(("spread", chunk - 2))
    order.append(("finish", total - 1))
    return order + [("spread", c) for c in range(total) if ("spread", c) not in order]


def peaks_body(values_ref, out_ref):
    out_ref[0] = jnp.max(values_ref[:8, :])
    out_ref[1] = jnp.max(values_ref[8:, :])


def fold_body(plan, passed, ins, outs):
    for i in range(passed):
        outs[len(plan) + i][...] = ins[len(ins) - passed + i][...]
    for out, (slots, low) in zip(outs, plan):
        rows = out.shape[1]
        for slot, terms in enumerate(slots):
            total = 0.0
            for at, i in terms:
                total = total + ins[at][i, low : low + rows, :].astype(F32)
            out[slot] = total.astype(BF16)


def fold(args, terms, masks, lows, rows, bits, follow, passed=()):
    plan, shapes, lefts = [], [], []
    width = args[0].shape[2]
    for h, bit in enumerate(bits):
        for side in (0, 1):
            chosen = [m for m in masks[h] if m >> bit & 1 == side]
            plan.append(([terms[h][m] for m in chosen], lows[h]))
            shapes.append(((len(chosen), rows, width), BF16))
        lefts.append([m for m in masks[h] if not m >> bit & 1])
    shapes += [(x.shape, x.dtype) for x in passed]
    made = small(
        lambda ins, outs: fold_body(plan, len(passed), ins, outs),
        [*args, *passed],
        shapes,
        "fold",
        follow,
    )
    state = [
        (made[2 * h], across(made[2 * h + 1], bit), lefts[h]) for h, bit in enumerate(bits)
    ]
    return state, made[len(plan) :]


def fold_cores(same, came, bits, follow):
    half = same.shape[1] // 2
    masks = [2 * i for i in range(same.shape[0])]
    terms = {m: ((0, i), (1, i)) for i, m in enumerate(masks)}
    return fold([same, came], [terms] * 2, [masks] * 2, [0, half], half, bits, follow)[0]


def finish(state, stages, follow, passed=()):
    for bits in stages[1:]:
        args = [x for keep, recv, _ in state for x in (keep, recv)]
        masks = [left for _, _, left in state]
        terms = [
            {m: ((2 * h, i), (2 * h + 1, i)) for i, m in enumerate(left)}
            for h, left in enumerate(masks)
        ]
        state, passed = fold(
            args, terms, masks, [0, 0], args[0].shape[1], bits, follow, passed
        )
    return state, passed


def solution(mesh):
    in_specs = (
        P("dp", "tensor"),
        P("dp", None),
        P("dp", None),
        P(None, "tensor"),
        P(None, "tensor"),
        P("tensor", None),
    )
    out_specs = (P("dp", "tensor"), P())
    return jax.shard_map(
        on_device, mesh=mesh, in_specs=in_specs, out_specs=out_specs, check_vma=False
    )
```

```python
import math

import jax
import jax.numpy as jnp
from jax import lax
from jax.experimental import pallas as pl
from jax.experimental.pallas import tpu as pltpu
from jax.sharding import PartitionSpec as P

CAP = 768
CLIP_SHARE = 0.25
LANES = 128
ROW_CHUNKS = 2
BF16 = jnp.bfloat16
F32 = jnp.float32
MIB = 1 << 20
EXPAND_MIB = 24
AHEAD = 3


def params(mib):
    return pltpu.CompilerParams(vmem_limit_bytes=mib * MIB)


TINY = pl.CostEstimate(flops=1, bytes_accessed=1, transcendentals=0)


def across(block, bit):
    count = lax.axis_size("tensor")
    return lax.ppermute(block, "tensor", [(r, r ^ 1 << bit) for r in range(count)])


def iota(shape, dim):
    return lax.broadcasted_iota(jnp.int32, shape, dim)


def slots_of(ids_ref):
    tokens = ids_ref.shape[1]
    rows = tokens // LANES
    padded = (rows + 15) // 16 * 16
    hit = jnp.where((ids_ref[0:1, :] == 0) | (ids_ref[1:2, :] == 0), 1.0, 0.0)
    grid = jnp.concatenate(
        [hit[:, LANES * k : LANES * (k + 1)] for k in range(rows)]
        + [jnp.zeros((padded - rows, LANES), F32)],
        axis=0,
    )
    flat = grid.astype(BF16)
    upto = (iota((LANES, LANES), 0) <= iota((LANES, LANES), 1)).astype(F32).astype(BF16)
    before = (iota((padded, padded), 1) < iota((padded, padded), 0)).astype(F32).astype(BF16)
    within = jnp.dot(flat, upto, preferred_element_type=F32)
    offset = jnp.sum(jnp.dot(before, flat, preferred_element_type=F32), axis=1, keepdims=True)
    return jnp.where(grid > 0.0, within + offset - 1.0, -1.0)


def pick_body(first, ids_hbm, tokens_hbm, *refs):
    picked_ref, peak_ref, ids_ref, tokens_ref, loaded = refs[-5:]
    rows = picked_ref.shape[0]
    count = tokens_ref.shape[0]
    pieces = loaded.shape[0] - 1
    step = count // pieces
    ids_copy = pltpu.make_async_copy(ids_hbm, ids_ref, loaded.at[pieces])
    ids_copy.start()
    copies = [
        pltpu.make_async_copy(
            tokens_hbm.at[pl.ds(i * step, step), :],
            tokens_ref.at[pl.ds(i * step, step), :],
            loaded.at[i],
        )
        for i in range(pieces)
    ]
    for copy in copies:
        copy.start()
    ids_copy.wait()
    slots = slots_of(ids_ref).astype(jnp.int32)
    wanted = iota((rows, LANES), 0) + first
    picked = jnp.zeros(picked_ref.shape, F32)
    for i, copy in enumerate(copies):
        hot = jnp.concatenate(
            [
                jnp.where(wanted == slots[k : k + 1, :], 1.0, 0.0).astype(BF16)
                for k in range(i * step // LANES, (i + 1) * step // LANES)
            ],
            axis=1,
        )
        copy.wait()
        picked += jnp.dot(
            hot, tokens_ref[i * step : (i + 1) * step, :], preferred_element_type=F32
        )
    picked_ref[...] = picked.astype(BF16)
    peak_ref[...] = jnp.broadcast_to(jnp.max(jnp.abs(picked)), peak_ref.shape)


def pick_rows(ids, tokens, first, rows, follow=()):
    count, width = tokens.shape
    blocks = count // LANES
    pieces = math.gcd(blocks, 4)
    in_hbm = [pltpu.with_memory_space_constraint(x, pltpu.HBM) for x in (ids, tokens)]
    return pl.pallas_call(
        lambda *refs: pick_body(first, *refs),
        out_shape=(
            jax.ShapeDtypeStruct((rows, width), BF16),
            jax.ShapeDtypeStruct((8, LANES), F32),
        ),
        in_specs=[pl.BlockSpec(memory_space=pltpu.HBM)] * 2 + follows(follow),
        out_specs=[pl.BlockSpec(memory_space=pltpu.VMEM)] * 2,
        scratch_shapes=[
            pltpu.VMEM(ids.shape, ids.dtype),
            pltpu.VMEM(tokens.shape, tokens.dtype),
            pltpu.SemaphoreType.DMA((pieces + 1,)),
        ],
        compiler_params=params(16),
        cost_estimate=TINY,
        name="pick_rows",
    )(*in_hbm, *follow)


def signs(size):
    common = iota((size, size), 0) & iota((size, size), 1)
    shift = 1
    while shift < size.bit_length():
        shift *= 2
    while shift > 1:
        shift //= 2
        common = common ^ (common >> shift)
    return (1 - 2 * (common & 1)).astype(F32).astype(BF16)


def expand_body(first, cuts, last, me_ref, *refs):
    count = len(cuts)
    parts = []
    for pieces in cuts:
        parts.append(refs[:pieces])
        refs = refs[pieces:]
    before_ref = None
    if last:
        before_ref, refs = refs[0], refs[1:]
    gate_hbm, up_hbm, *outs, total, held, loaded = refs
    width = parts[0][0].shape[1]
    columns = total.shape[2]
    tile = min(256, columns)

    def load(mask):
        rows = pl.ds(pl.multiple_of((me_ref[0] ^ mask) * width, LANES), width)
        return [
            pltpu.make_async_copy(
                weight.at[rows, pl.ds(first, columns)], held.at[mask, at], loaded.at[mask, at]
            )
            for at, weight in enumerate((gate_hbm, up_hbm))
        ]

    loads = [load(mask) for mask in range(count)]
    for copies in loads[:AHEAD]:
        for copy in copies:
            copy.start()
    table = signs(tile)
    for mask, pieces in enumerate(parts):
        part = jnp.concatenate([piece[...] for piece in pieces], axis=0)
        for copies in loads[mask + AHEAD : mask + AHEAD + 1]:
            for copy in copies:
                copy.start()
        for at in range(2):
            loads[mask][at].wait()
            term = jnp.dot(part, held[mask, at], preferred_element_type=F32)
            if mask == 0:
                total[at] = term
            else:
                total[at] += term
    values = []
    for i in range(columns // tile):
        gate = total[0, :, i * tile : (i + 1) * tile]
        up = total[1, :, i * tile : (i + 1) * tile]
        hidden = (gate * (1.0 / (1.0 + jnp.exp(-gate))) * up).astype(BF16)
        values.append(jnp.dot(hidden, table, preferred_element_type=F32))
        if not last:
            outs[0][i] = values[i]
    if not last:
        return
    values = [before_ref[i] for i in range(before_ref.shape[0])] + values
    steps = len(values)
    gap = 1
    while gap < steps:
        values = [
            values[i] + values[i ^ gap] if not i & gap else values[i ^ gap] - values[i]
            for i in range(steps)
        ]
        gap *= 2
    for i in range(steps):
        low = 0
        for out in outs:
            rows = out.shape[0]
            out[:, i * tile : (i + 1) * tile] = values[i][low : low + rows].astype(BF16)
            low += rows


def expand(parts, rows, me, gate_weight, up_weight, before=None, follow=()):
    depth, width = gate_weight.shape
    last = before is not None
    columns = width // 2
    first = columns if last else 0
    tile = min(256, columns)
    parts = [x if isinstance(x, (list, tuple)) else [x] for x in parts]
    cuts = [len(x) for x in parts]
    parts = [x for pieces in parts for x in pieces]
    count = len(cuts)
    vmem = pl.BlockSpec(memory_space=pltpu.VMEM)
    in_hbm = [pltpu.with_memory_space_constraint(x, pltpu.HBM) for x in (gate_weight, up_weight)]
    args = [me, *parts] + ([before] if last else [])
    used = len(args) + 2
    if last:
        out_shape = [jax.ShapeDtypeStruct((rows // 2, width), BF16)] * 2
    else:
        out_shape = [jax.ShapeDtypeStruct((columns // tile, rows, tile), F32)]
    return pl.pallas_call(
        lambda *refs: expand_body(first, cuts, last, *refs[:used], *refs[used + len(follow) :]),
        in_specs=[pl.BlockSpec(memory_space=pltpu.SMEM)]
        + [vmem] * (used - 3)
        + [pl.BlockSpec(memory_space=pltpu.HBM)] * 2
        + follows(follow),
        out_specs=[vmem] * len(out_shape),
        out_shape=out_shape,
        scratch_shapes=[
            pltpu.VMEM((2, rows, columns), F32),
            pltpu.VMEM((count, 2, depth // count, columns), BF16),
            pltpu.SemaphoreType.DMA((count, 2)),
        ],
        compiler_params=params(EXPAND_MIB),
        cost_estimate=TINY,
        name="expand_last" if last else "expand_first",
    )(*args, *in_hbm, *follow)


def clip_body(ins, outs):
    level = CLIP_SHARE * jnp.max(ins[0][8:, :])
    low = 0
    for part in ins[1:]:
        rows = part.shape[0]
        outs[0][low : low + rows, :] = jnp.clip(part[...].astype(F32), -level, level).astype(BF16)
        low += rows


def down_body(first, me_ref, clipped_ref, weight_hbm, *refs):
    owners = lax.axis_size("tensor")
    half = owners // 2
    other_ref, same_ref, held, loaded = refs[-4:]
    fc = same_ref.shape[2]
    stride = weight_hbm.shape[1] // owners
    masks = [2 * i + 1 for i in range(half)] + [2 * i for i in range(half)]

    def load(i):
        column = pl.multiple_of((me_ref[0] ^ masks[i]) * stride + first, LANES)
        return pltpu.make_async_copy(
            weight_hbm.at[:, pl.ds(column, fc)],
            held.at[i // 2, :, pl.ds(i % 2 * fc, fc)],
            loaded.at[i],
        )

    loads = [load(i) for i in range(owners)]
    for copy in loads[: 2 * AHEAD]:
        copy.start()
    for pair in range(half):
        for copy in loads[2 * (pair + AHEAD) : 2 * (pair + AHEAD + 1)]:
            copy.start()
        for copy in loads[2 * pair : 2 * pair + 2]:
            copy.wait()
        terms = jnp.dot(clipped_ref[...], held[pair], preferred_element_type=F32).astype(BF16)
        for side in range(2):
            i = 2 * pair + side
            term = terms[:, side * fc : (side + 1) * fc]
            if i < half:
                other_ref[i] = term
            else:
                same_ref[i - half] = term


def down(clipped, weight, me, units, first, follow=()):
    depth = weight.shape[0]
    owners = lax.axis_size("tensor")
    half = owners // 2
    rows = clipped.shape[0]
    fc = units * LANES
    vmem = pl.BlockSpec(memory_space=pltpu.VMEM)
    shape = jax.ShapeDtypeStruct((half, rows, fc), BF16)
    return pl.pallas_call(
        lambda *refs: down_body(first * LANES, *refs),
        in_specs=[
            pl.BlockSpec(memory_space=pltpu.SMEM),
            vmem,
            pl.BlockSpec(memory_space=pltpu.HBM),
        ]
        + follows(follow),
        out_specs=[vmem] * 2,
        out_shape=[shape] * 2,
        scratch_shapes=[
            pltpu.VMEM((half, depth, 2 * fc), BF16),
            pltpu.SemaphoreType.DMA((owners,)),
        ],
        compiler_params=params(16),
        cost_estimate=TINY,
        name="down",
    )(me, clipped, pltpu.with_memory_space_constraint(weight, pltpu.HBM), *follow)


def spread_body(count, ids_ref, probs_ref, *refs):
    mine, theirs = refs[:count], refs[count : 2 * count]
    out_ref, mark_ref = refs[-2:]
    mark_ref[...] = jnp.zeros_like(mark_ref)
    tokens = ids_ref.shape[1]
    summed = jnp.concatenate(
        [(a[0].astype(F32) + b[0].astype(F32)).astype(BF16) for a, b in zip(mine, theirs)], axis=0
    )
    slots = slots_of(ids_ref)
    share = jnp.where(ids_ref[0:1, :] == 0, probs_ref[0:1, :], 0.0) + jnp.where(
        ids_ref[1:2, :] == 0, probs_ref[1:2, :], 0.0
    )
    blocks = tokens // LANES
    share = jnp.concatenate(
        [share[:, LANES * k : LANES * (k + 1)] for k in range(blocks)]
        + [jnp.zeros((LANES - blocks, LANES), F32)],
        axis=0,
    ).T
    slots = jnp.concatenate(
        [slots, jnp.zeros((LANES - slots.shape[0], LANES), F32)], axis=0
    ).T.astype(jnp.int32)
    at = iota((LANES, summed.shape[0]), 1)
    for k in range(blocks):
        hot = jnp.where(at == slots[:, k : k + 1], 1.0, 0.0).astype(BF16)
        rows = jnp.dot(hot, summed, preferred_element_type=F32)
        out_ref[LANES * k : LANES * (k + 1), :] = (rows * share[:, k : k + 1]).astype(BF16)


def spread(ids, probs, state, first, features, out, follow=()):
    mine, theirs = [x[0] for x in state], [x[1] for x in state]
    tokens = ids.shape[1]
    count = len(mine)
    _, rows, fc = mine[0].shape
    args = [ids, probs, *mine, *theirs]
    in_specs = [pl.BlockSpec(x.shape, lambda i, d=x.ndim: (0,) * d) for x in args]
    aliases = {}
    if out is not None:
        aliases = {len(args): 0}
        follow = [out, *follow]
    return pl.pallas_call(
        lambda *refs: spread_body(count, *refs[: 2 + 2 * count], *refs[-2:]),
        grid=(1,),
        in_specs=in_specs + follows(follow),
        out_specs=[
            pl.BlockSpec((pl.Element(tokens), pl.Element(fc)), lambda i: (0, first * LANES)),
            pl.BlockSpec((8, LANES), lambda i: (0, 0)),
        ],
        out_shape=[
            jax.ShapeDtypeStruct((tokens, features), BF16),
            jax.ShapeDtypeStruct((8, LANES), F32),
        ],
        input_output_aliases=aliases,
        compiler_params=params(16),
        cost_estimate=TINY,
        name="spread",
    )(*args, *follow)


def follows(arrays):
    return [pl.BlockSpec(memory_space=pl.ANY)] * len(arrays)


def small(body, args, shapes, name, follow=()):
    vmem = pl.BlockSpec(memory_space=pltpu.VMEM)
    count = len(args)
    specs = [pl.BlockSpec(memory_space=pltpu.SMEM) if x.ndim == 1 else vmem for x in args]
    return pl.pallas_call(
        lambda *refs: body(refs[:count], refs[count + len(follow) :]),
        in_specs=specs + follows(follow),
        out_specs=[vmem] * len(shapes),
        out_shape=[jax.ShapeDtypeStruct(*x) for x in shapes],
        compiler_params=params(16),
        cost_estimate=TINY,
        name=name,
    )(*args, *follow)


def gather_near(own, orders):
    return {0: own} | {1 << bit: across(own, bit) for bit in orders[0]}


def cut_body(firsts, ins, outs):
    for h, at in enumerate(firsts):
        rows = outs[h].shape[0]
        outs[h][...] = ins[at][h * rows : (h + 1) * rows, :]
    for block, out in zip(ins, outs[2:]):
        out[...] = block[...]


def join_body(ins, outs):
    pieces = 2 * len(outs) // len(ins)
    for i in range(len(ins) // 2):
        whole = jnp.concatenate([ins[2 * i][...], ins[2 * i + 1][...]], axis=0)
        for k in range(pieces):
            out = outs[pieces * i + k]
            rows = out.shape[0]
            out[...] = whole[k * rows : (k + 1) * rows, :]


def cut(full, orders, follow, passed=False):
    rows, width = full[0].shape
    masks = [mask for mask in full if mask]
    firsts = [masks.index(1 << order[0]) for order in orders]
    shapes = [((rows // 2, width), BF16)] * 2 + [((rows, width), BF16)] * len(masks) * passed
    outs = small(
        lambda ins, outs: cut_body(firsts, ins, outs),
        [full[mask] for mask in masks],
        shapes,
        "cut",
        follow,
    )
    return outs[:2], full | dict(zip(masks, outs[2:]))


def gather_far(full, cuts, orders):
    half = full[0].shape[0] // len(orders)
    firsts = [1 << order[0] for order in orders]
    part = {}

    def get(mask, h):
        if (mask, h) in part:
            return part[mask, h]
        return cuts[h] if mask == firsts[h] else full[mask][h * half : (h + 1) * half]

    have = [[0, first] for first in firsts]
    for at in range(1, len(orders[0])):
        for h, order in enumerate(orders):
            bit = order[at]
            for mask in list(have[h]):
                there = mask | 1 << bit
                if there not in full:
                    part[there, h] = across(get(mask, h), bit)
                have[h].append(there)
    return part


def join(part, follow, pieces):
    masks = sorted({mask for mask, _ in part})
    halves = [part[mask, h] for mask in masks for h in range(2)]
    half, width = halves[0].shape
    shapes = [((2 * half // pieces, width), BF16)] * (pieces * len(masks))
    joined = small(join_body, halves, shapes, "join", follow)
    return {mask: joined[pieces * i : pieces * (i + 1)] for i, mask in enumerate(masks)}


def paired(pieces):
    return pieces | {
        mask | 1: [across(x, 0) for x in block] if isinstance(block, list) else across(block, 0)
        for mask, block in pieces.items()
    }


def turn_body(bits, scale, ins, outs):
    me_ref, ins = ins[0], ins[1:]
    count = len(bits)
    for h, bit in enumerate(bits):
        flip = (1 - 2 * ((me_ref[0] >> bit) & 1)).astype(F32)
        own = ins[2 * h][...].astype(F32)
        came = ins[2 * h + 1][...].astype(F32)
        value = came + own * flip
        if scale is not None:
            value = value * scale
            top = jnp.max(jnp.abs(own) + jnp.abs(came), axis=0, keepdims=True) * scale
            wide = top[:, :LANES]
            for k in range(1, top.shape[1] // LANES):
                wide = jnp.maximum(wide, top[:, k * LANES : (k + 1) * LANES])
            outs[count + h][...] = jnp.broadcast_to(wide, outs[count + h].shape)
        outs[h][...] = value.astype(BF16)


def turn(me, blocks, came, bits, follow=(), scale=None):
    args = [me] + [x for pair in zip(blocks, came) for x in pair]
    shapes = [(x.shape, BF16) for x in blocks]
    if scale is not None:
        shapes += [((8, LANES), F32)] * len(blocks)
    return small(
        lambda ins, outs: turn_body(bits, scale, ins, outs), args, shapes, "turn", follow
    )


def largest(top_in, tops, lasts):
    bits = range(lax.axis_size("tensor").bit_length() - 1)
    values = jnp.concatenate([top_in, *tops], axis=0)
    for bit in bits:
        if bit not in lasts:
            values = jnp.maximum(values, across(values, bit))
    n = top_in.shape[0]
    top_in, first, second = values[:n], values[n : 2 * n], values[2 * n :]
    if lasts[0] != lasts[1]:
        pair = jnp.concatenate([top_in, second], axis=0)
        came_first, came_pair = across(first, lasts[1]), across(pair, lasts[0])
        first = jnp.maximum(first, came_first)
        pair = jnp.maximum(pair, came_pair)
        top_in, second = pair[:n], pair[n:]
    values = jnp.concatenate([top_in, jnp.maximum(first, second)], axis=0)
    blocks = lax.axis_size("dp")
    far = 1
    while far < blocks:
        pairs = [(r, r ^ far) for r in range(blocks)]
        values = jnp.maximum(values, lax.ppermute(values, "dp", pairs))
        far *= 2
    return values


def on_device(tokens, expert_ids, gate_probs, gate_weight, up_weight, down_weight):
    count = lax.axis_size("tensor")
    bits = count.bit_length() - 1
    outer = list(range(1, bits))
    orders = [outer, outer[::-1]]
    me = lax.axis_index("tensor")
    me_arr = me.astype(jnp.int32).reshape(1)
    ids, probs = expert_ids.T, gate_probs.T
    rows = CAP // ROW_CHUNKS
    half = rows // 2
    scale = 1.0 / math.sqrt(gate_weight.shape[1] * count)
    stages = [[order[at] for order in orders] for at in range(len(outer))]
    early_bit = stages[-1][1]

    def send(blocks, bits):
        return [across(x, bit) for x, bit in zip(blocks, bits)]

    def start_turn(halves, follow=()):
        blocks = turn(me_arr, halves, send(halves, [0, 0]), [0, 0], follow)
        return blocks, send(blocks, stages[0])

    def go_on(blocks, came, at, follow=()):
        blocks = turn(me_arr, blocks, came, stages[at], follow)
        return blocks, send(blocks, stages[at + 1])

    def end_turn(blocks, came, follow=()):
        made = turn(me_arr, blocks, came, stages[-1], follow, scale)
        return made[: len(blocks)], made[len(blocks) :]

    own_a, top_a = pick_rows(ids, tokens, 0, rows, [me_arr])
    near_a = gather_near(own_a, orders)
    weights = (me_arr, gate_weight, up_weight)
    cuts_a, near_a = cut(near_a, orders, [])
    own_b, top_b = pick_rows(ids, tokens, rows, rows, cuts_a)
    top_in = jnp.maximum(top_a, top_b)
    top_in = jnp.maximum(top_in, across(top_in, early_bit))
    far_a = join(gather_far(near_a, cuts_a, orders), [own_b, top_in], 1)
    near_b = gather_near(own_b, orders)
    parts_a = paired(near_a | far_a)
    parts_a = [parts_a[mask] for mask in range(count)]
    first_a = expand(parts_a, rows, *weights)
    local_a = expand(parts_a, rows, *weights, *first_a)
    cuts_b, near_b = cut(near_b, orders, local_a, True)
    parts_b = paired(near_b)
    theirs_b = [block for mask, block in parts_b.items() if mask & 1]
    blocks_a, came_a = start_turn(local_a)
    far_b = join(gather_far(near_b, cuts_b, orders), list(blocks_a) + theirs_b, 3)
    parts_b |= paired(far_b)
    parts_b = [parts_b[mask] for mask in range(count)]
    first_b = expand(parts_b, rows, *weights, None, blocks_a)
    for at in range(len(outer) - 1):
        blocks_a, came_a = go_on(blocks_a, came_a, at, first_b)
    local_b = expand(parts_b, rows, *weights, *first_b, blocks_a)
    turned_a, rot_a = end_turn(blocks_a, came_a, local_b)
    blocks_b, came_b = start_turn(local_b, rot_a)
    for at in range(len(outer) - 1):
        blocks_b, came_b = go_on(blocks_b, came_b, at)
    turned_b, rot_b = end_turn(blocks_b, came_b)
    rotated = turned_a + turned_b

    peaks = largest(top_in, [jnp.maximum(x, y) for x, y in zip(rot_a, rot_b)], stages[-1])
    clipped = small(
        clip_body, [peaks, *rotated], [((CAP, gate_weight.shape[1]), BF16)], "clip"
    )[0]

    tops = pl.pallas_call(
        peaks_body,
        out_specs=pl.BlockSpec(memory_space=pltpu.SMEM),
        out_shape=jax.ShapeDtypeStruct((2,), F32),
        name="peaks",
    )(peaks)
    units = tokens.shape[1] // LANES
    sizes = chunks_of(units)
    firsts = [sum(sizes[:i]) for i in range(len(sizes))]
    total = len(sizes)
    products, begun, ended, out, last = {}, {}, {}, None, []
    for step, chunk in sums_order(total):
        if step == "product":
            products[chunk] = down(
                clipped, down_weight, me_arr, sizes[chunk], firsts[chunk], last
            )
            last = [products[chunk][1]]
        elif step == "begin":
            other, same = products[chunk]
            begun[chunk] = fold_cores(same, across(other, 0), stages[0], last)
            last = [keep for keep, _, _ in begun[chunk]]
        elif step == "finish":
            ahead = [c for c in products if c not in begun]
            passed = [products[c][0] for c in ahead]
            ended[chunk], passed = finish(begun[chunk], stages, last, passed)
            for c, other in zip(ahead, passed):
                products[c] = (other, products[c][1])
            last = [keep for keep, _, _ in ended[chunk]]
        else:
            out, mark = spread(
                ids, probs, ended[chunk], firsts[chunk], tokens.shape[1], out, last
            )
            last = [mark]
    return out, tops


def chunks_of(units):
    return [2] * (units // 2) + [1] * (units % 2)


def sums_order(total):
    order = [("product", 0)]
    for chunk in range(total):
        if chunk + 1 < total:
            order.append(("product", chunk + 1))
        order.append(("begin", chunk))
        if chunk > 0:
            order.append(("finish", chunk - 1))
        if chunk > 1 and chunk + 1 < total:
            order.append(("spread", chunk - 2))
    order.append(("finish", total - 1))
    return order + [("spread", c) for c in range(total) if ("spread", c) not in order]


def peaks_body(values_ref, out_ref):
    out_ref[0] = jnp.max(values_ref[:8, :])
    out_ref[1] = jnp.max(values_ref[8:, :])


def fold_body(plan, passed, ins, outs):
    for i in range(passed):
        outs[len(plan) + i][...] = ins[len(ins) - passed + i][...]
    for out, (slots, low) in zip(outs, plan):
        rows = out.shape[1]
        for slot, terms in enumerate(slots):
            total = 0.0
            for at, i in terms:
                total = total + ins[at][i, low : low + rows, :].astype(F32)
            out[slot] = total.astype(BF16)


def fold(args, terms, masks, lows, rows, bits, follow, passed=()):
    plan, shapes, lefts = [], [], []
    width = args[0].shape[2]
    for h, bit in enumerate(bits):
        for side in (0, 1):
            chosen = [m for m in masks[h] if m >> bit & 1 == side]
            plan.append(([terms[h][m] for m in chosen], lows[h]))
            shapes.append(((len(chosen), rows, width), BF16))
        lefts.append([m for m in masks[h] if not m >> bit & 1])
    shapes += [(x.shape, x.dtype) for x in passed]
    made = small(
        lambda ins, outs: fold_body(plan, len(passed), ins, outs),
        [*args, *passed],
        shapes,
        "fold",
        follow,
    )
    state = [
        (made[2 * h], across(made[2 * h + 1], bit), lefts[h]) for h, bit in enumerate(bits)
    ]
    return state, made[len(plan) :]


def fold_cores(same, came, bits, follow):
    half = same.shape[1] // 2
    masks = [2 * i for i in range(same.shape[0])]
    terms = {m: ((0, i), (1, i)) for i, m in enumerate(masks)}
    return fold([same, came], [terms] * 2, [masks] * 2, [0, half], half, bits, follow)[0]


def finish(state, stages, follow, passed=()):
    for bits in stages[1:]:
        args = [x for keep, recv, _ in state for x in (keep, recv)]
        masks = [left for _, _, left in state]
        terms = [
            {m: ((2 * h, i), (2 * h + 1, i)) for i, m in enumerate(left)}
            for h, left in enumerate(masks)
        ]
        state, passed = fold(
            args, terms, masks, [0, 0], args[0].shape[1], bits, follow, passed
        )
    return state, passed


def solution(mesh):
    in_specs = (
        P("dp", "tensor"),
        P("dp", None),
        P("dp", None),
        P(None, "tensor"),
        P(None, "tensor"),
        P("tensor", None),
    )
    out_specs = (P("dp", "tensor"), P())
    return jax.shard_map(
        on_device, mesh=mesh, in_specs=in_specs, out_specs=out_specs, check_vma=False
    )
```

```python
import math

import jax
import jax.numpy as jnp
from jax import lax
from jax.experimental import pallas as pl
from jax.experimental.pallas import tpu as pltpu
from jax.sharding import PartitionSpec as P

CAP = 768
CLIP_SHARE = 0.25
LANES = 128
ROW_CHUNKS = 2
BF16 = jnp.bfloat16
F32 = jnp.float32
MIB = 1 << 20
EXPAND_MIB = 24
AHEAD = 3


def params(mib):
    return pltpu.CompilerParams(vmem_limit_bytes=mib * MIB)


TINY = pl.CostEstimate(flops=1, bytes_accessed=1, transcendentals=0)


def across(block, bit):
    count = lax.axis_size("tensor")
    return lax.ppermute(block, "tensor", [(r, r ^ 1 << bit) for r in range(count)])


def iota(shape, dim):
    return lax.broadcasted_iota(jnp.int32, shape, dim)


def slots_of(ids_ref):
    tokens = ids_ref.shape[1]
    rows = tokens // LANES
    padded = (rows + 15) // 16 * 16
    hit = jnp.where((ids_ref[0:1, :] == 0) | (ids_ref[1:2, :] == 0), 1.0, 0.0)
    grid = jnp.concatenate(
        [hit[:, LANES * k : LANES * (k + 1)] for k in range(rows)]
        + [jnp.zeros((padded - rows, LANES), F32)],
        axis=0,
    )
    flat = grid.astype(BF16)
    upto = (iota((LANES, LANES), 0) <= iota((LANES, LANES), 1)).astype(F32).astype(BF16)
    before = (iota((padded, padded), 1) < iota((padded, padded), 0)).astype(F32).astype(BF16)
    within = jnp.dot(flat, upto, preferred_element_type=F32)
    offset = jnp.sum(jnp.dot(before, flat, preferred_element_type=F32), axis=1, keepdims=True)
    return jnp.where(grid > 0.0, within + offset - 1.0, -1.0)


def pick_body(first, ids_hbm, tokens_hbm, *refs):
    picked_ref, peak_ref, ids_ref, tokens_ref, loaded = refs[-5:]
    rows = picked_ref.shape[0]
    count = tokens_ref.shape[0]
    pieces = loaded.shape[0] - 1
    step = count // pieces
    ids_copy = pltpu.make_async_copy(ids_hbm, ids_ref, loaded.at[pieces])
    ids_copy.start()
    copies = [
        pltpu.make_async_copy(
            tokens_hbm.at[pl.ds(i * step, step), :],
            tokens_ref.at[pl.ds(i * step, step), :],
            loaded.at[i],
        )
        for i in range(pieces)
    ]
    for copy in copies:
        copy.start()
    ids_copy.wait()
    slots = slots_of(ids_ref).astype(jnp.int32)
    wanted = iota((rows, LANES), 0) + first
    picked = jnp.zeros(picked_ref.shape, F32)
    for i, copy in enumerate(copies):
        hot = jnp.concatenate(
            [
                jnp.where(wanted == slots[k : k + 1, :], 1.0, 0.0).astype(BF16)
                for k in range(i * step // LANES, (i + 1) * step // LANES)
            ],
            axis=1,
        )
        copy.wait()
        picked += jnp.dot(
            hot, tokens_ref[i * step : (i + 1) * step, :], preferred_element_type=F32
        )
    picked_ref[...] = picked.astype(BF16)
    peak_ref[...] = jnp.broadcast_to(jnp.max(jnp.abs(picked)), peak_ref.shape)


def pick_rows(ids, tokens, first, rows, follow=()):
    count, width = tokens.shape
    blocks = count // LANES
    pieces = math.gcd(blocks, 4)
    in_hbm = [pltpu.with_memory_space_constraint(x, pltpu.HBM) for x in (ids, tokens)]
    return pl.pallas_call(
        lambda *refs: pick_body(first, *refs),
        out_shape=(
            jax.ShapeDtypeStruct((rows, width), BF16),
            jax.ShapeDtypeStruct((8, LANES), F32),
        ),
        in_specs=[pl.BlockSpec(memory_space=pltpu.HBM)] * 2 + follows(follow),
        out_specs=[pl.BlockSpec(memory_space=pltpu.VMEM)] * 2,
        scratch_shapes=[
            pltpu.VMEM(ids.shape, ids.dtype),
            pltpu.VMEM(tokens.shape, tokens.dtype),
            pltpu.SemaphoreType.DMA((pieces + 1,)),
        ],
        compiler_params=params(16),
        cost_estimate=TINY,
        name="pick_rows",
    )(*in_hbm, *follow)


def signs(size):
    common = iota((size, size), 0) & iota((size, size), 1)
    shift = 1
    while shift < size.bit_length():
        shift *= 2
    while shift > 1:
        shift //= 2
        common = common ^ (common >> shift)
    return (1 - 2 * (common & 1)).astype(F32).astype(BF16)


def expand_body(first, cuts, last, me_ref, *refs):
    count = len(cuts)
    parts = []
    for pieces in cuts:
        parts.append(refs[:pieces])
        refs = refs[pieces:]
    before_ref = None
    if last:
        before_ref, refs = refs[0], refs[1:]
    gate_hbm, up_hbm, *outs, total, held, loaded = refs
    width = parts[0][0].shape[1]
    columns = total.shape[2]
    tile = min(256, columns)

    def load(mask):
        rows = pl.ds(pl.multiple_of((me_ref[0] ^ mask) * width, LANES), width)
        return [
            pltpu.make_async_copy(
                weight.at[rows, pl.ds(first, columns)], held.at[mask, at], loaded.at[mask, at]
            )
            for at, weight in enumerate((gate_hbm, up_hbm))
        ]

    loads = [load(mask) for mask in range(count)]
    for copies in loads[:AHEAD]:
        for copy in copies:
            copy.start()
    table = signs(tile)
    for mask, pieces in enumerate(parts):
        part = jnp.concatenate([piece[...] for piece in pieces], axis=0)
        for copies in loads[mask + AHEAD : mask + AHEAD + 1]:
            for copy in copies:
                copy.start()
        for at in range(2):
            loads[mask][at].wait()
            term = jnp.dot(part, held[mask, at], preferred_element_type=F32)
            if mask == 0:
                total[at] = term
            else:
                total[at] += term
    values = []
    for i in range(columns // tile):
        gate = total[0, :, i * tile : (i + 1) * tile]
        up = total[1, :, i * tile : (i + 1) * tile]
        hidden = (gate * (1.0 / (1.0 + jnp.exp(-gate))) * up).astype(BF16)
        values.append(jnp.dot(hidden, table, preferred_element_type=F32))
        if not last:
            outs[0][i] = values[i]
    if not last:
        return
    values = [before_ref[i] for i in range(before_ref.shape[0])] + values
    steps = len(values)
    gap = 1
    while gap < steps:
        values = [
            values[i] + values[i ^ gap] if not i & gap else values[i ^ gap] - values[i]
            for i in range(steps)
        ]
        gap *= 2
    for i in range(steps):
        low = 0
        for out in outs:
            rows = out.shape[0]
            out[:, i * tile : (i + 1) * tile] = values[i][low : low + rows].astype(BF16)
            low += rows


def expand(parts, rows, me, gate_weight, up_weight, before=None, follow=()):
    depth, width = gate_weight.shape
    last = before is not None
    columns = width // 2
    first = columns if last else 0
    tile = min(256, columns)
    parts = [x if isinstance(x, (list, tuple)) else [x] for x in parts]
    cuts = [len(x) for x in parts]
    parts = [x for pieces in parts for x in pieces]
    count = len(cuts)
    vmem = pl.BlockSpec(memory_space=pltpu.VMEM)
    in_hbm = [pltpu.with_memory_space_constraint(x, pltpu.HBM) for x in (gate_weight, up_weight)]
    args = [me, *parts] + ([before] if last else [])
    used = len(args) + 2
    if last:
        out_shape = [jax.ShapeDtypeStruct((rows // 2, width), BF16)] * 2
    else:
        out_shape = [jax.ShapeDtypeStruct((columns // tile, rows, tile), F32)]
    return pl.pallas_call(
        lambda *refs: expand_body(first, cuts, last, *refs[:used], *refs[used + len(follow) :]),
        in_specs=[pl.BlockSpec(memory_space=pltpu.SMEM)]
        + [vmem] * (used - 3)
        + [pl.BlockSpec(memory_space=pltpu.HBM)] * 2
        + follows(follow),
        out_specs=[vmem] * len(out_shape),
        out_shape=out_shape,
        scratch_shapes=[
            pltpu.VMEM((2, rows, columns), F32),
            pltpu.VMEM((count, 2, depth // count, columns), BF16),
            pltpu.SemaphoreType.DMA((count, 2)),
        ],
        compiler_params=params(EXPAND_MIB),
        cost_estimate=TINY,
        name="expand_last" if last else "expand_first",
    )(*args, *in_hbm, *follow)


def clip_body(ins, outs):
    level = CLIP_SHARE * jnp.max(ins[0][8:, :])
    low = 0
    for part in ins[1:]:
        rows = part.shape[0]
        outs[0][low : low + rows, :] = jnp.clip(part[...].astype(F32), -level, level).astype(BF16)
        low += rows


def down_body(first, me_ref, clipped_ref, weight_hbm, *refs):
    owners = lax.axis_size("tensor")
    half = owners // 2
    other_ref, same_ref, held, loaded = refs[-4:]
    fc = same_ref.shape[2]
    stride = weight_hbm.shape[1] // owners
    masks = [2 * i + 1 for i in range(half)] + [2 * i for i in range(half)]

    def load(i):
        column = pl.multiple_of((me_ref[0] ^ masks[i]) * stride + first, LANES)
        return pltpu.make_async_copy(
            weight_hbm.at[:, pl.ds(column, fc)],
            held.at[i // 2, :, pl.ds(i % 2 * fc, fc)],
            loaded.at[i],
        )

    loads = [load(i) for i in range(owners)]
    for copy in loads[: 2 * AHEAD]:
        copy.start()
    for pair in range(half):
        for copy in loads[2 * (pair + AHEAD) : 2 * (pair + AHEAD + 1)]:
            copy.start()
        for copy in loads[2 * pair : 2 * pair + 2]:
            copy.wait()
        terms = jnp.dot(clipped_ref[...], held[pair], preferred_element_type=F32).astype(BF16)
        for side in range(2):
            i = 2 * pair + side
            term = terms[:, side * fc : (side + 1) * fc]
            if i < half:
                other_ref[i] = term
            else:
                same_ref[i - half] = term


def down(clipped, weight, me, units, first, follow=()):
    depth = weight.shape[0]
    owners = lax.axis_size("tensor")
    half = owners // 2
    rows = clipped.shape[0]
    fc = units * LANES
    vmem = pl.BlockSpec(memory_space=pltpu.VMEM)
    shape = jax.ShapeDtypeStruct((half, rows, fc), BF16)
    return pl.pallas_call(
        lambda *refs: down_body(first * LANES, *refs),
        in_specs=[
            pl.BlockSpec(memory_space=pltpu.SMEM),
            vmem,
            pl.BlockSpec(memory_space=pltpu.HBM),
        ]
        + follows(follow),
        out_specs=[vmem] * 2,
        out_shape=[shape] * 2,
        scratch_shapes=[
            pltpu.VMEM((half, depth, 2 * fc), BF16),
            pltpu.SemaphoreType.DMA((owners,)),
        ],
        compiler_params=params(16),
        cost_estimate=TINY,
        name="down",
    )(me, clipped, pltpu.with_memory_space_constraint(weight, pltpu.HBM), *follow)


def spread_body(count, slot, ids_ref, probs_ref, *refs):
    mine, theirs = refs[:count], refs[count : 2 * count]
    out_ref, mark_ref = refs[-2:]
    mark_ref[...] = jnp.zeros_like(mark_ref)
    tokens = ids_ref.shape[1]
    summed = jnp.concatenate(
        [(a[0].astype(F32) + b[slot].astype(F32)).astype(BF16) for a, b in zip(mine, theirs)], axis=0
    )
    slots = slots_of(ids_ref)
    share = jnp.where(ids_ref[0:1, :] == 0, probs_ref[0:1, :], 0.0) + jnp.where(
        ids_ref[1:2, :] == 0, probs_ref[1:2, :], 0.0
    )
    blocks = tokens // LANES
    share = jnp.concatenate(
        [share[:, LANES * k : LANES * (k + 1)] for k in range(blocks)]
        + [jnp.zeros((LANES - blocks, LANES), F32)],
        axis=0,
    ).T
    slots = jnp.concatenate(
        [slots, jnp.zeros((LANES - slots.shape[0], LANES), F32)], axis=0
    ).T.astype(jnp.int32)
    at = iota((LANES, summed.shape[0]), 1)
    for k in range(blocks):
        hot = jnp.where(at == slots[:, k : k + 1], 1.0, 0.0).astype(BF16)
        rows = jnp.dot(hot, summed, preferred_element_type=F32)
        out_ref[LANES * k : LANES * (k + 1), :] = (rows * share[:, k : k + 1]).astype(BF16)


def spread(ids, probs, state, first, features, out, follow=(), held=-1):
    mine, theirs = [x[0] for x in state], [x[1] for x in state]
    slot = theirs[0].shape[0] - 1 if held < 0 else held
    tokens = ids.shape[1]
    count = len(mine)
    _, rows, fc = mine[0].shape
    args = [ids, probs, *mine, *theirs]
    in_specs = [pl.BlockSpec(x.shape, lambda i, d=x.ndim: (0,) * d) for x in args]
    aliases = {}
    if out is not None:
        aliases = {len(args): 0}
        follow = [out, *follow]
    return pl.pallas_call(
        lambda *refs: spread_body(count, slot, *refs[: 2 + 2 * count], *refs[-2:]),
        grid=(1,),
        in_specs=in_specs + follows(follow),
        out_specs=[
            pl.BlockSpec((pl.Element(tokens), pl.Element(fc)), lambda i: (0, first * LANES)),
            pl.BlockSpec((8, LANES), lambda i: (0, 0)),
        ],
        out_shape=[
            jax.ShapeDtypeStruct((tokens, features), BF16),
            jax.ShapeDtypeStruct((8, LANES), F32),
        ],
        input_output_aliases=aliases,
        compiler_params=params(16),
        cost_estimate=TINY,
        name="spread",
    )(*args, *follow)


def follows(arrays):
    return [pl.BlockSpec(memory_space=pl.ANY)] * len(arrays)


def small(body, args, shapes, name, follow=()):
    vmem = pl.BlockSpec(memory_space=pltpu.VMEM)
    count = len(args)
    specs = [pl.BlockSpec(memory_space=pltpu.SMEM) if x.ndim == 1 else vmem for x in args]
    return pl.pallas_call(
        lambda *refs: body(refs[:count], refs[count + len(follow) :]),
        in_specs=specs + follows(follow),
        out_specs=[vmem] * len(shapes),
        out_shape=[jax.ShapeDtypeStruct(*x) for x in shapes],
        compiler_params=params(16),
        cost_estimate=TINY,
        name=name,
    )(*args, *follow)


def gather_near(own, orders):
    return {0: own} | {1 << bit: across(own, bit) for bit in orders[0]}


def cut_body(firsts, ins, outs):
    for h, at in enumerate(firsts):
        rows = outs[h].shape[0]
        outs[h][...] = ins[at][h * rows : (h + 1) * rows, :]
    for block, out in zip(ins, outs[2:]):
        out[...] = block[...]


def join_body(ins, outs):
    pieces = 2 * len(outs) // len(ins)
    for i in range(len(ins) // 2):
        whole = jnp.concatenate([ins[2 * i][...], ins[2 * i + 1][...]], axis=0)
        for k in range(pieces):
            out = outs[pieces * i + k]
            rows = out.shape[0]
            out[...] = whole[k * rows : (k + 1) * rows, :]


def cut(full, orders, follow, passed=False):
    rows, width = full[0].shape
    masks = [mask for mask in full if mask]
    firsts = [masks.index(1 << order[0]) for order in orders]
    shapes = [((rows // 2, width), BF16)] * 2 + [((rows, width), BF16)] * len(masks) * passed
    outs = small(
        lambda ins, outs: cut_body(firsts, ins, outs),
        [full[mask] for mask in masks],
        shapes,
        "cut",
        follow,
    )
    return outs[:2], full | dict(zip(masks, outs[2:]))


def gather_far(full, cuts, orders):
    half = full[0].shape[0] // len(orders)
    firsts = [1 << order[0] for order in orders]
    part = {}

    def get(mask, h):
        if (mask, h) in part:
            return part[mask, h]
        return cuts[h] if mask == firsts[h] else full[mask][h * half : (h + 1) * half]

    have = [[0, first] for first in firsts]
    for at in range(1, len(orders[0])):
        for h, order in enumerate(orders):
            bit = order[at]
            for mask in list(have[h]):
                there = mask | 1 << bit
                if there not in full:
                    part[there, h] = across(get(mask, h), bit)
                have[h].append(there)
    return part


def join(part, follow, pieces):
    masks = sorted({mask for mask, _ in part})
    halves = [part[mask, h] for mask in masks for h in range(2)]
    half, width = halves[0].shape
    shapes = [((2 * half // pieces, width), BF16)] * (pieces * len(masks))
    joined = small(join_body, halves, shapes, "join", follow)
    return {mask: joined[pieces * i : pieces * (i + 1)] for i, mask in enumerate(masks)}


def paired(pieces):
    return pieces | {
        mask | 1: [across(x, 0) for x in block] if isinstance(block, list) else across(block, 0)
        for mask, block in pieces.items()
    }


def turn_body(bits, scale, ins, outs):
    me_ref, ins = ins[0], ins[1:]
    count = len(bits)
    for h, bit in enumerate(bits):
        flip = (1 - 2 * ((me_ref[0] >> bit) & 1)).astype(F32)
        own = ins[2 * h][...].astype(F32)
        came = ins[2 * h + 1][...].astype(F32)
        value = came + own * flip
        if scale is not None:
            value = value * scale
            top = jnp.max(jnp.abs(own) + jnp.abs(came), axis=0, keepdims=True) * scale
            wide = top[:, :LANES]
            for k in range(1, top.shape[1] // LANES):
                wide = jnp.maximum(wide, top[:, k * LANES : (k + 1) * LANES])
            outs[count + h][...] = jnp.broadcast_to(wide, outs[count + h].shape)
        outs[h][...] = value.astype(BF16)


def turn(me, blocks, came, bits, follow=(), scale=None):
    args = [me] + [x for pair in zip(blocks, came) for x in pair]
    shapes = [(x.shape, BF16) for x in blocks]
    if scale is not None:
        shapes += [((8, LANES), F32)] * len(blocks)
    return small(
        lambda ins, outs: turn_body(bits, scale, ins, outs), args, shapes, "turn", follow
    )


def largest(top_in, tops, lasts):
    bits = range(lax.axis_size("tensor").bit_length() - 1)
    values = jnp.concatenate([top_in, *tops], axis=0)
    for bit in bits:
        if bit not in lasts:
            values = jnp.maximum(values, across(values, bit))
    n = top_in.shape[0]
    top_in, first, second = values[:n], values[n : 2 * n], values[2 * n :]
    if lasts[0] != lasts[1]:
        pair = jnp.concatenate([top_in, second], axis=0)
        came_first, came_pair = across(first, lasts[1]), across(pair, lasts[0])
        first = jnp.maximum(first, came_first)
        pair = jnp.maximum(pair, came_pair)
        top_in, second = pair[:n], pair[n:]
    values = jnp.concatenate([top_in, jnp.maximum(first, second)], axis=0)
    blocks = lax.axis_size("dp")
    far = 1
    while far < blocks:
        pairs = [(r, r ^ far) for r in range(blocks)]
        values = jnp.maximum(values, lax.ppermute(values, "dp", pairs))
        far *= 2
    return values


def on_device(tokens, expert_ids, gate_probs, gate_weight, up_weight, down_weight):
    count = lax.axis_size("tensor")
    bits = count.bit_length() - 1
    outer = list(range(1, bits))
    orders = [outer, outer[::-1]]
    me = lax.axis_index("tensor")
    me_arr = me.astype(jnp.int32).reshape(1)
    ids, probs = expert_ids.T, gate_probs.T
    rows = CAP // ROW_CHUNKS
    half = rows // 2
    scale = 1.0 / math.sqrt(gate_weight.shape[1] * count)
    stages = [[order[at] for order in orders] for at in range(len(outer))]
    early_bit = stages[-1][1]

    def send(blocks, bits):
        return [across(x, bit) for x, bit in zip(blocks, bits)]

    def start_turn(halves, follow=()):
        blocks = turn(me_arr, halves, send(halves, [0, 0]), [0, 0], follow)
        return blocks, send(blocks, stages[0])

    def go_on(blocks, came, at, follow=()):
        blocks = turn(me_arr, blocks, came, stages[at], follow)
        return blocks, send(blocks, stages[at + 1])

    def end_turn(blocks, came, follow=()):
        made = turn(me_arr, blocks, came, stages[-1], follow, scale)
        return made[: len(blocks)], made[len(blocks) :]

    own_a, top_a = pick_rows(ids, tokens, 0, rows, [me_arr])
    near_a = gather_near(own_a, orders)
    weights = (me_arr, gate_weight, up_weight)
    cuts_a, near_a = cut(near_a, orders, [])
    own_b, top_b = pick_rows(ids, tokens, rows, rows, cuts_a)
    top_in = jnp.maximum(top_a, top_b)
    top_in = jnp.maximum(top_in, across(top_in, early_bit))
    far_a = join(gather_far(near_a, cuts_a, orders), [own_b, top_in], 1)
    near_b = gather_near(own_b, orders)
    parts_a = paired(near_a | far_a)
    parts_a = [parts_a[mask] for mask in range(count)]
    first_a = expand(parts_a, rows, *weights)
    local_a = expand(parts_a, rows, *weights, *first_a)
    cuts_b, near_b = cut(near_b, orders, local_a, True)
    parts_b = paired(near_b)
    theirs_b = [block for mask, block in parts_b.items() if mask & 1]
    blocks_a, came_a = start_turn(local_a)
    far_b = join(gather_far(near_b, cuts_b, orders), list(blocks_a) + theirs_b, 3)
    parts_b |= paired(far_b)
    parts_b = [parts_b[mask] for mask in range(count)]
    first_b = expand(parts_b, rows, *weights, None, blocks_a)
    for at in range(len(outer) - 1):
        blocks_a, came_a = go_on(blocks_a, came_a, at, first_b)
    local_b = expand(parts_b, rows, *weights, *first_b, blocks_a)
    turned_a, rot_a = end_turn(blocks_a, came_a, local_b)
    blocks_b, came_b = start_turn(local_b, rot_a)
    for at in range(len(outer) - 1):
        blocks_b, came_b = go_on(blocks_b, came_b, at)
    turned_b, rot_b = end_turn(blocks_b, came_b)
    rotated = turned_a + turned_b

    peaks = largest(top_in, [jnp.maximum(x, y) for x, y in zip(rot_a, rot_b)], stages[-1])
    clipped = small(
        clip_body, [peaks, *rotated], [((CAP, gate_weight.shape[1]), BF16)], "clip"
    )[0]

    tops = pl.pallas_call(
        peaks_body,
        out_specs=pl.BlockSpec(memory_space=pltpu.SMEM),
        out_shape=jax.ShapeDtypeStruct((2,), F32),
        name="peaks",
    )(peaks)
    units = tokens.shape[1] // LANES
    sizes = chunks_of(units)
    firsts = [sum(sizes[:i]) for i in range(len(sizes))]
    total = len(sizes)
    products, begun, ended, out, last = {}, {}, {}, None, []
    for step, chunk in sums_order(total):
        if step == "product":
            products[chunk] = down(
                clipped, down_weight, me_arr, sizes[chunk], firsts[chunk], last
            )
            last = [products[chunk][1]]
        elif step == "begin":
            other, same = products[chunk]
            begun[chunk] = fold_cores(same, across(other, 0), stages[0], last)
            last = [keep for keep, _, _ in begun[chunk]]
        elif step == "finish":
            ahead = [c for c in products if c not in begun]
            passed = [products[c][0] for c in ahead]
            held = chunk == 0 and total > 2
            stacked = [x for _, x, _ in ended[0]] if chunk == 1 and total > 2 else []
            ended[chunk], passed = finish(
                begun[chunk], stages, last, passed, stacked, not held
            )
            if stacked:
                ended[0] = [
                    (keep, both, left)
                    for (keep, _, left), (_, both, _) in zip(ended[0], ended[1])
                ]
            for c, other in zip(ahead, passed):
                products[c] = (other, products[c][1])
            last = [keep for keep, _, _ in ended[chunk]]
        else:
            out, mark = spread(
                ids,
                probs,
                ended[chunk],
                firsts[chunk],
                tokens.shape[1],
                out,
                last,
                0 if chunk == 0 else -1,
            )
            last = [mark]
    return out, tops


def chunks_of(units):
    return [2] * (units // 2) + [1] * (units % 2)


def sums_order(total):
    order = [("product", 0)]
    for chunk in range(total):
        if chunk + 1 < total:
            order.append(("product", chunk + 1))
        order.append(("begin", chunk))
        if chunk > 0:
            order.append(("finish", chunk - 1))
        if chunk > 1 and chunk + 1 < total:
            order.append(("spread", chunk - 2))
    order.append(("finish", total - 1))
    return order + [("spread", c) for c in range(total) if ("spread", c) not in order]


def peaks_body(values_ref, out_ref):
    out_ref[0] = jnp.max(values_ref[:8, :])
    out_ref[1] = jnp.max(values_ref[8:, :])


def fold_body(plan, passed, ins, outs):
    for i in range(passed):
        outs[len(plan) + i][...] = ins[len(ins) - passed + i][...]
    for out, (slots, low) in zip(outs, plan):
        rows = out.shape[1]
        for slot, terms in enumerate(slots):
            total = 0.0
            for at, i in terms:
                total = total + ins[at][i, low : low + rows, :].astype(F32)
            out[slot] = total.astype(BF16)


def fold(args, terms, masks, lows, rows, bits, follow, passed=(), stacked=(), sent=True):
    plan, shapes, lefts = [], [], []
    width = args[0].shape[2]
    for h, bit in enumerate(bits):
        for side in (0, 1):
            chosen = [m for m in masks[h] if m >> bit & 1 == side]
            slots = [terms[h][m] for m in chosen]
            if side and stacked:
                slots = [((len(args) + h, i),) for i in range(stacked[h].shape[0])] + slots
            plan.append((slots, lows[h]))
            shapes.append(((len(slots), rows, width), BF16))
        lefts.append([m for m in masks[h] if not m >> bit & 1])
    shapes += [(x.shape, x.dtype) for x in passed]
    made = small(
        lambda ins, outs: fold_body(plan, len(passed), ins, outs),
        [*args, *stacked, *passed],
        shapes,
        "fold",
        follow,
    )
    state = [
        (made[2 * h], across(made[2 * h + 1], bit) if sent else made[2 * h + 1], lefts[h])
        for h, bit in enumerate(bits)
    ]
    return state, made[len(plan) :]


def fold_cores(same, came, bits, follow):
    half = same.shape[1] // 2
    masks = [2 * i for i in range(same.shape[0])]
    terms = {m: ((0, i), (1, i)) for i, m in enumerate(masks)}
    return fold([same, came], [terms] * 2, [masks] * 2, [0, half], half, bits, follow)[0]


def finish(state, stages, follow, passed=(), stacked=(), sent=True):
    for bits in stages[1:]:
        args = [x for keep, recv, _ in state for x in (keep, recv)]
        masks = [left for _, _, left in state]
        terms = [
            {m: ((2 * h, i), (2 * h + 1, i)) for i, m in enumerate(left)}
            for h, left in enumerate(masks)
        ]
        last = bits is stages[-1]
        state, passed = fold(
            args,
            terms,
            masks,
            [0, 0],
            args[0].shape[1],
            bits,
            follow,
            passed,
            stacked if last else (),
            sent or not last,
        )
    return state, passed


def solution(mesh):
    in_specs = (
        P("dp", "tensor"),
        P("dp", None),
        P("dp", None),
        P(None, "tensor"),
        P(None, "tensor"),
        P("tensor", None),
    )
    out_specs = (P("dp", "tensor"), P())
    return jax.shard_map(
        on_device, mesh=mesh, in_specs=in_specs, out_specs=out_specs, check_vma=False
    )
```

```python
import math

import jax
import jax.numpy as jnp
from jax import lax
from jax.experimental import pallas as pl
from jax.experimental.pallas import tpu as pltpu
from jax.sharding import PartitionSpec as P

CAP = 768
CLIP_SHARE = 0.25
LANES = 128
ROW_CHUNKS = 2
BF16 = jnp.bfloat16
F32 = jnp.float32
MIB = 1 << 20
EXPAND_MIB = 24
AHEAD = 3


def params(mib):
    return pltpu.CompilerParams(vmem_limit_bytes=mib * MIB)


TINY = pl.CostEstimate(flops=1, bytes_accessed=1, transcendentals=0)


def across(block, bit):
    count = lax.axis_size("tensor")
    return lax.ppermute(block, "tensor", [(r, r ^ 1 << bit) for r in range(count)])


def iota(shape, dim):
    return lax.broadcasted_iota(jnp.int32, shape, dim)


def slots_of(ids_ref):
    tokens = ids_ref.shape[1]
    rows = tokens // LANES
    padded = (rows + 15) // 16 * 16
    hit = jnp.where((ids_ref[0:1, :] == 0) | (ids_ref[1:2, :] == 0), 1.0, 0.0)
    grid = jnp.concatenate(
        [hit[:, LANES * k : LANES * (k + 1)] for k in range(rows)]
        + [jnp.zeros((padded - rows, LANES), F32)],
        axis=0,
    )
    flat = grid.astype(BF16)
    upto = (iota((LANES, LANES), 0) <= iota((LANES, LANES), 1)).astype(F32).astype(BF16)
    before = (iota((padded, padded), 1) < iota((padded, padded), 0)).astype(F32).astype(BF16)
    within = jnp.dot(flat, upto, preferred_element_type=F32)
    offset = jnp.sum(jnp.dot(before, flat, preferred_element_type=F32), axis=1, keepdims=True)
    return jnp.where(grid > 0.0, within + offset - 1.0, -1.0)


def pick_body(first, ids_hbm, tokens_hbm, *refs):
    picked_ref, peak_ref, ids_ref, tokens_ref, loaded = refs[-5:]
    rows = picked_ref.shape[0]
    count = tokens_ref.shape[0]
    pieces = loaded.shape[0] - 1
    step = count // pieces
    ids_copy = pltpu.make_async_copy(ids_hbm, ids_ref, loaded.at[pieces])
    ids_copy.start()
    copies = [
        pltpu.make_async_copy(
            tokens_hbm.at[pl.ds(i * step, step), :],
            tokens_ref.at[pl.ds(i * step, step), :],
            loaded.at[i],
        )
        for i in range(pieces)
    ]
    for copy in copies:
        copy.start()
    ids_copy.wait()
    slots = slots_of(ids_ref).astype(jnp.int32)
    wanted = iota((rows, LANES), 0) + first
    picked = jnp.zeros(picked_ref.shape, F32)
    for i, copy in enumerate(copies):
        hot = jnp.concatenate(
            [
                jnp.where(wanted == slots[k : k + 1, :], 1.0, 0.0).astype(BF16)
                for k in range(i * step // LANES, (i + 1) * step // LANES)
            ],
            axis=1,
        )
        copy.wait()
        picked += jnp.dot(
            hot, tokens_ref[i * step : (i + 1) * step, :], preferred_element_type=F32
        )
    picked_ref[...] = picked.astype(BF16)
    peak_ref[...] = jnp.broadcast_to(jnp.max(jnp.abs(picked)), peak_ref.shape)


def pick_rows(ids, tokens, first, rows, follow=()):
    count, width = tokens.shape
    blocks = count // LANES
    pieces = math.gcd(blocks, 4)
    in_hbm = [pltpu.with_memory_space_constraint(x, pltpu.HBM) for x in (ids, tokens)]
    return pl.pallas_call(
        lambda *refs: pick_body(first, *refs),
        out_shape=(
            jax.ShapeDtypeStruct((rows, width), BF16),
            jax.ShapeDtypeStruct((8, LANES), F32),
        ),
        in_specs=[pl.BlockSpec(memory_space=pltpu.HBM)] * 2 + follows(follow),
        out_specs=[pl.BlockSpec(memory_space=pltpu.VMEM)] * 2,
        scratch_shapes=[
            pltpu.VMEM(ids.shape, ids.dtype),
            pltpu.VMEM(tokens.shape, tokens.dtype),
            pltpu.SemaphoreType.DMA((pieces + 1,)),
        ],
        compiler_params=params(16),
        cost_estimate=TINY,
        name="pick_rows",
    )(*in_hbm, *follow)


def signs(size):
    common = iota((size, size), 0) & iota((size, size), 1)
    shift = 1
    while shift < size.bit_length():
        shift *= 2
    while shift > 1:
        shift //= 2
        common = common ^ (common >> shift)
    return (1 - 2 * (common & 1)).astype(F32).astype(BF16)


def whole(pieces):
    if len(pieces) == 1:
        return pieces[0][...]
    return jnp.concatenate([piece[...] for piece in pieces], axis=0)


def expand_body(first, cuts, last, me_ref, *refs):
    count = len(cuts)
    parts = []
    for pieces in cuts:
        parts.append(refs[:pieces])
        refs = refs[pieces:]
    before_ref = None
    if last:
        before_ref, refs = refs[0], refs[1:]
    gate_hbm, up_hbm, *outs, total, held, loaded = refs
    width = parts[0][0].shape[1]
    columns = total.shape[2]
    tile = min(256, columns)

    def load(mask):
        rows = pl.ds(pl.multiple_of((me_ref[0] ^ mask) * width, LANES), width)
        return [
            pltpu.make_async_copy(
                weight.at[rows, pl.ds(first, columns)], held.at[mask, at], loaded.at[mask, at]
            )
            for at, weight in enumerate((gate_hbm, up_hbm))
        ]

    loads = [load(mask) for mask in range(count)]
    for copies in loads[:AHEAD]:
        for copy in copies:
            copy.start()
    table = signs(tile)
    for mask, pieces in enumerate(parts):
        for copies in loads[mask + AHEAD : mask + AHEAD + 1]:
            for copy in copies:
                copy.start()
        for at in range(2):
            loads[mask][at].wait()
            term = jnp.dot(whole(pieces), held[mask, at], preferred_element_type=F32)
            if mask == 0:
                total[at] = term
            else:
                total[at] += term
    values = []
    for i in range(columns // tile):
        gate = total[0, :, i * tile : (i + 1) * tile]
        up = total[1, :, i * tile : (i + 1) * tile]
        hidden = (gate * (1.0 / (1.0 + jnp.exp(-gate))) * up).astype(BF16)
        values.append(jnp.dot(hidden, table, preferred_element_type=F32))
        if not last:
            outs[0][i] = values[i]
    if not last:
        return
    values = [before_ref[i] for i in range(before_ref.shape[0])] + values
    steps = len(values)
    gap = 1
    while gap < steps:
        values = [
            values[i] + values[i ^ gap] if not i & gap else values[i ^ gap] - values[i]
            for i in range(steps)
        ]
        gap *= 2
    for i in range(steps):
        low = 0
        for out in outs:
            rows = out.shape[0]
            out[:, i * tile : (i + 1) * tile] = values[i][low : low + rows].astype(BF16)
            low += rows


def expand(parts, rows, me, gate_weight, up_weight, before=None, follow=()):
    depth, width = gate_weight.shape
    last = before is not None
    columns = width // 2
    first = columns if last else 0
    tile = min(256, columns)
    parts = [x if isinstance(x, (list, tuple)) else [x] for x in parts]
    cuts = [len(x) for x in parts]
    parts = [x for pieces in parts for x in pieces]
    count = len(cuts)
    vmem = pl.BlockSpec(memory_space=pltpu.VMEM)
    in_hbm = [pltpu.with_memory_space_constraint(x, pltpu.HBM) for x in (gate_weight, up_weight)]
    args = [me, *parts] + ([before] if last else [])
    used = len(args) + 2
    if last:
        out_shape = [jax.ShapeDtypeStruct((rows // 2, width), BF16)] * 2
    else:
        out_shape = [jax.ShapeDtypeStruct((columns // tile, rows, tile), F32)]
    return pl.pallas_call(
        lambda *refs: expand_body(first, cuts, last, *refs[:used], *refs[used + len(follow) :]),
        in_specs=[pl.BlockSpec(memory_space=pltpu.SMEM)]
        + [vmem] * (used - 3)
        + [pl.BlockSpec(memory_space=pltpu.HBM)] * 2
        + follows(follow),
        out_specs=[vmem] * len(out_shape),
        out_shape=out_shape,
        scratch_shapes=[
            pltpu.VMEM((2, rows, columns), F32),
            pltpu.VMEM((count, 2, depth // count, columns), BF16),
            pltpu.SemaphoreType.DMA((count, 2)),
        ],
        compiler_params=params(EXPAND_MIB),
        cost_estimate=TINY,
        name="expand_last" if last else "expand_first",
    )(*args, *in_hbm, *follow)


def clip_body(ins, outs):
    level = CLIP_SHARE * jnp.max(ins[0][8:, :])
    low = 0
    for part in ins[1:]:
        rows = part.shape[0]
        outs[0][low : low + rows, :] = jnp.clip(part[...].astype(F32), -level, level).astype(BF16)
        low += rows


def down_body(first, me_ref, clipped_ref, weight_hbm, *refs):
    owners = lax.axis_size("tensor")
    half = owners // 2
    other_ref, same_ref, held, loaded = refs[-4:]
    fc = same_ref.shape[2]
    stride = weight_hbm.shape[1] // owners
    masks = [2 * i + 1 for i in range(half)] + [2 * i for i in range(half)]

    def load(i):
        column = pl.multiple_of((me_ref[0] ^ masks[i]) * stride + first, LANES)
        return pltpu.make_async_copy(
            weight_hbm.at[:, pl.ds(column, fc)],
            held.at[i // 2, :, pl.ds(i % 2 * fc, fc)],
            loaded.at[i],
        )

    loads = [load(i) for i in range(owners)]
    for copy in loads[: 2 * AHEAD]:
        copy.start()
    for pair in range(half):
        for copy in loads[2 * (pair + AHEAD) : 2 * (pair + AHEAD + 1)]:
            copy.start()
        for copy in loads[2 * pair : 2 * pair + 2]:
            copy.wait()
        terms = jnp.dot(clipped_ref[...], held[pair], preferred_element_type=F32).astype(BF16)
        for side in range(2):
            i = 2 * pair + side
            term = terms[:, side * fc : (side + 1) * fc]
            if i < half:
                other_ref[i] = term
            else:
                same_ref[i - half] = term


def down(clipped, weight, me, units, first, follow=()):
    depth = weight.shape[0]
    owners = lax.axis_size("tensor")
    half = owners // 2
    rows = clipped.shape[0]
    fc = units * LANES
    vmem = pl.BlockSpec(memory_space=pltpu.VMEM)
    shape = jax.ShapeDtypeStruct((half, rows, fc), BF16)
    return pl.pallas_call(
        lambda *refs: down_body(first * LANES, *refs),
        in_specs=[
            pl.BlockSpec(memory_space=pltpu.SMEM),
            vmem,
            pl.BlockSpec(memory_space=pltpu.HBM),
        ]
        + follows(follow),
        out_specs=[vmem] * 2,
        out_shape=[shape] * 2,
        scratch_shapes=[
            pltpu.VMEM((half, depth, 2 * fc), BF16),
            pltpu.SemaphoreType.DMA((owners,)),
        ],
        compiler_params=params(16),
        cost_estimate=TINY,
        name="down",
    )(me, clipped, pltpu.with_memory_space_constraint(weight, pltpu.HBM), *follow)


def spots_body(ins, outs):
    ids_ref, probs_ref = ins
    hot_ref, share_ref = outs
    blocks = ids_ref.shape[1] // LANES
    slots = slots_of(ids_ref)
    share = jnp.where(ids_ref[0:1, :] == 0, probs_ref[0:1, :], 0.0) + jnp.where(
        ids_ref[1:2, :] == 0, probs_ref[1:2, :], 0.0
    )
    share_ref[...] = jnp.concatenate(
        [share[:, LANES * k : LANES * (k + 1)] for k in range(blocks)]
        + [jnp.zeros((LANES - blocks, LANES), F32)],
        axis=0,
    ).T
    slots = jnp.concatenate(
        [slots, jnp.zeros((LANES - slots.shape[0], LANES), F32)], axis=0
    ).T.astype(jnp.int32)
    at = iota((LANES, hot_ref.shape[1]), 1)
    for k in range(blocks):
        hot_ref[LANES * k : LANES * (k + 1), :] = jnp.where(
            at == slots[:, k : k + 1], 1.0, 0.0
        ).astype(BF16)


def spread_body(count, slot, first, hot_ref, share_ref, *refs):
    mine, theirs = refs[:count], refs[count : 2 * count]
    out_hbm, mark_ref, staged, sent = refs[-4:]
    mark_ref[...] = jnp.zeros_like(mark_ref)
    summed = jnp.concatenate(
        [(a[0].astype(F32) + b[slot].astype(F32)).astype(BF16) for a, b in zip(mine, theirs)], axis=0
    )
    pieces = sent.shape[0]
    rows = hot_ref.shape[0] // pieces
    columns = pl.ds(first, staged.shape[1])
    copies = []
    for i in range(pieces):
        here = slice(rows * i, rows * (i + 1))
        found = jnp.dot(hot_ref[here, :], summed, preferred_element_type=F32)
        for j in range(rows // LANES):
            k = i * (rows // LANES) + j
            part = found[LANES * j : LANES * (j + 1), :] * share_ref[:, k : k + 1]
            staged[LANES * k : LANES * (k + 1), :] = part.astype(BF16)
        span = pl.ds(rows * i, rows)
        copies.append(
            pltpu.make_async_copy(staged.at[span, :], out_hbm.at[span, columns], sent.at[i])
        )
        copies[i].start()
    for copy in copies:
        copy.wait()


def spread(hot, share, state, first, features, out, follow=(), held=-1):
    mine, theirs = [x[0] for x in state], [x[1] for x in state]
    slot = theirs[0].shape[0] - 1 if held < 0 else held
    tokens = hot.shape[0]
    count = len(mine)
    fc = mine[0].shape[2]
    args = [hot, share, *mine, *theirs]
    used = len(args)
    vmem = pl.BlockSpec(memory_space=pltpu.VMEM)
    aliases = {}
    if out is not None:
        aliases = {used: 0}
        follow = [out, *follow]
    return pl.pallas_call(
        lambda *refs: spread_body(count, slot, first * LANES, *refs[:used], *refs[-4:]),
        in_specs=[vmem] * used
        + [pl.BlockSpec(memory_space=pltpu.HBM)] * len(aliases)
        + follows(follow[len(aliases) :]),
        out_specs=[pl.BlockSpec(memory_space=pltpu.HBM), vmem],
        out_shape=[
            jax.ShapeDtypeStruct((tokens, features), BF16),
            jax.ShapeDtypeStruct((8, LANES), F32),
        ],
        scratch_shapes=[
            pltpu.VMEM((tokens, fc), BF16),
            pltpu.SemaphoreType.DMA((math.gcd(tokens // LANES, 4),)),
        ],
        input_output_aliases=aliases,
        compiler_params=params(16),
        cost_estimate=TINY,
        name="spread",
    )(*args, *follow)


def follows(arrays):
    return [pl.BlockSpec(memory_space=pl.ANY)] * len(arrays)


def small(body, args, shapes, name, follow=()):
    vmem = pl.BlockSpec(memory_space=pltpu.VMEM)
    count = len(args)
    specs = [pl.BlockSpec(memory_space=pltpu.SMEM) if x.ndim == 1 else vmem for x in args]
    return pl.pallas_call(
        lambda *refs: body(refs[:count], refs[count + len(follow) :]),
        in_specs=specs + follows(follow),
        out_specs=[vmem] * len(shapes),
        out_shape=[jax.ShapeDtypeStruct(*x) for x in shapes],
        compiler_params=params(16),
        cost_estimate=TINY,
        name=name,
    )(*args, *follow)


def gather_near(own, orders):
    return {0: own} | {1 << bit: across(own, bit) for bit in orders[0]}


def cut_body(firsts, ins, outs):
    for h, at in enumerate(firsts):
        rows = outs[h].shape[0]
        outs[h][...] = ins[at][h * rows : (h + 1) * rows, :]
    for block, out in zip(ins, outs[2:]):
        out[...] = block[...]


def join_body(ins, outs):
    pieces = 2 * len(outs) // len(ins)
    for i in range(len(ins) // 2):
        whole = jnp.concatenate([ins[2 * i][...], ins[2 * i + 1][...]], axis=0)
        for k in range(pieces):
            out = outs[pieces * i + k]
            rows = out.shape[0]
            out[...] = whole[k * rows : (k + 1) * rows, :]


def cut(full, orders, follow, passed=False):
    rows, width = full[0].shape
    masks = [mask for mask in full if mask]
    firsts = [masks.index(1 << order[0]) for order in orders]
    shapes = [((rows // 2, width), BF16)] * 2 + [((rows, width), BF16)] * len(masks) * passed
    outs = small(
        lambda ins, outs: cut_body(firsts, ins, outs),
        [full[mask] for mask in masks],
        shapes,
        "cut",
        follow,
    )
    return outs[:2], full | dict(zip(masks, outs[2:]))


def gather_far(full, cuts, orders):
    half = full[0].shape[0] // len(orders)
    firsts = [1 << order[0] for order in orders]
    part = {}

    def get(mask, h):
        if (mask, h) in part:
            return part[mask, h]
        return cuts[h] if mask == firsts[h] else full[mask][h * half : (h + 1) * half]

    have = [[0, first] for first in firsts]
    for at in range(1, len(orders[0])):
        for h, order in enumerate(orders):
            bit = order[at]
            for mask in list(have[h]):
                there = mask | 1 << bit
                if there not in full:
                    part[there, h] = across(get(mask, h), bit)
                have[h].append(there)
    return part


def join(part, follow, pieces):
    masks = sorted({mask for mask, _ in part})
    halves = [part[mask, h] for mask in masks for h in range(2)]
    half, width = halves[0].shape
    shapes = [((2 * half // pieces, width), BF16)] * (pieces * len(masks))
    joined = small(join_body, halves, shapes, "join", follow)
    return {mask: joined[pieces * i : pieces * (i + 1)] for i, mask in enumerate(masks)}


def paired(pieces):
    return pieces | {
        mask | 1: [across(x, 0) for x in block] if isinstance(block, list) else across(block, 0)
        for mask, block in pieces.items()
    }


def turn_body(bits, scale, ins, outs):
    me_ref, ins = ins[0], ins[1:]
    count = len(bits)
    for h, bit in enumerate(bits):
        flip = (1 - 2 * ((me_ref[0] >> bit) & 1)).astype(F32)
        own = ins[2 * h][...].astype(F32)
        came = ins[2 * h + 1][...].astype(F32)
        value = came + own * flip
        if scale is not None:
            value = value * scale
            top = jnp.max(jnp.abs(own) + jnp.abs(came), axis=0, keepdims=True) * scale
            wide = top[:, :LANES]
            for k in range(1, top.shape[1] // LANES):
                wide = jnp.maximum(wide, top[:, k * LANES : (k + 1) * LANES])
            outs[count + h][...] = jnp.broadcast_to(wide, outs[count + h].shape)
        outs[h][...] = value.astype(BF16)


def turn(me, blocks, came, bits, follow=(), scale=None):
    args = [me] + [x for pair in zip(blocks, came) for x in pair]
    shapes = [(x.shape, BF16) for x in blocks]
    if scale is not None:
        shapes += [((8, LANES), F32)] * len(blocks)
    return small(
        lambda ins, outs: turn_body(bits, scale, ins, outs), args, shapes, "turn", follow
    )


def largest(top_in, tops, lasts):
    bits = range(lax.axis_size("tensor").bit_length() - 1)
    values = jnp.concatenate([top_in, *tops], axis=0)
    for bit in bits:
        if bit not in lasts:
            values = jnp.maximum(values, across(values, bit))
    n = top_in.shape[0]
    top_in, first, second = values[:n], values[n : 2 * n], values[2 * n :]
    if lasts[0] != lasts[1]:
        pair = jnp.concatenate([top_in, second], axis=0)
        came_first, came_pair = across(first, lasts[1]), across(pair, lasts[0])
        first = jnp.maximum(first, came_first)
        pair = jnp.maximum(pair, came_pair)
        top_in, second = pair[:n], pair[n:]
    values = jnp.concatenate([top_in, jnp.maximum(first, second)], axis=0)
    blocks = lax.axis_size("dp")
    far = 1
    while far < blocks:
        pairs = [(r, r ^ far) for r in range(blocks)]
        values = jnp.maximum(values, lax.ppermute(values, "dp", pairs))
        far *= 2
    return values


def on_device(tokens, expert_ids, gate_probs, gate_weight, up_weight, down_weight):
    count = lax.axis_size("tensor")
    bits = count.bit_length() - 1
    outer = list(range(1, bits))
    orders = [outer, outer[::-1]]
    me = lax.axis_index("tensor")
    me_arr = me.astype(jnp.int32).reshape(1)
    ids, probs = expert_ids.T, gate_probs.T
    rows = CAP // ROW_CHUNKS
    half = rows // 2
    scale = 1.0 / math.sqrt(gate_weight.shape[1] * count)
    stages = [[order[at] for order in orders] for at in range(len(outer))]
    early_bit = stages[-1][1]

    def send(blocks, bits):
        return [across(x, bit) for x, bit in zip(blocks, bits)]

    def start_turn(halves, follow=()):
        blocks = turn(me_arr, halves, send(halves, [0, 0]), [0, 0], follow)
        return blocks, send(blocks, stages[0])

    def go_on(blocks, came, at, follow=()):
        blocks = turn(me_arr, blocks, came, stages[at], follow)
        return blocks, send(blocks, stages[at + 1])

    def end_turn(blocks, came, follow=()):
        made = turn(me_arr, blocks, came, stages[-1], follow, scale)
        return made[: len(blocks)], made[len(blocks) :]

    own_a, top_a = pick_rows(ids, tokens, 0, rows, [me_arr])
    near_a = gather_near(own_a, orders)
    weights = (me_arr, gate_weight, up_weight)
    cuts_a, near_a = cut(near_a, orders, [])
    own_b, top_b = pick_rows(ids, tokens, rows, rows, cuts_a)
    top_in = jnp.maximum(top_a, top_b)
    top_in = jnp.maximum(top_in, across(top_in, early_bit))
    far_a = join(gather_far(near_a, cuts_a, orders), [own_b, top_in], 1)
    near_b = gather_near(own_b, orders)
    parts_a = paired(near_a | far_a)
    parts_a = [parts_a[mask] for mask in range(count)]
    first_a = expand(parts_a, rows, *weights)
    local_a = expand(parts_a, rows, *weights, *first_a)
    cuts_b, near_b = cut(near_b, orders, local_a, True)
    parts_b = paired(near_b)
    theirs_b = [block for mask, block in parts_b.items() if mask & 1]
    blocks_a, came_a = start_turn(local_a)
    far_b = join(gather_far(near_b, cuts_b, orders), list(blocks_a) + theirs_b, 3)
    parts_b |= paired(far_b)
    parts_b = [parts_b[mask] for mask in range(count)]
    first_b = expand(parts_b, rows, *weights, None, blocks_a)
    for at in range(len(outer) - 1):
        blocks_a, came_a = go_on(blocks_a, came_a, at, first_b)
    local_b = expand(parts_b, rows, *weights, *first_b, blocks_a)
    turned_a, rot_a = end_turn(blocks_a, came_a, local_b)
    blocks_b, came_b = start_turn(local_b, rot_a)
    for at in range(len(outer) - 1):
        blocks_b, came_b = go_on(blocks_b, came_b, at)
    turned_b, rot_b = end_turn(blocks_b, came_b)
    rotated = turned_a + turned_b

    peaks = largest(top_in, [jnp.maximum(x, y) for x, y in zip(rot_a, rot_b)], stages[-1])
    clipped = small(
        clip_body, [peaks, *rotated], [((CAP, gate_weight.shape[1]), BF16)], "clip"
    )[0]

    tops = pl.pallas_call(
        peaks_body,
        out_specs=pl.BlockSpec(memory_space=pltpu.SMEM),
        out_shape=jax.ShapeDtypeStruct((2,), F32),
        name="peaks",
    )(peaks)
    units = tokens.shape[1] // LANES
    sizes = chunks_of(units)
    firsts = [sum(sizes[:i]) for i in range(len(sizes))]
    total = len(sizes)
    products, begun, ended, out, last = {}, {}, {}, None, []
    for step, chunk in sums_order(total):
        if step == "product":
            products[chunk] = down(
                clipped, down_weight, me_arr, sizes[chunk], firsts[chunk], last
            )
            last = [products[chunk][1]]
        elif step == "begin":
            other, same = products[chunk]
            begun[chunk] = fold_cores(same, across(other, 0), stages[0], last)
            last = [keep for keep, _, _ in begun[chunk]]
        elif step == "spots":
            shapes = [((tokens.shape[0], CAP), BF16), ((LANES, LANES), F32)]
            hot, share = small(spots_body, [ids, probs], shapes, "spots", last)
            last = [share]
        elif step == "finish":
            ahead = [c for c in products if c not in begun]
            passed = [products[c][0] for c in ahead]
            held = chunk == 0 and total > 2
            stacked = [x for _, x, _ in ended[0]] if chunk == 1 and total > 2 else []
            ended[chunk], passed = finish(
                begun[chunk], stages, last, passed, stacked, not held
            )
            if stacked:
                ended[0] = [
                    (keep, both, left)
                    for (keep, _, left), (_, both, _) in zip(ended[0], ended[1])
                ]
            for c, other in zip(ahead, passed):
                products[c] = (other, products[c][1])
            last = [keep for keep, _, _ in ended[chunk]]
        else:
            out, mark = spread(
                hot,
                share,
                ended[chunk],
                firsts[chunk],
                tokens.shape[1],
                out,
                last,
                0 if chunk == 0 else -1,
            )
            last = [mark]
    return out, tops


def chunks_of(units):
    return [2] * (units // 2) + [1] * (units % 2)


def sums_order(total):
    order = [("product", 0)]
    for chunk in range(total):
        if chunk + 1 < total:
            order.append(("product", chunk + 1))
        order.append(("begin", chunk))
        if chunk == min(1, total - 1):
            order.append(("spots", 0))
        if chunk > 0:
            order.append(("finish", chunk - 1))
        if chunk > 1 and chunk + 1 < total:
            order.append(("spread", chunk - 2))
    order.append(("finish", total - 1))
    return order + [("spread", c) for c in range(total) if ("spread", c) not in order]


def peaks_body(values_ref, out_ref):
    out_ref[0] = jnp.max(values_ref[:8, :])
    out_ref[1] = jnp.max(values_ref[8:, :])


def fold_body(plan, passed, ins, outs):
    for i in range(passed):
        outs[len(plan) + i][...] = ins[len(ins) - passed + i][...]
    for out, (slots, low) in zip(outs, plan):
        rows = out.shape[1]
        for slot, terms in enumerate(slots):
            total = 0.0
            for at, i in terms:
                total = total + ins[at][i, low : low + rows, :].astype(F32)
            out[slot] = total.astype(BF16)


def fold(args, terms, masks, lows, rows, bits, follow, passed=(), stacked=(), sent=True):
    plan, shapes, lefts = [], [], []
    width = args[0].shape[2]
    for h, bit in enumerate(bits):
        for side in (0, 1):
            chosen = [m for m in masks[h] if m >> bit & 1 == side]
            slots = [terms[h][m] for m in chosen]
            if side and stacked:
                slots = [((len(args) + h, i),) for i in range(stacked[h].shape[0])] + slots
            plan.append((slots, lows[h]))
            shapes.append(((len(slots), rows, width), BF16))
        lefts.append([m for m in masks[h] if not m >> bit & 1])
    shapes += [(x.shape, x.dtype) for x in passed]
    made = small(
        lambda ins, outs: fold_body(plan, len(passed), ins, outs),
        [*args, *stacked, *passed],
        shapes,
        "fold",
        follow,
    )
    state = [
        (made[2 * h], across(made[2 * h + 1], bit) if sent else made[2 * h + 1], lefts[h])
        for h, bit in enumerate(bits)
    ]
    return state, made[len(plan) :]


def fold_cores(same, came, bits, follow):
    half = same.shape[1] // 2
    masks = [2 * i for i in range(same.shape[0])]
    terms = {m: ((0, i), (1, i)) for i, m in enumerate(masks)}
    return fold([same, came], [terms] * 2, [masks] * 2, [0, half], half, bits, follow)[0]


def finish(state, stages, follow, passed=(), stacked=(), sent=True):
    for bits in stages[1:]:
        args = [x for keep, recv, _ in state for x in (keep, recv)]
        masks = [left for _, _, left in state]
        terms = [
            {m: ((2 * h, i), (2 * h + 1, i)) for i, m in enumerate(left)}
            for h, left in enumerate(masks)
        ]
        last = bits is stages[-1]
        state, passed = fold(
            args,
            terms,
            masks,
            [0, 0],
            args[0].shape[1],
            bits,
            follow,
            passed,
            stacked if last else (),
            sent or not last,
        )
    return state, passed


def solution(mesh):
    in_specs = (
        P("dp", "tensor"),
        P("dp", None),
        P("dp", None),
        P(None, "tensor"),
        P(None, "tensor"),
        P("tensor", None),
    )
    out_specs = (P("dp", "tensor"), P())
    return jax.shard_map(
        on_device, mesh=mesh, in_specs=in_specs, out_specs=out_specs, check_vma=False
    )
```

```python
import math

import jax
import jax.numpy as jnp
from jax import lax
from jax.experimental import pallas as pl
from jax.experimental.pallas import tpu as pltpu
from jax.sharding import PartitionSpec as P

CAP = 768
CLIP_SHARE = 0.25
LANES = 128
ROW_CHUNKS = 2
BF16 = jnp.bfloat16
F32 = jnp.float32
MIB = 1 << 20
EXPAND_MIB = 24
AHEAD = 3


def params(mib):
    return pltpu.CompilerParams(vmem_limit_bytes=mib * MIB)


TINY = pl.CostEstimate(flops=1, bytes_accessed=1, transcendentals=0)


def across(block, bit):
    count = lax.axis_size("tensor")
    return lax.ppermute(block, "tensor", [(r, r ^ 1 << bit) for r in range(count)])


def iota(shape, dim):
    return lax.broadcasted_iota(jnp.int32, shape, dim)


def slots_of(ids_ref):
    tokens = ids_ref.shape[1]
    rows = tokens // LANES
    padded = (rows + 15) // 16 * 16
    hit = jnp.where((ids_ref[0:1, :] == 0) | (ids_ref[1:2, :] == 0), 1.0, 0.0)
    grid = jnp.concatenate(
        [hit[:, LANES * k : LANES * (k + 1)] for k in range(rows)]
        + [jnp.zeros((padded - rows, LANES), F32)],
        axis=0,
    )
    flat = grid.astype(BF16)
    upto = (iota((LANES, LANES), 0) <= iota((LANES, LANES), 1)).astype(F32).astype(BF16)
    before = (iota((padded, padded), 1) < iota((padded, padded), 0)).astype(F32).astype(BF16)
    within = jnp.dot(flat, upto, preferred_element_type=F32)
    offset = jnp.sum(jnp.dot(before, flat, preferred_element_type=F32), axis=1, keepdims=True)
    return jnp.where(grid > 0.0, within + offset - 1.0, -1.0)


def pick_body(first, ids_hbm, tokens_hbm, *refs):
    picked_ref, peak_ref, ids_ref, tokens_ref, loaded = refs[-5:]
    rows = picked_ref.shape[0]
    count = tokens_ref.shape[0]
    pieces = loaded.shape[0] - 1
    step = count // pieces
    ids_copy = pltpu.make_async_copy(ids_hbm, ids_ref, loaded.at[pieces])
    ids_copy.start()
    copies = [
        pltpu.make_async_copy(
            tokens_hbm.at[pl.ds(i * step, step), :],
            tokens_ref.at[pl.ds(i * step, step), :],
            loaded.at[i],
        )
        for i in range(pieces)
    ]
    for copy in copies:
        copy.start()
    ids_copy.wait()
    slots = slots_of(ids_ref).astype(jnp.int32)
    wanted = iota((rows, LANES), 0) + first
    picked = jnp.zeros(picked_ref.shape, F32)
    for i, copy in enumerate(copies):
        hot = jnp.concatenate(
            [
                jnp.where(wanted == slots[k : k + 1, :], 1.0, 0.0).astype(BF16)
                for k in range(i * step // LANES, (i + 1) * step // LANES)
            ],
            axis=1,
        )
        copy.wait()
        picked += jnp.dot(
            hot, tokens_ref[i * step : (i + 1) * step, :], preferred_element_type=F32
        )
    picked_ref[...] = picked.astype(BF16)
    peak_ref[...] = jnp.broadcast_to(jnp.max(jnp.abs(picked)), peak_ref.shape)


def pick_rows(ids, tokens, first, rows, follow=()):
    count, width = tokens.shape
    blocks = count // LANES
    pieces = math.gcd(blocks, 4)
    in_hbm = [pltpu.with_memory_space_constraint(x, pltpu.HBM) for x in (ids, tokens)]
    return pl.pallas_call(
        lambda *refs: pick_body(first, *refs),
        out_shape=(
            jax.ShapeDtypeStruct((rows, width), BF16),
            jax.ShapeDtypeStruct((8, LANES), F32),
        ),
        in_specs=[pl.BlockSpec(memory_space=pltpu.HBM)] * 2 + follows(follow),
        out_specs=[pl.BlockSpec(memory_space=pltpu.VMEM)] * 2,
        scratch_shapes=[
            pltpu.VMEM(ids.shape, ids.dtype),
            pltpu.VMEM(tokens.shape, tokens.dtype),
            pltpu.SemaphoreType.DMA((pieces + 1,)),
        ],
        compiler_params=params(16),
        cost_estimate=TINY,
        name="pick_rows",
    )(*in_hbm, *follow)


def signs(size):
    common = iota((size, size), 0) & iota((size, size), 1)
    shift = 1
    while shift < size.bit_length():
        shift *= 2
    while shift > 1:
        shift //= 2
        common = common ^ (common >> shift)
    return (1 - 2 * (common & 1)).astype(F32).astype(BF16)


def whole(pieces):
    if len(pieces) == 1:
        return pieces[0][...]
    return jnp.concatenate([piece[...] for piece in pieces], axis=0)


def expand_body(first, cuts, last, me_ref, *refs):
    count = len(cuts)
    parts = []
    for pieces in cuts:
        parts.append(refs[:pieces])
        refs = refs[pieces:]
    before_ref = None
    if last:
        before_ref, refs = refs[0], refs[1:]
    gate_hbm, up_hbm, *outs, total, held, loaded = refs
    width = parts[0][0].shape[1]
    columns = total.shape[2]
    tile = min(256, columns)

    def load(mask):
        rows = pl.ds(pl.multiple_of((me_ref[0] ^ mask) * width, LANES), width)
        return [
            pltpu.make_async_copy(
                weight.at[rows, pl.ds(first, columns)], held.at[mask, at], loaded.at[mask, at]
            )
            for at, weight in enumerate((gate_hbm, up_hbm))
        ]

    loads = [load(mask) for mask in range(count)]
    for copies in loads[:AHEAD]:
        for copy in copies:
            copy.start()
    table = signs(tile)
    for mask, pieces in enumerate(parts):
        for copies in loads[mask + AHEAD : mask + AHEAD + 1]:
            for copy in copies:
                copy.start()
        for at in range(2):
            loads[mask][at].wait()
            term = jnp.dot(whole(pieces), held[mask, at], preferred_element_type=F32)
            if mask == 0:
                total[at] = term
            else:
                total[at] += term
    values = []
    for i in range(columns // tile):
        gate = total[0, :, i * tile : (i + 1) * tile]
        up = total[1, :, i * tile : (i + 1) * tile]
        hidden = (gate * (1.0 / (1.0 + jnp.exp(-gate))) * up).astype(BF16)
        values.append(jnp.dot(hidden, table, preferred_element_type=F32))
        if not last:
            outs[0][i] = values[i]
    if not last:
        return
    values = [before_ref[i] for i in range(before_ref.shape[0])] + values
    steps = len(values)
    gap = 1
    while gap < steps:
        values = [
            values[i] + values[i ^ gap] if not i & gap else values[i ^ gap] - values[i]
            for i in range(steps)
        ]
        gap *= 2
    for i in range(steps):
        low = 0
        for out in outs:
            rows = out.shape[0]
            out[:, i * tile : (i + 1) * tile] = values[i][low : low + rows].astype(BF16)
            low += rows


def expand(parts, rows, me, gate_weight, up_weight, before=None, follow=()):
    depth, width = gate_weight.shape
    last = before is not None
    columns = width // 2
    first = columns if last else 0
    tile = min(256, columns)
    parts = [x if isinstance(x, (list, tuple)) else [x] for x in parts]
    cuts = [len(x) for x in parts]
    parts = [x for pieces in parts for x in pieces]
    count = len(cuts)
    vmem = pl.BlockSpec(memory_space=pltpu.VMEM)
    in_hbm = [pltpu.with_memory_space_constraint(x, pltpu.HBM) for x in (gate_weight, up_weight)]
    args = [me, *parts] + ([before] if last else [])
    used = len(args) + 2
    if last:
        out_shape = [jax.ShapeDtypeStruct((rows // 2, width), BF16)] * 2
    else:
        out_shape = [jax.ShapeDtypeStruct((columns // tile, rows, tile), F32)]
    return pl.pallas_call(
        lambda *refs: expand_body(first, cuts, last, *refs[:used], *refs[used + len(follow) :]),
        in_specs=[pl.BlockSpec(memory_space=pltpu.SMEM)]
        + [vmem] * (used - 3)
        + [pl.BlockSpec(memory_space=pltpu.HBM)] * 2
        + follows(follow),
        out_specs=[vmem] * len(out_shape),
        out_shape=out_shape,
        scratch_shapes=[
            pltpu.VMEM((2, rows, columns), F32),
            pltpu.VMEM((count, 2, depth // count, columns), BF16),
            pltpu.SemaphoreType.DMA((count, 2)),
        ],
        compiler_params=params(EXPAND_MIB),
        cost_estimate=TINY,
        name="expand_last" if last else "expand_first",
    )(*args, *in_hbm, *follow)


def clip_body(ins, outs):
    level = CLIP_SHARE * jnp.max(ins[0][8:, :])
    low = 0
    for part in ins[1:]:
        rows = part.shape[0]
        outs[0][low : low + rows, :] = jnp.clip(part[...].astype(F32), -level, level).astype(BF16)
        low += rows


def down_body(first, me_ref, clipped_ref, weight_hbm, *refs):
    owners = lax.axis_size("tensor")
    half = owners // 2
    other_ref, same_ref, held, loaded = refs[-4:]
    fc = same_ref.shape[2]
    stride = weight_hbm.shape[1] // owners
    masks = [2 * i + 1 for i in range(half)] + [2 * i for i in range(half)]

    def load(i):
        column = pl.multiple_of((me_ref[0] ^ masks[i]) * stride + first, LANES)
        return pltpu.make_async_copy(
            weight_hbm.at[:, pl.ds(column, fc)],
            held.at[i // 2, :, pl.ds(i % 2 * fc, fc)],
            loaded.at[i],
        )

    loads = [load(i) for i in range(owners)]
    for copy in loads[: 2 * AHEAD]:
        copy.start()
    for pair in range(half):
        for copy in loads[2 * (pair + AHEAD) : 2 * (pair + AHEAD + 1)]:
            copy.start()
        for copy in loads[2 * pair : 2 * pair + 2]:
            copy.wait()
        terms = jnp.dot(clipped_ref[...], held[pair], preferred_element_type=F32).astype(BF16)
        for side in range(2):
            i = 2 * pair + side
            term = terms[:, side * fc : (side + 1) * fc]
            if i < half:
                other_ref[i] = term
            else:
                same_ref[i - half] = term


def down(clipped, weight, me, units, first, follow=()):
    depth = weight.shape[0]
    owners = lax.axis_size("tensor")
    half = owners // 2
    rows = clipped.shape[0]
    fc = units * LANES
    vmem = pl.BlockSpec(memory_space=pltpu.VMEM)
    shape = jax.ShapeDtypeStruct((half, rows, fc), BF16)
    return pl.pallas_call(
        lambda *refs: down_body(first * LANES, *refs),
        in_specs=[
            pl.BlockSpec(memory_space=pltpu.SMEM),
            vmem,
            pl.BlockSpec(memory_space=pltpu.HBM),
        ]
        + follows(follow),
        out_specs=[vmem] * 2,
        out_shape=[shape] * 2,
        scratch_shapes=[
            pltpu.VMEM((half, depth, 2 * fc), BF16),
            pltpu.SemaphoreType.DMA((owners,)),
        ],
        compiler_params=params(16),
        cost_estimate=TINY,
        name="down",
    )(me, clipped, pltpu.with_memory_space_constraint(weight, pltpu.HBM), *follow)


def spread_body(counts, slots_at, ids_ref, probs_ref, *refs):
    out_ref = refs[-1]
    tokens = ids_ref.shape[1]
    summed = []
    for count, slot in zip(counts, slots_at):
        mine, theirs = refs[:count], refs[count : 2 * count]
        refs = refs[2 * count :]
        rows = [(a[0].astype(F32) + b[slot].astype(F32)).astype(BF16) for a, b in zip(mine, theirs)]
        summed.append(jnp.concatenate(rows, axis=0))
    summed = jnp.concatenate(summed, axis=1)
    slots = slots_of(ids_ref)
    share = jnp.where(ids_ref[0:1, :] == 0, probs_ref[0:1, :], 0.0) + jnp.where(
        ids_ref[1:2, :] == 0, probs_ref[1:2, :], 0.0
    )
    blocks = tokens // LANES
    share = jnp.concatenate(
        [share[:, LANES * k : LANES * (k + 1)] for k in range(blocks)]
        + [jnp.zeros((LANES - blocks, LANES), F32)],
        axis=0,
    ).T
    slots = jnp.concatenate(
        [slots, jnp.zeros((LANES - slots.shape[0], LANES), F32)], axis=0
    ).T.astype(jnp.int32)
    at = iota((LANES, summed.shape[0]), 1)
    for k in range(blocks):
        hot = jnp.where(at == slots[:, k : k + 1], 1.0, 0.0).astype(BF16)
        rows = jnp.dot(hot, summed, preferred_element_type=F32)
        out_ref[LANES * k : LANES * (k + 1), :] = (rows * share[:, k : k + 1]).astype(BF16)


def spread(ids, probs, states, slots_at, first, features, out):
    tokens = ids.shape[1]
    fc = sum(state[0][0].shape[2] for state in states)
    args = [ids, probs]
    for state in states:
        args += [x[0] for x in state] + [x[1] for x in state]
    counts = [len(state) for state in states]
    used = len(args)
    in_specs = [pl.BlockSpec(x.shape, lambda i, d=x.ndim: (0,) * d) for x in args]
    earlier = [] if out is None else [out]
    return pl.pallas_call(
        lambda *refs: spread_body(counts, slots_at, *refs[:used], refs[-1]),
        grid=(1,),
        in_specs=in_specs + follows(earlier),
        out_specs=pl.BlockSpec((pl.Element(tokens), pl.Element(fc)), lambda i: (0, first * LANES)),
        out_shape=jax.ShapeDtypeStruct((tokens, features), BF16),
        input_output_aliases={used: 0} if earlier else {},
        compiler_params=params(24),
        cost_estimate=TINY,
        name="spread",
    )(*args, *earlier)


def follows(arrays):
    return [pl.BlockSpec(memory_space=pl.ANY)] * len(arrays)


def small(body, args, shapes, name, follow=()):
    vmem = pl.BlockSpec(memory_space=pltpu.VMEM)
    count = len(args)
    specs = [pl.BlockSpec(memory_space=pltpu.SMEM) if x.ndim == 1 else vmem for x in args]
    return pl.pallas_call(
        lambda *refs: body(refs[:count], refs[count + len(follow) :]),
        in_specs=specs + follows(follow),
        out_specs=[vmem] * len(shapes),
        out_shape=[jax.ShapeDtypeStruct(*x) for x in shapes],
        compiler_params=params(16),
        cost_estimate=TINY,
        name=name,
    )(*args, *follow)


def gather_near(own, orders):
    return {0: own} | {1 << bit: across(own, bit) for bit in orders[0]}


def cut_body(firsts, ins, outs):
    for h, at in enumerate(firsts):
        rows = outs[h].shape[0]
        outs[h][...] = ins[at][h * rows : (h + 1) * rows, :]
    for block, out in zip(ins, outs[2:]):
        out[...] = block[...]


def join_body(ins, outs):
    pieces = 2 * len(outs) // len(ins)
    for i in range(len(ins) // 2):
        whole = jnp.concatenate([ins[2 * i][...], ins[2 * i + 1][...]], axis=0)
        for k in range(pieces):
            out = outs[pieces * i + k]
            rows = out.shape[0]
            out[...] = whole[k * rows : (k + 1) * rows, :]


def cut(full, orders, follow, passed=False):
    rows, width = full[0].shape
    masks = [mask for mask in full if mask]
    firsts = [masks.index(1 << order[0]) for order in orders]
    shapes = [((rows // 2, width), BF16)] * 2 + [((rows, width), BF16)] * len(masks) * passed
    outs = small(
        lambda ins, outs: cut_body(firsts, ins, outs),
        [full[mask] for mask in masks],
        shapes,
        "cut",
        follow,
    )
    return outs[:2], full | dict(zip(masks, outs[2:]))


def gather_far(full, cuts, orders):
    half = full[0].shape[0] // len(orders)
    firsts = [1 << order[0] for order in orders]
    part = {}

    def get(mask, h):
        if (mask, h) in part:
            return part[mask, h]
        return cuts[h] if mask == firsts[h] else full[mask][h * half : (h + 1) * half]

    have = [[0, first] for first in firsts]
    for at in range(1, len(orders[0])):
        for h, order in enumerate(orders):
            bit = order[at]
            for mask in list(have[h]):
                there = mask | 1 << bit
                if there not in full:
                    part[there, h] = across(get(mask, h), bit)
                have[h].append(there)
    return part


def join(part, follow, pieces):
    masks = sorted({mask for mask, _ in part})
    halves = [part[mask, h] for mask in masks for h in range(2)]
    half, width = halves[0].shape
    shapes = [((2 * half // pieces, width), BF16)] * (pieces * len(masks))
    joined = small(join_body, halves, shapes, "join", follow)
    return {mask: joined[pieces * i : pieces * (i + 1)] for i, mask in enumerate(masks)}


def paired(pieces):
    return pieces | {
        mask | 1: [across(x, 0) for x in block] if isinstance(block, list) else across(block, 0)
        for mask, block in pieces.items()
    }


def turn_body(bits, scale, ins, outs):
    me_ref, ins = ins[0], ins[1:]
    count = len(bits)
    for h, bit in enumerate(bits):
        flip = (1 - 2 * ((me_ref[0] >> bit) & 1)).astype(F32)
        own = ins[2 * h][...].astype(F32)
        came = ins[2 * h + 1][...].astype(F32)
        value = came + own * flip
        if scale is not None:
            value = value * scale
            top = jnp.max(jnp.abs(own) + jnp.abs(came), axis=0, keepdims=True) * scale
            wide = top[:, :LANES]
            for k in range(1, top.shape[1] // LANES):
                wide = jnp.maximum(wide, top[:, k * LANES : (k + 1) * LANES])
            outs[count + h][...] = jnp.broadcast_to(wide, outs[count + h].shape)
        outs[h][...] = value.astype(BF16)


def turn(me, blocks, came, bits, follow=(), scale=None):
    args = [me] + [x for pair in zip(blocks, came) for x in pair]
    shapes = [(x.shape, BF16) for x in blocks]
    if scale is not None:
        shapes += [((8, LANES), F32)] * len(blocks)
    return small(
        lambda ins, outs: turn_body(bits, scale, ins, outs), args, shapes, "turn", follow
    )


def largest(top_in, tops, lasts):
    bits = range(lax.axis_size("tensor").bit_length() - 1)
    values = jnp.concatenate([top_in, *tops], axis=0)
    for bit in bits:
        if bit not in lasts:
            values = jnp.maximum(values, across(values, bit))
    n = top_in.shape[0]
    top_in, first, second = values[:n], values[n : 2 * n], values[2 * n :]
    if lasts[0] != lasts[1]:
        pair = jnp.concatenate([top_in, second], axis=0)
        came_first, came_pair = across(first, lasts[1]), across(pair, lasts[0])
        first = jnp.maximum(first, came_first)
        pair = jnp.maximum(pair, came_pair)
        top_in, second = pair[:n], pair[n:]
    values = jnp.concatenate([top_in, jnp.maximum(first, second)], axis=0)
    blocks = lax.axis_size("dp")
    far = 1
    while far < blocks:
        pairs = [(r, r ^ far) for r in range(blocks)]
        values = jnp.maximum(values, lax.ppermute(values, "dp", pairs))
        far *= 2
    return values


def on_device(tokens, expert_ids, gate_probs, gate_weight, up_weight, down_weight):
    count = lax.axis_size("tensor")
    bits = count.bit_length() - 1
    outer = list(range(1, bits))
    orders = [outer, outer[::-1]]
    me = lax.axis_index("tensor")
    me_arr = me.astype(jnp.int32).reshape(1)
    ids, probs = expert_ids.T, gate_probs.T
    rows = CAP // ROW_CHUNKS
    half = rows // 2
    scale = 1.0 / math.sqrt(gate_weight.shape[1] * count)
    stages = [[order[at] for order in orders] for at in range(len(outer))]
    early_bit = stages[-1][1]

    def send(blocks, bits):
        return [across(x, bit) for x, bit in zip(blocks, bits)]

    def start_turn(halves, follow=()):
        blocks = turn(me_arr, halves, send(halves, [0, 0]), [0, 0], follow)
        return blocks, send(blocks, stages[0])

    def go_on(blocks, came, at, follow=()):
        blocks = turn(me_arr, blocks, came, stages[at], follow)
        return blocks, send(blocks, stages[at + 1])

    def end_turn(blocks, came, follow=()):
        made = turn(me_arr, blocks, came, stages[-1], follow, scale)
        return made[: len(blocks)], made[len(blocks) :]

    own_a, top_a = pick_rows(ids, tokens, 0, rows, [me_arr])
    near_a = gather_near(own_a, orders)
    weights = (me_arr, gate_weight, up_weight)
    cuts_a, near_a = cut(near_a, orders, [])
    own_b, top_b = pick_rows(ids, tokens, rows, rows, cuts_a)
    top_in = jnp.maximum(top_a, top_b)
    top_in = jnp.maximum(top_in, across(top_in, early_bit))
    far_a = join(gather_far(near_a, cuts_a, orders), [own_b, top_in], 1)
    near_b = gather_near(own_b, orders)
    parts_a = paired(near_a | far_a)
    parts_a = [parts_a[mask] for mask in range(count)]
    first_a = expand(parts_a, rows, *weights)
    local_a = expand(parts_a, rows, *weights, *first_a)
    cuts_b, near_b = cut(near_b, orders, local_a, True)
    parts_b = paired(near_b)
    theirs_b = [block for mask, block in parts_b.items() if mask & 1]
    blocks_a, came_a = start_turn(local_a)
    far_b = join(gather_far(near_b, cuts_b, orders), list(blocks_a) + theirs_b, 3)
    parts_b |= paired(far_b)
    parts_b = [parts_b[mask] for mask in range(count)]
    first_b = expand(parts_b, rows, *weights, None, blocks_a)
    for at in range(len(outer) - 1):
        blocks_a, came_a = go_on(blocks_a, came_a, at, first_b)
    local_b = expand(parts_b, rows, *weights, *first_b, blocks_a)
    turned_a, rot_a = end_turn(blocks_a, came_a, local_b)
    blocks_b, came_b = start_turn(local_b, rot_a)
    for at in range(len(outer) - 1):
        blocks_b, came_b = go_on(blocks_b, came_b, at)
    turned_b, rot_b = end_turn(blocks_b, came_b)
    rotated = turned_a + turned_b

    peaks = largest(top_in, [jnp.maximum(x, y) for x, y in zip(rot_a, rot_b)], stages[-1])
    clipped = small(
        clip_body, [peaks, *rotated], [((CAP, gate_weight.shape[1]), BF16)], "clip"
    )[0]

    tops = pl.pallas_call(
        peaks_body,
        out_specs=pl.BlockSpec(memory_space=pltpu.SMEM),
        out_shape=jax.ShapeDtypeStruct((2,), F32),
        name="peaks",
    )(peaks)
    units = tokens.shape[1] // LANES
    sizes = chunks_of(units)
    firsts = [sum(sizes[:i]) for i in range(len(sizes))]
    total = len(sizes)
    products, begun, ended, out, last = {}, {}, {}, None, []
    for step, chunk in sums_order(total):
        if step == "product":
            products[chunk] = down(
                clipped, down_weight, me_arr, sizes[chunk], firsts[chunk], last
            )
            last = [products[chunk][1]]
        elif step == "begin":
            other, same = products[chunk]
            begun[chunk] = fold_cores(same, across(other, 0), stages[0], last)
            last = [keep for keep, _, _ in begun[chunk]]
        elif step == "finish":
            ahead = [c for c in products if c not in begun]
            passed = [products[c][0] for c in ahead]
            held = chunk == 0 and total > 2
            stacked = [x for _, x, _ in ended[0]] if chunk == 1 and total > 2 else []
            ended[chunk], passed = finish(
                begun[chunk], stages, last, passed, stacked, not held
            )
            if stacked:
                ended[0] = [
                    (keep, both, left)
                    for (keep, _, left), (_, both, _) in zip(ended[0], ended[1])
                ]
            for c, other in zip(ahead, passed):
                products[c] = (other, products[c][1])
            last = [keep for keep, _, _ in ended[chunk]]
        else:
            chunks = [0, 1] if chunk == 0 and total > 2 else [chunk]
            slots_at = [0 if c == 0 else ended[c][0][1].shape[0] - 1 for c in chunks]
            out = spread(
                ids,
                probs,
                [ended[c] for c in chunks],
                slots_at,
                firsts[chunk],
                tokens.shape[1],
                out,
            )
    return out, tops


def chunks_of(units):
    return [2] * (units // 2) + [1] * (units % 2)


def sums_order(total):
    order = [("product", 0)]
    for chunk in range(total):
        if chunk + 1 < total:
            order.append(("product", chunk + 1))
        order.append(("begin", chunk))
        if chunk > 0:
            order.append(("finish", chunk - 1))
    order.append(("finish", total - 1))
    return order + [("spread", c) for c in range(total) if c != 1 or total < 3]


def peaks_body(values_ref, out_ref):
    out_ref[0] = jnp.max(values_ref[:8, :])
    out_ref[1] = jnp.max(values_ref[8:, :])


def fold_body(plan, passed, ins, outs):
    for i in range(passed):
        outs[len(plan) + i][...] = ins[len(ins) - passed + i][...]
    for out, (slots, low) in zip(outs, plan):
        rows = out.shape[1]
        for slot, terms in enumerate(slots):
            total = 0.0
            for at, i in terms:
                total = total + ins[at][i, low : low + rows, :].astype(F32)
            out[slot] = total.astype(BF16)


def fold(args, terms, masks, lows, rows, bits, follow, passed=(), stacked=(), sent=True):
    plan, shapes, lefts = [], [], []
    width = args[0].shape[2]
    for h, bit in enumerate(bits):
        for side in (0, 1):
            chosen = [m for m in masks[h] if m >> bit & 1 == side]
            slots = [terms[h][m] for m in chosen]
            if side and stacked:
                slots = [((len(args) + h, i),) for i in range(stacked[h].shape[0])] + slots
            plan.append((slots, lows[h]))
            shapes.append(((len(slots), rows, width), BF16))
        lefts.append([m for m in masks[h] if not m >> bit & 1])
    shapes += [(x.shape, x.dtype) for x in passed]
    made = small(
        lambda ins, outs: fold_body(plan, len(passed), ins, outs),
        [*args, *stacked, *passed],
        shapes,
        "fold",
        follow,
    )
    state = [
        (made[2 * h], across(made[2 * h + 1], bit) if sent else made[2 * h + 1], lefts[h])
        for h, bit in enumerate(bits)
    ]
    return state, made[len(plan) :]


def fold_cores(same, came, bits, follow):
    half = same.shape[1] // 2
    masks = [2 * i for i in range(same.shape[0])]
    terms = {m: ((0, i), (1, i)) for i, m in enumerate(masks)}
    return fold([same, came], [terms] * 2, [masks] * 2, [0, half], half, bits, follow)[0]


def finish(state, stages, follow, passed=(), stacked=(), sent=True):
    for bits in stages[1:]:
        args = [x for keep, recv, _ in state for x in (keep, recv)]
        masks = [left for _, _, left in state]
        terms = [
            {m: ((2 * h, i), (2 * h + 1, i)) for i, m in enumerate(left)}
            for h, left in enumerate(masks)
        ]
        last = bits is stages[-1]
        state, passed = fold(
            args,
            terms,
            masks,
            [0, 0],
            args[0].shape[1],
            bits,
            follow,
            passed,
            stacked if last else (),
            sent or not last,
        )
    return state, passed


def solution(mesh):
    in_specs = (
        P("dp", "tensor"),
        P("dp", None),
        P("dp", None),
        P(None, "tensor"),
        P(None, "tensor"),
        P("tensor", None),
    )
    out_specs = (P("dp", "tensor"), P())
    return jax.shard_map(
        on_device, mesh=mesh, in_specs=in_specs, out_specs=out_specs, check_vma=False
    )
```

```python
import math

import jax
import jax.numpy as jnp
from jax import lax
from jax.experimental import pallas as pl
from jax.experimental.pallas import tpu as pltpu
from jax.sharding import PartitionSpec as P

CAP = 768
CLIP_SHARE = 0.25
LANES = 128
ROW_CHUNKS = 2
BF16 = jnp.bfloat16
F32 = jnp.float32
MIB = 1 << 20
EXPAND_MIB = 24
AHEAD = 3


def params(mib):
    return pltpu.CompilerParams(vmem_limit_bytes=mib * MIB)


TINY = pl.CostEstimate(flops=1, bytes_accessed=1, transcendentals=0)


def across(block, bit):
    count = lax.axis_size("tensor")
    return lax.ppermute(block, "tensor", [(r, r ^ 1 << bit) for r in range(count)])


def iota(shape, dim):
    return lax.broadcasted_iota(jnp.int32, shape, dim)


def slots_of(ids_ref):
    tokens = ids_ref.shape[1]
    rows = tokens // LANES
    padded = (rows + 15) // 16 * 16
    hit = jnp.where((ids_ref[0:1, :] == 0) | (ids_ref[1:2, :] == 0), 1.0, 0.0)
    grid = jnp.concatenate(
        [hit[:, LANES * k : LANES * (k + 1)] for k in range(rows)]
        + [jnp.zeros((padded - rows, LANES), F32)],
        axis=0,
    )
    flat = grid.astype(BF16)
    upto = (iota((LANES, LANES), 0) <= iota((LANES, LANES), 1)).astype(F32).astype(BF16)
    before = (iota((padded, padded), 1) < iota((padded, padded), 0)).astype(F32).astype(BF16)
    within = jnp.dot(flat, upto, preferred_element_type=F32)
    offset = jnp.sum(jnp.dot(before, flat, preferred_element_type=F32), axis=1, keepdims=True)
    return jnp.where(grid > 0.0, within + offset - 1.0, -1.0)


def pick_body(first, ids_hbm, tokens_hbm, *refs):
    picked_ref, peak_ref, ids_ref, tokens_ref, loaded = refs[-5:]
    rows = picked_ref.shape[0]
    count = tokens_ref.shape[0]
    pieces = loaded.shape[0] - 1
    step = count // pieces
    ids_copy = pltpu.make_async_copy(ids_hbm, ids_ref, loaded.at[pieces])
    ids_copy.start()
    copies = [
        pltpu.make_async_copy(
            tokens_hbm.at[pl.ds(i * step, step), :],
            tokens_ref.at[pl.ds(i * step, step), :],
            loaded.at[i],
        )
        for i in range(pieces)
    ]
    for copy in copies:
        copy.start()
    ids_copy.wait()
    slots = slots_of(ids_ref).astype(jnp.int32)
    wanted = iota((rows, LANES), 0) + first
    picked = jnp.zeros(picked_ref.shape, F32)
    for i, copy in enumerate(copies):
        hot = jnp.concatenate(
            [
                jnp.where(wanted == slots[k : k + 1, :], 1.0, 0.0).astype(BF16)
                for k in range(i * step // LANES, (i + 1) * step // LANES)
            ],
            axis=1,
        )
        copy.wait()
        picked += jnp.dot(
            hot, tokens_ref[i * step : (i + 1) * step, :], preferred_element_type=F32
        )
    picked_ref[...] = picked.astype(BF16)
    peak_ref[...] = jnp.broadcast_to(jnp.max(jnp.abs(picked)), peak_ref.shape)


def pick_rows(ids, tokens, first, rows, follow=()):
    count, width = tokens.shape
    blocks = count // LANES
    pieces = math.gcd(blocks, 4)
    in_hbm = [pltpu.with_memory_space_constraint(x, pltpu.HBM) for x in (ids, tokens)]
    return pl.pallas_call(
        lambda *refs: pick_body(first, *refs),
        out_shape=(
            jax.ShapeDtypeStruct((rows, width), BF16),
            jax.ShapeDtypeStruct((8, LANES), F32),
        ),
        in_specs=[pl.BlockSpec(memory_space=pltpu.HBM)] * 2 + follows(follow),
        out_specs=[pl.BlockSpec(memory_space=pltpu.VMEM)] * 2,
        scratch_shapes=[
            pltpu.VMEM(ids.shape, ids.dtype),
            pltpu.VMEM(tokens.shape, tokens.dtype),
            pltpu.SemaphoreType.DMA((pieces + 1,)),
        ],
        compiler_params=params(16),
        cost_estimate=TINY,
        name="pick_rows",
    )(*in_hbm, *follow)


def signs(size):
    common = iota((size, size), 0) & iota((size, size), 1)
    shift = 1
    while shift < size.bit_length():
        shift *= 2
    while shift > 1:
        shift //= 2
        common = common ^ (common >> shift)
    return (1 - 2 * (common & 1)).astype(F32).astype(BF16)


def whole(pieces):
    if len(pieces) == 1:
        return pieces[0][...]
    return jnp.concatenate([piece[...] for piece in pieces], axis=0)


def expand_body(first, cuts, last, me_ref, *refs):
    count = len(cuts)
    parts = []
    for pieces in cuts:
        parts.append(refs[:pieces])
        refs = refs[pieces:]
    before_ref = None
    if last:
        before_ref, refs = refs[0], refs[1:]
    gate_hbm, up_hbm, *outs, total, held, loaded = refs
    width = parts[0][0].shape[1]
    columns = total.shape[2]
    tile = min(256, columns)

    def load(mask):
        rows = pl.ds(pl.multiple_of((me_ref[0] ^ mask) * width, LANES), width)
        return [
            pltpu.make_async_copy(
                weight.at[rows, pl.ds(first, columns)], held.at[mask, at], loaded.at[mask, at]
            )
            for at, weight in enumerate((gate_hbm, up_hbm))
        ]

    loads = [load(mask) for mask in range(count)]
    for copies in loads[:AHEAD]:
        for copy in copies:
            copy.start()
    table = signs(tile)
    for mask, pieces in enumerate(parts):
        for copies in loads[mask + AHEAD : mask + AHEAD + 1]:
            for copy in copies:
                copy.start()
        for at in range(2):
            loads[mask][at].wait()
            term = jnp.dot(whole(pieces), held[mask, at], preferred_element_type=F32)
            if mask == 0:
                total[at] = term
            else:
                total[at] += term
    values = []
    for i in range(columns // tile):
        gate = total[0, :, i * tile : (i + 1) * tile]
        up = total[1, :, i * tile : (i + 1) * tile]
        hidden = (gate * (1.0 / (1.0 + jnp.exp(-gate))) * up).astype(BF16)
        values.append(jnp.dot(hidden, table, preferred_element_type=F32))
        if not last:
            outs[0][i] = values[i]
    if not last:
        return
    values = [before_ref[i] for i in range(before_ref.shape[0])] + values
    steps = len(values)
    gap = 1
    while gap < steps:
        values = [
            values[i] + values[i ^ gap] if not i & gap else values[i ^ gap] - values[i]
            for i in range(steps)
        ]
        gap *= 2
    for i in range(steps):
        low = 0
        for out in outs:
            rows = out.shape[0]
            out[:, i * tile : (i + 1) * tile] = values[i][low : low + rows].astype(BF16)
            low += rows


def expand(parts, rows, me, gate_weight, up_weight, before=None, follow=()):
    depth, width = gate_weight.shape
    last = before is not None
    columns = width // 2
    first = columns if last else 0
    tile = min(256, columns)
    parts = [x if isinstance(x, (list, tuple)) else [x] for x in parts]
    cuts = [len(x) for x in parts]
    parts = [x for pieces in parts for x in pieces]
    count = len(cuts)
    vmem = pl.BlockSpec(memory_space=pltpu.VMEM)
    in_hbm = [pltpu.with_memory_space_constraint(x, pltpu.HBM) for x in (gate_weight, up_weight)]
    args = [me, *parts] + ([before] if last else [])
    used = len(args) + 2
    if last:
        out_shape = [jax.ShapeDtypeStruct((rows // 2, width), BF16)] * 2
    else:
        out_shape = [jax.ShapeDtypeStruct((columns // tile, rows, tile), F32)]
    return pl.pallas_call(
        lambda *refs: expand_body(first, cuts, last, *refs[:used], *refs[used + len(follow) :]),
        in_specs=[pl.BlockSpec(memory_space=pltpu.SMEM)]
        + [vmem] * (used - 3)
        + [pl.BlockSpec(memory_space=pltpu.HBM)] * 2
        + follows(follow),
        out_specs=[vmem] * len(out_shape),
        out_shape=out_shape,
        scratch_shapes=[
            pltpu.VMEM((2, rows, columns), F32),
            pltpu.VMEM((count, 2, depth // count, columns), BF16),
            pltpu.SemaphoreType.DMA((count, 2)),
        ],
        compiler_params=params(EXPAND_MIB),
        cost_estimate=TINY,
        name="expand_last" if last else "expand_first",
    )(*args, *in_hbm, *follow)


def multiply_body(masks, cuts, resumed, last, me_ref, *refs):
    count = len(masks)
    parts = []
    for pieces in cuts:
        parts.append(refs[:pieces])
        refs = refs[pieces:]
    before_ref = None
    if resumed:
        before_ref, refs = refs[0], refs[1:]
    gate_hbm, up_hbm, *outs, held, loaded = refs
    if last:
        *outs, total = outs
    else:
        total = outs[0]
    features = parts[0][0].shape[1]
    width = total.shape[2]

    def load(i):
        rows = pl.ds(pl.multiple_of((me_ref[0] ^ masks[i]) * features, LANES), features)
        return [
            pltpu.make_async_copy(weight.at[rows, :], held.at[i, at], loaded.at[i, at])
            for at, weight in enumerate((gate_hbm, up_hbm))
        ]

    loads = [load(i) for i in range(count)]
    for copies in loads[:AHEAD]:
        for copy in copies:
            copy.start()
    columns = min(512, width)
    for i, pieces in enumerate(parts):
        for copies in loads[i + AHEAD : i + AHEAD + 1]:
            for copy in copies:
                copy.start()
        for at in range(2):
            loads[i][at].wait()
            for low in range(0, width, columns):
                span = slice(low, low + columns)
                term = jnp.dot(whole(pieces), held[i, at, :, span], preferred_element_type=F32)
                if i > 0:
                    term += total[at, :, span]
                elif resumed:
                    term += before_ref[at, :, span]
                total[at, :, span] = term
    if not last:
        return
    tile = min(256, width)
    steps = width // tile
    table = signs(tile)
    values = []
    for i in range(steps):
        gate = total[0, :, i * tile : (i + 1) * tile]
        up = total[1, :, i * tile : (i + 1) * tile]
        hidden = (gate * (1.0 / (1.0 + jnp.exp(-gate))) * up).astype(BF16)
        values.append(jnp.dot(hidden, table, preferred_element_type=F32))
    gap = 1
    while gap < steps:
        values = [
            values[i] + values[i ^ gap] if not i & gap else values[i ^ gap] - values[i]
            for i in range(steps)
        ]
        gap *= 2
    for i in range(steps):
        low = 0
        for out in outs:
            rows = out.shape[0]
            out[:, i * tile : (i + 1) * tile] = values[i][low : low + rows].astype(BF16)
            low += rows


def multiply(parts, me, gate_weight, up_weight, before=None, last=False, follow=()):
    masks = sorted(parts)
    depth, width = gate_weight.shape
    count = len(masks)
    pieces = [x if isinstance(x, (list, tuple)) else [x] for x in (parts[m] for m in masks)]
    cuts = [len(x) for x in pieces]
    rows, features = sum(x.shape[0] for x in pieces[0]), pieces[0][0].shape[1]
    vmem = pl.BlockSpec(memory_space=pltpu.VMEM)
    resumed = before is not None
    in_hbm = [pltpu.with_memory_space_constraint(x, pltpu.HBM) for x in (gate_weight, up_weight)]
    args = [me, *[x for group in pieces for x in group]] + ([before] if resumed else [])
    used = len(args) + 2
    scratch = [
        pltpu.VMEM((count, 2, features, width), BF16),
        pltpu.SemaphoreType.DMA((count, 2)),
    ]
    if last:
        out_shape = [jax.ShapeDtypeStruct((rows // 2, width), BF16)] * 2
        scratch.insert(0, pltpu.VMEM((2, rows, width), F32))
    else:
        out_shape = [jax.ShapeDtypeStruct((2, rows, width), F32)]
    made = pl.pallas_call(
        lambda *refs: multiply_body(
            masks, cuts, resumed, last, *refs[:used], *refs[used + len(follow) :]
        ),
        in_specs=[pl.BlockSpec(memory_space=pltpu.SMEM)]
        + [vmem] * (used - 3)
        + [pl.BlockSpec(memory_space=pltpu.HBM)] * 2
        + follows(follow),
        out_specs=[vmem] * len(out_shape),
        out_shape=out_shape,
        scratch_shapes=scratch,
        compiler_params=params(EXPAND_MIB + 8),
        cost_estimate=TINY,
        name="multiply_last" if last else "multiply",
    )(*args, *in_hbm, *follow)
    return made if last else made[0]


def clip_body(ins, outs):
    level = CLIP_SHARE * jnp.max(ins[0][8:, :])
    low = 0
    for part in ins[1:]:
        rows = part.shape[0]
        outs[0][low : low + rows, :] = jnp.clip(part[...].astype(F32), -level, level).astype(BF16)
        low += rows


def down_body(first, me_ref, clipped_ref, weight_hbm, *refs):
    owners = lax.axis_size("tensor")
    half = owners // 2
    other_ref, same_ref, held, loaded = refs[-4:]
    fc = same_ref.shape[2]
    stride = weight_hbm.shape[1] // owners
    masks = [2 * i + 1 for i in range(half)] + [2 * i for i in range(half)]

    def load(i):
        column = pl.multiple_of((me_ref[0] ^ masks[i]) * stride + first, LANES)
        return pltpu.make_async_copy(
            weight_hbm.at[:, pl.ds(column, fc)],
            held.at[i // 2, :, pl.ds(i % 2 * fc, fc)],
            loaded.at[i],
        )

    loads = [load(i) for i in range(owners)]
    for copy in loads[: 2 * AHEAD]:
        copy.start()
    for pair in range(half):
        for copy in loads[2 * (pair + AHEAD) : 2 * (pair + AHEAD + 1)]:
            copy.start()
        for copy in loads[2 * pair : 2 * pair + 2]:
            copy.wait()
        terms = jnp.dot(clipped_ref[...], held[pair], preferred_element_type=F32).astype(BF16)
        for side in range(2):
            i = 2 * pair + side
            term = terms[:, side * fc : (side + 1) * fc]
            if i < half:
                other_ref[i] = term
            else:
                same_ref[i - half] = term


def down(clipped, weight, me, units, first, follow=()):
    depth = weight.shape[0]
    owners = lax.axis_size("tensor")
    half = owners // 2
    rows = clipped.shape[0]
    fc = units * LANES
    vmem = pl.BlockSpec(memory_space=pltpu.VMEM)
    shape = jax.ShapeDtypeStruct((half, rows, fc), BF16)
    return pl.pallas_call(
        lambda *refs: down_body(first * LANES, *refs),
        in_specs=[
            pl.BlockSpec(memory_space=pltpu.SMEM),
            vmem,
            pl.BlockSpec(memory_space=pltpu.HBM),
        ]
        + follows(follow),
        out_specs=[vmem] * 2,
        out_shape=[shape] * 2,
        scratch_shapes=[
            pltpu.VMEM((half, depth, 2 * fc), BF16),
            pltpu.SemaphoreType.DMA((owners,)),
        ],
        compiler_params=params(16),
        cost_estimate=TINY,
        name="down",
    )(me, clipped, pltpu.with_memory_space_constraint(weight, pltpu.HBM), *follow)


def spread_body(counts, slots_at, ids_ref, probs_ref, *refs):
    out_ref = refs[-1]
    tokens = ids_ref.shape[1]
    summed = []
    for count, slot in zip(counts, slots_at):
        mine, theirs = refs[:count], refs[count : 2 * count]
        refs = refs[2 * count :]
        rows = [(a[0].astype(F32) + b[slot].astype(F32)).astype(BF16) for a, b in zip(mine, theirs)]
        summed.append(jnp.concatenate(rows, axis=0))
    summed = jnp.concatenate(summed, axis=1)
    slots = slots_of(ids_ref)
    share = jnp.where(ids_ref[0:1, :] == 0, probs_ref[0:1, :], 0.0) + jnp.where(
        ids_ref[1:2, :] == 0, probs_ref[1:2, :], 0.0
    )
    blocks = tokens // LANES
    share = jnp.concatenate(
        [share[:, LANES * k : LANES * (k + 1)] for k in range(blocks)]
        + [jnp.zeros((LANES - blocks, LANES), F32)],
        axis=0,
    ).T
    slots = jnp.concatenate(
        [slots, jnp.zeros((LANES - slots.shape[0], LANES), F32)], axis=0
    ).T.astype(jnp.int32)
    at = iota((LANES, summed.shape[0]), 1)
    for k in range(blocks):
        hot = jnp.where(at == slots[:, k : k + 1], 1.0, 0.0).astype(BF16)
        rows = jnp.dot(hot, summed, preferred_element_type=F32)
        out_ref[LANES * k : LANES * (k + 1), :] = (rows * share[:, k : k + 1]).astype(BF16)


def spread(ids, probs, states, slots_at, first, features, out):
    tokens = ids.shape[1]
    fc = sum(state[0][0].shape[2] for state in states)
    args = [ids, probs]
    for state in states:
        args += [x[0] for x in state] + [x[1] for x in state]
    counts = [len(state) for state in states]
    used = len(args)
    in_specs = [pl.BlockSpec(x.shape, lambda i, d=x.ndim: (0,) * d) for x in args]
    earlier = [] if out is None else [out]
    return pl.pallas_call(
        lambda *refs: spread_body(counts, slots_at, *refs[:used], refs[-1]),
        grid=(1,),
        in_specs=in_specs + follows(earlier),
        out_specs=pl.BlockSpec((pl.Element(tokens), pl.Element(fc)), lambda i: (0, first * LANES)),
        out_shape=jax.ShapeDtypeStruct((tokens, features), BF16),
        input_output_aliases={used: 0} if earlier else {},
        compiler_params=params(24),
        cost_estimate=TINY,
        name="spread",
    )(*args, *earlier)


def follows(arrays):
    return [pl.BlockSpec(memory_space=pl.ANY)] * len(arrays)


def small(body, args, shapes, name, follow=()):
    vmem = pl.BlockSpec(memory_space=pltpu.VMEM)
    count = len(args)
    specs = [pl.BlockSpec(memory_space=pltpu.SMEM) if x.ndim == 1 else vmem for x in args]
    return pl.pallas_call(
        lambda *refs: body(refs[:count], refs[count + len(follow) :]),
        in_specs=specs + follows(follow),
        out_specs=[vmem] * len(shapes),
        out_shape=[jax.ShapeDtypeStruct(*x) for x in shapes],
        compiler_params=params(16),
        cost_estimate=TINY,
        name=name,
    )(*args, *follow)


def gather_near(own, orders):
    return {0: own} | {1 << bit: across(own, bit) for bit in orders[0]}


def cut_body(firsts, ins, outs):
    for h, at in enumerate(firsts):
        rows = outs[h].shape[0]
        outs[h][...] = ins[at][h * rows : (h + 1) * rows, :]
    for block, out in zip(ins, outs[2:]):
        out[...] = block[...]


def join_body(ins, outs):
    pieces = 2 * len(outs) // len(ins)
    for i in range(len(ins) // 2):
        whole = jnp.concatenate([ins[2 * i][...], ins[2 * i + 1][...]], axis=0)
        for k in range(pieces):
            out = outs[pieces * i + k]
            rows = out.shape[0]
            out[...] = whole[k * rows : (k + 1) * rows, :]


def cut(full, orders, follow, passed=False):
    rows, width = full[0].shape
    masks = [mask for mask in full if mask]
    firsts = [masks.index(1 << order[0]) for order in orders]
    shapes = [((rows // 2, width), BF16)] * 2 + [((rows, width), BF16)] * len(masks) * passed
    outs = small(
        lambda ins, outs: cut_body(firsts, ins, outs),
        [full[mask] for mask in masks],
        shapes,
        "cut",
        follow,
    )
    return outs[:2], full | dict(zip(masks, outs[2:]))


def gather_far(full, cuts, orders):
    half = full[0].shape[0] // len(orders)
    firsts = [1 << order[0] for order in orders]
    part = {}

    def get(mask, h):
        if (mask, h) in part:
            return part[mask, h]
        return cuts[h] if mask == firsts[h] else full[mask][h * half : (h + 1) * half]

    have = [[0, first] for first in firsts]
    for at in range(1, len(orders[0])):
        for h, order in enumerate(orders):
            bit = order[at]
            for mask in list(have[h]):
                there = mask | 1 << bit
                if there not in full:
                    part[there, h] = across(get(mask, h), bit)
                have[h].append(there)
    return part


def join(part, follow, pieces):
    masks = sorted({mask for mask, _ in part})
    halves = [part[mask, h] for mask in masks for h in range(2)]
    half, width = halves[0].shape
    shapes = [((2 * half // pieces, width), BF16)] * (pieces * len(masks))
    joined = small(join_body, halves, shapes, "join", follow)
    return {mask: joined[pieces * i : pieces * (i + 1)] for i, mask in enumerate(masks)}


def paired(pieces):
    return pieces | {
        mask | 1: [across(x, 0) for x in block] if isinstance(block, list) else across(block, 0)
        for mask, block in pieces.items()
    }


def turn_body(bits, scale, ins, outs):
    me_ref, ins = ins[0], ins[1:]
    count = len(bits)
    for h, bit in enumerate(bits):
        flip = (1 - 2 * ((me_ref[0] >> bit) & 1)).astype(F32)
        own = ins[2 * h][...].astype(F32)
        came = ins[2 * h + 1][...].astype(F32)
        value = came + own * flip
        if scale is not None:
            value = value * scale
            top = jnp.max(jnp.abs(own) + jnp.abs(came), axis=0, keepdims=True) * scale
            wide = top[:, :LANES]
            for k in range(1, top.shape[1] // LANES):
                wide = jnp.maximum(wide, top[:, k * LANES : (k + 1) * LANES])
            outs[count + h][...] = jnp.broadcast_to(wide, outs[count + h].shape)
        outs[h][...] = value.astype(BF16)


def turn(me, blocks, came, bits, follow=(), scale=None):
    args = [me] + [x for pair in zip(blocks, came) for x in pair]
    shapes = [(x.shape, BF16) for x in blocks]
    if scale is not None:
        shapes += [((8, LANES), F32)] * len(blocks)
    return small(
        lambda ins, outs: turn_body(bits, scale, ins, outs), args, shapes, "turn", follow
    )


def largest(top_in, tops, lasts):
    bits = range(lax.axis_size("tensor").bit_length() - 1)
    values = jnp.concatenate([top_in, *tops], axis=0)
    for bit in bits:
        if bit not in lasts:
            values = jnp.maximum(values, across(values, bit))
    n = top_in.shape[0]
    top_in, first, second = values[:n], values[n : 2 * n], values[2 * n :]
    if lasts[0] != lasts[1]:
        pair = jnp.concatenate([top_in, second], axis=0)
        came_first, came_pair = across(first, lasts[1]), across(pair, lasts[0])
        first = jnp.maximum(first, came_first)
        pair = jnp.maximum(pair, came_pair)
        top_in, second = pair[:n], pair[n:]
    values = jnp.concatenate([top_in, jnp.maximum(first, second)], axis=0)
    blocks = lax.axis_size("dp")
    far = 1
    while far < blocks:
        pairs = [(r, r ^ far) for r in range(blocks)]
        values = jnp.maximum(values, lax.ppermute(values, "dp", pairs))
        far *= 2
    return values


def on_device(tokens, expert_ids, gate_probs, gate_weight, up_weight, down_weight):
    count = lax.axis_size("tensor")
    bits = count.bit_length() - 1
    outer = list(range(1, bits))
    orders = [outer, outer[::-1]]
    me = lax.axis_index("tensor")
    me_arr = me.astype(jnp.int32).reshape(1)
    ids, probs = expert_ids.T, gate_probs.T
    rows = CAP // ROW_CHUNKS
    half = rows // 2
    scale = 1.0 / math.sqrt(gate_weight.shape[1] * count)
    stages = [[order[at] for order in orders] for at in range(len(outer))]
    early_bit = stages[-1][1]

    def send(blocks, bits):
        return [across(x, bit) for x, bit in zip(blocks, bits)]

    def start_turn(halves, follow=()):
        blocks = turn(me_arr, halves, send(halves, [0, 0]), [0, 0], follow)
        return blocks, send(blocks, stages[0])

    def go_on(blocks, came, at, follow=()):
        blocks = turn(me_arr, blocks, came, stages[at], follow)
        return blocks, send(blocks, stages[at + 1])

    def end_turn(blocks, came, follow=()):
        made = turn(me_arr, blocks, came, stages[-1], follow, scale)
        return made[: len(blocks)], made[len(blocks) :]

    own_a, top_a = pick_rows(ids, tokens, 0, rows, [me_arr])
    near_a = gather_near(own_a, orders)
    weights = (me_arr, gate_weight, up_weight)
    cuts_a, near_a = cut(near_a, orders, [])
    own_b, top_b = pick_rows(ids, tokens, rows, rows, cuts_a)
    top_in = jnp.maximum(top_a, top_b)
    top_in = jnp.maximum(top_in, across(top_in, early_bit))
    far_a = join(gather_far(near_a, cuts_a, orders), [own_b, top_in], 1)
    near_b = gather_near(own_b, orders)
    parts_a = paired(near_a | far_a)
    parts_a = [parts_a[mask] for mask in range(count)]
    first_a = expand(parts_a, rows, *weights)
    local_a = expand(parts_a, rows, *weights, *first_a)
    cuts_b, near_b = cut(near_b, orders, local_a, True)
    parts_b = paired(near_b)
    theirs_b = [block for mask, block in parts_b.items() if mask & 1]
    blocks_a, came_a = start_turn(local_a, theirs_b)
    total_b = multiply(parts_b, *weights, follow=blocks_a)
    far_b = join(gather_far(near_b, cuts_b, orders), [total_b], 3)
    for at in range(len(outer) - 1):
        blocks_a, came_a = go_on(blocks_a, came_a, at, [total_b])
    local_b = multiply(paired(far_b), *weights, total_b, True, blocks_a)
    turned_a, rot_a = end_turn(blocks_a, came_a, local_b)
    blocks_b, came_b = start_turn(local_b, rot_a)
    for at in range(len(outer) - 1):
        blocks_b, came_b = go_on(blocks_b, came_b, at)
    turned_b, rot_b = end_turn(blocks_b, came_b)
    rotated = turned_a + turned_b

    peaks = largest(top_in, [jnp.maximum(x, y) for x, y in zip(rot_a, rot_b)], stages[-1])
    clipped = small(
        clip_body, [peaks, *rotated], [((CAP, gate_weight.shape[1]), BF16)], "clip"
    )[0]

    tops = pl.pallas_call(
        peaks_body,
        out_specs=pl.BlockSpec(memory_space=pltpu.SMEM),
        out_shape=jax.ShapeDtypeStruct((2,), F32),
        name="peaks",
    )(peaks)
    units = tokens.shape[1] // LANES
    sizes = chunks_of(units)
    firsts = [sum(sizes[:i]) for i in range(len(sizes))]
    total = len(sizes)
    products, begun, ended, out, last = {}, {}, {}, None, []
    for step, chunk in sums_order(total):
        if step == "product":
            products[chunk] = down(
                clipped, down_weight, me_arr, sizes[chunk], firsts[chunk], last
            )
            last = [products[chunk][1]]
        elif step == "begin":
            other, same = products[chunk]
            begun[chunk] = fold_cores(same, across(other, 0), stages[0], last)
            last = [keep for keep, _, _ in begun[chunk]]
        elif step == "finish":
            ahead = [c for c in products if c not in begun]
            passed = [products[c][0] for c in ahead]
            held = chunk == 0 and total > 2
            stacked = [x for _, x, _ in ended[0]] if chunk == 1 and total > 2 else []
            ended[chunk], passed = finish(
                begun[chunk], stages, last, passed, stacked, not held
            )
            if stacked:
                ended[0] = [
                    (keep, both, left)
                    for (keep, _, left), (_, both, _) in zip(ended[0], ended[1])
                ]
            for c, other in zip(ahead, passed):
                products[c] = (other, products[c][1])
            last = [keep for keep, _, _ in ended[chunk]]
        else:
            chunks = [0, 1] if chunk == 0 and total > 2 else [chunk]
            slots_at = [0 if c == 0 else ended[c][0][1].shape[0] - 1 for c in chunks]
            out = spread(
                ids,
                probs,
                [ended[c] for c in chunks],
                slots_at,
                firsts[chunk],
                tokens.shape[1],
                out,
            )
    return out, tops


def chunks_of(units):
    return [2] * (units // 2) + [1] * (units % 2)


def sums_order(total):
    order = [("product", 0)]
    for chunk in range(total):
        if chunk + 1 < total:
            order.append(("product", chunk + 1))
        order.append(("begin", chunk))
        if chunk > 0:
            order.append(("finish", chunk - 1))
    order.append(("finish", total - 1))
    return order + [("spread", c) for c in range(total) if c != 1 or total < 3]


def peaks_body(values_ref, out_ref):
    out_ref[0] = jnp.max(values_ref[:8, :])
    out_ref[1] = jnp.max(values_ref[8:, :])


def fold_body(plan, passed, ins, outs):
    for i in range(passed):
        outs[len(plan) + i][...] = ins[len(ins) - passed + i][...]
    for out, (slots, low) in zip(outs, plan):
        rows = out.shape[1]
        for slot, terms in enumerate(slots):
            total = 0.0
            for at, i in terms:
                total = total + ins[at][i, low : low + rows, :].astype(F32)
            out[slot] = total.astype(BF16)


def fold(args, terms, masks, lows, rows, bits, follow, passed=(), stacked=(), sent=True):
    plan, shapes, lefts = [], [], []
    width = args[0].shape[2]
    for h, bit in enumerate(bits):
        for side in (0, 1):
            chosen = [m for m in masks[h] if m >> bit & 1 == side]
            slots = [terms[h][m] for m in chosen]
            if side and stacked:
                slots = [((len(args) + h, i),) for i in range(stacked[h].shape[0])] + slots
            plan.append((slots, lows[h]))
            shapes.append(((len(slots), rows, width), BF16))
        lefts.append([m for m in masks[h] if not m >> bit & 1])
    shapes += [(x.shape, x.dtype) for x in passed]
    made = small(
        lambda ins, outs: fold_body(plan, len(passed), ins, outs),
        [*args, *stacked, *passed],
        shapes,
        "fold",
        follow,
    )
    state = [
        (made[2 * h], across(made[2 * h + 1], bit) if sent else made[2 * h + 1], lefts[h])
        for h, bit in enumerate(bits)
    ]
    return state, made[len(plan) :]


def fold_cores(same, came, bits, follow):
    half = same.shape[1] // 2
    masks = [2 * i for i in range(same.shape[0])]
    terms = {m: ((0, i), (1, i)) for i, m in enumerate(masks)}
    return fold([same, came], [terms] * 2, [masks] * 2, [0, half], half, bits, follow)[0]


def finish(state, stages, follow, passed=(), stacked=(), sent=True):
    for bits in stages[1:]:
        args = [x for keep, recv, _ in state for x in (keep, recv)]
        masks = [left for _, _, left in state]
        terms = [
            {m: ((2 * h, i), (2 * h + 1, i)) for i, m in enumerate(left)}
            for h, left in enumerate(masks)
        ]
        last = bits is stages[-1]
        state, passed = fold(
            args,
            terms,
            masks,
            [0, 0],
            args[0].shape[1],
            bits,
            follow,
            passed,
            stacked if last else (),
            sent or not last,
        )
    return state, passed


def solution(mesh):
    in_specs = (
        P("dp", "tensor"),
        P("dp", None),
        P("dp", None),
        P(None, "tensor"),
        P(None, "tensor"),
        P("tensor", None),
    )
    out_specs = (P("dp", "tensor"), P())
    return jax.shard_map(
        on_device, mesh=mesh, in_specs=in_specs, out_specs=out_specs, check_vma=False
    )
```

```python
import math

import jax
import jax.numpy as jnp
from jax import lax
from jax.experimental import pallas as pl
from jax.experimental.pallas import tpu as pltpu
from jax.sharding import PartitionSpec as P

CAP = 768
CLIP_SHARE = 0.25
LANES = 128
ROW_CHUNKS = 2
BF16 = jnp.bfloat16
F32 = jnp.float32
MIB = 1 << 20
EXPAND_MIB = 24
AHEAD = 3


def params(mib):
    return pltpu.CompilerParams(vmem_limit_bytes=mib * MIB)


TINY = pl.CostEstimate(flops=1, bytes_accessed=1, transcendentals=0)


def across(block, bit):
    count = lax.axis_size("tensor")
    return lax.ppermute(block, "tensor", [(r, r ^ 1 << bit) for r in range(count)])


def iota(shape, dim):
    return lax.broadcasted_iota(jnp.int32, shape, dim)


def slots_of(ids_ref):
    tokens = ids_ref.shape[1]
    rows = tokens // LANES
    padded = (rows + 15) // 16 * 16
    hit = jnp.where((ids_ref[0:1, :] == 0) | (ids_ref[1:2, :] == 0), 1.0, 0.0)
    grid = jnp.concatenate(
        [hit[:, LANES * k : LANES * (k + 1)] for k in range(rows)]
        + [jnp.zeros((padded - rows, LANES), F32)],
        axis=0,
    )
    flat = grid.astype(BF16)
    upto = (iota((LANES, LANES), 0) <= iota((LANES, LANES), 1)).astype(F32).astype(BF16)
    before = (iota((padded, padded), 1) < iota((padded, padded), 0)).astype(F32).astype(BF16)
    within = jnp.dot(flat, upto, preferred_element_type=F32)
    offset = jnp.sum(jnp.dot(before, flat, preferred_element_type=F32), axis=1, keepdims=True)
    return jnp.where(grid > 0.0, within + offset - 1.0, -1.0)


def pick_body(first, ids_hbm, tokens_hbm, *refs):
    picked_ref, peak_ref, ids_ref, tokens_ref, loaded = refs[-5:]
    rows = picked_ref.shape[0]
    count = tokens_ref.shape[0]
    pieces = loaded.shape[0] - 1
    step = count // pieces
    ids_copy = pltpu.make_async_copy(ids_hbm, ids_ref, loaded.at[pieces])
    ids_copy.start()
    copies = [
        pltpu.make_async_copy(
            tokens_hbm.at[pl.ds(i * step, step), :],
            tokens_ref.at[pl.ds(i * step, step), :],
            loaded.at[i],
        )
        for i in range(pieces)
    ]
    for copy in copies:
        copy.start()
    ids_copy.wait()
    slots = slots_of(ids_ref).astype(jnp.int32)
    wanted = iota((rows, LANES), 0) + first
    picked = jnp.zeros(picked_ref.shape, F32)
    for i, copy in enumerate(copies):
        hot = jnp.concatenate(
            [
                jnp.where(wanted == slots[k : k + 1, :], 1.0, 0.0).astype(BF16)
                for k in range(i * step // LANES, (i + 1) * step // LANES)
            ],
            axis=1,
        )
        copy.wait()
        picked += jnp.dot(
            hot, tokens_ref[i * step : (i + 1) * step, :], preferred_element_type=F32
        )
    picked_ref[...] = picked.astype(BF16)
    peak_ref[...] = jnp.broadcast_to(jnp.max(jnp.abs(picked)), peak_ref.shape)


def pick_rows(ids, tokens, first, rows, follow=()):
    count, width = tokens.shape
    blocks = count // LANES
    pieces = math.gcd(blocks, 4)
    in_hbm = [pltpu.with_memory_space_constraint(x, pltpu.HBM) for x in (ids, tokens)]
    return pl.pallas_call(
        lambda *refs: pick_body(first, *refs),
        out_shape=(
            jax.ShapeDtypeStruct((rows, width), BF16),
            jax.ShapeDtypeStruct((8, LANES), F32),
        ),
        in_specs=[pl.BlockSpec(memory_space=pltpu.HBM)] * 2 + follows(follow),
        out_specs=[pl.BlockSpec(memory_space=pltpu.VMEM)] * 2,
        scratch_shapes=[
            pltpu.VMEM(ids.shape, ids.dtype),
            pltpu.VMEM(tokens.shape, tokens.dtype),
            pltpu.SemaphoreType.DMA((pieces + 1,)),
        ],
        compiler_params=params(16),
        cost_estimate=TINY,
        name="pick_rows",
    )(*in_hbm, *follow)


def signs(size):
    common = iota((size, size), 0) & iota((size, size), 1)
    shift = 1
    while shift < size.bit_length():
        shift *= 2
    while shift > 1:
        shift //= 2
        common = common ^ (common >> shift)
    return (1 - 2 * (common & 1)).astype(F32).astype(BF16)


def whole(pieces):
    if len(pieces) == 1:
        return pieces[0][...]
    return jnp.concatenate([piece[...] for piece in pieces], axis=0)


def expand_body(first, cuts, last, me_ref, *refs):
    count = len(cuts)
    parts = []
    for pieces in cuts:
        parts.append(refs[:pieces])
        refs = refs[pieces:]
    before_ref = None
    if last:
        before_ref, refs = refs[0], refs[1:]
    gate_hbm, up_hbm, *outs, total, held, loaded = refs
    width = parts[0][0].shape[1]
    columns = total.shape[2]
    tile = min(256, columns)

    def load(mask):
        rows = pl.ds(pl.multiple_of((me_ref[0] ^ mask) * width, LANES), width)
        return [
            pltpu.make_async_copy(
                weight.at[rows, pl.ds(first, columns)], held.at[mask, at], loaded.at[mask, at]
            )
            for at, weight in enumerate((gate_hbm, up_hbm))
        ]

    loads = [load(mask) for mask in range(count)]
    for copies in loads[:AHEAD]:
        for copy in copies:
            copy.start()
    table = signs(tile)
    for mask, pieces in enumerate(parts):
        for copies in loads[mask + AHEAD : mask + AHEAD + 1]:
            for copy in copies:
                copy.start()
        for at in range(2):
            loads[mask][at].wait()
            term = jnp.dot(whole(pieces), held[mask, at], preferred_element_type=F32)
            if mask == 0:
                total[at] = term
            else:
                total[at] += term
    values = []
    for i in range(columns // tile):
        gate = total[0, :, i * tile : (i + 1) * tile]
        up = total[1, :, i * tile : (i + 1) * tile]
        hidden = (gate * (1.0 / (1.0 + jnp.exp(-gate))) * up).astype(BF16)
        values.append(jnp.dot(hidden, table, preferred_element_type=F32))
        if not last:
            outs[0][i] = values[i]
    if not last:
        return
    values = [before_ref[i] for i in range(before_ref.shape[0])] + values
    steps = len(values)
    gap = 1
    while gap < steps:
        values = [
            values[i] + values[i ^ gap] if not i & gap else values[i ^ gap] - values[i]
            for i in range(steps)
        ]
        gap *= 2
    for i in range(steps):
        low = 0
        for out in outs:
            rows = out.shape[0]
            out[:, i * tile : (i + 1) * tile] = values[i][low : low + rows].astype(BF16)
            low += rows


def expand(parts, rows, me, gate_weight, up_weight, before=None, follow=()):
    depth, width = gate_weight.shape
    last = before is not None
    columns = width // 2
    first = columns if last else 0
    tile = min(256, columns)
    parts = [x if isinstance(x, (list, tuple)) else [x] for x in parts]
    cuts = [len(x) for x in parts]
    parts = [x for pieces in parts for x in pieces]
    count = len(cuts)
    vmem = pl.BlockSpec(memory_space=pltpu.VMEM)
    in_hbm = [pltpu.with_memory_space_constraint(x, pltpu.HBM) for x in (gate_weight, up_weight)]
    args = [me, *parts] + ([before] if last else [])
    used = len(args) + 2
    if last:
        out_shape = [jax.ShapeDtypeStruct((rows // 2, width), BF16)] * 2
    else:
        out_shape = [jax.ShapeDtypeStruct((columns // tile, rows, tile), F32)]
    return pl.pallas_call(
        lambda *refs: expand_body(first, cuts, last, *refs[:used], *refs[used + len(follow) :]),
        in_specs=[pl.BlockSpec(memory_space=pltpu.SMEM)]
        + [vmem] * (used - 3)
        + [pl.BlockSpec(memory_space=pltpu.HBM)] * 2
        + follows(follow),
        out_specs=[vmem] * len(out_shape),
        out_shape=out_shape,
        scratch_shapes=[
            pltpu.VMEM((2, rows, columns), F32),
            pltpu.VMEM((count, 2, depth // count, columns), BF16),
            pltpu.SemaphoreType.DMA((count, 2)),
        ],
        compiler_params=params(EXPAND_MIB),
        cost_estimate=TINY,
        name="expand_last" if last else "expand_first",
    )(*args, *in_hbm, *follow)


def multiply_body(masks, cuts, resumed, last, me_ref, *refs):
    count = len(masks)
    parts = []
    for pieces in cuts:
        parts.append(refs[:pieces])
        refs = refs[pieces:]
    before_ref = None
    if resumed:
        before_ref, refs = refs[0], refs[1:]
    gate_hbm, up_hbm, *outs, held, loaded = refs
    if last:
        *outs, total = outs
    else:
        total = outs[0]
    features = parts[0][0].shape[1]
    width = total.shape[2]

    def load(i):
        rows = pl.ds(pl.multiple_of((me_ref[0] ^ masks[i]) * features, LANES), features)
        return [
            pltpu.make_async_copy(weight.at[rows, :], held.at[i, at], loaded.at[i, at])
            for at, weight in enumerate((gate_hbm, up_hbm))
        ]

    loads = [load(i) for i in range(count)]
    for copies in loads[:AHEAD]:
        for copy in copies:
            copy.start()
    columns = min(512, width)
    for i, pieces in enumerate(parts):
        for copies in loads[i + AHEAD : i + AHEAD + 1]:
            for copy in copies:
                copy.start()
        for at in range(2):
            loads[i][at].wait()
            for low in range(0, width, columns):
                span = slice(low, low + columns)
                term = jnp.dot(whole(pieces), held[i, at, :, span], preferred_element_type=F32)
                if i > 0:
                    term += total[at, :, span]
                elif resumed:
                    term += before_ref[at, :, span]
                total[at, :, span] = term
    if not last:
        return
    tile = min(256, width)
    steps = width // tile
    table = signs(tile)
    values = []
    for i in range(steps):
        gate = total[0, :, i * tile : (i + 1) * tile]
        up = total[1, :, i * tile : (i + 1) * tile]
        hidden = (gate * (1.0 / (1.0 + jnp.exp(-gate))) * up).astype(BF16)
        values.append(jnp.dot(hidden, table, preferred_element_type=F32))
    gap = 1
    while gap < steps:
        values = [
            values[i] + values[i ^ gap] if not i & gap else values[i ^ gap] - values[i]
            for i in range(steps)
        ]
        gap *= 2
    for i in range(steps):
        low = 0
        for out in outs:
            rows = out.shape[0]
            out[:, i * tile : (i + 1) * tile] = values[i][low : low + rows].astype(BF16)
            low += rows


def multiply(parts, me, gate_weight, up_weight, before=None, last=False, follow=()):
    masks = sorted(parts)
    depth, width = gate_weight.shape
    count = len(masks)
    pieces = [x if isinstance(x, (list, tuple)) else [x] for x in (parts[m] for m in masks)]
    cuts = [len(x) for x in pieces]
    rows, features = sum(x.shape[0] for x in pieces[0]), pieces[0][0].shape[1]
    vmem = pl.BlockSpec(memory_space=pltpu.VMEM)
    resumed = before is not None
    in_hbm = [pltpu.with_memory_space_constraint(x, pltpu.HBM) for x in (gate_weight, up_weight)]
    args = [me, *[x for group in pieces for x in group]] + ([before] if resumed else [])
    used = len(args) + 2
    scratch = [
        pltpu.VMEM((count, 2, features, width), BF16),
        pltpu.SemaphoreType.DMA((count, 2)),
    ]
    if last:
        out_shape = [jax.ShapeDtypeStruct((rows // 2, width), BF16)] * 2
        scratch.insert(0, pltpu.VMEM((2, rows, width), F32))
    else:
        out_shape = [jax.ShapeDtypeStruct((2, rows, width), F32)]
    made = pl.pallas_call(
        lambda *refs: multiply_body(
            masks, cuts, resumed, last, *refs[:used], *refs[used + len(follow) :]
        ),
        in_specs=[pl.BlockSpec(memory_space=pltpu.SMEM)]
        + [vmem] * (used - 3)
        + [pl.BlockSpec(memory_space=pltpu.HBM)] * 2
        + follows(follow),
        out_specs=[vmem] * len(out_shape),
        out_shape=out_shape,
        scratch_shapes=scratch,
        compiler_params=params(EXPAND_MIB + 8),
        cost_estimate=TINY,
        name="multiply_last" if last else "multiply",
    )(*args, *in_hbm, *follow)
    return made if last else made[0]


def clip_rows(peaks_ref, rotated, clipped_ref):
    level = CLIP_SHARE * jnp.max(peaks_ref[8:, :])
    low = 0
    for part in rotated:
        rows = part.shape[0]
        clipped_ref[low : low + rows, :] = jnp.clip(
            part[...].astype(F32), -level, level
        ).astype(BF16)
        low += rows


def down_body(first, fresh, me_ref, *refs):
    if fresh:
        peaks_ref, rotated, weight_hbm = refs[0], refs[1:fresh], refs[fresh]
        clipped_ref, refs = refs[-5], refs[:-5] + refs[-4:]
    else:
        clipped_ref, weight_hbm = refs[:2]
    owners = lax.axis_size("tensor")
    half = owners // 2
    other_ref, same_ref, held, loaded = refs[-4:]
    fc = same_ref.shape[2]
    stride = weight_hbm.shape[1] // owners
    masks = [2 * i + 1 for i in range(half)] + [2 * i for i in range(half)]

    def load(i):
        column = pl.multiple_of((me_ref[0] ^ masks[i]) * stride + first, LANES)
        return pltpu.make_async_copy(
            weight_hbm.at[:, pl.ds(column, fc)],
            held.at[i // 2, :, pl.ds(i % 2 * fc, fc)],
            loaded.at[i],
        )

    loads = [load(i) for i in range(owners)]
    for copy in loads[: 2 * AHEAD]:
        copy.start()
    if fresh:
        clip_rows(peaks_ref, rotated, clipped_ref)
    for pair in range(half):
        for copy in loads[2 * (pair + AHEAD) : 2 * (pair + AHEAD + 1)]:
            copy.start()
        for copy in loads[2 * pair : 2 * pair + 2]:
            copy.wait()
        terms = jnp.dot(clipped_ref[...], held[pair], preferred_element_type=F32).astype(BF16)
        for side in range(2):
            i = 2 * pair + side
            term = terms[:, side * fc : (side + 1) * fc]
            if i < half:
                other_ref[i] = term
            else:
                same_ref[i - half] = term


def down(clipped, weight, me, units, first, follow=(), fresh=()):
    depth = weight.shape[0]
    owners = lax.axis_size("tensor")
    half = owners // 2
    args = list(fresh) if fresh else [clipped]
    rows = sum(x.shape[0] for x in (fresh[1:] if fresh else [clipped]))
    fc = units * LANES
    vmem = pl.BlockSpec(memory_space=pltpu.VMEM)
    shapes = [jax.ShapeDtypeStruct((rows, depth), BF16)] * bool(fresh)
    shapes += [jax.ShapeDtypeStruct((half, rows, fc), BF16)] * 2
    return pl.pallas_call(
        lambda *refs: down_body(first * LANES, len(fresh), *refs),
        in_specs=[pl.BlockSpec(memory_space=pltpu.SMEM)]
        + [vmem] * len(args)
        + [pl.BlockSpec(memory_space=pltpu.HBM)]
        + follows(follow),
        out_specs=[vmem] * len(shapes),
        out_shape=shapes,
        scratch_shapes=[
            pltpu.VMEM((half, depth, 2 * fc), BF16),
            pltpu.SemaphoreType.DMA((owners,)),
        ],
        compiler_params=params(16),
        cost_estimate=TINY,
        name="down",
    )(me, *args, pltpu.with_memory_space_constraint(weight, pltpu.HBM), *follow)


def spread_body(counts, slots_at, ids_ref, probs_ref, *refs):
    out_ref = refs[-1]
    tokens = ids_ref.shape[1]
    summed = []
    for count, slot in zip(counts, slots_at):
        mine, theirs = refs[:count], refs[count : 2 * count]
        refs = refs[2 * count :]
        rows = [(a[0].astype(F32) + b[slot].astype(F32)).astype(BF16) for a, b in zip(mine, theirs)]
        summed.append(jnp.concatenate(rows, axis=0))
    summed = jnp.concatenate(summed, axis=1)
    slots = slots_of(ids_ref)
    share = jnp.where(ids_ref[0:1, :] == 0, probs_ref[0:1, :], 0.0) + jnp.where(
        ids_ref[1:2, :] == 0, probs_ref[1:2, :], 0.0
    )
    blocks = tokens // LANES
    share = jnp.concatenate(
        [share[:, LANES * k : LANES * (k + 1)] for k in range(blocks)]
        + [jnp.zeros((LANES - blocks, LANES), F32)],
        axis=0,
    ).T
    slots = jnp.concatenate(
        [slots, jnp.zeros((LANES - slots.shape[0], LANES), F32)], axis=0
    ).T.astype(jnp.int32)
    at = iota((LANES, summed.shape[0]), 1)
    for k in range(blocks):
        hot = jnp.where(at == slots[:, k : k + 1], 1.0, 0.0).astype(BF16)
        rows = jnp.dot(hot, summed, preferred_element_type=F32)
        out_ref[LANES * k : LANES * (k + 1), :] = (rows * share[:, k : k + 1]).astype(BF16)


def spread(ids, probs, states, slots_at, first, features, out):
    tokens = ids.shape[1]
    fc = sum(state[0][0].shape[2] for state in states)
    args = [ids, probs]
    for state in states:
        args += [x[0] for x in state] + [x[1] for x in state]
    counts = [len(state) for state in states]
    used = len(args)
    in_specs = [pl.BlockSpec(x.shape, lambda i, d=x.ndim: (0,) * d) for x in args]
    earlier = [] if out is None else [out]
    return pl.pallas_call(
        lambda *refs: spread_body(counts, slots_at, *refs[:used], refs[-1]),
        grid=(1,),
        in_specs=in_specs + follows(earlier),
        out_specs=pl.BlockSpec((pl.Element(tokens), pl.Element(fc)), lambda i: (0, first * LANES)),
        out_shape=jax.ShapeDtypeStruct((tokens, features), BF16),
        input_output_aliases={used: 0} if earlier else {},
        compiler_params=params(24),
        cost_estimate=TINY,
        name="spread",
    )(*args, *earlier)


def follows(arrays):
    return [pl.BlockSpec(memory_space=pl.ANY)] * len(arrays)


def small(body, args, shapes, name, follow=()):
    vmem = pl.BlockSpec(memory_space=pltpu.VMEM)
    count = len(args)
    specs = [pl.BlockSpec(memory_space=pltpu.SMEM) if x.ndim == 1 else vmem for x in args]
    return pl.pallas_call(
        lambda *refs: body(refs[:count], refs[count + len(follow) :]),
        in_specs=specs + follows(follow),
        out_specs=[vmem] * len(shapes),
        out_shape=[jax.ShapeDtypeStruct(*x) for x in shapes],
        compiler_params=params(16),
        cost_estimate=TINY,
        name=name,
    )(*args, *follow)


def gather_near(own, orders):
    return {0: own} | {1 << bit: across(own, bit) for bit in orders[0]}


def cut_body(firsts, ins, outs):
    for h, at in enumerate(firsts):
        rows = outs[h].shape[0]
        outs[h][...] = ins[at][h * rows : (h + 1) * rows, :]
    for block, out in zip(ins, outs[2:]):
        out[...] = block[...]


def join_body(ins, outs):
    pieces = 2 * len(outs) // len(ins)
    for i in range(len(ins) // 2):
        whole = jnp.concatenate([ins[2 * i][...], ins[2 * i + 1][...]], axis=0)
        for k in range(pieces):
            out = outs[pieces * i + k]
            rows = out.shape[0]
            out[...] = whole[k * rows : (k + 1) * rows, :]


def cut(full, orders, follow, passed=False):
    rows, width = full[0].shape
    masks = [mask for mask in full if mask]
    firsts = [masks.index(1 << order[0]) for order in orders]
    shapes = [((rows // 2, width), BF16)] * 2 + [((rows, width), BF16)] * len(masks) * passed
    outs = small(
        lambda ins, outs: cut_body(firsts, ins, outs),
        [full[mask] for mask in masks],
        shapes,
        "cut",
        follow,
    )
    return outs[:2], full | dict(zip(masks, outs[2:]))


def gather_far(full, cuts, orders):
    half = full[0].shape[0] // len(orders)
    firsts = [1 << order[0] for order in orders]
    part = {}

    def get(mask, h):
        if (mask, h) in part:
            return part[mask, h]
        return cuts[h] if mask == firsts[h] else full[mask][h * half : (h + 1) * half]

    have = [[0, first] for first in firsts]
    for at in range(1, len(orders[0])):
        for h, order in enumerate(orders):
            bit = order[at]
            for mask in list(have[h]):
                there = mask | 1 << bit
                if there not in full:
                    part[there, h] = across(get(mask, h), bit)
                have[h].append(there)
    return part


def join(part, follow, pieces):
    masks = sorted({mask for mask, _ in part})
    halves = [part[mask, h] for mask in masks for h in range(2)]
    half, width = halves[0].shape
    shapes = [((2 * half // pieces, width), BF16)] * (pieces * len(masks))
    joined = small(join_body, halves, shapes, "join", follow)
    return {mask: joined[pieces * i : pieces * (i + 1)] for i, mask in enumerate(masks)}


def paired(pieces):
    return pieces | {
        mask | 1: [across(x, 0) for x in block] if isinstance(block, list) else across(block, 0)
        for mask, block in pieces.items()
    }


def turn_body(bits, scale, ins, outs):
    me_ref, ins = ins[0], ins[1:]
    count = len(bits)
    for h, bit in enumerate(bits):
        flip = (1 - 2 * ((me_ref[0] >> bit) & 1)).astype(F32)
        own = ins[2 * h][...].astype(F32)
        came = ins[2 * h + 1][...].astype(F32)
        value = came + own * flip
        if scale is not None:
            value = value * scale
            top = jnp.max(jnp.abs(own) + jnp.abs(came), axis=0, keepdims=True) * scale
            wide = top[:, :LANES]
            for k in range(1, top.shape[1] // LANES):
                wide = jnp.maximum(wide, top[:, k * LANES : (k + 1) * LANES])
            outs[count + h][...] = jnp.broadcast_to(wide, outs[count + h].shape)
        outs[h][...] = value.astype(BF16)


def turn(me, blocks, came, bits, follow=(), scale=None):
    args = [me] + [x for pair in zip(blocks, came) for x in pair]
    shapes = [(x.shape, BF16) for x in blocks]
    if scale is not None:
        shapes += [((8, LANES), F32)] * len(blocks)
    return small(
        lambda ins, outs: turn_body(bits, scale, ins, outs), args, shapes, "turn", follow
    )


def largest(top_in, tops, lasts):
    bits = range(lax.axis_size("tensor").bit_length() - 1)
    values = jnp.concatenate([top_in, *tops], axis=0)
    for bit in bits:
        if bit not in lasts:
            values = jnp.maximum(values, across(values, bit))
    n = top_in.shape[0]
    top_in, first, second = values[:n], values[n : 2 * n], values[2 * n :]
    if lasts[0] != lasts[1]:
        pair = jnp.concatenate([top_in, second], axis=0)
        came_first, came_pair = across(first, lasts[1]), across(pair, lasts[0])
        first = jnp.maximum(first, came_first)
        pair = jnp.maximum(pair, came_pair)
        top_in, second = pair[:n], pair[n:]
    values = jnp.concatenate([top_in, jnp.maximum(first, second)], axis=0)
    blocks = lax.axis_size("dp")
    far = 1
    while far < blocks:
        pairs = [(r, r ^ far) for r in range(blocks)]
        values = jnp.maximum(values, lax.ppermute(values, "dp", pairs))
        far *= 2
    return values


def on_device(tokens, expert_ids, gate_probs, gate_weight, up_weight, down_weight):
    count = lax.axis_size("tensor")
    bits = count.bit_length() - 1
    outer = list(range(1, bits))
    orders = [outer, outer[::-1]]
    me = lax.axis_index("tensor")
    me_arr = me.astype(jnp.int32).reshape(1)
    ids, probs = expert_ids.T, gate_probs.T
    rows = CAP // ROW_CHUNKS
    half = rows // 2
    scale = 1.0 / math.sqrt(gate_weight.shape[1] * count)
    stages = [[order[at] for order in orders] for at in range(len(outer))]
    early_bit = stages[-1][1]

    def send(blocks, bits):
        return [across(x, bit) for x, bit in zip(blocks, bits)]

    def start_turn(halves, follow=()):
        blocks = turn(me_arr, halves, send(halves, [0, 0]), [0, 0], follow)
        return blocks, send(blocks, stages[0])

    def go_on(blocks, came, at, follow=()):
        blocks = turn(me_arr, blocks, came, stages[at], follow)
        return blocks, send(blocks, stages[at + 1])

    def end_turn(blocks, came, follow=()):
        made = turn(me_arr, blocks, came, stages[-1], follow, scale)
        return made[: len(blocks)], made[len(blocks) :]

    own_a, top_a = pick_rows(ids, tokens, 0, rows, [me_arr])
    near_a = gather_near(own_a, orders)
    weights = (me_arr, gate_weight, up_weight)
    cuts_a, near_a = cut(near_a, orders, [])
    own_b, top_b = pick_rows(ids, tokens, rows, rows, cuts_a)
    top_in = jnp.maximum(top_a, top_b)
    top_in = jnp.maximum(top_in, across(top_in, early_bit))
    far_a = join(gather_far(near_a, cuts_a, orders), [own_b, top_in], 1)
    near_b = gather_near(own_b, orders)
    parts_a = paired(near_a | far_a)
    parts_a = [parts_a[mask] for mask in range(count)]
    first_a = expand(parts_a, rows, *weights)
    local_a = expand(parts_a, rows, *weights, *first_a)
    cuts_b, near_b = cut(near_b, orders, local_a, True)
    parts_b = paired(near_b)
    theirs_b = [block for mask, block in parts_b.items() if mask & 1]
    blocks_a, came_a = start_turn(local_a, theirs_b)
    total_b = multiply(parts_b, *weights, follow=blocks_a)
    far_b = join(gather_far(near_b, cuts_b, orders), [total_b], 3)
    for at in range(len(outer) - 1):
        blocks_a, came_a = go_on(blocks_a, came_a, at, [total_b])
    local_b = multiply(paired(far_b), *weights, total_b, True, blocks_a)
    turned_a, rot_a = end_turn(blocks_a, came_a, local_b)
    blocks_b, came_b = start_turn(local_b, rot_a)
    for at in range(len(outer) - 1):
        blocks_b, came_b = go_on(blocks_b, came_b, at)
    turned_b, rot_b = end_turn(blocks_b, came_b)
    rotated = turned_a + turned_b

    peaks = largest(top_in, [jnp.maximum(x, y) for x, y in zip(rot_a, rot_b)], stages[-1])
    tops = pl.pallas_call(
        peaks_body,
        out_specs=pl.BlockSpec(memory_space=pltpu.SMEM),
        out_shape=jax.ShapeDtypeStruct((2,), F32),
        name="peaks",
    )(peaks)
    units = tokens.shape[1] // LANES
    sizes = chunks_of(units)
    firsts = [sum(sizes[:i]) for i in range(len(sizes))]
    total = len(sizes)
    products, begun, ended, out, last, clipped = {}, {}, {}, None, [], None
    for step, chunk in sums_order(total):
        if step == "product":
            fresh = [peaks, *rotated] if chunk == 0 else []
            made = down(clipped, down_weight, me_arr, sizes[chunk], firsts[chunk], last, fresh)
            if fresh:
                clipped, made = made[0], made[1:]
            products[chunk] = made
            last = [products[chunk][1]]
        elif step == "begin":
            other, same = products[chunk]
            begun[chunk] = fold_cores(same, across(other, 0), stages[0], last)
            last = [keep for keep, _, _ in begun[chunk]]
        elif step == "finish":
            ahead = [c for c in products if c not in begun]
            passed = [products[c][0] for c in ahead]
            held = chunk == 0 and total > 2
            stacked = [x for _, x, _ in ended[0]] if chunk == 1 and total > 2 else []
            ended[chunk], passed = finish(
                begun[chunk], stages, last, passed, stacked, not held
            )
            if stacked:
                ended[0] = [
                    (keep, both, left)
                    for (keep, _, left), (_, both, _) in zip(ended[0], ended[1])
                ]
            for c, other in zip(ahead, passed):
                products[c] = (other, products[c][1])
            last = [keep for keep, _, _ in ended[chunk]]
        else:
            chunks = [0, 1] if chunk == 0 and total > 2 else [chunk]
            slots_at = [0 if c == 0 else ended[c][0][1].shape[0] - 1 for c in chunks]
            out = spread(
                ids,
                probs,
                [ended[c] for c in chunks],
                slots_at,
                firsts[chunk],
                tokens.shape[1],
                out,
            )
    return out, tops


def chunks_of(units):
    return [2] * (units // 2) + [1] * (units % 2)


def sums_order(total):
    order = [("product", 0)]
    for chunk in range(total):
        if chunk + 1 < total:
            order.append(("product", chunk + 1))
        order.append(("begin", chunk))
        if chunk > 0:
            order.append(("finish", chunk - 1))
    order.append(("finish", total - 1))
    return order + [("spread", c) for c in range(total) if c != 1 or total < 3]


def peaks_body(values_ref, out_ref):
    out_ref[0] = jnp.max(values_ref[:8, :])
    out_ref[1] = jnp.max(values_ref[8:, :])


def fold_body(plan, passed, ins, outs):
    for i in range(passed):
        outs[len(plan) + i][...] = ins[len(ins) - passed + i][...]
    for out, (slots, low) in zip(outs, plan):
        rows = out.shape[1]
        for slot, terms in enumerate(slots):
            total = 0.0
            for at, i in terms:
                total = total + ins[at][i, low : low + rows, :].astype(F32)
            out[slot] = total.astype(BF16)


def fold(args, terms, masks, lows, rows, bits, follow, passed=(), stacked=(), sent=True):
    plan, shapes, lefts = [], [], []
    width = args[0].shape[2]
    for h, bit in enumerate(bits):
        for side in (0, 1):
            chosen = [m for m in masks[h] if m >> bit & 1 == side]
            slots = [terms[h][m] for m in chosen]
            if side and stacked:
                slots = [((len(args) + h, i),) for i in range(stacked[h].shape[0])] + slots
            plan.append((slots, lows[h]))
            shapes.append(((len(slots), rows, width), BF16))
        lefts.append([m for m in masks[h] if not m >> bit & 1])
    shapes += [(x.shape, x.dtype) for x in passed]
    made = small(
        lambda ins, outs: fold_body(plan, len(passed), ins, outs),
        [*args, *stacked, *passed],
        shapes,
        "fold",
        follow,
    )
    state = [
        (made[2 * h], across(made[2 * h + 1], bit) if sent else made[2 * h + 1], lefts[h])
        for h, bit in enumerate(bits)
    ]
    return state, made[len(plan) :]


def fold_cores(same, came, bits, follow):
    half = same.shape[1] // 2
    masks = [2 * i for i in range(same.shape[0])]
    terms = {m: ((0, i), (1, i)) for i, m in enumerate(masks)}
    return fold([same, came], [terms] * 2, [masks] * 2, [0, half], half, bits, follow)[0]


def finish(state, stages, follow, passed=(), stacked=(), sent=True):
    for bits in stages[1:]:
        args = [x for keep, recv, _ in state for x in (keep, recv)]
        masks = [left for _, _, left in state]
        terms = [
            {m: ((2 * h, i), (2 * h + 1, i)) for i, m in enumerate(left)}
            for h, left in enumerate(masks)
        ]
        last = bits is stages[-1]
        state, passed = fold(
            args,
            terms,
            masks,
            [0, 0],
            args[0].shape[1],
            bits,
            follow,
            passed,
            stacked if last else (),
            sent or not last,
        )
    return state, passed


def solution(mesh):
    in_specs = (
        P("dp", "tensor"),
        P("dp", None),
        P("dp", None),
        P(None, "tensor"),
        P(None, "tensor"),
        P("tensor", None),
    )
    out_specs = (P("dp", "tensor"), P())
    return jax.shard_map(
        on_device, mesh=mesh, in_specs=in_specs, out_specs=out_specs, check_vma=False
    )
```

```python
import math

import jax
import jax.numpy as jnp
from jax import lax
from jax.experimental import pallas as pl
from jax.experimental.pallas import tpu as pltpu
from jax.sharding import PartitionSpec as P

CAP = 768
CLIP_SHARE = 0.25
LANES = 128
ROW_CHUNKS = 2
BF16 = jnp.bfloat16
F32 = jnp.float32
MIB = 1 << 20
EXPAND_MIB = 24
AHEAD = 2


def params(mib):
    return pltpu.CompilerParams(vmem_limit_bytes=mib * MIB)


TINY = pl.CostEstimate(flops=1, bytes_accessed=1, transcendentals=0)


def across(block, bit):
    count = lax.axis_size("tensor")
    return lax.ppermute(block, "tensor", [(r, r ^ 1 << bit) for r in range(count)])


def iota(shape, dim):
    return lax.broadcasted_iota(jnp.int32, shape, dim)


def slots_of(ids_ref):
    tokens = ids_ref.shape[1]
    rows = tokens // LANES
    padded = (rows + 15) // 16 * 16
    hit = jnp.where((ids_ref[0:1, :] == 0) | (ids_ref[1:2, :] == 0), 1.0, 0.0)
    grid = jnp.concatenate(
        [hit[:, LANES * k : LANES * (k + 1)] for k in range(rows)]
        + [jnp.zeros((padded - rows, LANES), F32)],
        axis=0,
    )
    flat = grid.astype(BF16)
    upto = (iota((LANES, LANES), 0) <= iota((LANES, LANES), 1)).astype(F32).astype(BF16)
    before = (iota((padded, padded), 1) < iota((padded, padded), 0)).astype(F32).astype(BF16)
    within = jnp.dot(flat, upto, preferred_element_type=F32)
    offset = jnp.sum(jnp.dot(before, flat, preferred_element_type=F32), axis=1, keepdims=True)
    return jnp.where(grid > 0.0, within + offset - 1.0, -1.0)


def pick_body(first, ids_hbm, tokens_hbm, *refs):
    picked_ref, peak_ref, ids_ref, tokens_ref, loaded = refs[-5:]
    rows = picked_ref.shape[0]
    count = tokens_ref.shape[0]
    pieces = loaded.shape[0] - 1
    step = count // pieces
    ids_copy = pltpu.make_async_copy(ids_hbm, ids_ref, loaded.at[pieces])
    ids_copy.start()
    copies = [
        pltpu.make_async_copy(
            tokens_hbm.at[pl.ds(i * step, step), :],
            tokens_ref.at[pl.ds(i * step, step), :],
            loaded.at[i],
        )
        for i in range(pieces)
    ]
    for copy in copies:
        copy.start()
    ids_copy.wait()
    slots = slots_of(ids_ref).astype(jnp.int32)
    wanted = iota((rows, LANES), 0) + first
    picked = jnp.zeros(picked_ref.shape, F32)
    for i, copy in enumerate(copies):
        hot = jnp.concatenate(
            [
                jnp.where(wanted == slots[k : k + 1, :], 1.0, 0.0).astype(BF16)
                for k in range(i * step // LANES, (i + 1) * step // LANES)
            ],
            axis=1,
        )
        copy.wait()
        picked += jnp.dot(
            hot, tokens_ref[i * step : (i + 1) * step, :], preferred_element_type=F32
        )
    picked_ref[...] = picked.astype(BF16)
    peak_ref[...] = jnp.broadcast_to(jnp.max(jnp.abs(picked)), peak_ref.shape)


def pick_rows(ids, tokens, first, rows, follow=()):
    count, width = tokens.shape
    blocks = count // LANES
    pieces = math.gcd(blocks, 4)
    in_hbm = [pltpu.with_memory_space_constraint(x, pltpu.HBM) for x in (ids, tokens)]
    return pl.pallas_call(
        lambda *refs: pick_body(first, *refs),
        out_shape=(
            jax.ShapeDtypeStruct((rows, width), BF16),
            jax.ShapeDtypeStruct((8, LANES), F32),
        ),
        in_specs=[pl.BlockSpec(memory_space=pltpu.HBM)] * 2 + follows(follow),
        out_specs=[pl.BlockSpec(memory_space=pltpu.VMEM)] * 2,
        scratch_shapes=[
            pltpu.VMEM(ids.shape, ids.dtype),
            pltpu.VMEM(tokens.shape, tokens.dtype),
            pltpu.SemaphoreType.DMA((pieces + 1,)),
        ],
        compiler_params=params(16),
        cost_estimate=TINY,
        name="pick_rows",
    )(*in_hbm, *follow)


def signs(size):
    common = iota((size, size), 0) & iota((size, size), 1)
    shift = 1
    while shift < size.bit_length():
        shift *= 2
    while shift > 1:
        shift //= 2
        common = common ^ (common >> shift)
    return (1 - 2 * (common & 1)).astype(F32).astype(BF16)


def whole(pieces):
    if len(pieces) == 1:
        return pieces[0][...]
    return jnp.concatenate([piece[...] for piece in pieces], axis=0)


def expand_body(first, cuts, last, me_ref, *refs):
    count = len(cuts)
    parts = []
    for pieces in cuts:
        parts.append(refs[:pieces])
        refs = refs[pieces:]
    before_ref = None
    if last:
        before_ref, refs = refs[0], refs[1:]
    gate_hbm, up_hbm, *outs, total, held, loaded = refs
    width = parts[0][0].shape[1]
    columns = total.shape[2]
    tile = min(256, columns)

    def load(mask):
        rows = pl.ds(pl.multiple_of((me_ref[0] ^ mask) * width, LANES), width)
        return [
            pltpu.make_async_copy(
                weight.at[rows, pl.ds(first, columns)], held.at[mask, at], loaded.at[mask, at]
            )
            for at, weight in enumerate((gate_hbm, up_hbm))
        ]

    loads = [load(mask) for mask in range(count)]
    for copies in loads[:AHEAD]:
        for copy in copies:
            copy.start()
    table = signs(tile)
    for mask, pieces in enumerate(parts):
        for copies in loads[mask + AHEAD : mask + AHEAD + 1]:
            for copy in copies:
                copy.start()
        for at in range(2):
            loads[mask][at].wait()
            term = jnp.dot(whole(pieces), held[mask, at], preferred_element_type=F32)
            if mask == 0:
                total[at] = term
            else:
                total[at] += term
    values = []
    for i in range(columns // tile):
        gate = total[0, :, i * tile : (i + 1) * tile]
        up = total[1, :, i * tile : (i + 1) * tile]
        hidden = (gate * (1.0 / (1.0 + jnp.exp(-gate))) * up).astype(BF16)
        values.append(jnp.dot(hidden, table, preferred_element_type=F32))
        if not last:
            outs[0][i] = values[i]
    if not last:
        return
    values = [before_ref[i] for i in range(before_ref.shape[0])] + values
    steps = len(values)
    gap = 1
    while gap < steps:
        values = [
            values[i] + values[i ^ gap] if not i & gap else values[i ^ gap] - values[i]
            for i in range(steps)
        ]
        gap *= 2
    for i in range(steps):
        low = 0
        for out in outs:
            rows = out.shape[0]
            out[:, i * tile : (i + 1) * tile] = values[i][low : low + rows].astype(BF16)
            low += rows


def expand(parts, rows, me, gate_weight, up_weight, before=None, follow=()):
    depth, width = gate_weight.shape
    last = before is not None
    columns = width // 2
    first = columns if last else 0
    tile = min(256, columns)
    parts = [x if isinstance(x, (list, tuple)) else [x] for x in parts]
    cuts = [len(x) for x in parts]
    parts = [x for pieces in parts for x in pieces]
    count = len(cuts)
    vmem = pl.BlockSpec(memory_space=pltpu.VMEM)
    in_hbm = [pltpu.with_memory_space_constraint(x, pltpu.HBM) for x in (gate_weight, up_weight)]
    args = [me, *parts] + ([before] if last else [])
    used = len(args) + 2
    if last:
        out_shape = [jax.ShapeDtypeStruct((rows // 2, width), BF16)] * 2
    else:
        out_shape = [jax.ShapeDtypeStruct((columns // tile, rows, tile), F32)]
    return pl.pallas_call(
        lambda *refs: expand_body(first, cuts, last, *refs[:used], *refs[used + len(follow) :]),
        in_specs=[pl.BlockSpec(memory_space=pltpu.SMEM)]
        + [vmem] * (used - 3)
        + [pl.BlockSpec(memory_space=pltpu.HBM)] * 2
        + follows(follow),
        out_specs=[vmem] * len(out_shape),
        out_shape=out_shape,
        scratch_shapes=[
            pltpu.VMEM((2, rows, columns), F32),
            pltpu.VMEM((count, 2, depth // count, columns), BF16),
            pltpu.SemaphoreType.DMA((count, 2)),
        ],
        compiler_params=params(EXPAND_MIB),
        cost_estimate=TINY,
        name="expand_last" if last else "expand_first",
    )(*args, *in_hbm, *follow)


def multiply_body(masks, cuts, resumed, last, me_ref, *refs):
    count = len(masks)
    parts = []
    for pieces in cuts:
        parts.append(refs[:pieces])
        refs = refs[pieces:]
    before_ref = None
    if resumed:
        before_ref, refs = refs[0], refs[1:]
    gate_hbm, up_hbm, *outs, held, loaded = refs
    if last:
        *outs, total = outs
    else:
        total = outs[0]
    features = parts[0][0].shape[1]
    width = total.shape[2]

    def load(i):
        rows = pl.ds(pl.multiple_of((me_ref[0] ^ masks[i]) * features, LANES), features)
        return [
            pltpu.make_async_copy(weight.at[rows, :], held.at[i, at], loaded.at[i, at])
            for at, weight in enumerate((gate_hbm, up_hbm))
        ]

    loads = [load(i) for i in range(count)]
    for copies in loads[:AHEAD]:
        for copy in copies:
            copy.start()
    columns = min(512, width)
    for i, pieces in enumerate(parts):
        for copies in loads[i + AHEAD : i + AHEAD + 1]:
            for copy in copies:
                copy.start()
        for at in range(2):
            loads[i][at].wait()
            for low in range(0, width, columns):
                span = slice(low, low + columns)
                term = jnp.dot(whole(pieces), held[i, at, :, span], preferred_element_type=F32)
                if i > 0:
                    term += total[at, :, span]
                elif resumed:
                    term += before_ref[at, :, span]
                total[at, :, span] = term
    if not last:
        return
    tile = min(256, width)
    steps = width // tile
    table = signs(tile)
    values = []
    for i in range(steps):
        gate = total[0, :, i * tile : (i + 1) * tile]
        up = total[1, :, i * tile : (i + 1) * tile]
        hidden = (gate * (1.0 / (1.0 + jnp.exp(-gate))) * up).astype(BF16)
        values.append(jnp.dot(hidden, table, preferred_element_type=F32))
    gap = 1
    while gap < steps:
        values = [
            values[i] + values[i ^ gap] if not i & gap else values[i ^ gap] - values[i]
            for i in range(steps)
        ]
        gap *= 2
    for i in range(steps):
        low = 0
        for out in outs:
            rows = out.shape[0]
            out[:, i * tile : (i + 1) * tile] = values[i][low : low + rows].astype(BF16)
            low += rows


def multiply(parts, me, gate_weight, up_weight, before=None, last=False, follow=()):
    masks = sorted(parts)
    depth, width = gate_weight.shape
    count = len(masks)
    pieces = [x if isinstance(x, (list, tuple)) else [x] for x in (parts[m] for m in masks)]
    cuts = [len(x) for x in pieces]
    rows, features = sum(x.shape[0] for x in pieces[0]), pieces[0][0].shape[1]
    vmem = pl.BlockSpec(memory_space=pltpu.VMEM)
    resumed = before is not None
    in_hbm = [pltpu.with_memory_space_constraint(x, pltpu.HBM) for x in (gate_weight, up_weight)]
    args = [me, *[x for group in pieces for x in group]] + ([before] if resumed else [])
    used = len(args) + 2
    scratch = [
        pltpu.VMEM((count, 2, features, width), BF16),
        pltpu.SemaphoreType.DMA((count, 2)),
    ]
    if last:
        out_shape = [jax.ShapeDtypeStruct((rows // 2, width), BF16)] * 2
        scratch.insert(0, pltpu.VMEM((2, rows, width), F32))
    else:
        out_shape = [jax.ShapeDtypeStruct((2, rows, width), F32)]
    made = pl.pallas_call(
        lambda *refs: multiply_body(
            masks, cuts, resumed, last, *refs[:used], *refs[used + len(follow) :]
        ),
        in_specs=[pl.BlockSpec(memory_space=pltpu.SMEM)]
        + [vmem] * (used - 3)
        + [pl.BlockSpec(memory_space=pltpu.HBM)] * 2
        + follows(follow),
        out_specs=[vmem] * len(out_shape),
        out_shape=out_shape,
        scratch_shapes=scratch,
        compiler_params=params(EXPAND_MIB + 8),
        cost_estimate=TINY,
        name="multiply_last" if last else "multiply",
    )(*args, *in_hbm, *follow)
    return made if last else made[0]


def clip_rows(peaks_ref, rotated, clipped_ref):
    level = CLIP_SHARE * jnp.max(peaks_ref[8:, :])
    low = 0
    for part in rotated:
        rows = part.shape[0]
        clipped_ref[low : low + rows, :] = jnp.clip(
            part[...].astype(F32), -level, level
        ).astype(BF16)
        low += rows


def down_body(first, fresh, me_ref, *refs):
    if fresh:
        peaks_ref, rotated, weight_hbm = refs[0], refs[1:fresh], refs[fresh]
        clipped_ref, refs = refs[-5], refs[:-5] + refs[-4:]
    else:
        clipped_ref, weight_hbm = refs[:2]
    owners = lax.axis_size("tensor")
    half = owners // 2
    other_ref, same_ref, held, loaded = refs[-4:]
    fc = same_ref.shape[2]
    stride = weight_hbm.shape[1] // owners
    masks = [2 * i + 1 for i in range(half)] + [2 * i for i in range(half)]

    def load(i):
        column = pl.multiple_of((me_ref[0] ^ masks[i]) * stride + first, LANES)
        return pltpu.make_async_copy(
            weight_hbm.at[:, pl.ds(column, fc)],
            held.at[i // 2, :, pl.ds(i % 2 * fc, fc)],
            loaded.at[i],
        )

    loads = [load(i) for i in range(owners)]
    for copy in loads[: 2 * AHEAD]:
        copy.start()
    if fresh:
        clip_rows(peaks_ref, rotated, clipped_ref)
    for pair in range(half):
        for copy in loads[2 * (pair + AHEAD) : 2 * (pair + AHEAD + 1)]:
            copy.start()
        for copy in loads[2 * pair : 2 * pair + 2]:
            copy.wait()
        terms = jnp.dot(clipped_ref[...], held[pair], preferred_element_type=F32).astype(BF16)
        for side in range(2):
            i = 2 * pair + side
            term = terms[:, side * fc : (side + 1) * fc]
            if i < half:
                other_ref[i] = term
            else:
                same_ref[i - half] = term


def down(clipped, weight, me, units, first, follow=(), fresh=()):
    depth = weight.shape[0]
    owners = lax.axis_size("tensor")
    half = owners // 2
    args = list(fresh) if fresh else [clipped]
    rows = sum(x.shape[0] for x in (fresh[1:] if fresh else [clipped]))
    fc = units * LANES
    vmem = pl.BlockSpec(memory_space=pltpu.VMEM)
    shapes = [jax.ShapeDtypeStruct((rows, depth), BF16)] * bool(fresh)
    shapes += [jax.ShapeDtypeStruct((half, rows, fc), BF16)] * 2
    return pl.pallas_call(
        lambda *refs: down_body(first * LANES, len(fresh), *refs),
        in_specs=[pl.BlockSpec(memory_space=pltpu.SMEM)]
        + [vmem] * len(args)
        + [pl.BlockSpec(memory_space=pltpu.HBM)]
        + follows(follow),
        out_specs=[vmem] * len(shapes),
        out_shape=shapes,
        scratch_shapes=[
            pltpu.VMEM((half, depth, 2 * fc), BF16),
            pltpu.SemaphoreType.DMA((owners,)),
        ],
        compiler_params=params(16),
        cost_estimate=TINY,
        name="down",
    )(me, *args, pltpu.with_memory_space_constraint(weight, pltpu.HBM), *follow)


def spread_body(counts, slots_at, ids_ref, probs_ref, *refs):
    out_ref = refs[-1]
    tokens = ids_ref.shape[1]
    summed = []
    for count, slot in zip(counts, slots_at):
        mine, theirs = refs[:count], refs[count : 2 * count]
        refs = refs[2 * count :]
        rows = [(a[0].astype(F32) + b[slot].astype(F32)).astype(BF16) for a, b in zip(mine, theirs)]
        summed.append(jnp.concatenate(rows, axis=0))
    summed = jnp.concatenate(summed, axis=1)
    slots = slots_of(ids_ref)
    share = jnp.where(ids_ref[0:1, :] == 0, probs_ref[0:1, :], 0.0) + jnp.where(
        ids_ref[1:2, :] == 0, probs_ref[1:2, :], 0.0
    )
    blocks = tokens // LANES
    share = jnp.concatenate(
        [share[:, LANES * k : LANES * (k + 1)] for k in range(blocks)]
        + [jnp.zeros((LANES - blocks, LANES), F32)],
        axis=0,
    ).T
    slots = jnp.concatenate(
        [slots, jnp.zeros((LANES - slots.shape[0], LANES), F32)], axis=0
    ).T.astype(jnp.int32)
    at = iota((LANES, summed.shape[0]), 1)
    for k in range(blocks):
        hot = jnp.where(at == slots[:, k : k + 1], 1.0, 0.0).astype(BF16)
        rows = jnp.dot(hot, summed, preferred_element_type=F32)
        out_ref[LANES * k : LANES * (k + 1), :] = (rows * share[:, k : k + 1]).astype(BF16)


def spread(ids, probs, states, slots_at, first, features, out):
    tokens = ids.shape[1]
    fc = sum(state[0][0].shape[2] for state in states)
    args = [ids, probs]
    for state in states:
        args += [x[0] for x in state] + [x[1] for x in state]
    counts = [len(state) for state in states]
    used = len(args)
    in_specs = [pl.BlockSpec(x.shape, lambda i, d=x.ndim: (0,) * d) for x in args]
    earlier = [] if out is None else [out]
    return pl.pallas_call(
        lambda *refs: spread_body(counts, slots_at, *refs[:used], refs[-1]),
        grid=(1,),
        in_specs=in_specs + follows(earlier),
        out_specs=pl.BlockSpec((pl.Element(tokens), pl.Element(fc)), lambda i: (0, first * LANES)),
        out_shape=jax.ShapeDtypeStruct((tokens, features), BF16),
        input_output_aliases={used: 0} if earlier else {},
        compiler_params=params(24),
        cost_estimate=TINY,
        name="spread",
    )(*args, *earlier)


def follows(arrays):
    return [pl.BlockSpec(memory_space=pl.ANY)] * len(arrays)


def small(body, args, shapes, name, follow=()):
    vmem = pl.BlockSpec(memory_space=pltpu.VMEM)
    count = len(args)
    specs = [pl.BlockSpec(memory_space=pltpu.SMEM) if x.ndim == 1 else vmem for x in args]
    return pl.pallas_call(
        lambda *refs: body(refs[:count], refs[count + len(follow) :]),
        in_specs=specs + follows(follow),
        out_specs=[vmem] * len(shapes),
        out_shape=[jax.ShapeDtypeStruct(*x) for x in shapes],
        compiler_params=params(16),
        cost_estimate=TINY,
        name=name,
    )(*args, *follow)


def gather_near(own, orders):
    return {0: own} | {1 << bit: across(own, bit) for bit in orders[0]}


def cut_body(firsts, ins, outs):
    for h, at in enumerate(firsts):
        rows = outs[h].shape[0]
        outs[h][...] = ins[at][h * rows : (h + 1) * rows, :]
    for block, out in zip(ins, outs[2:]):
        out[...] = block[...]


def join_body(ins, outs):
    pieces = 2 * len(outs) // len(ins)
    for i in range(len(ins) // 2):
        whole = jnp.concatenate([ins[2 * i][...], ins[2 * i + 1][...]], axis=0)
        for k in range(pieces):
            out = outs[pieces * i + k]
            rows = out.shape[0]
            out[...] = whole[k * rows : (k + 1) * rows, :]


def cut(full, orders, follow, passed=False):
    rows, width = full[0].shape
    masks = [mask for mask in full if mask]
    firsts = [masks.index(1 << order[0]) for order in orders]
    shapes = [((rows // 2, width), BF16)] * 2 + [((rows, width), BF16)] * len(masks) * passed
    outs = small(
        lambda ins, outs: cut_body(firsts, ins, outs),
        [full[mask] for mask in masks],
        shapes,
        "cut",
        follow,
    )
    return outs[:2], full | dict(zip(masks, outs[2:]))


def gather_far(full, cuts, orders):
    half = full[0].shape[0] // len(orders)
    firsts = [1 << order[0] for order in orders]
    part = {}

    def get(mask, h):
        if (mask, h) in part:
            return part[mask, h]
        return cuts[h] if mask == firsts[h] else full[mask][h * half : (h + 1) * half]

    have = [[0, first] for first in firsts]
    for at in range(1, len(orders[0])):
        for h, order in enumerate(orders):
            bit = order[at]
            for mask in list(have[h]):
                there = mask | 1 << bit
                if there not in full:
                    part[there, h] = across(get(mask, h), bit)
                have[h].append(there)
    return part


def join(part, follow, pieces):
    masks = sorted({mask for mask, _ in part})
    halves = [part[mask, h] for mask in masks for h in range(2)]
    half, width = halves[0].shape
    shapes = [((2 * half // pieces, width), BF16)] * (pieces * len(masks))
    joined = small(join_body, halves, shapes, "join", follow)
    return {mask: joined[pieces * i : pieces * (i + 1)] for i, mask in enumerate(masks)}


def paired(pieces):
    return pieces | {
        mask | 1: [across(x, 0) for x in block] if isinstance(block, list) else across(block, 0)
        for mask, block in pieces.items()
    }


def turn_body(bits, scale, ins, outs):
    me_ref, ins = ins[0], ins[1:]
    count = len(bits)
    for h, bit in enumerate(bits):
        flip = (1 - 2 * ((me_ref[0] >> bit) & 1)).astype(F32)
        own = ins[2 * h][...].astype(F32)
        came = ins[2 * h + 1][...].astype(F32)
        value = came + own * flip
        if scale is not None:
            value = value * scale
            top = jnp.max(jnp.abs(own) + jnp.abs(came), axis=0, keepdims=True) * scale
            wide = top[:, :LANES]
            for k in range(1, top.shape[1] // LANES):
                wide = jnp.maximum(wide, top[:, k * LANES : (k + 1) * LANES])
            outs[count + h][...] = jnp.broadcast_to(wide, outs[count + h].shape)
        outs[h][...] = value.astype(BF16)


def turn(me, blocks, came, bits, follow=(), scale=None):
    args = [me] + [x for pair in zip(blocks, came) for x in pair]
    shapes = [(x.shape, BF16) for x in blocks]
    if scale is not None:
        shapes += [((8, LANES), F32)] * len(blocks)
    return small(
        lambda ins, outs: turn_body(bits, scale, ins, outs), args, shapes, "turn", follow
    )


def largest(top_in, tops, lasts):
    bits = range(lax.axis_size("tensor").bit_length() - 1)
    values = jnp.concatenate([top_in, *tops], axis=0)
    for bit in bits:
        if bit not in lasts:
            values = jnp.maximum(values, across(values, bit))
    n = top_in.shape[0]
    top_in, first, second = values[:n], values[n : 2 * n], values[2 * n :]
    if lasts[0] != lasts[1]:
        pair = jnp.concatenate([top_in, second], axis=0)
        came_first, came_pair = across(first, lasts[1]), across(pair, lasts[0])
        first = jnp.maximum(first, came_first)
        pair = jnp.maximum(pair, came_pair)
        top_in, second = pair[:n], pair[n:]
    values = jnp.concatenate([top_in, jnp.maximum(first, second)], axis=0)
    blocks = lax.axis_size("dp")
    far = 1
    while far < blocks:
        pairs = [(r, r ^ far) for r in range(blocks)]
        values = jnp.maximum(values, lax.ppermute(values, "dp", pairs))
        far *= 2
    return values


def on_device(tokens, expert_ids, gate_probs, gate_weight, up_weight, down_weight):
    count = lax.axis_size("tensor")
    bits = count.bit_length() - 1
    outer = list(range(1, bits))
    orders = [outer, outer[::-1]]
    me = lax.axis_index("tensor")
    me_arr = me.astype(jnp.int32).reshape(1)
    ids, probs = expert_ids.T, gate_probs.T
    rows = CAP // ROW_CHUNKS
    half = rows // 2
    scale = 1.0 / math.sqrt(gate_weight.shape[1] * count)
    stages = [[order[at] for order in orders] for at in range(len(outer))]
    early_bit = stages[-1][1]

    def send(blocks, bits):
        return [across(x, bit) for x, bit in zip(blocks, bits)]

    def start_turn(halves, follow=()):
        blocks = turn(me_arr, halves, send(halves, [0, 0]), [0, 0], follow)
        return blocks, send(blocks, stages[0])

    def go_on(blocks, came, at, follow=()):
        blocks = turn(me_arr, blocks, came, stages[at], follow)
        return blocks, send(blocks, stages[at + 1])

    def end_turn(blocks, came, follow=()):
        made = turn(me_arr, blocks, came, stages[-1], follow, scale)
        return made[: len(blocks)], made[len(blocks) :]

    own_a, top_a = pick_rows(ids, tokens, 0, rows, [me_arr])
    near_a = gather_near(own_a, orders)
    weights = (me_arr, gate_weight, up_weight)
    cuts_a, near_a = cut(near_a, orders, [])
    own_b, top_b = pick_rows(ids, tokens, rows, rows, cuts_a)
    top_in = jnp.maximum(top_a, top_b)
    top_in = jnp.maximum(top_in, across(top_in, early_bit))
    far_a = join(gather_far(near_a, cuts_a, orders), [own_b, top_in], 1)
    near_b = gather_near(own_b, orders)
    parts_a = paired(near_a | far_a)
    parts_a = [parts_a[mask] for mask in range(count)]
    first_a = expand(parts_a, rows, *weights)
    local_a = expand(parts_a, rows, *weights, *first_a)
    cuts_b, near_b = cut(near_b, orders, local_a, True)
    parts_b = paired(near_b)
    theirs_b = [block for mask, block in parts_b.items() if mask & 1]
    blocks_a, came_a = start_turn(local_a, theirs_b)
    total_b = multiply(parts_b, *weights, follow=blocks_a)
    far_b = join(gather_far(near_b, cuts_b, orders), [total_b], 3)
    for at in range(len(outer) - 1):
        blocks_a, came_a = go_on(blocks_a, came_a, at, [total_b])
    local_b = multiply(paired(far_b), *weights, total_b, True, blocks_a)
    turned_a, rot_a = end_turn(blocks_a, came_a, local_b)
    blocks_b, came_b = start_turn(local_b, rot_a)
    for at in range(len(outer) - 1):
        blocks_b, came_b = go_on(blocks_b, came_b, at)
    turned_b, rot_b = end_turn(blocks_b, came_b)
    rotated = turned_a + turned_b

    peaks = largest(top_in, [jnp.maximum(x, y) for x, y in zip(rot_a, rot_b)], stages[-1])
    tops = pl.pallas_call(
        peaks_body,
        out_specs=pl.BlockSpec(memory_space=pltpu.SMEM),
        out_shape=jax.ShapeDtypeStruct((2,), F32),
        name="peaks",
    )(peaks)
    units = tokens.shape[1] // LANES
    sizes = chunks_of(units)
    firsts = [sum(sizes[:i]) for i in range(len(sizes))]
    total = len(sizes)
    products, begun, ended, out, last, clipped = {}, {}, {}, None, [], None
    for step, chunk in sums_order(total):
        if step == "product":
            fresh = [peaks, *rotated] if chunk == 0 else []
            made = down(clipped, down_weight, me_arr, sizes[chunk], firsts[chunk], last, fresh)
            if fresh:
                clipped, made = made[0], made[1:]
            products[chunk] = made
            last = [products[chunk][1]]
        elif step == "begin":
            other, same = products[chunk]
            begun[chunk] = fold_cores(same, across(other, 0), stages[0], last)
            last = [keep for keep, _, _ in begun[chunk]]
        elif step == "finish":
            ahead = [c for c in products if c not in begun]
            passed = [products[c][0] for c in ahead]
            held = chunk == 0 and total > 2
            stacked = [x for _, x, _ in ended[0]] if chunk == 1 and total > 2 else []
            ended[chunk], passed = finish(
                begun[chunk], stages, last, passed, stacked, not held
            )
            if stacked:
                ended[0] = [
                    (keep, both, left)
                    for (keep, _, left), (_, both, _) in zip(ended[0], ended[1])
                ]
            for c, other in zip(ahead, passed):
                products[c] = (other, products[c][1])
            last = [keep for keep, _, _ in ended[chunk]]
        else:
            chunks = [0, 1] if chunk == 0 and total > 2 else [chunk]
            slots_at = [0 if c == 0 else ended[c][0][1].shape[0] - 1 for c in chunks]
            out = spread(
                ids,
                probs,
                [ended[c] for c in chunks],
                slots_at,
                firsts[chunk],
                tokens.shape[1],
                out,
            )
    return out, tops


def chunks_of(units):
    return [2] * (units // 2) + [1] * (units % 2)


def sums_order(total):
    order = [("product", 0)]
    for chunk in range(total):
        if chunk + 1 < total:
            order.append(("product", chunk + 1))
        order.append(("begin", chunk))
        if chunk > 0:
            order.append(("finish", chunk - 1))
    order.append(("finish", total - 1))
    return order + [("spread", c) for c in range(total) if c != 1 or total < 3]


def peaks_body(values_ref, out_ref):
    out_ref[0] = jnp.max(values_ref[:8, :])
    out_ref[1] = jnp.max(values_ref[8:, :])


def fold_body(plan, passed, ins, outs):
    for i in range(passed):
        outs[len(plan) + i][...] = ins[len(ins) - passed + i][...]
    for out, (slots, low) in zip(outs, plan):
        rows = out.shape[1]
        for slot, terms in enumerate(slots):
            total = 0.0
            for at, i in terms:
                total = total + ins[at][i, low : low + rows, :].astype(F32)
            out[slot] = total.astype(BF16)


def fold(args, terms, masks, lows, rows, bits, follow, passed=(), stacked=(), sent=True):
    plan, shapes, lefts = [], [], []
    width = args[0].shape[2]
    for h, bit in enumerate(bits):
        for side in (0, 1):
            chosen = [m for m in masks[h] if m >> bit & 1 == side]
            slots = [terms[h][m] for m in chosen]
            if side and stacked:
                slots = [((len(args) + h, i),) for i in range(stacked[h].shape[0])] + slots
            plan.append((slots, lows[h]))
            shapes.append(((len(slots), rows, width), BF16))
        lefts.append([m for m in masks[h] if not m >> bit & 1])
    shapes += [(x.shape, x.dtype) for x in passed]
    made = small(
        lambda ins, outs: fold_body(plan, len(passed), ins, outs),
        [*args, *stacked, *passed],
        shapes,
        "fold",
        follow,
    )
    state = [
        (made[2 * h], across(made[2 * h + 1], bit) if sent else made[2 * h + 1], lefts[h])
        for h, bit in enumerate(bits)
    ]
    return state, made[len(plan) :]


def fold_cores(same, came, bits, follow):
    half = same.shape[1] // 2
    masks = [2 * i for i in range(same.shape[0])]
    terms = {m: ((0, i), (1, i)) for i, m in enumerate(masks)}
    return fold([same, came], [terms] * 2, [masks] * 2, [0, half], half, bits, follow)[0]


def finish(state, stages, follow, passed=(), stacked=(), sent=True):
    for bits in stages[1:]:
        args = [x for keep, recv, _ in state for x in (keep, recv)]
        masks = [left for _, _, left in state]
        terms = [
            {m: ((2 * h, i), (2 * h + 1, i)) for i, m in enumerate(left)}
            for h, left in enumerate(masks)
        ]
        last = bits is stages[-1]
        state, passed = fold(
            args,
            terms,
            masks,
            [0, 0],
            args[0].shape[1],
            bits,
            follow,
            passed,
            stacked if last else (),
            sent or not last,
        )
    return state, passed


def solution(mesh):
    in_specs = (
        P("dp", "tensor"),
        P("dp", None),
        P("dp", None),
        P(None, "tensor"),
        P(None, "tensor"),
        P("tensor", None),
    )
    out_specs = (P("dp", "tensor"), P())
    return jax.shard_map(
        on_device, mesh=mesh, in_specs=in_specs, out_specs=out_specs, check_vma=False
    )
```
